32 devices in a mesh: shard: 4 (over z), ctx: 4 (over y, core), tp: 2 (over x).
Axes of the slice: x: 2, y: 2, z: 4, core: 2. Of those that a mesh axis runs over, the one named last changes fastest.
Arguments:
- inputs: bfloat16 [8, 2048, 1024], P('shard', 'ctx', 'tp'), may hold values from -6 to 6
- ln1_gain: bfloat16 [1024], replicated, may hold values from 0.099609375 to 1.8984375
- ln1_bias: bfloat16 [1024], replicated, may hold values from -3 to 3
- w_qkv: bfloat16 [1024, 3, 1024], P('shard', None, 'tp'), may hold values from -0.1875 to 0.1875
- b_qkv: bfloat16 [3, 1024], P(None, 'tp'), may hold values from -3 to 3
- w_out: bfloat16 [1024, 1024], P('tp', 'shard'), may hold values from -3 to 3
- b_out: bfloat16 [1024], P('tp'), may hold values from -3 to 3
- ln2_gain: bfloat16 [1024], replicated, may hold values from 0.099609375 to 1.8984375
- ln2_bias: bfloat16 [1024], replicated, may hold values from -3 to 3
- w_in: bfloat16 [1024, 4096], P('shard', 'tp'), may hold values from -0.1875 to 0.1875
- b_in: bfloat16 [4096], P('tp'), may hold values from -3 to 3
- w_back: bfloat16 [4096, 1024], P('tp', 'shard'), may hold values from -0.1875 to 0.1875
- b_back: bfloat16 [1024], P('tp'), may hold values from -3 to 3
- cotangent: bfloat16 [8, 2048, 1024], P('shard', 'ctx', 'tp'), may hold values from -6 to 6
Outputs:
- output: bfloat16 [8, 2048, 1024], P('shard', 'ctx', 'tp')
- input_grad: float32 [8, 2048, 1024], P('shard', 'ctx', 'tp')
- grad_ln1_gain: float32 [1024], replicated
- grad_ln1_bias: float32 [1024], replicated
- grad_w_qkv: float32 [1024, 3, 1024], P('shard', None, 'tp')
- grad_b_qkv: float32 [3, 1024], P(None, 'tp')
- grad_w_out: float32 [1024, 1024], P('tp', 'shard')
- grad_b_out: float32 [1024], P('tp')
- grad_ln2_gain: float32 [1024], replicated
- grad_ln2_bias: float32 [1024], replicated
- grad_w_in: float32 [1024, 4096], P('shard', 'tp')
- grad_b_in: float32 [4096], P('tp')
- grad_w_back: float32 [4096, 1024], P('tp', 'shard')
- grad_b_back: float32 [1024], P('tp')
The draws below stay inside these ranges and needn't reach their ends.
All inputs are finite; a program needn't handle non-finite values.
Results may differ from the reference program's by a relative error of at most 0.023.
Values may be sent and summed in bfloat16 or wider, within the bound.
A program may use at most 192 MiB of HBM per device.

```python
import math
import jax
import jax.numpy as jnp
from jax import lax

D = 1024
HEADS = 16
HEAD_DIM = 64
FF = 4096
GH = 16
GW = 16
LEN = 2048
CLIPS = 8


def steps_of(stream_key, dims, cuts, least, top_value):
    def one(dim, blocks):
        heights = jax.random.uniform(jax.random.fold_in(jax.random.fold_in(stream_key, 6), dim), (blocks,), jnp.float32, least / len(cuts), top_value / len(cuts))
        return jnp.repeat(jnp.exp(heights), dims[dim] // blocks).reshape((-1,) + (1,) * (len(dims) - dim - 1))

    level = one(*cuts[0])
    for cut in cuts[1:]:
        level = level * one(*cut)
    return level


def noise(stream_key, extent, scale, bound, cuts=(), kind=jnp.bfloat16):
    entries = jax.random.normal(stream_key, extent, jnp.float32) * scale
    if len(cuts) > 0:
        entries = steps_of(stream_key, extent, cuts, -0.22, 0.18) * entries
    return jnp.clip(entries, min=-bound, max=bound).astype(kind)


def setup_inputs(seed: int = 0) -> dict:
    arg_keys = jax.random.split(jax.random.key(seed), 15)
    return {
        "inputs": noise(arg_keys[0], (CLIPS, LEN, D), 1.0, 6.0, ((0, 4), (1, 4), (2, 2))),
        "ln1_gain": jnp.clip(1.0 + 0.18 * jax.random.normal(arg_keys[1], (D,), jnp.float32), 0.099609375, 1.8984375).astype(jnp.bfloat16),
        "ln1_bias": noise(arg_keys[2], (D,), 0.3, 3.0),
        "w_qkv": noise(arg_keys[3], (D, 3, D), D ** -0.5, 0.1875, ((0, 4), (2, 2))),
        "b_qkv": noise(arg_keys[4], (3, D), 0.3, 3.0, ((1, 2),)),
        "w_out": noise(arg_keys[5], (D, D), (max(D // 256, 1)) ** -0.5, 3.0, ((0, 2), (1, 4))),
        "b_out": noise(arg_keys[6], (D,), 0.3, 3.0, ((0, 2),)),
        "ln2_gain": jnp.clip(1.0 + 0.18 * jax.random.normal(arg_keys[7], (D,), jnp.float32), 0.099609375, 1.8984375).astype(jnp.bfloat16),
        "ln2_bias": noise(arg_keys[8], (D,), 0.3, 3.0),
        "w_in": noise(arg_keys[9], (D, FF), D ** -0.5, 0.1875, ((0, 4), (1, 2))),
        "b_in": noise(arg_keys[10], (FF,), 0.3, 3.0, ((0, 2),)),
        "w_back": noise(arg_keys[11], (FF, D), (FF // 4) ** -0.5, 0.1875, ((0, 2), (1, 4))),
        "b_back": noise(arg_keys[12], (D,), 0.3, 3.0, ((0, 2),)),
        "cotangent": noise(arg_keys[13], (CLIPS, LEN, D), 1.0, 6.0, ((0, 4), (1, 4), (2, 2))),
    }


EPSILON = 1e-06
HIGHEST = lax.Precision.HIGHEST

@jax.custom_vjp
def low(v):
    return lax.optimization_barrier(v.astype(jnp.bfloat16)).astype(jnp.float32)

@jax.custom_vjp
def low_back(v):
    return v

def low_keep(v):
    return (low(v), None)

def low_pass(kept, grad):
    return (grad,)

def back_keep(v):
    return (v, None)

def back_low(kept, grad):
    return (low(grad),)
low.defvjp(low_keep, low_pass)
low_back.defvjp(back_keep, back_low)

def rotary_tables(first_row, row_count):
    segment = 2 * (HEAD_DIM // 3 // 2)
    halfway = segment // 2
    places = first_row + jnp.arange(row_count, dtype=jnp.int32)
    frames = places // (GH * GW)
    rows_at = places // GW % GH
    cols_at = places % GW
    column = jnp.arange(HEAD_DIM, dtype=jnp.int32)
    segment_of = column // segment
    within = column % segment
    frequency = jnp.power(10000.0, -(within % halfway).astype(jnp.float32) / halfway)
    position = jnp.where(segment_of[None, :] == 0, frames[:, None], jnp.where(segment_of[None, :] == 1, rows_at[:, None], cols_at[:, None]))
    angles = position.astype(jnp.float32) * frequency[None, :]
    active = (column < 3 * segment)[None, :]
    cosines = jnp.where(active, jnp.cos(angles), 1.0)
    sine_table = jnp.where(active, jnp.where((within < halfway)[None, :], -jnp.sin(angles), jnp.sin(angles)), 0.0)
    return (cosines, sine_table)

def partner(tensor):
    segment = 2 * (HEAD_DIM // 3 // 2)
    halfway = segment // 2
    pieces = []
    for number in range(3):
        offset = number * segment
        pieces.append(tensor[..., offset + halfway:offset + segment])
        pieces.append(tensor[..., offset:offset + halfway])
    pieces.append(tensor[..., 3 * segment:])
    return jnp.concatenate(pieces, axis=-1)

def rotate(tensor, cosines, sine_table):
    return tensor * cosines + partner(tensor) * sine_table

def layer_norm(tensor, gain, shift):
    center = tensor - lax.optimization_barrier(jnp.mean(tensor, axis=-1, keepdims=True))
    spread = lax.optimization_barrier(jnp.mean(center * center, axis=-1, keepdims=True))
    return center * lax.rsqrt(spread + EPSILON) * gain + shift

def attend(queries, key_rows, values):
    length = queries.shape[0]
    block_size = math.gcd(length, 512)
    score_scale = HEAD_DIM ** (-0.5)
    blocks = queries.reshape(length // block_size, block_size, HEADS, HEAD_DIM)

    def one_block(query_block):
        scores = low_back(jnp.einsum('qhd,khd->hqk', query_block, key_rows, precision=HIGHEST) * score_scale)
        prob_block = low(jax.nn.softmax(scores, axis=-1))
        return jnp.einsum('hqk,khd->qhd', prob_block, values, precision=HIGHEST)
    return lax.map(jax.checkpoint(one_block), blocks).reshape(length, HEADS, HEAD_DIM)

def vit_layer(tokens, params):
    gain_one, shift_one, w_qkv, b_qkv, w_out, b_out, gain_two, shift_two, w_in, b_in, w_back, b_back = params
    length = tokens.shape[0]
    cosines, sine_table = rotary_tables(0, length)
    cosines = cosines[:, None, :]
    sine_table = sine_table[:, None, :]
    normed = low(layer_norm(tokens, gain_one, shift_one))
    joined = low_back(jnp.einsum('td,dkc->tkc', normed, w_qkv, precision=HIGHEST) + b_qkv)
    shaped = joined.reshape(length, 3, HEADS, HEAD_DIM)
    queries = low(rotate(shaped[:, 0], cosines, sine_table))
    key_rows = low(rotate(shaped[:, 1], cosines, sine_table))
    values = low(shaped[:, 2])
    mixed_heads = low(low_back(attend(queries, key_rows, values))).reshape(length, D)
    branch = low_back(jnp.dot(mixed_heads, w_out, precision=HIGHEST) + b_out)
    middle = tokens + branch
    second = low(layer_norm(middle, gain_two, shift_two))
    inner_pre = low_back(jnp.dot(second, w_in, precision=HIGHEST) + b_in)
    active = low(jax.nn.gelu(inner_pre, approximate=False))
    return middle + jnp.dot(active, w_back, precision=HIGHEST) + b_back

def reference(inputs, ln1_gain, ln1_bias, w_qkv, b_qkv, w_out, b_out, ln2_gain, ln2_bias, w_in, b_in, w_back, b_back, cotangent):
    params = tuple((parameter.astype(jnp.float32) for parameter in (ln1_gain, ln1_bias, w_qkv, b_qkv, w_out, b_out, ln2_gain, ln2_bias, w_in, b_in, w_back, b_back)))

    def one_clip(totals, clip_pair):
        clip_rows, grad_out = clip_pair
        result, pullback = jax.vjp(vit_layer, clip_rows.astype(jnp.float32), params)
        grad_clip, grad_params = pullback(grad_out.astype(jnp.float32))
        totals = jax.tree.map(lambda running, latest: running + latest, totals, grad_params)
        return (totals, (result.astype(jnp.bfloat16), grad_clip))
    zero_grads = jax.tree.map(jnp.zeros_like, params)
    totals, (output, input_grad) = lax.scan(one_clip, zero_grads, (inputs, cotangent))
    return (output, input_grad.astype(jnp.float32), totals[0], totals[1], totals[2], totals[3], totals[4], totals[5], totals[6], totals[7], totals[8], totals[9], totals[10], totals[11])
```

```python
import functools
import math

import jax
import jax.numpy as jnp
from jax import lax
from jax.experimental import pallas as pl
from jax.experimental.pallas import tpu as pltpu
from jax.sharding import PartitionSpec as P

HEAD_DIM = 64
GH = 16
GW = 16


EPSILON = 1e-06
NEG_LARGE = -1e30


def rotary_tables(first_row, row_count):
    segment = 2 * (HEAD_DIM // 3 // 2)
    halfway = segment // 2
    places = first_row + jnp.arange(row_count, dtype=jnp.int32)
    frames = places // (GH * GW)
    rows_at = places // GW % GH
    cols_at = places % GW
    column = jnp.arange(HEAD_DIM, dtype=jnp.int32)
    segment_of = column // segment
    within = column % segment
    frequency = jnp.power(10000.0, -(within % halfway).astype(jnp.float32) / halfway)
    position = jnp.where(
        segment_of[None, :] == 0,
        frames[:, None],
        jnp.where(segment_of[None, :] == 1, rows_at[:, None], cols_at[:, None]),
    )
    angles = position.astype(jnp.float32) * frequency[None, :]
    active = (column < 3 * segment)[None, :]
    cosines = jnp.where(active, jnp.cos(angles), 1.0)
    sine_table = jnp.where(
        active, jnp.where((within < halfway)[None, :], -jnp.sin(angles), jnp.sin(angles)), 0.0
    )
    return (cosines, sine_table)


def partner(tensor):
    segment = 2 * (HEAD_DIM // 3 // 2)
    halfway = segment // 2
    pieces = []
    for number in range(3):
        offset = number * segment
        pieces.append(tensor[..., offset + halfway : offset + segment])
        pieces.append(tensor[..., offset : offset + halfway])
    pieces.append(tensor[..., 3 * segment :])
    return jnp.concatenate(pieces, axis=-1)


def rotate(tensor, cosines, sine_table):
    return tensor * cosines + partner(tensor) * sine_table


def rotate_back(gradient, cosines, sine_table):
    return gradient * cosines + partner(gradient * sine_table)


def normalize(tensor, gain, shift):
    center = tensor - jnp.mean(tensor, axis=-1, keepdims=True)
    spread = jnp.mean(center * center, axis=-1, keepdims=True)
    inv_std = lax.rsqrt(spread + EPSILON)
    scaled = center * inv_std
    return (scaled * gain + shift, scaled, inv_std)


def norm_back(grad_out, scaled, inv_std, gain):
    grad_scaled = grad_out * gain
    mean_one = jnp.mean(grad_scaled, axis=-1, keepdims=True)
    mean_two = jnp.mean(grad_scaled * scaled, axis=-1, keepdims=True)
    return inv_std * (grad_scaled - mean_one - scaled * mean_two)


def tp_rows(sharded):
    return lax.all_gather(sharded, "tp", axis=2, tiled=True)


def tensor_sum(summand):
    return lax.psum_scatter(
        summand.astype(jnp.bfloat16), "tp", scatter_dimension=2, tiled=True
    ).astype(jnp.float32)


def back_total(summand):
    return lax.psum(summand.astype(jnp.bfloat16), "tp").astype(jnp.float32)


def fetch_weights(w_qkv, w_out, w_in, w_back):
    return (
        lax.all_gather(w_qkv, "shard", axis=0, tiled=True),
        lax.all_gather(w_out, "shard", axis=1, tiled=True),
        lax.all_gather(w_in, "shard", axis=0, tiled=True),
        lax.all_gather(w_back, "shard", axis=1, tiled=True),
    )


def forward(inputs, params, weights, cosines, sine_table):
    gain_one, shift_one, b_qkv, b_out, gain_two, shift_two, b_in, b_back = params
    w_qkv_all, w_out_all, w_in_all, w_back_all = weights
    clip_count, row_count, width_local = inputs.shape
    heads_local = width_local // HEAD_DIM
    score_scale = HEAD_DIM ** (-0.5)
    tokens = tp_rows(inputs).astype(jnp.float32)
    normed, scaled_one, inv_one = normalize(tokens, gain_one, shift_one)
    normed_low = normed.astype(jnp.bfloat16)
    joined = (
        jnp.einsum("csd,dkh->cskh", normed_low, w_qkv_all, preferred_element_type=jnp.float32)
        + b_qkv
    )
    shaped = joined.reshape(clip_count, row_count, 3, heads_local, HEAD_DIM)
    queries = rotate(shaped[:, :, 0], cosines, sine_table).astype(jnp.bfloat16)
    key_rows = rotate(shaped[:, :, 1], cosines, sine_table).astype(jnp.bfloat16)
    values = shaped[:, :, 2].astype(jnp.bfloat16)
    key_flat = key_rows.reshape(clip_count, row_count, width_local)
    value_flat = values.reshape(clip_count, row_count, width_local)

    def absorb_block(running, block_pair):
        row_max, row_sum, weighted = running
        key_piece, value_piece = block_pair
        scores = (
            jnp.einsum("cqhd,ckhd->chqk", queries, key_piece, preferred_element_type=jnp.float32)
            * score_scale
        )
        next_max = jnp.maximum(row_max, jnp.max(scores, axis=-1))
        factor = jnp.exp(row_max - next_max)
        weights_now = jnp.exp(scores - next_max[..., None])
        row_sum = row_sum * factor + jnp.sum(weights_now, axis=-1)
        weighted = weighted * factor[..., None] + jnp.einsum(
            "chqk,ckhd->chqd",
            weights_now.astype(jnp.bfloat16),
            value_piece,
            preferred_element_type=jnp.float32,
        )
        return ((next_max, row_sum, weighted), None)

    initial = (
        jnp.full((clip_count, heads_local, row_count), NEG_LARGE, jnp.float32),
        jnp.zeros((clip_count, heads_local, row_count), jnp.float32),
        jnp.zeros((clip_count, heads_local, row_count, HEAD_DIM), jnp.float32),
    )
    running = initial
    pieces = (
        lax.all_gather(key_flat, "ctx", axis=1, tiled=True),
        lax.all_gather(value_flat, "ctx", axis=1, tiled=True),
    )
    piece_rows = pieces[0].shape[1]
    block_size = math.gcd(piece_rows, 512)
    block_count = piece_rows // block_size
    key_blocks = jnp.moveaxis(
        pieces[0].reshape(clip_count, block_count, block_size, heads_local, HEAD_DIM), 1, 0
    )
    value_blocks = jnp.moveaxis(
        pieces[1].reshape(clip_count, block_count, block_size, heads_local, HEAD_DIM), 1, 0
    )
    running, unused = lax.scan(absorb_block, running, (key_blocks, value_blocks))
    row_max, row_sum, weighted = running
    log_total = row_max + jnp.log(row_sum)
    mixed_heads = jnp.transpose(weighted / row_sum[..., None], (0, 2, 1, 3))
    mixed_low = mixed_heads.reshape(clip_count, row_count, width_local).astype(jnp.bfloat16)
    branch = tensor_sum(
        jnp.einsum("csh,hd->csd", mixed_low, w_out_all, preferred_element_type=jnp.float32)
    )
    middle = inputs.astype(jnp.float32) + branch + b_out
    middle_all = lax.all_gather(middle.astype(jnp.bfloat16), "tp", axis=2, tiled=True).astype(
        middle.dtype
    )
    second, scaled_two, inv_two = normalize(middle_all, gain_two, shift_two)
    second_low = second.astype(jnp.bfloat16)
    inner_pre = (
        jnp.einsum("csd,df->csf", second_low, w_in_all, preferred_element_type=jnp.float32) + b_in
    )
    active_low = jax.nn.gelu(inner_pre, approximate=False).astype(jnp.bfloat16)
    return {
        "normed_low": normed_low,
        "scaled_one": scaled_one,
        "inv_one": inv_one,
        "queries": queries,
        "key_flat": key_flat,
        "value_flat": value_flat,
        "mixed_heads": mixed_heads,
        "mixed_low": mixed_low,
        "log_total": log_total,
        "middle": middle,
        "scaled_two": scaled_two,
        "inv_two": inv_two,
        "second_low": second_low,
        "inner_pre": inner_pre,
        "active_low": active_low,
    }


def per_device(
    inputs,
    ln1_gain,
    ln1_bias,
    w_qkv,
    b_qkv,
    w_out,
    b_out,
    ln2_gain,
    ln2_bias,
    w_in,
    b_in,
    w_back,
    b_back,
    cotangent,
):
    params = tuple(
        (
            parameter.astype(jnp.float32)
            for parameter in (ln1_gain, ln1_bias, b_qkv, b_out, ln2_gain, ln2_bias, b_in, b_back)
        )
    )
    gain_one = params[0]
    gain_two = params[4]
    clip_count, row_count, width_local = inputs.shape
    heads_local = width_local // HEAD_DIM
    score_scale = HEAD_DIM ** (-0.5)
    tp_index = lax.axis_index("tp")
    share_start = tp_index * width_local
    cosines, sine_table = rotary_tables(lax.axis_index("ctx") * row_count, row_count)
    cosines = cosines[:, None, :]
    sine_table = sine_table[:, None, :]
    weights = fetch_weights(w_qkv, w_out, w_in, w_back)
    stored_acts = forward(inputs, params, weights, cosines, sine_table)
    output = (
        stored_acts["middle"]
        + tensor_sum(
            jnp.einsum(
                "csf,fd->csd",
                stored_acts["active_low"],
                weights[3],
                preferred_element_type=jnp.float32,
            )
        )
        + params[7]
    ).astype(jnp.bfloat16)
    weights = fetch_weights(w_qkv, w_out, w_in, w_back)
    stored_acts = forward(inputs, params, weights, cosines, sine_table)
    w_qkv_all, w_out_all, w_in_all, w_back_all = weights
    grad_low = tp_rows(cotangent)
    grad_full = grad_low.astype(jnp.float32)
    grad_active = jnp.einsum(
        "csd,fd->csf", grad_low, w_back_all, preferred_element_type=jnp.float32
    )
    unused, gelu_back = jax.vjp(
        lambda argument: jax.nn.gelu(argument, approximate=False), stored_acts["inner_pre"]
    )
    grad_inner = gelu_back(grad_active)[0].astype(jnp.bfloat16)
    grad_w_back = jnp.einsum(
        "csf,csd->fd", stored_acts["active_low"], grad_low, preferred_element_type=jnp.float32
    )
    grad_b_back = jnp.sum(cotangent.astype(jnp.float32), axis=(0, 1))
    grad_w_in = jnp.einsum(
        "csd,csf->df", stored_acts["second_low"], grad_inner, preferred_element_type=jnp.float32
    )
    grad_b_in = jnp.sum(grad_inner.astype(jnp.float32), axis=(0, 1))
    grad_second = back_total(
        jnp.einsum("csf,df->csd", grad_inner, w_in_all, preferred_element_type=jnp.float32)
    )
    grad_gain_two = jnp.sum(grad_second * stored_acts["scaled_two"], axis=(0, 1))
    grad_shift_two = jnp.sum(grad_second, axis=(0, 1))
    grad_middle = grad_full + norm_back(
        grad_second, stored_acts["scaled_two"], stored_acts["inv_two"], gain_two
    )
    grad_branch = grad_middle.astype(jnp.bfloat16)
    grad_b_out = lax.dynamic_slice_in_dim(
        jnp.sum(grad_branch.astype(jnp.float32), axis=(0, 1)), share_start, width_local
    )
    grad_w_out = jnp.einsum(
        "csh,csd->hd", stored_acts["mixed_low"], grad_branch, preferred_element_type=jnp.float32
    )
    grad_mixed = jnp.einsum(
        "csd,hd->csh", grad_branch, w_out_all, preferred_element_type=jnp.float32
    ).astype(jnp.bfloat16)
    key_all, value_all = (
        lax.all_gather(stored_acts["key_flat"], "ctx", axis=1, tiled=True),
        lax.all_gather(stored_acts["value_flat"], "ctx", axis=1, tiled=True),
    )
    length = key_all.shape[1]
    block_size = math.gcd(length, 512)
    block_count = length // block_size
    grad_heads = grad_mixed.reshape(clip_count, row_count, heads_local, HEAD_DIM)
    queries = stored_acts["queries"]
    log_total = stored_acts["log_total"]
    row_delta = jnp.einsum(
        "cqhd,chqd->chq",
        grad_heads.astype(jnp.float32),
        jnp.transpose(stored_acts["mixed_heads"], (0, 2, 1, 3)),
    )
    key_blocks = jnp.moveaxis(
        key_all.reshape(clip_count, block_count, block_size, heads_local, HEAD_DIM), 1, 0
    )
    value_blocks = jnp.moveaxis(
        value_all.reshape(clip_count, block_count, block_size, heads_local, HEAD_DIM), 1, 0
    )

    def key_step(grad_query, block_pair):
        key_piece, value_piece = block_pair
        scores = (
            jnp.einsum("cqhd,ckhd->chqk", queries, key_piece, preferred_element_type=jnp.float32)
            * score_scale
        )
        prob_block = jnp.exp(scores - log_total[..., None])
        grad_probs = jnp.einsum(
            "cqhd,ckhd->chqk", grad_heads, value_piece, preferred_element_type=jnp.float32
        )
        grad_scores = (prob_block * (grad_probs - row_delta[..., None])).astype(jnp.bfloat16)
        grad_query = grad_query + jnp.einsum(
            "chqk,ckhd->cqhd", grad_scores, key_piece, preferred_element_type=jnp.float32
        )
        grad_key = (
            jnp.einsum("chqk,cqhd->ckhd", grad_scores, queries, preferred_element_type=jnp.float32)
            * score_scale
        )
        grad_value = jnp.einsum(
            "chqk,cqhd->ckhd",
            prob_block.astype(jnp.bfloat16),
            grad_heads,
            preferred_element_type=jnp.float32,
        )
        return (grad_query, (grad_key, grad_value))

    grad_query, (key_terms, value_terms) = lax.scan(
        key_step,
        jnp.zeros((clip_count, row_count, heads_local, HEAD_DIM), jnp.float32),
        (key_blocks, value_blocks),
    )
    grad_query = grad_query * score_scale
    key_terms = jnp.moveaxis(key_terms, 0, 1).reshape(clip_count, length, width_local)
    value_terms = jnp.moveaxis(value_terms, 0, 1).reshape(clip_count, length, width_local)
    grad_keys, grad_values = (
        lax.psum_scatter(
            key_terms.astype(jnp.bfloat16), "ctx", scatter_dimension=1, tiled=True
        ).astype(jnp.float32),
        lax.psum_scatter(
            value_terms.astype(jnp.bfloat16), "ctx", scatter_dimension=1, tiled=True
        ).astype(jnp.float32),
    )
    grad_q_pre = rotate_back(grad_query, cosines, sine_table).reshape(
        clip_count, row_count, width_local
    )
    grad_k_pre = rotate_back(
        grad_keys.reshape(clip_count, row_count, heads_local, HEAD_DIM), cosines, sine_table
    ).reshape(clip_count, row_count, width_local)
    grad_joined = jnp.stack([grad_q_pre, grad_k_pre, grad_values], axis=2).astype(jnp.bfloat16)
    grad_w_qkv = jnp.einsum(
        "csd,cskh->dkh", stored_acts["normed_low"], grad_joined, preferred_element_type=jnp.float32
    )
    grad_b_qkv = jnp.sum(grad_joined.astype(jnp.float32), axis=(0, 1))
    normed_term = jnp.einsum(
        "cskh,dkh->csd", grad_joined, w_qkv_all, preferred_element_type=jnp.float32
    )
    grad_normed = back_total(normed_term)
    grad_gain_one = jnp.sum(grad_normed * stored_acts["scaled_one"], axis=(0, 1))
    grad_shift_one = jnp.sum(grad_normed, axis=(0, 1))
    grad_tokens = grad_middle + norm_back(
        grad_normed, stored_acts["scaled_one"], stored_acts["inv_one"], gain_one
    )
    input_grad = lax.dynamic_slice_in_dim(grad_tokens, share_start, width_local, axis=2)
    summed = (
        lax.psum(grad_w_qkv.astype(jnp.bfloat16), "ctx").astype(jnp.float32),
        lax.psum(grad_w_out.astype(jnp.bfloat16), "ctx").astype(jnp.float32),
        lax.psum(grad_w_in.astype(jnp.bfloat16), "ctx").astype(jnp.float32),
        lax.psum(grad_w_back.astype(jnp.bfloat16), "ctx").astype(jnp.float32),
    )
    owned_grads = (
        lax.psum_scatter(
            summed[0].astype(jnp.bfloat16), "shard", scatter_dimension=0, tiled=True
        ).astype(jnp.float32),
        lax.psum_scatter(
            summed[1].astype(jnp.bfloat16), "shard", scatter_dimension=1, tiled=True
        ).astype(jnp.float32),
        lax.psum_scatter(
            summed[2].astype(jnp.bfloat16), "shard", scatter_dimension=0, tiled=True
        ).astype(jnp.float32),
        lax.psum_scatter(
            summed[3].astype(jnp.bfloat16), "shard", scatter_dimension=1, tiled=True
        ).astype(jnp.float32),
    )
    small_sums = lax.psum(
        (
            grad_gain_one,
            grad_shift_one,
            grad_b_qkv,
            grad_b_out,
            grad_gain_two,
            grad_shift_two,
            grad_b_in,
            grad_b_back,
        ),
        ("shard", "ctx"),
    )
    return (
        output,
        input_grad,
        small_sums[0],
        small_sums[1],
        owned_grads[0],
        small_sums[2],
        owned_grads[1],
        small_sums[3],
        small_sums[4],
        small_sums[5],
        owned_grads[2],
        small_sums[6],
        owned_grads[3],
        small_sums[7],
    )


LOG2E = 1.4426950408889634
BF = jnp.bfloat16
F32 = jnp.float32
VMEM_BYTES = 56 * 2**20


def dot_nt(a, b):
    return lax.dot_general(a, b, (((1,), (1,)), ((), ())), preferred_element_type=F32)


def dot_nn(a, b):
    return lax.dot_general(a, b, (((1,), (0,)), ((), ())), preferred_element_type=F32)


def dot_tn(a, b):
    return lax.dot_general(a, b, (((0,), (0,)), ((), ())), preferred_element_type=F32)


def whole(shape):
    return pl.BlockSpec(shape, lambda *_: (0,) * len(shape))


SMEM = pl.BlockSpec(memory_space=pltpu.SMEM)


def call(body, args, outs, name, scratch=(), flops=0, grid=None, in_specs=None, out_specs=None):
    shapes = [jax.ShapeDtypeStruct(shape, kind) for shape, kind in outs]
    moved = sum(a.size * a.dtype.itemsize for a in args)
    moved += sum(math.prod(s.shape) * jnp.dtype(s.dtype).itemsize for s in shapes)
    extra = {} if grid is None else {"grid": grid}
    return pl.pallas_call(
        body,
        in_specs=in_specs or [SMEM] + [whole(a.shape) for a in args[1:]],
        out_specs=out_specs or [whole(s.shape) for s in shapes],
        out_shape=shapes,
        scratch_shapes=list(scratch),
        compiler_params=pltpu.CompilerParams(vmem_limit_bytes=VMEM_BYTES),
        cost_estimate=pl.CostEstimate(
            flops=int(flops), bytes_accessed=int(moved), transcendentals=0
        ),
        name=name,
        **extra,
    )(*args)


def piece_index(ids_ref, half, part):
    shard, tp = ids_ref[0], ids_ref[2]
    return shard ^ (2 * (tp ^ half) + part)


CHUNKS = ((0, 0), (0, 1), (1, 0), (1, 1))


def partner_lanes(tensor):
    segment = 2 * (HEAD_DIM // 3 // 2)
    halfway = segment // 2
    width = tensor.shape[1]
    lane = lax.broadcasted_iota(jnp.int32, tensor.shape, 1) % HEAD_DIM
    first = lane % segment < halfway
    return jnp.where(
        first, pltpu.roll(tensor, width - halfway, 1), pltpu.roll(tensor, halfway, 1)
    )


def norm_parts(own, other):
    total = 2 * own.shape[1]
    mean = (jnp.sum(own, 1, keepdims=True) + jnp.sum(other, 1, keepdims=True)) / total
    own, other = own - mean, other - mean
    spread = (
        jnp.sum(own * own, 1, keepdims=True) + jnp.sum(other * other, 1, keepdims=True)
    ) / total
    inv = lax.rsqrt(spread + EPSILON)
    return own * inv, other * inv, inv


def qkv_body(ids_ref, *refs):
    blocks, (w_ref, b_ref, ln_ref, cos_ref, sin_ref, n_ref, q_ref, k_ref, v_ref) = (
        refs[:10],
        refs[10:],
    )
    step = pl.program_id(0)
    own = [blocks[m][...] for m in range(4)]
    other = [
        blocks[4][...],
        blocks[5][...],
        jnp.where(step == 0, blocks[6][...], blocks[7][...]),
        jnp.where(step == 0, blocks[8][...], blocks[9][...]),
    ]
    half = own[0].shape[1]
    width = half // 2
    for m in range(4):
        one, two, unused = norm_parts(own[m].astype(F32), other[m].astype(F32))
        n_ref[m, :, :half] = (one * ln_ref[0:1, :half] + ln_ref[1:2, :half]).astype(BF)
        n_ref[m, :, half:] = (two * ln_ref[0:1, half:] + ln_ref[1:2, half:]).astype(BF)
    for m in range(4):
        acc = b_ref[...]
        for h, j in CHUNKS:
            at = (2 * h + j) * width
            acc = acc + dot_nn(n_ref[m, :, at : at + width], w_ref[piece_index(ids_ref, h, j)])
        cosines, sines = cos_ref[m], sin_ref[m]
        lanes = cosines.shape[1]
        q, k = acc[:, :lanes], acc[:, lanes : 2 * lanes]
        q_ref[m] = (q * cosines + partner_lanes(q) * sines).astype(BF)
        k_ref[m] = (k * cosines + partner_lanes(k) * sines).astype(BF)
        v_ref[m] = acc[:, 2 * lanes :].astype(BF)


def qkv_call(ids, blocks, w, b, ln, cosines, sines):
    rows, half = blocks[0].shape
    lanes = cosines.shape[2]
    block = rows // 2
    row_spec = pl.BlockSpec((block, half), lambda i: (i, 0))
    held = whole((block, half))
    four = lambda cols: pl.BlockSpec((4, block, cols), lambda i: (0, i, 0))
    args = [ids, *blocks, w, b, ln, cosines, sines]
    return call(
        qkv_body,
        args,
        [((4, rows, 2 * half), BF)] + [((4, rows, lanes), BF)] * 3,
        "qkv",
        grid=(2,),
        in_specs=[SMEM]
        + [row_spec] * 6
        + [held] * 4
        + [whole(w.shape), whole(b.shape), whole(ln.shape), four(lanes), four(lanes)],
        out_specs=[four(2 * half), four(lanes), four(lanes), four(lanes)],
        flops=2 * 4 * rows * 2 * half * 3 * lanes * 3,
    )


def attend_body(block, q_ref, k_ref, v_ref, o0, o1, o2, o3, ot_ref, lse_ref, vt_ref):
    step = pl.program_id(0)
    keys, width = k_ref.shape
    rows = q_ref.shape[0]

    @pl.when(step == 0)
    def _():
        vt_ref[:width, :] = v_ref[...].T
        vt_ref[width:, :] = jnp.ones((vt_ref.shape[0] - width, keys), BF)

    q = q_ref[...]
    head = lax.broadcasted_iota(jnp.int32, (rows, width), 1) // HEAD_DIM
    scale = HEAD_DIM ** (-0.5) * LOG2E
    outs = []
    for h in range(width // HEAD_DIM):
        q_head = jnp.where(head == h, q, jnp.zeros_like(q))
        top = None
        for start in range(0, keys, block):
            part = slice(start, start + block)
            scores = dot_nt(k_ref[part, :], q_head)
            latest = jnp.max(scores, axis=0, keepdims=True)
            latest = latest if top is None else jnp.maximum(top, latest)
            probs = jnp.exp2(scores * scale - latest * scale).astype(BF)
            term = dot_nn(vt_ref[:, part], probs)
            acc = term if top is None else acc * jnp.exp2((top - latest) * scale) + term
            top = latest
        total = acc[width : width + 1, :]
        outs.append(acc[h * HEAD_DIM : (h + 1) * HEAD_DIM, :] / total)
        lse_ref[h : h + 1, :] = top * scale + jnp.log2(total)
    result = jnp.concatenate(outs, axis=0)
    ot_ref[...] = result
    low = result.T.astype(BF)

    @pl.when(step == 0)
    def _():
        o0[...] = low[: rows // 2]
        o1[...] = low[rows // 2 :]

    @pl.when(step == 1)
    def _():
        o2[...] = low[: rows // 2]
        o3[...] = low[rows // 2 :]


def attend_call(q, k, v):
    count, width = q.shape
    rows = count // 2
    heads = width // HEAD_DIM
    piece = (count // 4, width)
    return call(
        functools.partial(attend_body, count),
        [q, k, v],
        [(piece, BF)] * 4 + [((width, count), F32), ((heads, count), F32)],
        "attend",
        scratch=[pltpu.VMEM((width + 16, count), BF)],
        grid=(2,),
        in_specs=[pl.BlockSpec((rows, width), lambda i: (i, 0)), whole(k.shape), whole(v.shape)],
        out_specs=[whole(piece)] * 4
        + [
            pl.BlockSpec((width, rows), lambda i: (0, i)),
            pl.BlockSpec((heads, rows), lambda i: (0, i)),
        ],
        flops=4 * count * count * 256 * heads,
    )


def block_body(ids_ref, *refs):
    (x_ref, xp_ref, mo_ref, mp_ref, c_ref, cp_ref, ln_ref, bin_ref) = refs[:8]
    wo, wi, wb = refs[8:12], refs[12:16], refs[16:20]
    mid_ref, sec_ref, act_ref, gin_ref, out_own, out_other, gs_ref, sums_ref = refs[20:]
    rows, half = x_ref.shape
    width = half // 2
    hidden = wi[0].shape[2]
    ctx = ids_ref[1]
    mixed = jnp.concatenate([mo_ref[...], mp_ref[...]], axis=1)
    for h, j in CHUNKS:
        k = piece_index(ids_ref, h, j)
        at = (2 * h + j) * width
        source = (x_ref, xp_ref)[h][:, j * width : (j + 1) * width].astype(F32)
        weight = jnp.concatenate([wo[m][k, side] for side in range(2) for m in range(4)], axis=0)
        mid_ref[:, at : at + width] = (
            source + dot_nn(mixed, weight) + ln_ref[4:5, at : at + width]
        )
    one, two, unused = norm_parts(mid_ref[:, :half], mid_ref[:, half:])
    sec_ref[:, :half] = (one * ln_ref[2:3, :half] + ln_ref[3:4, :half]).astype(BF)
    sec_ref[:, half:] = (two * ln_ref[2:3, half:] + ln_ref[3:4, half:]).astype(BF)
    for m in range(4):
        at = m * hidden
        inner = bin_ref[pl.ds(ctx ^ m, 1), :]
        grad = None
        for h, j in CHUNKS:
            k = piece_index(ids_ref, h, j)
            cols = slice((2 * h + j) * width, (2 * h + j + 1) * width)
            inner = inner + dot_nn(sec_ref[:, cols], wi[m][k])
            part = (c_ref, cp_ref)[h][:, j * width : (j + 1) * width]
            term = dot_nt(part, wb[m][k])
            grad = term if grad is None else grad + term
        phi = 0.5 + 0.5 * lax.erf(inner * (0.5**0.5))
        act_ref[:, at : at + hidden] = (inner * phi).astype(BF)
        slope = phi + inner * (jnp.exp(-0.5 * inner * inner) * ((2 * math.pi) ** -0.5))
        grad = (grad * slope).astype(BF)
        gin_ref[:, at : at + hidden] = grad
        sums_ref[0:1, at : at + hidden] = jnp.sum(grad.astype(F32), axis=0, keepdims=True)
    for h, j in CHUNKS:
        k = piece_index(ids_ref, h, j)
        cols = slice((2 * h + j) * width, (2 * h + j + 1) * width)
        back = None
        out = None
        for m in range(4):
            wide = slice(m * hidden, (m + 1) * hidden)
            term = dot_nt(gin_ref[:, wide], wi[m][k])
            back = term if back is None else back + term
            term = dot_nn(act_ref[:, wide], wb[m][k])
            out = term if out is None else out + term
        gs_ref[:, cols] = back.astype(BF)
        (out_own, out_other)[h][:, j * width : (j + 1) * width] = out.astype(BF)


def block_call(ids, x, xp, mo, mp, c, cp, ln, b_in, wo, wi, wb):
    rows, half = x.shape
    hidden = 4 * wi[0].shape[2]
    return call(
        block_body,
        [ids, x, xp, mo, mp, c, cp, ln, b_in, *wo, *wi, *wb],
        [
            ((rows, 2 * half), F32),
            ((rows, 2 * half), BF),
            ((rows, hidden), BF),
            ((rows, hidden), BF),
            ((rows, half), BF),
            ((rows, half), BF),
            ((rows, 2 * half), BF),
            ((1, hidden), F32),
        ],
        "block",
        flops=2 * rows * 2 * half * (2 * half + 4 * hidden) * 2,
    )


def branch_body(ids_ref, gs_ref, gsp_ref, c_ref, cp_ref, mid_ref, ln_ref, *refs):
    wo = refs[:4]
    gmid_ref, gb_ref, m0, m1, m2, m3, sums_ref = refs[4:]
    half = c_ref.shape[1]
    width = half // 2
    own_u, other_u, inv = norm_parts(mid_ref[:, :half], mid_ref[:, half:])
    own = gs_ref[:, :half].astype(F32) + gsp_ref[:, half:].astype(F32)
    other = gs_ref[:, half:].astype(F32) + gsp_ref[:, :half].astype(F32)
    sums_ref[0:1, :half] = jnp.sum(own * own_u, 0, keepdims=True)
    sums_ref[0:1, half:] = jnp.sum(other * other_u, 0, keepdims=True)
    sums_ref[1:2, :half] = jnp.sum(own, 0, keepdims=True)
    sums_ref[1:2, half:] = jnp.sum(other, 0, keepdims=True)
    own = own * ln_ref[2:3, :half]
    other = other * ln_ref[2:3, half:]
    total = 2 * half
    mean_one = (jnp.sum(own, 1, keepdims=True) + jnp.sum(other, 1, keepdims=True)) / total
    mean_two = (
        jnp.sum(own * own_u, 1, keepdims=True) + jnp.sum(other * other_u, 1, keepdims=True)
    ) / total
    cot = c_ref[...].astype(F32)
    own = cot + inv * (own - mean_one - own_u * mean_two)
    other = cp_ref[...].astype(F32) + inv * (other - mean_one - other_u * mean_two)
    gmid_ref[...] = own
    gb_ref[:, :half] = own.astype(BF)
    gb_ref[:, half:] = other.astype(BF)
    sums_ref[2:3, :half] = jnp.sum(own.astype(BF).astype(F32), 0, keepdims=True)
    sums_ref[2:3, half:] = jnp.sum(cot, 0, keepdims=True)
    mixed = None
    for h, j in CHUNKS:
        k = piece_index(ids_ref, h, j)
        at = (2 * h + j) * width
        weight = jnp.concatenate([wo[m][k, 0] for m in range(4)], axis=0)
        term = dot_nt(gb_ref[:, at : at + width], weight)
        mixed = term if mixed is None else mixed + term
    mixed = mixed.astype(BF)
    lanes = m0.shape[1]
    for m, ref in enumerate((m0, m1, m2, m3)):
        ref[...] = mixed[:, m * lanes : (m + 1) * lanes]


def branch_call(ids, gs, gsp, c, cp, mid, ln, wo):
    rows, half = c.shape
    lanes = wo[0].shape[2]
    return call(
        branch_body,
        [ids, gs, gsp, c, cp, mid, ln, *wo],
        [((rows, half), F32), ((rows, 2 * half), BF)]
        + [((rows, lanes), BF)] * 4
        + [((3, 2 * half), F32)],
        "branch",
        flops=2 * rows * 2 * half * 4 * lanes * 3,
    )


def attend_back_body(rows, q_ref, k_ref, v_ref, d0, d1, d2, d3, ot_ref, lse_ref, *refs):
    dq_ref, dk_ref, dv_ref, qh_ref, dh_ref, delta_ref, dqt_ref = refs
    step = pl.program_id(0)
    count, width = q_ref.shape
    heads = width // HEAD_DIM
    scale = HEAD_DIM ** (-0.5)

    @pl.when(step == 0)
    def _():
        quarter = count // 4
        head = lax.broadcasted_iota(jnp.int32, (quarter, width), 1) // HEAD_DIM
        for m, d_ref in enumerate((d0, d1, d2, d3)):
            part = slice(m * quarter, (m + 1) * quarter)
            q, d = q_ref[part, :], d_ref[...]
            for h in range(heads):
                qh_ref[h, part, :] = jnp.where(head == h, q, jnp.zeros_like(q))
                dh_ref[h, part, :] = jnp.where(head == h, d, jnp.zeros_like(d))
            products = d.astype(F32).T * ot_ref[:, part]
            for h in range(heads):
                delta_ref[h : h + 1, part] = jnp.sum(
                    products[h * HEAD_DIM : (h + 1) * HEAD_DIM], axis=0, keepdims=True
                )
        dqt_ref[...] = jnp.zeros_like(dqt_ref)

    keys, values = k_ref[...], v_ref[...]
    turned = keys.T
    row = lax.broadcasted_iota(jnp.int32, turned.shape, 0) // HEAD_DIM
    dk = dv = None
    for h in range(heads):
        turned_head = jnp.where(row == h, turned, jnp.zeros_like(turned))
        for start in range(0, count, rows):
            part = slice(start, start + rows)
            q, d = qh_ref[h, part, :], dh_ref[h, part, :]
            probs = jnp.exp2(dot_nt(keys, q) * (scale * LOG2E) - lse_ref[h : h + 1, part])
            grad = (probs * (dot_nt(values, d) - delta_ref[h : h + 1, part])).astype(BF)
            value_term, key_term = dot_nn(probs.astype(BF), d), dot_nn(grad, q)
            dk = key_term if dk is None else dk + key_term
            dv = value_term if dv is None else dv + value_term
            dqt_ref[:, part] += dot_nn(turned_head, grad)
    dk_ref[...] = dk * scale
    dv_ref[...] = dv

    @pl.when(step == pl.num_programs(0) - 1)
    def _():
        dq_ref[...] = (dqt_ref[...] * scale).T


def attend_back_call(q, k, v, d, ot, lse):
    count, width = q.shape
    heads = width // HEAD_DIM
    rows = 512
    block = 512
    part = pl.BlockSpec((block, width), lambda i: (i, 0))
    return call(
        functools.partial(attend_back_body, rows),
        [q, k, v, *d, ot, lse],
        [((count, width), F32)] * 3,
        "attend_back",
        scratch=[
            pltpu.VMEM((heads, count, width), BF),
            pltpu.VMEM((heads, count, width), BF),
            pltpu.VMEM((heads, count), F32),
            pltpu.VMEM((width, count), F32),
        ],
        grid=(count // block,),
        in_specs=[whole(q.shape), part, part]
        + [whole(d[0].shape)] * 4
        + [whole(ot.shape), whole(lse.shape)],
        out_specs=[whole(q.shape), part, part],
        flops=10 * count * count * 256 * heads,
    )


def joined_body(ids_ref, dq_ref, dk_ref, dv_ref, cos_ref, sin_ref, w_ref, *refs):
    gj_ref, keep_ref, send_ref, sums_ref = refs
    lanes = dq_ref.shape[2]
    half = keep_ref.shape[2]
    width = half // 2
    sums = [0.0, 0.0, 0.0]
    for m in range(4):
        cosines, sines = cos_ref[m], sin_ref[m]
        dq, dk = dq_ref[m], dk_ref[m]
        parts = (
            dq * cosines + partner_lanes(dq * sines),
            dk * cosines + partner_lanes(dk * sines),
            dv_ref[m],
        )
        for i, part in enumerate(parts):
            low = part.astype(BF)
            gj_ref[m, :, i * lanes : (i + 1) * lanes] = low
            sums[i] = sums[i] + jnp.sum(low.astype(F32), axis=0, keepdims=True)
    for i in range(3):
        sums_ref[i : i + 1, :] = sums[i]
    for m in range(4):
        target = (keep_ref, send_ref)[m % 2]
        for h, j in CHUNKS:
            term = dot_nt(gj_ref[m], w_ref[piece_index(ids_ref, h, j)])
            target[2 * (m // 2) + h, :, j * width : (j + 1) * width] = term.astype(BF)


def joined_call(ids, dq, dk, dv, cosines, sines, w):
    four, rows, lanes = dq.shape
    half = 2 * w.shape[1]
    return call(
        joined_body,
        [ids, dq, dk, dv, cosines, sines, w],
        [
            ((4, rows, 3 * lanes), BF),
            ((4, rows, half), BF),
            ((4, rows, half), BF),
            ((3, lanes), F32),
        ],
        "joined_back",
        flops=2 * 4 * rows * 3 * lanes * 2 * half * 2,
    )


def qkv_grad_body(ids_ref, na_ref, ga_ref, nb_ref, gb_ref, out_ref):
    width = out_ref.shape[1]
    for h, j in CHUNKS:
        at = (2 * h + j) * width
        total = dot_tn(na_ref[:, at : at + width], ga_ref[...]) + dot_tn(
            nb_ref[:, at : at + width], gb_ref[...]
        )
        out_ref[piece_index(ids_ref, h, j)] = total.astype(BF)


def weight_grad_body(ids_ref, *refs):
    act, gin, mo = refs[0:2], refs[2:4], refs[4:6]
    c, cp, sec, gb = refs[6:8], refs[8:10], refs[10:12], refs[12:14]
    keep_ref, send_ref = refs[14:]
    half = c[0].shape[1]
    width = half // 2
    hidden = act[0].shape[1] // 2
    lanes = mo[0].shape[1] // 2
    for side, out_ref in enumerate((keep_ref, send_ref)):
        wide = slice(side * hidden, (side + 1) * hidden)
        narrow = slice(side * lanes, (side + 1) * lanes)
        for h, j in CHUNKS:
            k = piece_index(ids_ref, h, j)
            cols = slice((2 * h + j) * width, (2 * h + j + 1) * width)
            part = slice(j * width, (j + 1) * width)
            back = own = out = 0.0
            for b in range(2):
                cot = (c[b], cp[b])[h][:, part]
                back = back + dot_tn(act[b][:, wide], cot)
                own = own + dot_tn(sec[b][:, cols], gin[b][:, wide])
                out = out + dot_tn(mo[b][:, narrow], gb[b][:, cols])
            out_ref[0, k, :hidden, :] = back.astype(BF)
            out_ref[0, k, hidden : hidden + width, :] = own[:, :width].astype(BF)
            out_ref[0, k, hidden + width : hidden + 2 * width, :] = own[:, width:].astype(BF)
            out_ref[0, k, hidden + 2 * width :, :] = out.astype(BF)


def weight_grad_call(ids, act, gin, mo, c, cp, sec, gb):
    rows, half = c[0].shape
    width = half // 2
    hidden = act[0].shape[1] // 4
    lanes = mo[0].shape[1] // 4
    shape = (2, 4, hidden + 2 * width + lanes, width)
    pair = lambda cols: pl.BlockSpec((rows, cols), lambda i: (0, i))
    args = [ids, *act, *gin, *mo, *c, *cp, *sec, *gb]
    out = pl.BlockSpec((1,) + shape[1:], lambda i: (i, 0, 0, 0))
    return call(
        weight_grad_body,
        args,
        [(shape, BF)] * 2,
        "weight_grads",
        grid=(2,),
        in_specs=[SMEM]
        + [pair(2 * hidden)] * 4
        + [pair(2 * lanes)] * 2
        + [whole(a.shape) for a in args[7:]],
        out_specs=[out, out],
        flops=2 * 2 * rows * 2 * half * (8 * hidden + 4 * lanes) * 1.5,
    )


def across(axis, size, distance):
    pairs = [(i, i ^ distance) for i in range(size)]
    return lambda value: lax.ppermute(value, axis, pairs)


def fast_device(
    inputs,
    ln1_gain,
    ln1_bias,
    w_qkv,
    b_qkv,
    w_out,
    b_out,
    ln2_gain,
    ln2_bias,
    w_in,
    b_in,
    w_back,
    b_back,
    cotangent,
):
    clips, rows, half = inputs.shape
    width = half // 2
    lanes = half // 4
    hidden = w_in.shape[1] // 4
    shard, ctx, tp = (lax.axis_index(name) for name in ("shard", "ctx", "tp"))
    ids = jnp.stack([shard, ctx, tp]).astype(jnp.int32)
    px = across("tp", 2, 1)
    p1, p2, p3 = (across("ctx", 4, k) for k in (1, 2, 3))
    pz = [across("shard", 4, k) for k in (1, 2, 3)]

    def from_shards(piece):
        return jnp.stack([piece] + [p(piece) for p in pz])

    def from_ctx(stack):
        far = p2(stack)
        return [stack, p1(stack), far, p1(far)]

    blocks = []
    for b in range(clips):
        own = inputs[b]
        other = px(own)
        far = p2(own)
        low = p2(other[: rows // 2])
        high = px(far[rows // 2 :])
        near = p1(own)
        other_near = p1(other)
        far_near = p1(far)
        low_near, high_near = p1(low), p1(high)
        blocks.append(
            (own, near, far, far_near, other, other_near, low, high, low_near, high_near)
        )

    qkv_piece = lax.dynamic_slice_in_dim(w_qkv, ctx * lanes, lanes, axis=2).reshape(
        width, 3 * lanes
    )
    wq = from_shards(qkv_piece)
    out_piece = lax.dynamic_slice_in_dim(w_out, ctx * lanes, lanes, axis=0)
    wo = from_ctx(from_shards(jnp.stack([out_piece, px(out_piece)])))
    wi = from_ctx(from_shards(lax.dynamic_slice_in_dim(w_in, ctx * hidden, hidden, axis=1)))
    wb = from_ctx(from_shards(lax.dynamic_slice_in_dim(w_back, ctx * hidden, hidden, axis=0)))

    def halves(vector):
        vector = vector.astype(F32)
        return jnp.concatenate(
            [
                lax.dynamic_slice_in_dim(vector, tp * half, half),
                lax.dynamic_slice_in_dim(vector, (1 - tp) * half, half),
            ]
        )

    bias_out = jnp.concatenate([b_out, px(b_out)]).astype(F32)
    ln_qkv = jnp.stack([halves(ln1_gain), halves(ln1_bias)])
    ln = jnp.stack(
        [ln_qkv[0], ln_qkv[1], halves(ln2_gain), halves(ln2_bias), bias_out]
    )
    bias_qkv = (
        lax.dynamic_slice_in_dim(b_qkv, ctx * lanes, lanes, axis=1)
        .reshape(1, 3 * lanes)
        .astype(F32)
    )
    bias_in = b_in.reshape(4, hidden).astype(F32)

    tables = [rotary_tables((ctx ^ m) * rows, rows) for m in range(4)]
    cosines = jnp.stack([jnp.tile(one, (1, lanes // HEAD_DIM)) for one, _ in tables])
    sines = jnp.stack([jnp.tile(two, (1, lanes // HEAD_DIM)) for _, two in tables])

    cots = [(cotangent[b], px(cotangent[b])) for b in range(clips)]

    flat = lambda a: a.reshape(4 * rows, -1)
    stage = []
    for b in range(clips):
        normed, q, k, v = qkv_call(ids, blocks[b], wq, bias_qkv, ln_qkv, cosines, sines)
        q, k, v = flat(q), flat(k), flat(v)
        o0, o1, o2, o3, ot, lse = attend_call(q, k, v)
        mo = jnp.concatenate([o0, p1(o1), p2(o2), p3(o3)], axis=1)
        stage.append((normed, q, k, v, ot, lse, mo, px(mo)))
    mids, acts, gins, secs, gbs, gmids, backs = [], [], [], [], [], [], []
    outputs, in_sums, mid_sums = [], [], []
    for b in range(clips):
        mo, mp = stage[b][6:]
        mid, sec, act, gin, out_own, out_other, gs, in_sum = block_call(
            ids, blocks[b][0], blocks[b][4], mo, mp, *cots[b], ln, bias_in, wo, wi, wb
        )
        gsp = px(gs)
        arrived = px(out_other)
        outputs.append(
            (
                mid[:, :half]
                + out_own.astype(F32)
                + arrived.astype(F32)
                + b_back.astype(F32)
            ).astype(BF)
        )
        gmid, gb, g0, g1, g2, g3, sums = branch_call(ids, gs, gsp, *cots[b], mid, ln, wo)
        backs.append((g0, p1(g1), p2(g2), p3(g3)))
        for group, item in zip(
            (mids, acts, gins, secs, gbs, gmids, in_sums, mid_sums),
            (mid, act, gin, sec, gb, gmid, in_sum, sums),
        ):
            group.append(item)

    keep, send = weight_grad_call(
        ids,
        acts,
        gins,
        [s[6] for s in stage],
        [c for c, _ in cots],
        [c for _, c in cots],
        secs,
        gbs,
    )

    def add(*terms):
        return sum(term.astype(F32) for term in terms)

    def over_ctx(keep, send):
        near = p1(send)
        far = p2(add(keep[1], near[1]).astype(BF))
        return add(keep[0], near[0], far).astype(BF)

    def over_shards(stack):
        return add(stack[0], *(p(stack[k + 1]) for k, p in enumerate(pz)))

    def spread(piece):
        far = p2(piece)
        return [piece, p1(piece), far, p1(far)]

    dense = spread(over_shards(over_ctx(keep, send)).astype(BF))

    joins, q_sums, grads_normed = [], [], []
    for b in range(clips):
        normed, q, k, v, ot, lse, mo, mp = stage[b]
        dq, dk, dv = attend_back_call(q, k, v, backs[b], ot, lse)
        gj, kept, sent, q_sum = joined_call(
            ids, *(a.reshape(4, rows, lanes) for a in (dq, dk, dv)), cosines, sines, wq
        )
        near = p1(sent)
        cut = rows // 2
        across_low = px(add(kept[3, :cut], near[3, :cut]).astype(BF))
        across_high = p2(add(kept[3, cut:], near[3, cut:]).astype(BF))
        far = add(kept[2], near[2])
        far = jnp.concatenate([far[:cut] + across_low.astype(F32), far[cut:]]).astype(BF)
        other = add(kept[1], near[1])
        other = jnp.concatenate([other[:cut], other[cut:] + across_high.astype(F32)]).astype(BF)
        grads_normed.append(add(kept[0], near[0], p2(far), px(other)))
        joins.append(gj)
        q_sums.append(q_sum)

    qkv_sum = call(
        qkv_grad_body,
        [ids, flat(stage[0][0]), flat(joins[0]), flat(stage[1][0]), flat(joins[1])],
        [((4, width, 3 * lanes), BF)],
        "qkv_grad",
        flops=2 * 8 * rows * 2 * half * 3 * lanes * 1.5,
    )[0]
    qkv_dense = spread(over_shards(qkv_sum).astype(BF))

    gain_own = ln_qkv[0, :half]
    input_grads, gain_sum, shift_sum = [], 0.0, 0.0
    for b in range(clips):
        one, unused, inv = norm_parts(blocks[b][0].astype(F32), blocks[b][4].astype(F32))
        grad = grads_normed[b]
        gain_sum = gain_sum + jnp.sum(grad * one, axis=0)
        shift_sum = shift_sum + jnp.sum(grad, axis=0)
        scaled = grad * gain_own
        stats = jnp.stack([jnp.sum(scaled, axis=1), jnp.sum(scaled * one, axis=1)])
        stats = (stats + px(stats)) / (2 * half)
        input_grads.append(
            gmids[b] + inv * (scaled - stats[0][:, None] - one * stats[1][:, None])
        )

    def all_sum(vector):
        vector = vector + sum(p(vector) for p in pz)
        return vector + p1(vector) + p2(vector) + p3(vector)

    def unroll(pieces):
        return [lax.dynamic_index_in_dim(pieces, ctx ^ m, 0, False) for m in range(4)]

    in_total = in_sums[0] + in_sums[1]
    in_total = jnp.concatenate(unroll(in_total.reshape(4, hidden)))
    mid_total = mid_sums[0] + mid_sums[1]
    q_total = q_sums[0] + q_sums[1]
    q_total = lax.dynamic_update_slice(
        jnp.zeros((4, 3, lanes), F32), q_total[None], (ctx, 0, 0)
    )
    early = all_sum(jnp.concatenate([in_total, mid_total.reshape(-1)]))
    late = all_sum(jnp.concatenate([gain_sum, shift_sum, q_total.reshape(-1)]))
    grad_b_in = early[: 4 * hidden]
    mid_total = early[4 * hidden :].reshape(3, 2 * half)
    grad_b_out, grad_b_back = mid_total[2, :half], mid_total[2, half:]
    grad_b_qkv = (
        late[2 * half :].reshape(4, 3, lanes).transpose(1, 0, 2).reshape(3, 4 * lanes)
    )
    own_ln1 = late[: 2 * half].reshape(2, half)
    other_ln1 = px(own_ln1)

    def in_order(own, other):
        return jnp.where(tp == 0, jnp.concatenate([own, other]), jnp.concatenate([other, own]))

    grad_ln1 = [in_order(own_ln1[i], other_ln1[i]) for i in range(2)]
    grad_ln2 = [in_order(mid_total[i, :half], mid_total[i, half:]) for i in range(2)]

    ordered = unroll(jnp.stack(dense))
    grad_w_back = jnp.concatenate([p[:hidden] for p in ordered], axis=0).astype(F32)
    grad_w_in = jnp.concatenate(
        [p[hidden + i * width : hidden + (i + 1) * width] for p in ordered for i in range(2)],
        axis=1,
    ).astype(F32)
    grad_w_out = jnp.concatenate([p[hidden + 2 * width :] for p in ordered], axis=0).astype(F32)
    ordered = unroll(jnp.stack(qkv_dense))
    grad_w_qkv = jnp.concatenate(
        [p.reshape(width, 3, lanes) for p in ordered], axis=2
    ).astype(F32)
    return (
        jnp.stack(outputs),
        jnp.stack(input_grads),
        grad_ln1[0],
        grad_ln1[1],
        grad_w_qkv,
        grad_b_qkv,
        grad_w_out,
        grad_b_out,
        grad_ln2[0],
        grad_ln2[1],
        grad_w_in,
        grad_b_in,
        grad_w_back,
        grad_b_back,
    )


def quick_form_fits(mesh):
    return (mesh.shape["shard"], mesh.shape["ctx"], mesh.shape["tp"]) == (4, 4, 2)


def solution(mesh):
    placed = (
        P("shard", "ctx", "tp"),
        P(),
        P(),
        P("shard", None, "tp"),
        P(None, "tp"),
        P("tp", "shard"),
        P("tp"),
        P(),
        P(),
        P("shard", "tp"),
        P("tp"),
        P("tp", "shard"),
        P("tp"),
        P("shard", "ctx", "tp"),
    )
    return jax.shard_map(
        fast_device if quick_form_fits(mesh) else per_device,
        mesh=mesh,
        in_specs=placed,
        out_specs=(
            P("shard", "ctx", "tp"),
            P("shard", "ctx", "tp"),
            P(),
            P(),
            P("shard", None, "tp"),
            P(None, "tp"),
            P("tp", "shard"),
            P("tp"),
            P(),
            P(),
            P("shard", "tp"),
            P("tp"),
            P("tp", "shard"),
            P("tp"),
        ),
        check_vma=False,
    )
```

```python
import functools
import math

import jax
import jax.numpy as jnp
from jax import lax
from jax.experimental import pallas as pl
from jax.experimental.pallas import tpu as pltpu
from jax.sharding import PartitionSpec as P

HEAD_DIM = 64
GH = 16
GW = 16


EPSILON = 1e-06
NEG_LARGE = -1e30


def rotary_tables(first_row, row_count):
    segment = 2 * (HEAD_DIM // 3 // 2)
    halfway = segment // 2
    places = first_row + jnp.arange(row_count, dtype=jnp.int32)
    frames = places // (GH * GW)
    rows_at = places // GW % GH
    cols_at = places % GW
    column = jnp.arange(HEAD_DIM, dtype=jnp.int32)
    segment_of = column // segment
    within = column % segment
    frequency = jnp.power(10000.0, -(within % halfway).astype(jnp.float32) / halfway)
    position = jnp.where(
        segment_of[None, :] == 0,
        frames[:, None],
        jnp.where(segment_of[None, :] == 1, rows_at[:, None], cols_at[:, None]),
    )
    angles = position.astype(jnp.float32) * frequency[None, :]
    active = (column < 3 * segment)[None, :]
    cosines = jnp.where(active, jnp.cos(angles), 1.0)
    sine_table = jnp.where(
        active, jnp.where((within < halfway)[None, :], -jnp.sin(angles), jnp.sin(angles)), 0.0
    )
    return (cosines, sine_table)


def partner(tensor):
    segment = 2 * (HEAD_DIM // 3 // 2)
    halfway = segment // 2
    pieces = []
    for number in range(3):
        offset = number * segment
        pieces.append(tensor[..., offset + halfway : offset + segment])
        pieces.append(tensor[..., offset : offset + halfway])
    pieces.append(tensor[..., 3 * segment :])
    return jnp.concatenate(pieces, axis=-1)


def rotate(tensor, cosines, sine_table):
    return tensor * cosines + partner(tensor) * sine_table


def rotate_back(gradient, cosines, sine_table):
    return gradient * cosines + partner(gradient * sine_table)


def normalize(tensor, gain, shift):
    center = tensor - jnp.mean(tensor, axis=-1, keepdims=True)
    spread = jnp.mean(center * center, axis=-1, keepdims=True)
    inv_std = lax.rsqrt(spread + EPSILON)
    scaled = center * inv_std
    return (scaled * gain + shift, scaled, inv_std)


def norm_back(grad_out, scaled, inv_std, gain):
    grad_scaled = grad_out * gain
    mean_one = jnp.mean(grad_scaled, axis=-1, keepdims=True)
    mean_two = jnp.mean(grad_scaled * scaled, axis=-1, keepdims=True)
    return inv_std * (grad_scaled - mean_one - scaled * mean_two)


def tp_rows(sharded):
    return lax.all_gather(sharded, "tp", axis=2, tiled=True)


def tensor_sum(summand):
    return lax.psum_scatter(
        summand.astype(jnp.bfloat16), "tp", scatter_dimension=2, tiled=True
    ).astype(jnp.float32)


def back_total(summand):
    return lax.psum(summand.astype(jnp.bfloat16), "tp").astype(jnp.float32)


def fetch_weights(w_qkv, w_out, w_in, w_back):
    return (
        lax.all_gather(w_qkv, "shard", axis=0, tiled=True),
        lax.all_gather(w_out, "shard", axis=1, tiled=True),
        lax.all_gather(w_in, "shard", axis=0, tiled=True),
        lax.all_gather(w_back, "shard", axis=1, tiled=True),
    )


def forward(inputs, params, weights, cosines, sine_table):
    gain_one, shift_one, b_qkv, b_out, gain_two, shift_two, b_in, b_back = params
    w_qkv_all, w_out_all, w_in_all, w_back_all = weights
    clip_count, row_count, width_local = inputs.shape
    heads_local = width_local // HEAD_DIM
    score_scale = HEAD_DIM ** (-0.5)
    tokens = tp_rows(inputs).astype(jnp.float32)
    normed, scaled_one, inv_one = normalize(tokens, gain_one, shift_one)
    normed_low = normed.astype(jnp.bfloat16)
    joined = (
        jnp.einsum("csd,dkh->cskh", normed_low, w_qkv_all, preferred_element_type=jnp.float32)
        + b_qkv
    )
    shaped = joined.reshape(clip_count, row_count, 3, heads_local, HEAD_DIM)
    queries = rotate(shaped[:, :, 0], cosines, sine_table).astype(jnp.bfloat16)
    key_rows = rotate(shaped[:, :, 1], cosines, sine_table).astype(jnp.bfloat16)
    values = shaped[:, :, 2].astype(jnp.bfloat16)
    key_flat = key_rows.reshape(clip_count, row_count, width_local)
    value_flat = values.reshape(clip_count, row_count, width_local)

    def absorb_block(running, block_pair):
        row_max, row_sum, weighted = running
        key_piece, value_piece = block_pair
        scores = (
            jnp.einsum("cqhd,ckhd->chqk", queries, key_piece, preferred_element_type=jnp.float32)
            * score_scale
        )
        next_max = jnp.maximum(row_max, jnp.max(scores, axis=-1))
        factor = jnp.exp(row_max - next_max)
        weights_now = jnp.exp(scores - next_max[..., None])
        row_sum = row_sum * factor + jnp.sum(weights_now, axis=-1)
        weighted = weighted * factor[..., None] + jnp.einsum(
            "chqk,ckhd->chqd",
            weights_now.astype(jnp.bfloat16),
            value_piece,
            preferred_element_type=jnp.float32,
        )
        return ((next_max, row_sum, weighted), None)

    initial = (
        jnp.full((clip_count, heads_local, row_count), NEG_LARGE, jnp.float32),
        jnp.zeros((clip_count, heads_local, row_count), jnp.float32),
        jnp.zeros((clip_count, heads_local, row_count, HEAD_DIM), jnp.float32),
    )
    running = initial
    pieces = (
        lax.all_gather(key_flat, "ctx", axis=1, tiled=True),
        lax.all_gather(value_flat, "ctx", axis=1, tiled=True),
    )
    piece_rows = pieces[0].shape[1]
    block_size = math.gcd(piece_rows, 512)
    block_count = piece_rows // block_size
    key_blocks = jnp.moveaxis(
        pieces[0].reshape(clip_count, block_count, block_size, heads_local, HEAD_DIM), 1, 0
    )
    value_blocks = jnp.moveaxis(
        pieces[1].reshape(clip_count, block_count, block_size, heads_local, HEAD_DIM), 1, 0
    )
    running, unused = lax.scan(absorb_block, running, (key_blocks, value_blocks))
    row_max, row_sum, weighted = running
    log_total = row_max + jnp.log(row_sum)
    mixed_heads = jnp.transpose(weighted / row_sum[..., None], (0, 2, 1, 3))
    mixed_low = mixed_heads.reshape(clip_count, row_count, width_local).astype(jnp.bfloat16)
    branch = tensor_sum(
        jnp.einsum("csh,hd->csd", mixed_low, w_out_all, preferred_element_type=jnp.float32)
    )
    middle = inputs.astype(jnp.float32) + branch + b_out
    middle_all = lax.all_gather(middle.astype(jnp.bfloat16), "tp", axis=2, tiled=True).astype(
        middle.dtype
    )
    second, scaled_two, inv_two = normalize(middle_all, gain_two, shift_two)
    second_low = second.astype(jnp.bfloat16)
    inner_pre = (
        jnp.einsum("csd,df->csf", second_low, w_in_all, preferred_element_type=jnp.float32) + b_in
    )
    active_low = jax.nn.gelu(inner_pre, approximate=False).astype(jnp.bfloat16)
    return {
        "normed_low": normed_low,
        "scaled_one": scaled_one,
        "inv_one": inv_one,
        "queries": queries,
        "key_flat": key_flat,
        "value_flat": value_flat,
        "mixed_heads": mixed_heads,
        "mixed_low": mixed_low,
        "log_total": log_total,
        "middle": middle,
        "scaled_two": scaled_two,
        "inv_two": inv_two,
        "second_low": second_low,
        "inner_pre": inner_pre,
        "active_low": active_low,
    }


def per_device(
    inputs,
    ln1_gain,
    ln1_bias,
    w_qkv,
    b_qkv,
    w_out,
    b_out,
    ln2_gain,
    ln2_bias,
    w_in,
    b_in,
    w_back,
    b_back,
    cotangent,
):
    params = tuple(
        (
            parameter.astype(jnp.float32)
            for parameter in (ln1_gain, ln1_bias, b_qkv, b_out, ln2_gain, ln2_bias, b_in, b_back)
        )
    )
    gain_one = params[0]
    gain_two = params[4]
    clip_count, row_count, width_local = inputs.shape
    heads_local = width_local // HEAD_DIM
    score_scale = HEAD_DIM ** (-0.5)
    tp_index = lax.axis_index("tp")
    share_start = tp_index * width_local
    cosines, sine_table = rotary_tables(lax.axis_index("ctx") * row_count, row_count)
    cosines = cosines[:, None, :]
    sine_table = sine_table[:, None, :]
    weights = fetch_weights(w_qkv, w_out, w_in, w_back)
    stored_acts = forward(inputs, params, weights, cosines, sine_table)
    output = (
        stored_acts["middle"]
        + tensor_sum(
            jnp.einsum(
                "csf,fd->csd",
                stored_acts["active_low"],
                weights[3],
                preferred_element_type=jnp.float32,
            )
        )
        + params[7]
    ).astype(jnp.bfloat16)
    weights = fetch_weights(w_qkv, w_out, w_in, w_back)
    stored_acts = forward(inputs, params, weights, cosines, sine_table)
    w_qkv_all, w_out_all, w_in_all, w_back_all = weights
    grad_low = tp_rows(cotangent)
    grad_full = grad_low.astype(jnp.float32)
    grad_active = jnp.einsum(
        "csd,fd->csf", grad_low, w_back_all, preferred_element_type=jnp.float32
    )
    unused, gelu_back = jax.vjp(
        lambda argument: jax.nn.gelu(argument, approximate=False), stored_acts["inner_pre"]
    )
    grad_inner = gelu_back(grad_active)[0].astype(jnp.bfloat16)
    grad_w_back = jnp.einsum(
        "csf,csd->fd", stored_acts["active_low"], grad_low, preferred_element_type=jnp.float32
    )
    grad_b_back = jnp.sum(cotangent.astype(jnp.float32), axis=(0, 1))
    grad_w_in = jnp.einsum(
        "csd,csf->df", stored_acts["second_low"], grad_inner, preferred_element_type=jnp.float32
    )
    grad_b_in = jnp.sum(grad_inner.astype(jnp.float32), axis=(0, 1))
    grad_second = back_total(
        jnp.einsum("csf,df->csd", grad_inner, w_in_all, preferred_element_type=jnp.float32)
    )
    grad_gain_two = jnp.sum(grad_second * stored_acts["scaled_two"], axis=(0, 1))
    grad_shift_two = jnp.sum(grad_second, axis=(0, 1))
    grad_middle = grad_full + norm_back(
        grad_second, stored_acts["scaled_two"], stored_acts["inv_two"], gain_two
    )
    grad_branch = grad_middle.astype(jnp.bfloat16)
    grad_b_out = lax.dynamic_slice_in_dim(
        jnp.sum(grad_branch.astype(jnp.float32), axis=(0, 1)), share_start, width_local
    )
    grad_w_out = jnp.einsum(
        "csh,csd->hd", stored_acts["mixed_low"], grad_branch, preferred_element_type=jnp.float32
    )
    grad_mixed = jnp.einsum(
        "csd,hd->csh", grad_branch, w_out_all, preferred_element_type=jnp.float32
    ).astype(jnp.bfloat16)
    key_all, value_all = (
        lax.all_gather(stored_acts["key_flat"], "ctx", axis=1, tiled=True),
        lax.all_gather(stored_acts["value_flat"], "ctx", axis=1, tiled=True),
    )
    length = key_all.shape[1]
    block_size = math.gcd(length, 512)
    block_count = length // block_size
    grad_heads = grad_mixed.reshape(clip_count, row_count, heads_local, HEAD_DIM)
    queries = stored_acts["queries"]
    log_total = stored_acts["log_total"]
    row_delta = jnp.einsum(
        "cqhd,chqd->chq",
        grad_heads.astype(jnp.float32),
        jnp.transpose(stored_acts["mixed_heads"], (0, 2, 1, 3)),
    )
    key_blocks = jnp.moveaxis(
        key_all.reshape(clip_count, block_count, block_size, heads_local, HEAD_DIM), 1, 0
    )
    value_blocks = jnp.moveaxis(
        value_all.reshape(clip_count, block_count, block_size, heads_local, HEAD_DIM), 1, 0
    )

    def key_step(grad_query, block_pair):
        key_piece, value_piece = block_pair
        scores = (
            jnp.einsum("cqhd,ckhd->chqk", queries, key_piece, preferred_element_type=jnp.float32)
            * score_scale
        )
        prob_block = jnp.exp(scores - log_total[..., None])
        grad_probs = jnp.einsum(
            "cqhd,ckhd->chqk", grad_heads, value_piece, preferred_element_type=jnp.float32
        )
        grad_scores = (prob_block * (grad_probs - row_delta[..., None])).astype(jnp.bfloat16)
        grad_query = grad_query + jnp.einsum(
            "chqk,ckhd->cqhd", grad_scores, key_piece, preferred_element_type=jnp.float32
        )
        grad_key = (
            jnp.einsum("chqk,cqhd->ckhd", grad_scores, queries, preferred_element_type=jnp.float32)
            * score_scale
        )
        grad_value = jnp.einsum(
            "chqk,cqhd->ckhd",
            prob_block.astype(jnp.bfloat16),
            grad_heads,
            preferred_element_type=jnp.float32,
        )
        return (grad_query, (grad_key, grad_value))

    grad_query, (key_terms, value_terms) = lax.scan(
        key_step,
        jnp.zeros((clip_count, row_count, heads_local, HEAD_DIM), jnp.float32),
        (key_blocks, value_blocks),
    )
    grad_query = grad_query * score_scale
    key_terms = jnp.moveaxis(key_terms, 0, 1).reshape(clip_count, length, width_local)
    value_terms = jnp.moveaxis(value_terms, 0, 1).reshape(clip_count, length, width_local)
    grad_keys, grad_values = (
        lax.psum_scatter(
            key_terms.astype(jnp.bfloat16), "ctx", scatter_dimension=1, tiled=True
        ).astype(jnp.float32),
        lax.psum_scatter(
            value_terms.astype(jnp.bfloat16), "ctx", scatter_dimension=1, tiled=True
        ).astype(jnp.float32),
    )
    grad_q_pre = rotate_back(grad_query, cosines, sine_table).reshape(
        clip_count, row_count, width_local
    )
    grad_k_pre = rotate_back(
        grad_keys.reshape(clip_count, row_count, heads_local, HEAD_DIM), cosines, sine_table
    ).reshape(clip_count, row_count, width_local)
    grad_joined = jnp.stack([grad_q_pre, grad_k_pre, grad_values], axis=2).astype(jnp.bfloat16)
    grad_w_qkv = jnp.einsum(
        "csd,cskh->dkh", stored_acts["normed_low"], grad_joined, preferred_element_type=jnp.float32
    )
    grad_b_qkv = jnp.sum(grad_joined.astype(jnp.float32), axis=(0, 1))
    normed_term = jnp.einsum(
        "cskh,dkh->csd", grad_joined, w_qkv_all, preferred_element_type=jnp.float32
    )
    grad_normed = back_total(normed_term)
    grad_gain_one = jnp.sum(grad_normed * stored_acts["scaled_one"], axis=(0, 1))
    grad_shift_one = jnp.sum(grad_normed, axis=(0, 1))
    grad_tokens = grad_middle + norm_back(
        grad_normed, stored_acts["scaled_one"], stored_acts["inv_one"], gain_one
    )
    input_grad = lax.dynamic_slice_in_dim(grad_tokens, share_start, width_local, axis=2)
    summed = (
        lax.psum(grad_w_qkv.astype(jnp.bfloat16), "ctx").astype(jnp.float32),
        lax.psum(grad_w_out.astype(jnp.bfloat16), "ctx").astype(jnp.float32),
        lax.psum(grad_w_in.astype(jnp.bfloat16), "ctx").astype(jnp.float32),
        lax.psum(grad_w_back.astype(jnp.bfloat16), "ctx").astype(jnp.float32),
    )
    owned_grads = (
        lax.psum_scatter(
            summed[0].astype(jnp.bfloat16), "shard", scatter_dimension=0, tiled=True
        ).astype(jnp.float32),
        lax.psum_scatter(
            summed[1].astype(jnp.bfloat16), "shard", scatter_dimension=1, tiled=True
        ).astype(jnp.float32),
        lax.psum_scatter(
            summed[2].astype(jnp.bfloat16), "shard", scatter_dimension=0, tiled=True
        ).astype(jnp.float32),
        lax.psum_scatter(
            summed[3].astype(jnp.bfloat16), "shard", scatter_dimension=1, tiled=True
        ).astype(jnp.float32),
    )
    small_sums = lax.psum(
        (
            grad_gain_one,
            grad_shift_one,
            grad_b_qkv,
            grad_b_out,
            grad_gain_two,
            grad_shift_two,
            grad_b_in,
            grad_b_back,
        ),
        ("shard", "ctx"),
    )
    return (
        output,
        input_grad,
        small_sums[0],
        small_sums[1],
        owned_grads[0],
        small_sums[2],
        owned_grads[1],
        small_sums[3],
        small_sums[4],
        small_sums[5],
        owned_grads[2],
        small_sums[6],
        owned_grads[3],
        small_sums[7],
    )


LOG2E = 1.4426950408889634
BF = jnp.bfloat16
F32 = jnp.float32
VMEM_BYTES = 56 * 2**20


def dot_nt(a, b):
    return lax.dot_general(a, b, (((1,), (1,)), ((), ())), preferred_element_type=F32)


def dot_nn(a, b):
    return lax.dot_general(a, b, (((1,), (0,)), ((), ())), preferred_element_type=F32)


def dot_tn(a, b):
    return lax.dot_general(a, b, (((0,), (0,)), ((), ())), preferred_element_type=F32)


def whole(shape):
    return pl.BlockSpec(shape, lambda *_: (0,) * len(shape))


SMEM = pl.BlockSpec(memory_space=pltpu.SMEM)


def call(body, args, outs, name, scratch=(), flops=0, grid=None, in_specs=None, out_specs=None):
    shapes = [jax.ShapeDtypeStruct(shape, kind) for shape, kind in outs]
    moved = sum(a.size * a.dtype.itemsize for a in args)
    moved += sum(math.prod(s.shape) * jnp.dtype(s.dtype).itemsize for s in shapes)
    extra = {} if grid is None else {"grid": grid}
    return pl.pallas_call(
        body,
        in_specs=in_specs or [SMEM] + [whole(a.shape) for a in args[1:]],
        out_specs=out_specs or [whole(s.shape) for s in shapes],
        out_shape=shapes,
        scratch_shapes=list(scratch),
        compiler_params=pltpu.CompilerParams(vmem_limit_bytes=VMEM_BYTES),
        cost_estimate=pl.CostEstimate(
            flops=int(flops), bytes_accessed=int(moved), transcendentals=0
        ),
        name=name,
        **extra,
    )(*args)


def piece_index(ids_ref, half, part):
    shard, tp = ids_ref[0], ids_ref[2]
    return shard ^ (2 * (tp ^ half) + part)


CHUNKS = ((0, 0), (0, 1), (1, 0), (1, 1))


def partner_lanes(tensor):
    segment = 2 * (HEAD_DIM // 3 // 2)
    halfway = segment // 2
    width = tensor.shape[1]
    lane = lax.broadcasted_iota(jnp.int32, tensor.shape, 1) % HEAD_DIM
    first = lane % segment < halfway
    return jnp.where(
        first, pltpu.roll(tensor, width - halfway, 1), pltpu.roll(tensor, halfway, 1)
    )


def norm_parts(own, other):
    total = 2 * own.shape[1]
    mean = (jnp.sum(own, 1, keepdims=True) + jnp.sum(other, 1, keepdims=True)) / total
    own, other = own - mean, other - mean
    spread = (
        jnp.sum(own * own, 1, keepdims=True) + jnp.sum(other * other, 1, keepdims=True)
    ) / total
    inv = lax.rsqrt(spread + EPSILON)
    return own * inv, other * inv, inv


def attend_back_body(rows, q_ref, k_ref, v_ref, d0, d1, d2, d3, ot_ref, lse_ref, *refs):
    dq_ref, dk_ref, dv_ref, qh_ref, dh_ref, delta_ref, dqt_ref = refs
    step = pl.program_id(0)
    count, width = q_ref.shape
    heads = width // HEAD_DIM
    scale = HEAD_DIM ** (-0.5)

    @pl.when(step == 0)
    def _():
        quarter = count // 4
        head = lax.broadcasted_iota(jnp.int32, (quarter, width), 1) // HEAD_DIM
        for m, d_ref in enumerate((d0, d1, d2, d3)):
            part = slice(m * quarter, (m + 1) * quarter)
            q, d = q_ref[part, :], d_ref[...]
            for h in range(heads):
                qh_ref[h, part, :] = jnp.where(head == h, q, jnp.zeros_like(q))
                dh_ref[h, part, :] = jnp.where(head == h, d, jnp.zeros_like(d))
            products = d.astype(F32).T * ot_ref[:, part]
            for h in range(heads):
                delta_ref[h : h + 1, part] = jnp.sum(
                    products[h * HEAD_DIM : (h + 1) * HEAD_DIM], axis=0, keepdims=True
                )
        dqt_ref[...] = jnp.zeros_like(dqt_ref)

    keys, values = k_ref[...], v_ref[...]
    turned = keys.T
    row = lax.broadcasted_iota(jnp.int32, turned.shape, 0) // HEAD_DIM
    dk = dv = None
    for h in range(heads):
        turned_head = jnp.where(row == h, turned, jnp.zeros_like(turned))
        for start in range(0, count, rows):
            part = slice(start, start + rows)
            q, d = qh_ref[h, part, :], dh_ref[h, part, :]
            probs = jnp.exp2(dot_nt(keys, q) * (scale * LOG2E) - lse_ref[h : h + 1, part])
            grad = (probs * (dot_nt(values, d) - delta_ref[h : h + 1, part])).astype(BF)
            value_term, key_term = dot_nn(probs.astype(BF), d), dot_nn(grad, q)
            dk = key_term if dk is None else dk + key_term
            dv = value_term if dv is None else dv + value_term
            dqt_ref[:, part] += dot_nn(turned_head, grad)
    dk_ref[...] = dk * scale
    dv_ref[...] = dv

    @pl.when(step == pl.num_programs(0) - 1)
    def _():
        dq_ref[...] = (dqt_ref[...] * scale).T


def attend_back_call(q, k, v, d, ot, lse):
    count, width = q.shape
    heads = width // HEAD_DIM
    rows = 512
    block = 512
    part = pl.BlockSpec((block, width), lambda i: (i, 0))
    return call(
        functools.partial(attend_back_body, rows),
        [q, k, v, *d, ot, lse],
        [((count, width), F32)] * 3,
        "attend_back",
        scratch=[
            pltpu.VMEM((heads, count, width), BF),
            pltpu.VMEM((heads, count, width), BF),
            pltpu.VMEM((heads, count), F32),
            pltpu.VMEM((width, count), F32),
        ],
        grid=(count // block,),
        in_specs=[whole(q.shape), part, part]
        + [whole(d[0].shape)] * 4
        + [whole(ot.shape), whole(lse.shape)],
        out_specs=[whole(q.shape), part, part],
        flops=10 * count * count * 256 * heads,
    )


def joined_body(ids_ref, dq_ref, dk_ref, dv_ref, cos_ref, sin_ref, w_ref, *refs):
    gj_ref, keep_ref, send_ref, sums_ref = refs
    lanes = dq_ref.shape[2]
    half = keep_ref.shape[2]
    width = half // 2
    sums = [0.0, 0.0, 0.0]
    for m in range(4):
        cosines, sines = cos_ref[m], sin_ref[m]
        dq, dk = dq_ref[m], dk_ref[m]
        parts = (
            dq * cosines + partner_lanes(dq * sines),
            dk * cosines + partner_lanes(dk * sines),
            dv_ref[m],
        )
        for i, part in enumerate(parts):
            low = part.astype(BF)
            gj_ref[m, :, i * lanes : (i + 1) * lanes] = low
            sums[i] = sums[i] + jnp.sum(low.astype(F32), axis=0, keepdims=True)
    for i in range(3):
        sums_ref[i : i + 1, :] = sums[i]
    for m in range(4):
        target = (keep_ref, send_ref)[m % 2]
        for h, j in CHUNKS:
            term = dot_nt(gj_ref[m], w_ref[piece_index(ids_ref, h, j)])
            target[2 * (m // 2) + h, :, j * width : (j + 1) * width] = term.astype(BF)


def joined_call(ids, dq, dk, dv, cosines, sines, w):
    four, rows, lanes = dq.shape
    half = 2 * w.shape[1]
    return call(
        joined_body,
        [ids, dq, dk, dv, cosines, sines, w],
        [
            ((4, rows, 3 * lanes), BF),
            ((4, rows, half), BF),
            ((4, rows, half), BF),
            ((3, lanes), F32),
        ],
        "joined_back",
        flops=2 * 4 * rows * 3 * lanes * 2 * half * 2,
    )


def qkv_grad_body(ids_ref, na_ref, ga_ref, nb_ref, gb_ref, out_ref):
    width = out_ref.shape[1]
    for h, j in CHUNKS:
        at = (2 * h + j) * width
        total = dot_tn(na_ref[:, at : at + width], ga_ref[...]) + dot_tn(
            nb_ref[:, at : at + width], gb_ref[...]
        )
        out_ref[piece_index(ids_ref, h, j)] = total.astype(BF)


def flip(value, bit):
    if bit == 1:
        return value + 1 - 2 * lax.rem(value, 2)
    return lax.rem(value + 2, 4)


def place():
    return tuple(lax.axis_index(name) for name in ("shard", "ctx", "tp"))


def piece_at(shard, tp, half, part):
    found = lax.rem(shard + 2 * lax.rem(tp + half, 2), 4)
    return flip(found, 1) if part else found


class Movers:
    def __init__(self, send_sems, recv_sems, local_sems):
        shard, ctx, tp = place()
        self.sems = (send_sems, recv_sems, local_sems)
        self.sent, self.kept = [], []
        self.partners = {
            "x": {"tp": 1 - tp},
            "core": {"ctx": flip(ctx, 1)},
            "y": {"ctx": flip(ctx, 2)},
            "ycore": {"ctx": flip(flip(ctx, 2), 1)},
            "z1": {"shard": flip(shard, 1)},
            "z2": {"shard": flip(shard, 2)},
            "z3": {"shard": flip(flip(shard, 2), 1)},
        }

    def barrier(self, names):
        barrier = pltpu.get_barrier_semaphore()
        for name in names:
            pl.semaphore_signal(
                barrier,
                inc=1,
                device_id=self.partners[name],
                device_id_type=pl.DeviceIdType.MESH,
            )
        pl.semaphore_wait(barrier, len(names))

    def send(self, source, target, name):
        at = len(self.sent)
        copy = pltpu.make_async_remote_copy(
            src_ref=source,
            dst_ref=target,
            send_sem=self.sems[0].at[at],
            recv_sem=self.sems[1].at[at],
            device_id=self.partners[name],
            device_id_type=pl.DeviceIdType.MESH,
        )
        copy.start()
        self.sent.append([copy, False])
        return at

    def arrive(self, *which):
        for at in which:
            if not self.sent[at][1]:
                self.sent[at][0].wait_recv()
                self.sent[at][1] = True

    def keep(self, source, target):
        at = len(self.kept)
        copy = pltpu.make_async_copy(source, target, self.sems[2].at[at])
        copy.start()
        self.kept.append([copy, False])
        return at

    def kept_done(self, *which):
        for at in which:
            if not self.kept[at][1]:
                self.kept[at][0].wait()
                self.kept[at][1] = True

    def finish(self):
        self.arrive(*range(len(self.sent)))
        for copy, _ in self.sent:
            copy.wait_send()
        self.kept_done(*range(len(self.kept)))


def first_body(*refs):
    (x_ref, cot_ref, wq_piece, wout_ref, win_ref, wback_ref, b_ref, ln_ref, bout_ref) = refs[:9]
    (xp_out, cp_out, n_out, qkv_out, ot_out, lse_out, mo_out, mp_out, wq_out, wo, wi, wb, boutp_out, table_out) = refs[
        9:23
    ]
    (xall, nbuf, qkv, ot, vt, osc, wq, tables, send_sems, recv_sems, local_sems) = refs[23:]
    clips, rows, half = x_ref.shape
    width = half // 2
    lanes = tables.shape[3]
    hidden = wi.shape[3]
    shard, ctx, tp = place()
    mv = Movers(send_sems, recv_sems, local_sems)
    mv.barrier(["x", "core", "y", "ycore", "z1", "z2", "z3"])
    zs = ("z1", "z2", "z3")
    cut = rows // 2

    x0 = [mv.send(x_ref.at[0], xall.at[0, 1, 0], "x")]
    y0 = [mv.send(x_ref.at[0], xall.at[0, 0, 2], "y")]
    wqz = [mv.send(wq_piece, wq.at[k + 1], name) for k, name in enumerate(zs)]
    c0 = [mv.send(x_ref.at[0], xall.at[0, 0, 1], "core")]
    own = [mv.keep(x_ref.at[b], xall.at[b, 0, 0]) for b in range(clips)]
    wq_own = mv.keep(wq_piece, wq.at[0])
    out_piece = wout_ref.at[pl.ds(pl.multiple_of(ctx * lanes, lanes), lanes), :]
    back_piece = wback_ref.at[pl.ds(pl.multiple_of(ctx * hidden, hidden), hidden), :]
    far_ctx = flip(ctx, 2)
    in_pieces = [
        win_ref.at[:, pl.ds(pl.multiple_of(at * hidden, hidden), hidden)] for at in (ctx, far_ctx)
    ]
    wo_x = mv.send(out_piece, wo.at[0, 0, 1], "x")
    mv.send(bout_ref, boutp_out, "x")
    wo_own = mv.keep(out_piece, wo.at[0, 0, 0])
    wi_own = [mv.keep(in_pieces[i], wi.at[2 * i, 0]) for i in range(2)]
    wb_own = mv.keep(back_piece, wb.at[0, 0])

    def forward(b, x, y):
        mv.arrive(x)
        low = mv.send(xall.at[b, 1, 0, :cut], xall.at[b, 1, 2, :cut], "y")
        near = [mv.send(xall.at[b, 1, 0], xall.at[b, 1, 1], "core")]
        mv.arrive(y)
        high = mv.send(xall.at[b, 0, 2, cut:], xall.at[b, 1, 2, cut:], "x")
        near.append(mv.send(xall.at[b, 0, 2], xall.at[b, 0, 3], "core"))
        return low, high, near

    def project(b, m):
        slot = m % 2
        for start in range(0, rows, cut):
            part = slice(start, start + cut)
            one, two, unused = norm_parts(
                xall[b, 0, m, part, :].astype(F32), xall[b, 1, m, part, :].astype(F32)
            )
            nbuf[slot, part, :half] = (one * ln_ref[0:1, :half] + ln_ref[1:2, :half]).astype(BF)
            nbuf[slot, part, half:] = (two * ln_ref[0:1, half:] + ln_ref[1:2, half:]).astype(BF)
        acc = b_ref[...]
        for h, j in CHUNKS:
            at = (2 * h + j) * width
            acc = acc + dot_nn(nbuf[slot, :, at : at + width], wq[piece_at(shard, tp, h, j)])
        cosines, sines = tables[0, m], tables[1, m]
        q, k = acc[:, :lanes], acc[:, lanes : 2 * lanes]
        place_rows = slice(m * rows, (m + 1) * rows)
        qkv[b, 0, place_rows, :] = (q * cosines + partner_lanes(q) * sines).astype(BF)
        qkv[b, 1, place_rows, :] = (k * cosines + partner_lanes(k) * sines).astype(BF)
        qkv[b, 2, place_rows, :] = acc[:, 2 * lanes :].astype(BF)
        return mv.keep(nbuf.at[slot], n_out.at[b, m])

    scale = HEAD_DIM ** (-0.5) * LOG2E
    head = lax.broadcasted_iota(jnp.int32, (rows, lanes), 1) // HEAD_DIM

    def turn_values(b):
        vt[:lanes, :] = qkv[b, 2].T
        vt[lanes:, :] = jnp.ones((vt.shape[0] - lanes, 4 * rows), BF)

    def attend(b, m):
        part = slice(m * rows, (m + 1) * rows)
        q = qkv[b, 0, part, :]
        keys = qkv[b, 1]
        outs = []
        for h in range(lanes // HEAD_DIM):
            q_head = jnp.where(head == h, q, jnp.zeros_like(q))
            scores = dot_nt(keys, q_head)
            top = jnp.max(scores, axis=0, keepdims=True) * scale
            probs = jnp.exp2(scores * scale - top).astype(BF)
            acc = dot_nn(vt[...], probs)
            total = acc[lanes : lanes + 1, :]
            outs.append(acc[h * HEAD_DIM : (h + 1) * HEAD_DIM, :] / total)
            lse_out[b, h : h + 1, part] = top + jnp.log2(total)
        result = jnp.concatenate(outs, axis=0)
        ot[b, :, part] = result
        osc[b, m] = result.T.astype(BF)
        if m == 0:
            return mv.keep(osc.at[b, 0], mo_out.at[b, 0])
        return mv.send(osc.at[b, m], mo_out.at[b, m], ("", "core", "y", "ycore")[m])

    token = lax.broadcasted_iota(jnp.int32, (rows, lanes), 0)
    column = lax.broadcasted_iota(jnp.int32, (rows, lanes), 1) % HEAD_DIM
    segment = 2 * (HEAD_DIM // 3 // 2)
    halfway = segment // 2
    within = column % segment
    frequency = jnp.exp(
        (within % halfway).astype(F32) * (-math.log(10000.0) / halfway)
    )
    sign = jnp.where(within < halfway, -1.0, 1.0)
    active = column < 3 * segment

    def turn(position):
        angle = position.astype(F32) * frequency
        return jnp.where(active, jnp.cos(angle), 1.0), jnp.where(active, jnp.sin(angle) * sign, 0.0)

    def turn_frame(frame):
        angle = frame.astype(F32) * frequency[:8]
        cosine, sine = jnp.cos(angle)[:1], (jnp.sin(angle) * sign[:8])[:1]
        return cosine, sine

    start = [at * rows for at in (ctx, flip(ctx, 1), flip(ctx, 2), flip(flip(ctx, 2), 1))]
    if rows % (GH * GW) == 0:
        tables_in = turn(
            jnp.where(column < 2 * segment, token // GW % GH, token % GW)
        )
        for m in range(4):
            for at in range(0, rows, GH * GW):
                part = slice(at, at + GH * GW)
                frame = turn_frame((start[m] + at) // (GH * GW))
                first = column[part] < segment
                for i in range(2):
                    tables[i, m, part, :] = jnp.where(first, frame[i], tables_in[i][part])
    else:
        for m in range(4):
            at = start[m] + token
            both = turn(
                jnp.where(
                    column < segment,
                    at // (GH * GW),
                    jnp.where(column < 2 * segment, at // GW % GH, at % GW),
                )
            )
            for i in range(2):
                tables[i, m] = both[i]
    mv.keep(tables, table_out)

    low0, high0, near0 = forward(0, x0[0], y0[0])
    x1 = mv.send(x_ref.at[1], xall.at[1, 1, 0], "x")
    y1 = mv.send(x_ref.at[1], xall.at[1, 0, 2], "y")
    c1 = mv.send(x_ref.at[1], xall.at[1, 0, 1], "core")
    mv.keep(xall.at[0, 1, 0], xp_out.at[0])
    mv.arrive(*wqz)
    wbz = [mv.send(back_piece, wb.at[0, k + 1], name) for k, name in enumerate(zs)]
    mv.kept_done(own[0], wq_own)
    mv.keep(wq, wq_out)
    n_copy = [project(0, 0)]
    mv.arrive(c0[0], near0[0])
    n_copy.append(project(0, 1))
    mv.arrive(low0, high0)
    near0.append(mv.send(xall.at[0, 1, 2], xall.at[0, 1, 3], "core"))
    mv.kept_done(n_copy[0])
    n_copy.append(project(0, 2))
    mv.arrive(wo_x)
    mv.kept_done(wo_own)
    woz = [mv.send(wo.at[0, 0], wo.at[0, k + 1], name) for k, name in enumerate(zs)]
    mv.arrive(near0[1], near0[2])
    mv.kept_done(n_copy[1])
    n_copy.append(project(0, 3))
    mv.keep(qkv.at[0], qkv_out.at[0])
    low1, high1, near1 = forward(1, x1, y1)
    mv.keep(xall.at[1, 1, 0], xp_out.at[1])
    cots = [mv.send(cot_ref.at[b], cp_out.at[b], "x") for b in range(clips)]
    turn_values(0)
    m0 = {2: attend(0, 2)}
    mv.arrive(low1, high1)
    near1.append(mv.send(xall.at[1, 1, 2], xall.at[1, 1, 3], "core"))
    mv.arrive(*wbz)
    mv.kept_done(wb_own)
    wiz = [
        mv.send(in_pieces[i], wi.at[2 * i, k + 1], name)
        for i in range(2)
        for k, name in enumerate(zs)
    ]
    wb_far = mv.send(wb.at[0], wb.at[2], "y")
    mv.send(wb.at[0], wb.at[1], "core")
    m0[3] = attend(0, 3)
    mv.arrive(*woz)
    wo_far = mv.send(wo.at[0], wo.at[2], "y")
    mv.send(wo.at[0], wo.at[1], "core")
    m0[1] = attend(0, 1)
    m0[0] = attend(0, 0)
    mv.keep(ot.at[0], ot_out.at[0])
    mv.arrive(c1, *near1)
    mv.kept_done(own[1], n_copy[2])
    n_copy.append(project(1, 0))
    mv.arrive(m0[2], m0[1], m0[3])
    mv.kept_done(m0[0])
    mv.send(mo_out.at[0], mp_out.at[0], "x")
    mv.kept_done(n_copy[3])
    n_copy.append(project(1, 1))
    mv.kept_done(n_copy[4])
    n_copy.append(project(1, 2))
    mv.kept_done(n_copy[5])
    n_copy.append(project(1, 3))
    mv.keep(qkv.at[1], qkv_out.at[1])
    turn_values(1)
    m1 = {2: attend(1, 2)}
    m1[3] = attend(1, 3)
    mv.arrive(wb_far)
    mv.send(wb.at[2], wb.at[3], "core")
    mv.arrive(wo_far)
    mv.send(wo.at[2], wo.at[3], "core")
    m1[1] = attend(1, 1)
    mv.arrive(*wiz[:3])
    mv.kept_done(wi_own[0])
    mv.send(wi.at[0], wi.at[1], "core")
    m1[0] = attend(1, 0)
    mv.keep(ot.at[1], ot_out.at[1])
    mv.kept_done(m1[0])
    mv.send(mo_out.at[1, 0], mp_out.at[1, 0], "x")
    for m in (1, 2, 3):
        mv.arrive(m1[m])
        mv.send(mo_out.at[1, m], mp_out.at[1, m], "x")
    mv.arrive(*wiz[3:])
    mv.kept_done(wi_own[1])
    mv.send(wi.at[2], wi.at[3], "core")
    mv.finish()


ANY = pl.BlockSpec(memory_space=pl.ANY)


def first_call(x, cot, wq_piece, w_out, w_in, w_back, b, ln, b_out):
    clips, rows, half = x.shape
    width = half // 2
    lanes = wq_piece.shape[1] // 3
    hidden = w_in.shape[1] // 4
    outs = [
        ((clips, rows, half), BF),
        ((clips, rows, half), BF),
        ((clips, 4, rows, 2 * half), BF),
        ((clips, 3, 4 * rows, lanes), BF),
        ((clips, lanes, 4 * rows), F32),
        ((clips, lanes // HEAD_DIM, 4 * rows), F32),
        ((clips, 4, rows, lanes), BF),
        ((clips, 4, rows, lanes), BF),
        ((4, width, 3 * lanes), BF),
        ((4, 4, 2, lanes, width), BF),
        ((4, 4, width, hidden), BF),
        ((4, 4, hidden, width), BF),
        (b_out.shape, BF),
        ((2, 4, rows, lanes), F32),
    ]
    out_specs = [ANY] * len(outs)
    out_specs[5] = whole(outs[5][0])
    return pl.pallas_call(
        first_body,
        in_specs=[ANY] * 6 + [whole(b.shape), whole(ln.shape), ANY],
        out_specs=out_specs,
        out_shape=[jax.ShapeDtypeStruct(shape, kind) for shape, kind in outs],
        scratch_shapes=[
            pltpu.VMEM((clips, 2, 4, rows, half), BF),
            pltpu.VMEM((2, rows, 2 * half), BF),
            pltpu.VMEM((clips, 3, 4 * rows, lanes), BF),
            pltpu.VMEM((clips, lanes, 4 * rows), F32),
            pltpu.VMEM((lanes + 16, 4 * rows), BF),
            pltpu.VMEM((clips, 4, rows, lanes), BF),
            pltpu.VMEM((4, width, 3 * lanes), BF),
            pltpu.VMEM((2, 4, rows, lanes), F32),
            pltpu.SemaphoreType.DMA((64,)),
            pltpu.SemaphoreType.DMA((64,)),
            pltpu.SemaphoreType.DMA((40,)),
        ],
        compiler_params=pltpu.CompilerParams(
            vmem_limit_bytes=VMEM_BYTES, collective_id=1, has_side_effects=True
        ),
        name="project_and_attend",
    )(x, cot, wq_piece, w_out, w_in, w_back, b, ln, b_out)


def chunk_of(shard, k):
    found = flip(shard, 2) if k & 2 else shard
    return flip(found, 1) if k & 1 else found


def side_by_side(parts):
    return jnp.concatenate(parts, axis=1)


def second_body(*refs):
    (x_ref, xp_ref, c_ref, cp_ref, mo_ref, mp_ref, wo_hbm, wi_hbm, wb_hbm) = refs[:9]
    (ln_ref, bin_ref, bout_ref, boutp_ref, bback_ref) = refs[9:14]
    (y_out, gmid_out, d_out, g_out, go_out, midsum_out, insum_out, backsum_out) = refs[14:22]
    (xs, cs, ms, wo, wi, wb, mid, sec, act, gin, outs, outr, gs, gsr, gmid, gb, gm) = refs[22:39]
    (wg, wgo, turned, send_sems, recv_sems, local_sems) = refs[39:]
    clips, rows, half = x_ref.shape
    width = half // 2
    lanes = mo_ref.shape[3]
    hidden = wi.shape[3]
    shard, ctx, tp = place()
    mv = Movers(send_sems, recv_sems, local_sems)
    ks = range(4)
    own_k = [piece_at(shard, tp, 0, j) for j in range(2)]
    other_k = [piece_at(shard, tp, 1, j) for j in range(2)]

    def fetch(b):
        return [
            mv.keep(mo_ref.at[b], ms.at[b, 0]),
            mv.keep(mp_ref.at[b], ms.at[b, 1]),
            mv.keep(x_ref.at[b], xs.at[b, 0]),
            mv.keep(xp_ref.at[b], xs.at[b, 1]),
            mv.keep(c_ref.at[b], cs.at[b, 0]),
            mv.keep(cp_ref.at[b], cs.at[b, 1]),
        ]

    got = [fetch(0)]
    got_wo = mv.keep(wo_hbm, wo)
    got_wi = [mv.keep(wi_hbm.at[m], wi.at[m]) for m in ks]
    got_wb = [mv.keep(wb_hbm.at[m], wb.at[m]) for m in ks]
    got.append(fetch(1))
    mv.barrier(["x", "core", "y", "ycore"])

    def row(which, k):
        return ln_ref[pl.ds(4 * which + chunk_of(shard, k), 1), :]

    def statistics(b):
        total = 4 * width
        mean = sum(jnp.sum(mid[b, k], 1, keepdims=True) for k in ks) / total
        spread = sum(jnp.sum((mid[b, k] - mean) ** 2, 1, keepdims=True) for k in ks) / total
        return mean, lax.rsqrt(spread + EPSILON)

    def block(b):
        mv.kept_done(*got[b])
        mv.kept_done(got_wo)
        mixed = side_by_side([ms[b, side, m] for side in range(2) for m in ks])
        for k in ks:
            weight = jnp.concatenate([wo[m, k, side] for side in range(2) for m in ks], axis=0)
            mid[b, k] = dot_nn(mixed, weight)
        for j in range(2):
            part = slice(j * width, (j + 1) * width)
            mid[b, own_k[j]] += xs[b, 0, :, part].astype(F32) + bout_ref[0:1, part].astype(F32)
            mid[b, other_k[j]] += xs[b, 1, :, part].astype(F32) + boutp_ref[0:1, part].astype(F32)
        mean, inv = statistics(b)
        for k in ks:
            sec[b, k] = ((mid[b, k] - mean) * inv * row(0, k) + row(1, k)).astype(BF)
        for j in range(2):
            part = slice(j * width, (j + 1) * width)
            gb[b, own_k[j]] = cs[b, 0, :, part]
            gb[b, other_k[j]] = cs[b, 1, :, part]
        normed = side_by_side([sec[b, k] for k in ks])
        cot = side_by_side([gb[b, k] for k in ks])
        for m in ks:
            mv.kept_done(got_wi[m])
            at = (ctx, flip(ctx, 1), flip(ctx, 2), flip(flip(ctx, 2), 1))[m]
            inner = bin_ref[pl.ds(at, 1), :] + dot_nn(normed, wi[m].reshape(4 * width, hidden))
            mv.kept_done(got_wb[m])
            grad = dot_nt(cot, side_by_side([wb[m, k] for k in ks]))
            phi = 0.5 + 0.5 * lax.erf(inner * (0.5**0.5))
            act[b, m] = (inner * phi).astype(BF)
            slope = phi + inner * (jnp.exp(-0.5 * inner * inner) * ((2 * math.pi) ** -0.5))
            grad = (grad * slope).astype(BF)
            gin[b, m] = grad
            sums = jnp.sum(grad.astype(F32), axis=0, keepdims=True)
            if b == 0:
                insum_out[pl.ds(at, 1), :] = sums
            else:
                insum_out[pl.ds(at, 1), :] += sums
        back = side_by_side([gin[b, m] for m in ks])
        sent = []
        for k in ks:
            gs[b, k] = dot_nt(back, side_by_side([wi[m, k] for m in ks])).astype(BF)
            sent.append(mv.send(gs.at[b, k], gsr.at[b, k], "x"))
        active = side_by_side([act[b, m] for m in ks])
        for h, which in enumerate((own_k, other_k)):
            for j in range(2):
                weight = jnp.concatenate([wb[m, which[j]] for m in ks], axis=0)
                outs[b, h, :, j * width : (j + 1) * width] = dot_nn(active, weight).astype(BF)
        sent.append(mv.send(outs.at[b, 1], outr.at[b], "x"))
        return sent

    put = []

    def branch(b, sent):
        mv.arrive(*sent[:4])
        mv.kept_done(*put)
        total = 4 * width
        mean, inv = statistics(b)
        mean_one = mean_two = 0.0
        for k in ks:
            unit = (mid[b, k] - mean) * inv
            grad = gs[b, k].astype(F32) + gsr[b, k].astype(F32)
            gain_sum = jnp.sum(grad * unit, 0, keepdims=True)
            shift_sum = jnp.sum(grad, 0, keepdims=True)
            for i, term in enumerate((gain_sum, shift_sum)):
                place_row = pl.ds(4 * i + chunk_of(shard, k), 1)
                if b == 0:
                    midsum_out[place_row, :] = term
                else:
                    midsum_out[place_row, :] += term
            scaled = grad * row(0, k)
            mean_one = mean_one + jnp.sum(scaled, 1, keepdims=True)
            mean_two = mean_two + jnp.sum(scaled * unit, 1, keepdims=True)
        mean_one, mean_two = mean_one / total, mean_two / total
        for k in ks:
            unit = (mid[b, k] - mean) * inv
            grad = gs[b, k].astype(F32) + gsr[b, k].astype(F32)
            full = gb[b, k].astype(F32) + inv * (grad * row(0, k) - mean_one - unit * mean_two)
            gmid[k] = full
            low = full.astype(BF)
            xs[b, k // 2, :, (k % 2) * width : (k % 2 + 1) * width] = low
            sec_sum = jnp.sum(low.astype(F32), 0, keepdims=True)
            place_row = pl.ds(8 + chunk_of(shard, k), 1)
            if b == 0:
                midsum_out[place_row, :] = sec_sum
            else:
                midsum_out[place_row, :] += sec_sum
        low = side_by_side([xs[b, 0], xs[b, 1]])
        weight = side_by_side([jnp.concatenate([wo[m, k, 0] for m in ks], axis=0) for k in ks])
        mixed = dot_nt(low, weight).astype(BF)
        for m in ks:
            gm[b, m] = mixed[:, m * lanes : (m + 1) * lanes]
        mv.send(gm.at[b, 2], d_out.at[b, 2], "y")
        mv.send(gm.at[b, 3], d_out.at[b, 3], "ycore")
        mv.send(gm.at[b, 1], d_out.at[b, 1], "core")
        mv.keep(gm.at[b, 0], d_out.at[b, 0])
        for j in range(2):
            put.append(mv.keep(gmid.at[own_k[j]], gmid_out.at[b, j]))
        cot_sum = jnp.sum(cs[b, 0].astype(F32), 0, keepdims=True)
        if b == 0:
            backsum_out[...] = cot_sum
        else:
            backsum_out[...] += cot_sum

    def tokens(ref, *at):
        return jnp.concatenate([ref[(b,) + at] for b in range(clips)], axis=0)

    def big_grads(m, slot):
        cot = side_by_side([tokens(gb, k) for k in ks])
        back = dot_tn(tokens(act, m), cot).astype(BF)
        own = dot_nn(turned[...], tokens(gin, m)).astype(BF)
        for k in ks:
            wg[slot, k, :hidden, :] = back[:, k * width : (k + 1) * width]
            wg[slot, k, hidden : hidden + width, :] = own[k * width : (k + 1) * width, :width]
            wg[slot, k, hidden + width :, :] = own[k * width : (k + 1) * width, width:]
        return mv.keep(wg.at[slot], g_out.at[m])

    first = block(0)
    second = block(1)
    for k in ks:
        turned[k * width : (k + 1) * width, :] = tokens(sec, k).T
    wrote = [big_grads(1, 0), big_grads(3, 1)]
    branch(0, first)
    mv.kept_done(wrote[0])
    wrote.append(big_grads(0, 0))
    mv.kept_done(wrote[1])
    wrote.append(big_grads(2, 1))
    branch(1, second)
    grads = side_by_side([tokens(xs, i) for i in range(2)])
    for m in ks:
        mixed = jnp.concatenate([ms[b, 0, m] for b in range(clips)], axis=0)
        out = dot_tn(mixed, grads).astype(BF)
        for k in ks:
            wgo[m, k] = out[:, k * width : (k + 1) * width]
    mv.keep(wgo, go_out)
    for b, sent in enumerate((first, second)):
        mv.arrive(sent[4])
        for j in range(2):
            part = slice(j * width, (j + 1) * width)
            y_out[b, :, part] = (
                mid[b, own_k[j]]
                + outs[b, 0, :, part].astype(F32)
                + outr[b, :, part].astype(F32)
                + bback_ref[0:1, part].astype(F32)
            ).astype(BF)
    mv.finish()


def second_call(x, xp, c, cp, mo, mp, wo, wi, wb, ln, b_in, b_out, b_out_other, b_back):
    clips, rows, half = x.shape
    width = half // 2
    lanes = mo.shape[3]
    hidden = wi.shape[3]
    tall = hidden + 2 * width
    outs = [
        ((clips, rows, half), BF),
        ((clips, 2, rows, width), F32),
        ((clips, 4, rows, lanes), BF),
        ((4, 4, tall, width), BF),
        ((4, 4, lanes, width), BF),
        ((12, width), F32),
        ((4, hidden), F32),
        ((1, half), F32),
    ]
    small = [ln, b_in, b_out, b_out_other, b_back]
    return pl.pallas_call(
        second_body,
        in_specs=[ANY] * 9 + [whole(a.shape) for a in small],
        out_specs=[whole(outs[0][0])] + [ANY] * 4 + [whole(o[0]) for o in outs[5:]],
        out_shape=[jax.ShapeDtypeStruct(shape, kind) for shape, kind in outs],
        scratch_shapes=[
            pltpu.VMEM((clips, 2, rows, half), BF),
            pltpu.VMEM((clips, 2, rows, half), BF),
            pltpu.VMEM((clips, 2, 4, rows, lanes), BF),
            pltpu.VMEM(wo.shape, BF),
            pltpu.VMEM(wi.shape, BF),
            pltpu.VMEM(wb.shape, BF),
            pltpu.VMEM((clips, 4, rows, width), F32),
            pltpu.VMEM((clips, 4, rows, width), BF),
            pltpu.VMEM((clips, 4, rows, hidden), BF),
            pltpu.VMEM((clips, 4, rows, hidden), BF),
            pltpu.VMEM((clips, 2, rows, half), BF),
            pltpu.VMEM((clips, rows, half), BF),
            pltpu.VMEM((clips, 4, rows, width), BF),
            pltpu.VMEM((clips, 4, rows, width), BF),
            pltpu.VMEM((4, rows, width), F32),
            pltpu.VMEM((clips, 4, rows, width), BF),
            pltpu.VMEM((clips, 4, rows, lanes), BF),
            pltpu.VMEM((2, 4, tall, width), BF),
            pltpu.VMEM((4, 4, lanes, width), BF),
            pltpu.VMEM((4 * width, clips * rows), BF),
            pltpu.SemaphoreType.DMA((24,)),
            pltpu.SemaphoreType.DMA((24,)),
            pltpu.SemaphoreType.DMA((40,)),
        ],
        compiler_params=pltpu.CompilerParams(
            vmem_limit_bytes=VMEM_BYTES, collective_id=2, has_side_effects=True
        ),
        name="layer_middle",
    )(x, xp, c, cp, mo, mp, wo, wi, wb, *small)


def across(axis, size, distance):
    pairs = [(i, i ^ distance) for i in range(size)]
    return lambda value: lax.ppermute(value, axis, pairs)


def fast_device(
    inputs,
    ln1_gain,
    ln1_bias,
    w_qkv,
    b_qkv,
    w_out,
    b_out,
    ln2_gain,
    ln2_bias,
    w_in,
    b_in,
    w_back,
    b_back,
    cotangent,
):
    clips, rows, half = inputs.shape
    width = half // 2
    lanes = half // 4
    hidden = w_in.shape[1] // 4
    shard, ctx, tp = (lax.axis_index(name) for name in ("shard", "ctx", "tp"))
    ids = jnp.stack([shard, ctx, tp]).astype(jnp.int32)
    px = across("tp", 2, 1)
    p1, p2, p3 = (across("ctx", 4, k) for k in (1, 2, 3))
    pz = [across("shard", 4, k) for k in (1, 2, 3)]

    def halves(vector):
        vector = vector.astype(F32)
        return jnp.concatenate(
            [
                lax.dynamic_slice_in_dim(vector, tp * half, half),
                lax.dynamic_slice_in_dim(vector, (1 - tp) * half, half),
            ]
        )

    ln_qkv = jnp.stack([halves(ln1_gain), halves(ln1_bias)])
    bias_qkv = (
        lax.dynamic_slice_in_dim(b_qkv, ctx * lanes, lanes, axis=1)
        .reshape(1, 3 * lanes)
        .astype(F32)
    )
    bias_in = b_in.reshape(4, hidden).astype(F32)

    flat = lambda a: a.reshape(4 * rows, -1)
    qkv_piece = lax.dynamic_slice_in_dim(w_qkv, ctx * lanes, lanes, axis=2).reshape(
        width, 3 * lanes
    )
    xp, cp, normed, qkv, ot, lse, mo, mp, wq, wo, wi, wb, bias_other, tables = first_call(
        inputs,
        cotangent,
        qkv_piece,
        w_out,
        w_in,
        w_back,
        bias_qkv,
        ln_qkv,
        jnp.broadcast_to(b_out, (16, half)),
    )
    cosines, sines = tables[0], tables[1]
    blocks = [(inputs[b], None, None, None, xp[b]) for b in range(clips)]
    ln_two = jnp.concatenate([ln2_gain, ln2_bias]).astype(F32).reshape(8, width)
    output, gmids, arrived, grads, grads_out, mid_total, in_total, back_total_own = second_call(
        inputs,
        xp,
        cotangent,
        cp,
        mo,
        mp,
        wo,
        wi,
        wb,
        ln_two,
        bias_in,
        b_out.reshape(1, half),
        bias_other,
        b_back.reshape(1, half),
    )
    backs = [[arrived[b, m] for m in range(4)] for b in range(clips)]
    stage = [
        (normed[b], qkv[b, 0], qkv[b, 1], qkv[b, 2], ot[b], lse[b], None, None)
        for b in range(clips)
    ]
    whole_grads = jnp.concatenate([grads, grads_out], axis=2)
    keep = jnp.stack([whole_grads[0], whole_grads[2]])
    send = jnp.stack([whole_grads[1], whole_grads[3]])

    def add(*terms):
        return sum(term.astype(F32) for term in terms)

    def over_ctx(keep, send):
        near = p1(send)
        far = p2(add(keep[1], near[1]).astype(BF))
        return add(keep[0], near[0], far).astype(BF)

    def over_shards(stack):
        return add(stack[0], *(p(stack[k + 1]) for k, p in enumerate(pz)))

    def spread(piece):
        far = p2(piece)
        return [piece, p1(piece), far, p1(far)]

    dense = spread(over_shards(over_ctx(keep, send)).astype(BF))

    joins, q_sums, grads_normed = [], [], []
    for b in range(clips):
        normed, q, k, v, ot, lse, mo, mp = stage[b]
        dq, dk, dv = attend_back_call(q, k, v, backs[b], ot, lse)
        gj, kept, sent, q_sum = joined_call(
            ids, *(a.reshape(4, rows, lanes) for a in (dq, dk, dv)), cosines, sines, wq
        )
        near = p1(sent)
        cut = rows // 2
        across_low = px(add(kept[3, :cut], near[3, :cut]).astype(BF))
        across_high = p2(add(kept[3, cut:], near[3, cut:]).astype(BF))
        far = add(kept[2], near[2])
        far = jnp.concatenate([far[:cut] + across_low.astype(F32), far[cut:]]).astype(BF)
        other = add(kept[1], near[1])
        other = jnp.concatenate([other[:cut], other[cut:] + across_high.astype(F32)]).astype(BF)
        grads_normed.append(add(kept[0], near[0], p2(far), px(other)))
        joins.append(gj)
        q_sums.append(q_sum)

    qkv_sum = call(
        qkv_grad_body,
        [ids, flat(stage[0][0]), flat(joins[0]), flat(stage[1][0]), flat(joins[1])],
        [((4, width, 3 * lanes), BF)],
        "qkv_grad",
        flops=2 * 8 * rows * 2 * half * 3 * lanes * 1.5,
    )[0]
    qkv_dense = spread(over_shards(qkv_sum).astype(BF))

    gain_own = ln_qkv[0, :half]
    input_grads, gain_sum, shift_sum = [], 0.0, 0.0
    for b in range(clips):
        one, unused, inv = norm_parts(blocks[b][0].astype(F32), blocks[b][4].astype(F32))
        grad = grads_normed[b]
        gain_sum = gain_sum + jnp.sum(grad * one, axis=0)
        shift_sum = shift_sum + jnp.sum(grad, axis=0)
        scaled = grad * gain_own
        stats = jnp.stack([jnp.sum(scaled, axis=1), jnp.sum(scaled * one, axis=1)])
        stats = (stats + px(stats)) / (2 * half)
        input_grads.append(
            jnp.concatenate([gmids[b, 0], gmids[b, 1]], axis=1) + inv * (scaled - stats[0][:, None] - one * stats[1][:, None])
        )

    def all_sum(vector):
        vector = vector + sum(p(vector) for p in pz)
        return vector + p1(vector) + p2(vector) + p3(vector)

    def unroll(pieces):
        return [lax.dynamic_index_in_dim(pieces, ctx ^ m, 0, False) for m in range(4)]

    q_total = q_sums[0] + q_sums[1]
    q_total = lax.dynamic_update_slice(
        jnp.zeros((4, 3, lanes), F32), q_total[None], (ctx, 0, 0)
    )
    early = all_sum(jnp.concatenate([in_total.reshape(-1), mid_total.reshape(-1), back_total_own[0]]))
    late = all_sum(jnp.concatenate([gain_sum, shift_sum, q_total.reshape(-1)]))
    grad_b_in = early[: 4 * hidden]
    mid_total = early[4 * hidden : 4 * hidden + 6 * half].reshape(3, 2 * half)
    grad_b_out = lax.dynamic_slice_in_dim(mid_total[2], tp * half, half)
    grad_b_back = early[4 * hidden + 6 * half :]
    grad_b_qkv = (
        late[2 * half :].reshape(4, 3, lanes).transpose(1, 0, 2).reshape(3, 4 * lanes)
    )
    own_ln1 = late[: 2 * half].reshape(2, half)
    other_ln1 = px(own_ln1)

    def in_order(own, other):
        return jnp.where(tp == 0, jnp.concatenate([own, other]), jnp.concatenate([other, own]))

    grad_ln1 = [in_order(own_ln1[i], other_ln1[i]) for i in range(2)]
    grad_ln2 = [mid_total[i] for i in range(2)]

    ordered = unroll(jnp.stack(dense))
    grad_w_back = jnp.concatenate([p[:hidden] for p in ordered], axis=0).astype(F32)
    grad_w_in = jnp.concatenate(
        [p[hidden + i * width : hidden + (i + 1) * width] for p in ordered for i in range(2)],
        axis=1,
    ).astype(F32)
    grad_w_out = jnp.concatenate([p[hidden + 2 * width :] for p in ordered], axis=0).astype(F32)
    ordered = unroll(jnp.stack(qkv_dense))
    grad_w_qkv = jnp.concatenate(
        [p.reshape(width, 3, lanes) for p in ordered], axis=2
    ).astype(F32)
    return (
        output,
        jnp.stack(input_grads),
        grad_ln1[0],
        grad_ln1[1],
        grad_w_qkv,
        grad_b_qkv,
        grad_w_out,
        grad_b_out,
        grad_ln2[0],
        grad_ln2[1],
        grad_w_in,
        grad_b_in,
        grad_w_back,
        grad_b_back,
    )


def quick_form_fits(mesh):
    return (mesh.shape["shard"], mesh.shape["ctx"], mesh.shape["tp"]) == (4, 4, 2)


def solution(mesh):
    placed = (
        P("shard", "ctx", "tp"),
        P(),
        P(),
        P("shard", None, "tp"),
        P(None, "tp"),
        P("tp", "shard"),
        P("tp"),
        P(),
        P(),
        P("shard", "tp"),
        P("tp"),
        P("tp", "shard"),
        P("tp"),
        P("shard", "ctx", "tp"),
    )
    return jax.shard_map(
        fast_device if quick_form_fits(mesh) else per_device,
        mesh=mesh,
        in_specs=placed,
        out_specs=(
            P("shard", "ctx", "tp"),
            P("shard", "ctx", "tp"),
            P(),
            P(),
            P("shard", None, "tp"),
            P(None, "tp"),
            P("tp", "shard"),
            P("tp"),
            P(),
            P(),
            P("shard", "tp"),
            P("tp"),
            P("tp", "shard"),
            P("tp"),
        ),
        check_vma=False,
    )
```

```python
import math

import jax
import jax.numpy as jnp
from jax import lax
from jax.experimental import pallas as pl
from jax.experimental.pallas import tpu as pltpu
from jax.sharding import PartitionSpec as P

HEAD_DIM = 64
GH = 16
GW = 16


EPSILON = 1e-06
NEG_LARGE = -1e30


def rotary_tables(first_row, row_count):
    segment = 2 * (HEAD_DIM // 3 // 2)
    halfway = segment // 2
    places = first_row + jnp.arange(row_count, dtype=jnp.int32)
    frames = places // (GH * GW)
    rows_at = places // GW % GH
    cols_at = places % GW
    column = jnp.arange(HEAD_DIM, dtype=jnp.int32)
    segment_of = column // segment
    within = column % segment
    frequency = jnp.power(10000.0, -(within % halfway).astype(jnp.float32) / halfway)
    position = jnp.where(
        segment_of[None, :] == 0,
        frames[:, None],
        jnp.where(segment_of[None, :] == 1, rows_at[:, None], cols_at[:, None]),
    )
    angles = position.astype(jnp.float32) * frequency[None, :]
    active = (column < 3 * segment)[None, :]
    cosines = jnp.where(active, jnp.cos(angles), 1.0)
    sine_table = jnp.where(
        active, jnp.where((within < halfway)[None, :], -jnp.sin(angles), jnp.sin(angles)), 0.0
    )
    return (cosines, sine_table)


def partner(tensor):
    segment = 2 * (HEAD_DIM // 3 // 2)
    halfway = segment // 2
    pieces = []
    for number in range(3):
        offset = number * segment
        pieces.append(tensor[..., offset + halfway : offset + segment])
        pieces.append(tensor[..., offset : offset + halfway])
    pieces.append(tensor[..., 3 * segment :])
    return jnp.concatenate(pieces, axis=-1)


def rotate(tensor, cosines, sine_table):
    return tensor * cosines + partner(tensor) * sine_table


def rotate_back(gradient, cosines, sine_table):
    return gradient * cosines + partner(gradient * sine_table)


def normalize(tensor, gain, shift):
    center = tensor - jnp.mean(tensor, axis=-1, keepdims=True)
    spread = jnp.mean(center * center, axis=-1, keepdims=True)
    inv_std = lax.rsqrt(spread + EPSILON)
    scaled = center * inv_std
    return (scaled * gain + shift, scaled, inv_std)


def norm_back(grad_out, scaled, inv_std, gain):
    grad_scaled = grad_out * gain
    mean_one = jnp.mean(grad_scaled, axis=-1, keepdims=True)
    mean_two = jnp.mean(grad_scaled * scaled, axis=-1, keepdims=True)
    return inv_std * (grad_scaled - mean_one - scaled * mean_two)


def tp_rows(sharded):
    return lax.all_gather(sharded, "tp", axis=2, tiled=True)


def tensor_sum(summand):
    return lax.psum_scatter(
        summand.astype(jnp.bfloat16), "tp", scatter_dimension=2, tiled=True
    ).astype(jnp.float32)


def back_total(summand):
    return lax.psum(summand.astype(jnp.bfloat16), "tp").astype(jnp.float32)


def fetch_weights(w_qkv, w_out, w_in, w_back):
    return (
        lax.all_gather(w_qkv, "shard", axis=0, tiled=True),
        lax.all_gather(w_out, "shard", axis=1, tiled=True),
        lax.all_gather(w_in, "shard", axis=0, tiled=True),
        lax.all_gather(w_back, "shard", axis=1, tiled=True),
    )


def forward(inputs, params, weights, cosines, sine_table):
    gain_one, shift_one, b_qkv, b_out, gain_two, shift_two, b_in, b_back = params
    w_qkv_all, w_out_all, w_in_all, w_back_all = weights
    clip_count, row_count, width_local = inputs.shape
    heads_local = width_local // HEAD_DIM
    score_scale = HEAD_DIM ** (-0.5)
    tokens = tp_rows(inputs).astype(jnp.float32)
    normed, scaled_one, inv_one = normalize(tokens, gain_one, shift_one)
    normed_low = normed.astype(jnp.bfloat16)
    joined = (
        jnp.einsum("csd,dkh->cskh", normed_low, w_qkv_all, preferred_element_type=jnp.float32)
        + b_qkv
    )
    shaped = joined.reshape(clip_count, row_count, 3, heads_local, HEAD_DIM)
    queries = rotate(shaped[:, :, 0], cosines, sine_table).astype(jnp.bfloat16)
    key_rows = rotate(shaped[:, :, 1], cosines, sine_table).astype(jnp.bfloat16)
    values = shaped[:, :, 2].astype(jnp.bfloat16)
    key_flat = key_rows.reshape(clip_count, row_count, width_local)
    value_flat = values.reshape(clip_count, row_count, width_local)

    def absorb_block(running, block_pair):
        row_max, row_sum, weighted = running
        key_piece, value_piece = block_pair
        scores = (
            jnp.einsum("cqhd,ckhd->chqk", queries, key_piece, preferred_element_type=jnp.float32)
            * score_scale
        )
        next_max = jnp.maximum(row_max, jnp.max(scores, axis=-1))
        factor = jnp.exp(row_max - next_max)
        weights_now = jnp.exp(scores - next_max[..., None])
        row_sum = row_sum * factor + jnp.sum(weights_now, axis=-1)
        weighted = weighted * factor[..., None] + jnp.einsum(
            "chqk,ckhd->chqd",
            weights_now.astype(jnp.bfloat16),
            value_piece,
            preferred_element_type=jnp.float32,
        )
        return ((next_max, row_sum, weighted), None)

    initial = (
        jnp.full((clip_count, heads_local, row_count), NEG_LARGE, jnp.float32),
        jnp.zeros((clip_count, heads_local, row_count), jnp.float32),
        jnp.zeros((clip_count, heads_local, row_count, HEAD_DIM), jnp.float32),
    )
    running = initial
    pieces = (
        lax.all_gather(key_flat, "ctx", axis=1, tiled=True),
        lax.all_gather(value_flat, "ctx", axis=1, tiled=True),
    )
    piece_rows = pieces[0].shape[1]
    block_size = math.gcd(piece_rows, 512)
    block_count = piece_rows // block_size
    key_blocks = jnp.moveaxis(
        pieces[0].reshape(clip_count, block_count, block_size, heads_local, HEAD_DIM), 1, 0
    )
    value_blocks = jnp.moveaxis(
        pieces[1].reshape(clip_count, block_count, block_size, heads_local, HEAD_DIM), 1, 0
    )
    running, unused = lax.scan(absorb_block, running, (key_blocks, value_blocks))
    row_max, row_sum, weighted = running
    log_total = row_max + jnp.log(row_sum)
    mixed_heads = jnp.transpose(weighted / row_sum[..., None], (0, 2, 1, 3))
    mixed_low = mixed_heads.reshape(clip_count, row_count, width_local).astype(jnp.bfloat16)
    branch = tensor_sum(
        jnp.einsum("csh,hd->csd", mixed_low, w_out_all, preferred_element_type=jnp.float32)
    )
    middle = inputs.astype(jnp.float32) + branch + b_out
    middle_all = lax.all_gather(middle.astype(jnp.bfloat16), "tp", axis=2, tiled=True).astype(
        middle.dtype
    )
    second, scaled_two, inv_two = normalize(middle_all, gain_two, shift_two)
    second_low = second.astype(jnp.bfloat16)
    inner_pre = (
        jnp.einsum("csd,df->csf", second_low, w_in_all, preferred_element_type=jnp.float32) + b_in
    )
    active_low = jax.nn.gelu(inner_pre, approximate=False).astype(jnp.bfloat16)
    return {
        "normed_low": normed_low,
        "scaled_one": scaled_one,
        "inv_one": inv_one,
        "queries": queries,
        "key_flat": key_flat,
        "value_flat": value_flat,
        "mixed_heads": mixed_heads,
        "mixed_low": mixed_low,
        "log_total": log_total,
        "middle": middle,
        "scaled_two": scaled_two,
        "inv_two": inv_two,
        "second_low": second_low,
        "inner_pre": inner_pre,
        "active_low": active_low,
    }


def per_device(
    inputs,
    ln1_gain,
    ln1_bias,
    w_qkv,
    b_qkv,
    w_out,
    b_out,
    ln2_gain,
    ln2_bias,
    w_in,
    b_in,
    w_back,
    b_back,
    cotangent,
):
    params = tuple(
        (
            parameter.astype(jnp.float32)
            for parameter in (ln1_gain, ln1_bias, b_qkv, b_out, ln2_gain, ln2_bias, b_in, b_back)
        )
    )
    gain_one = params[0]
    gain_two = params[4]
    clip_count, row_count, width_local = inputs.shape
    heads_local = width_local // HEAD_DIM
    score_scale = HEAD_DIM ** (-0.5)
    tp_index = lax.axis_index("tp")
    share_start = tp_index * width_local
    cosines, sine_table = rotary_tables(lax.axis_index("ctx") * row_count, row_count)
    cosines = cosines[:, None, :]
    sine_table = sine_table[:, None, :]
    weights = fetch_weights(w_qkv, w_out, w_in, w_back)
    stored_acts = forward(inputs, params, weights, cosines, sine_table)
    output = (
        stored_acts["middle"]
        + tensor_sum(
            jnp.einsum(
                "csf,fd->csd",
                stored_acts["active_low"],
                weights[3],
                preferred_element_type=jnp.float32,
            )
        )
        + params[7]
    ).astype(jnp.bfloat16)
    weights = fetch_weights(w_qkv, w_out, w_in, w_back)
    stored_acts = forward(inputs, params, weights, cosines, sine_table)
    w_qkv_all, w_out_all, w_in_all, w_back_all = weights
    grad_low = tp_rows(cotangent)
    grad_full = grad_low.astype(jnp.float32)
    grad_active = jnp.einsum(
        "csd,fd->csf", grad_low, w_back_all, preferred_element_type=jnp.float32
    )
    unused, gelu_back = jax.vjp(
        lambda argument: jax.nn.gelu(argument, approximate=False), stored_acts["inner_pre"]
    )
    grad_inner = gelu_back(grad_active)[0].astype(jnp.bfloat16)
    grad_w_back = jnp.einsum(
        "csf,csd->fd", stored_acts["active_low"], grad_low, preferred_element_type=jnp.float32
    )
    grad_b_back = jnp.sum(cotangent.astype(jnp.float32), axis=(0, 1))
    grad_w_in = jnp.einsum(
        "csd,csf->df", stored_acts["second_low"], grad_inner, preferred_element_type=jnp.float32
    )
    grad_b_in = jnp.sum(grad_inner.astype(jnp.float32), axis=(0, 1))
    grad_second = back_total(
        jnp.einsum("csf,df->csd", grad_inner, w_in_all, preferred_element_type=jnp.float32)
    )
    grad_gain_two = jnp.sum(grad_second * stored_acts["scaled_two"], axis=(0, 1))
    grad_shift_two = jnp.sum(grad_second, axis=(0, 1))
    grad_middle = grad_full + norm_back(
        grad_second, stored_acts["scaled_two"], stored_acts["inv_two"], gain_two
    )
    grad_branch = grad_middle.astype(jnp.bfloat16)
    grad_b_out = lax.dynamic_slice_in_dim(
        jnp.sum(grad_branch.astype(jnp.float32), axis=(0, 1)), share_start, width_local
    )
    grad_w_out = jnp.einsum(
        "csh,csd->hd", stored_acts["mixed_low"], grad_branch, preferred_element_type=jnp.float32
    )
    grad_mixed = jnp.einsum(
        "csd,hd->csh", grad_branch, w_out_all, preferred_element_type=jnp.float32
    ).astype(jnp.bfloat16)
    key_all, value_all = (
        lax.all_gather(stored_acts["key_flat"], "ctx", axis=1, tiled=True),
        lax.all_gather(stored_acts["value_flat"], "ctx", axis=1, tiled=True),
    )
    length = key_all.shape[1]
    block_size = math.gcd(length, 512)
    block_count = length // block_size
    grad_heads = grad_mixed.reshape(clip_count, row_count, heads_local, HEAD_DIM)
    queries = stored_acts["queries"]
    log_total = stored_acts["log_total"]
    row_delta = jnp.einsum(
        "cqhd,chqd->chq",
        grad_heads.astype(jnp.float32),
        jnp.transpose(stored_acts["mixed_heads"], (0, 2, 1, 3)),
    )
    key_blocks = jnp.moveaxis(
        key_all.reshape(clip_count, block_count, block_size, heads_local, HEAD_DIM), 1, 0
    )
    value_blocks = jnp.moveaxis(
        value_all.reshape(clip_count, block_count, block_size, heads_local, HEAD_DIM), 1, 0
    )

    def key_step(grad_query, block_pair):
        key_piece, value_piece = block_pair
        scores = (
            jnp.einsum("cqhd,ckhd->chqk", queries, key_piece, preferred_element_type=jnp.float32)
            * score_scale
        )
        prob_block = jnp.exp(scores - log_total[..., None])
        grad_probs = jnp.einsum(
            "cqhd,ckhd->chqk", grad_heads, value_piece, preferred_element_type=jnp.float32
        )
        grad_scores = (prob_block * (grad_probs - row_delta[..., None])).astype(jnp.bfloat16)
        grad_query = grad_query + jnp.einsum(
            "chqk,ckhd->cqhd", grad_scores, key_piece, preferred_element_type=jnp.float32
        )
        grad_key = (
            jnp.einsum("chqk,cqhd->ckhd", grad_scores, queries, preferred_element_type=jnp.float32)
            * score_scale
        )
        grad_value = jnp.einsum(
            "chqk,cqhd->ckhd",
            prob_block.astype(jnp.bfloat16),
            grad_heads,
            preferred_element_type=jnp.float32,
        )
        return (grad_query, (grad_key, grad_value))

    grad_query, (key_terms, value_terms) = lax.scan(
        key_step,
        jnp.zeros((clip_count, row_count, heads_local, HEAD_DIM), jnp.float32),
        (key_blocks, value_blocks),
    )
    grad_query = grad_query * score_scale
    key_terms = jnp.moveaxis(key_terms, 0, 1).reshape(clip_count, length, width_local)
    value_terms = jnp.moveaxis(value_terms, 0, 1).reshape(clip_count, length, width_local)
    grad_keys, grad_values = (
        lax.psum_scatter(
            key_terms.astype(jnp.bfloat16), "ctx", scatter_dimension=1, tiled=True
        ).astype(jnp.float32),
        lax.psum_scatter(
            value_terms.astype(jnp.bfloat16), "ctx", scatter_dimension=1, tiled=True
        ).astype(jnp.float32),
    )
    grad_q_pre = rotate_back(grad_query, cosines, sine_table).reshape(
        clip_count, row_count, width_local
    )
    grad_k_pre = rotate_back(
        grad_keys.reshape(clip_count, row_count, heads_local, HEAD_DIM), cosines, sine_table
    ).reshape(clip_count, row_count, width_local)
    grad_joined = jnp.stack([grad_q_pre, grad_k_pre, grad_values], axis=2).astype(jnp.bfloat16)
    grad_w_qkv = jnp.einsum(
        "csd,cskh->dkh", stored_acts["normed_low"], grad_joined, preferred_element_type=jnp.float32
    )
    grad_b_qkv = jnp.sum(grad_joined.astype(jnp.float32), axis=(0, 1))
    normed_term = jnp.einsum(
        "cskh,dkh->csd", grad_joined, w_qkv_all, preferred_element_type=jnp.float32
    )
    grad_normed = back_total(normed_term)
    grad_gain_one = jnp.sum(grad_normed * stored_acts["scaled_one"], axis=(0, 1))
    grad_shift_one = jnp.sum(grad_normed, axis=(0, 1))
    grad_tokens = grad_middle + norm_back(
        grad_normed, stored_acts["scaled_one"], stored_acts["inv_one"], gain_one
    )
    input_grad = lax.dynamic_slice_in_dim(grad_tokens, share_start, width_local, axis=2)
    summed = (
        lax.psum(grad_w_qkv.astype(jnp.bfloat16), "ctx").astype(jnp.float32),
        lax.psum(grad_w_out.astype(jnp.bfloat16), "ctx").astype(jnp.float32),
        lax.psum(grad_w_in.astype(jnp.bfloat16), "ctx").astype(jnp.float32),
        lax.psum(grad_w_back.astype(jnp.bfloat16), "ctx").astype(jnp.float32),
    )
    owned_grads = (
        lax.psum_scatter(
            summed[0].astype(jnp.bfloat16), "shard", scatter_dimension=0, tiled=True
        ).astype(jnp.float32),
        lax.psum_scatter(
            summed[1].astype(jnp.bfloat16), "shard", scatter_dimension=1, tiled=True
        ).astype(jnp.float32),
        lax.psum_scatter(
            summed[2].astype(jnp.bfloat16), "shard", scatter_dimension=0, tiled=True
        ).astype(jnp.float32),
        lax.psum_scatter(
            summed[3].astype(jnp.bfloat16), "shard", scatter_dimension=1, tiled=True
        ).astype(jnp.float32),
    )
    small_sums = lax.psum(
        (
            grad_gain_one,
            grad_shift_one,
            grad_b_qkv,
            grad_b_out,
            grad_gain_two,
            grad_shift_two,
            grad_b_in,
            grad_b_back,
        ),
        ("shard", "ctx"),
    )
    return (
        output,
        input_grad,
        small_sums[0],
        small_sums[1],
        owned_grads[0],
        small_sums[2],
        owned_grads[1],
        small_sums[3],
        small_sums[4],
        small_sums[5],
        owned_grads[2],
        small_sums[6],
        owned_grads[3],
        small_sums[7],
    )


LOG2E = 1.4426950408889634
BF = jnp.bfloat16
F32 = jnp.float32
VMEM_BYTES = 60 * 2**20


def dot_nt(a, b):
    return lax.dot_general(a, b, (((1,), (1,)), ((), ())), preferred_element_type=F32)


def dot_nn(a, b):
    return lax.dot_general(a, b, (((1,), (0,)), ((), ())), preferred_element_type=F32)


def dot_tn(a, b):
    return lax.dot_general(a, b, (((0,), (0,)), ((), ())), preferred_element_type=F32)


def whole(shape):
    return pl.BlockSpec(shape, lambda *_: (0,) * len(shape))


CHUNKS = ((0, 0), (0, 1), (1, 0), (1, 1))


def partner_lanes(tensor):
    segment = 2 * (HEAD_DIM // 3 // 2)
    halfway = segment // 2
    width = tensor.shape[1]
    lane = lax.broadcasted_iota(jnp.int32, tensor.shape, 1) % HEAD_DIM
    first = lane % segment < halfway
    return jnp.where(
        first, pltpu.roll(tensor, width - halfway, 1), pltpu.roll(tensor, halfway, 1)
    )


def norm_parts(own, other):
    total = 2 * own.shape[1]
    mean = (jnp.sum(own, 1, keepdims=True) + jnp.sum(other, 1, keepdims=True)) / total
    own, other = own - mean, other - mean
    spread = (
        jnp.sum(own * own, 1, keepdims=True) + jnp.sum(other * other, 1, keepdims=True)
    ) / total
    inv = lax.rsqrt(spread + EPSILON)
    return own * inv, other * inv, inv


def flip(value, bit):
    if bit == 1:
        return value + 1 - 2 * lax.rem(value, 2)
    return lax.rem(value + 2, 4)


def place():
    return tuple(lax.axis_index(name) for name in ("shard", "ctx", "tp"))


def piece_at(shard, tp, half, part):
    found = lax.rem(shard + 2 * lax.rem(tp + half, 2), 4)
    return flip(found, 1) if part else found


X, CORE, Y, YCORE, Z1, Z2, Z3 = range(7)


class Movers:
    def __init__(self, send_sems, recv_sems, local_sems):
        shard, ctx, tp = place()
        self.sems = (send_sems, recv_sems, local_sems)
        self.sent, self.kept = [], []
        self.partners = {
            X: {"tp": 1 - tp},
            CORE: {"ctx": flip(ctx, 1)},
            Y: {"ctx": flip(ctx, 2)},
            YCORE: {"ctx": flip(flip(ctx, 2), 1)},
            Z1: {"shard": flip(shard, 1)},
            Z2: {"shard": flip(shard, 2)},
            Z3: {"shard": flip(flip(shard, 2), 1)},
        }
        self.inner = jnp.logical_or(shard == 1, shard == 2)
        self.used = 0
        self.left = set()

    def barrier(self, names):
        barrier = pltpu.get_barrier_semaphore()
        for name in names:
            pl.semaphore_signal(
                barrier,
                inc=1,
                device_id=self.partners[name],
                device_id_type=pl.DeviceIdType.MESH,
            )
        pl.semaphore_wait(barrier, len(names))

    def remote(self, source, target, name, send_at, recv_at):
        return pltpu.make_async_remote_copy(
            src_ref=source,
            dst_ref=target,
            send_sem=self.sems[0].at[send_at],
            recv_sem=self.sems[1].at[recv_at],
            device_id=self.partners[name],
            device_id_type=pl.DeviceIdType.MESH,
        )

    def send(self, source, target, name):
        copy = self.remote(source, target, name, self.used, self.used)
        self.used += 1
        copy.start()
        self.sent.append([copy, False])
        return len(self.sent) - 1

    def arrive(self, *which):
        for at in which:
            if not self.sent[at][1]:
                self.sent[at][0].wait_recv()
                self.sent[at][1] = True

    def wait_sent(self, *which):
        for at in which:
            if at not in self.left:
                self.sent[at][0].wait_send()
                self.left.add(at)

    def keep(self, source, target):
        at = len(self.kept)
        copy = pltpu.make_async_copy(source, target, self.sems[2].at[at])
        copy.start()
        self.kept.append([copy, False])
        return at

    def kept_done(self, *which):
        for at in which:
            if not self.kept[at][1]:
                self.kept[at][0].wait()
                self.kept[at][1] = True

    def finish(self):
        self.arrive(*range(len(self.sent)))
        self.wait_sent(*range(len(self.sent)))
        self.kept_done(*range(len(self.kept)))


class Line:
    def __init__(self, mv, own, slot):
        self.mv, self.step = mv, 0
        at = mv.used
        mv.used += 5
        self.first = mv.remote(own, slot(1), Z1, at, at)
        self.middle = [
            mv.remote(own, slot(3), Z3, at + 1, at + 2),
            mv.remote(slot(1), slot(2), Z3, at + 2, at + 1),
            mv.remote(slot(3), slot(2), Z1, at + 3, at + 1),
            mv.remote(slot(2), slot(3), Z1, at + 4, at + 2),
        ]
        self.arrivals = {2: self.middle[1], 3: self.middle[0]}
        self.first.start()
        pl.when(mv.inner)(self.middle[0].start)

    def advance(self):
        self.step += 1
        if self.step == 1:
            self.first.wait_recv()
            pl.when(self.mv.inner)(self.middle[1].start)
            return
        arrival = self.arrivals[3 if self.step == 2 else 2]

        @pl.when(self.mv.inner)
        def _():
            arrival.wait_recv()
            self.middle[self.step].start()

    def done(self):
        while self.step < 3:
            self.advance()

        @pl.when(jnp.logical_not(self.mv.inner))
        def _():
            self.arrivals[2].wait_recv()
            self.arrivals[3].wait_recv()

    def finish(self):
        self.first.wait_send()

        @pl.when(self.mv.inner)
        def _():
            for copy in self.middle:
                copy.wait_send()


def first_body(*refs):
    (x_ref, wqkv_ref, wout_ref, win_ref, wback_ref, b_ref, ln_ref, bout_ref) = refs[:8]
    (xp_out, n_out, qkv_out, ot_out, lse_out, mo_out, mp_out, wq_out, wo, wi, wb, boutp_out, table_out) = refs[
        8:21
    ]
    (xall, nbuf, qkv, ot, vt, osc, wq, tables, send_sems, recv_sems, local_sems) = refs[21:]
    clips, rows, half = x_ref.shape
    width = half // 2
    lanes = tables.shape[3]
    hidden = wi.shape[3]
    shard, ctx, tp = place()
    mv = Movers(send_sems, recv_sems, local_sems)
    mv.barrier([X, CORE, Y, YCORE, Z1, Z2, Z3])
    cut = rows // 2

    x0 = [mv.send(x_ref.at[0], xall.at[0, 1, 0], X)]
    y0 = [mv.send(x_ref.at[0], xall.at[0, 0, 2], Y)]
    qkv_at = pl.ds(pl.multiple_of(ctx * lanes, lanes), lanes)
    wq_own = [
        mv.keep(wqkv_ref.at[i, :, qkv_at], wq.at[0, :, i * lanes : (i + 1) * lanes])
        for i in range(3)
    ]
    mv.kept_done(*wq_own)
    wq_line = Line(mv, wq.at[0], lambda k: wq.at[k])
    c0 = [mv.send(x_ref.at[0], xall.at[0, 0, 1], CORE)]
    own = [mv.keep(x_ref.at[b], xall.at[b, 0, 0]) for b in range(clips)]
    out_piece = wout_ref.at[pl.ds(pl.multiple_of(ctx * lanes, lanes), lanes), :]
    back_piece = wback_ref.at[pl.ds(pl.multiple_of(ctx * hidden, hidden), hidden), :]
    far_ctx = flip(ctx, 2)
    in_pieces = [
        win_ref.at[:, pl.ds(pl.multiple_of(at * hidden, hidden), hidden)] for at in (ctx, far_ctx)
    ]
    wo_x = mv.send(out_piece, wo.at[0, 0, 1], X)
    mv.send(bout_ref, boutp_out, X)
    wo_own = mv.keep(out_piece, wo.at[0, 0, 0])
    wi_own = [mv.keep(in_pieces[i], wi.at[2 * i, 0]) for i in range(2)]
    wb_own = mv.keep(back_piece, wb.at[0, 0])

    def forward(b, x, y):
        mv.arrive(x)
        size = cut if b == 0 else cut // 2
        low = mv.send(xall.at[b, 1, 0, :size], xall.at[b, 1, 2, :size], Y)
        near = [mv.send(xall.at[b, 1, 0], xall.at[b, 1, 1], CORE)]
        mv.arrive(y)
        high = mv.send(xall.at[b, 0, 2, size:], xall.at[b, 1, 2, size:], X)
        near.append(mv.send(xall.at[b, 0, 2], xall.at[b, 0, 3], CORE))
        return low, high, near

    def project(b, m):
        slot = m % 2
        for start in range(0, rows, cut):
            part = slice(start, start + cut)
            one, two, unused = norm_parts(
                xall[b, 0, m, part, :].astype(F32), xall[b, 1, m, part, :].astype(F32)
            )
            nbuf[slot, part, :half] = (one * ln_ref[0:1, :half] + ln_ref[1:2, :half]).astype(BF)
            nbuf[slot, part, half:] = (two * ln_ref[0:1, half:] + ln_ref[1:2, half:]).astype(BF)
        acc = b_ref[...]
        for h, j in CHUNKS:
            at = (2 * h + j) * width
            acc = acc + dot_nn(nbuf[slot, :, at : at + width], wq[piece_at(shard, tp, h, j)])
        cosines, sines = tables[0, m], tables[1, m]
        q, k = acc[:, :lanes], acc[:, lanes : 2 * lanes]
        place_rows = slice(m * rows, (m + 1) * rows)
        qkv[b, 0, place_rows, :] = (q * cosines + partner_lanes(q) * sines).astype(BF)
        qkv[b, 1, place_rows, :] = (k * cosines + partner_lanes(k) * sines).astype(BF)
        qkv[b, 2, place_rows, :] = acc[:, 2 * lanes :].astype(BF)
        return mv.keep(nbuf.at[slot], n_out.at[b, m])

    scale = HEAD_DIM ** (-0.5) * LOG2E
    head = lax.broadcasted_iota(jnp.int32, (rows, lanes), 1) // HEAD_DIM

    def turn_values(b):
        vt[:lanes, :] = qkv[b, 2].T
        vt[lanes:, :] = jnp.ones((vt.shape[0] - lanes, 4 * rows), BF)

    def attend(b, m):
        part = slice(m * rows, (m + 1) * rows)
        q = qkv[b, 0, part, :]
        keys = qkv[b, 1]
        outs = []
        for h in range(lanes // HEAD_DIM):
            q_head = jnp.where(head == h, q, jnp.zeros_like(q))
            scores = dot_nt(keys, q_head)
            top = jnp.max(scores, axis=0, keepdims=True) * scale
            probs = jnp.exp2(scores * scale - top).astype(BF)
            acc = dot_nn(vt[...], probs)
            total = acc[lanes : lanes + 1, :]
            outs.append(acc[h * HEAD_DIM : (h + 1) * HEAD_DIM, :] / total)
            lse_out[b, h : h + 1, part] = top + jnp.log2(total)
        result = jnp.concatenate(outs, axis=0)
        ot[b, :, part] = result
        osc[b, m] = result.T.astype(BF)
        if m == 0:
            return mv.keep(osc.at[b, 0], mo_out.at[b, 0])
        return mv.send(osc.at[b, m], mo_out.at[b, m], (None, CORE, Y, YCORE)[m])

    token = lax.broadcasted_iota(jnp.int32, (rows, lanes), 0)
    column = lax.broadcasted_iota(jnp.int32, (rows, lanes), 1) % HEAD_DIM
    segment = 2 * (HEAD_DIM // 3 // 2)
    halfway = segment // 2
    within = column % segment
    frequency = jnp.exp(
        (within % halfway).astype(F32) * (-math.log(10000.0) / halfway)
    )
    sign = jnp.where(within < halfway, -1.0, 1.0)
    active = column < 3 * segment

    def turn(position):
        angle = position.astype(F32) * frequency
        return jnp.where(active, jnp.cos(angle), 1.0), jnp.where(active, jnp.sin(angle) * sign, 0.0)

    def turn_frame(frame):
        angle = frame.astype(F32) * frequency[:8]
        cosine, sine = jnp.cos(angle)[:1], (jnp.sin(angle) * sign[:8])[:1]
        return cosine, sine

    start = [at * rows for at in (ctx, flip(ctx, 1), flip(ctx, 2), flip(flip(ctx, 2), 1))]
    if rows % (GH * GW) == 0:
        tables_in = turn(
            jnp.where(column < 2 * segment, token // GW % GH, token % GW)
        )
        for m in range(4):
            for at in range(0, rows, GH * GW):
                part = slice(at, at + GH * GW)
                frame = turn_frame((start[m] + at) // (GH * GW))
                first = column[part] < segment
                for i in range(2):
                    tables[i, m, part, :] = jnp.where(first, frame[i], tables_in[i][part])
    else:
        for m in range(4):
            at = start[m] + token
            both = turn(
                jnp.where(
                    column < segment,
                    at // (GH * GW),
                    jnp.where(column < 2 * segment, at // GW % GH, at % GW),
                )
            )
            for i in range(2):
                tables[i, m] = both[i]
    mv.keep(tables, table_out)

    wq_line.advance()
    wb_line = Line(mv, back_piece, lambda k: wb.at[0, k])
    wq_line.advance()
    low0, high0, near0 = forward(0, x0[0], y0[0])
    wq_line.advance()
    x1 = mv.send(x_ref.at[1], xall.at[1, 1, 0], X)
    y1 = mv.send(x_ref.at[1], xall.at[1, 0, 2], Y)
    c1 = mv.send(x_ref.at[1], xall.at[1, 0, 1], CORE)
    mv.keep(xall.at[0, 1, 0], xp_out.at[0])
    wb_line.advance()
    wi_near = Line(mv, in_pieces[0], lambda k: wi.at[0, k])
    wq_line.done()
    mv.kept_done(own[0])
    mv.keep(wq, wq_out)
    n_copy = [project(0, 0)]
    wb_line.advance()
    mv.arrive(c0[0], near0[0])
    n_copy.append(project(0, 1))
    mv.arrive(low0, high0)
    near0.append(mv.send(xall.at[0, 1, 2], xall.at[0, 1, 3], CORE))
    wb_line.advance()
    wi_near.advance()
    mv.kept_done(n_copy[0])
    n_copy.append(project(0, 2))
    mv.arrive(wo_x)
    mv.kept_done(wo_own)
    wo_line = Line(mv, wo.at[0, 0], lambda k: wo.at[0, k])
    mv.arrive(near0[1], near0[2])
    mv.kept_done(n_copy[1])
    n_copy.append(project(0, 3))
    mv.keep(qkv.at[0], qkv_out.at[0])
    low1, high1, near1 = forward(1, x1, y1)
    mv.keep(xall.at[1, 1, 0], xp_out.at[1])
    wi_near.advance()
    wi_far = Line(mv, in_pieces[1], lambda k: wi.at[2, k])
    turn_values(0)
    m0 = {2: attend(0, 2)}
    mv.arrive(low1, high1)
    near1.append(mv.send(xall.at[1, 1, 2], xall.at[1, 1, 3], CORE))
    wb_line.done()
    mv.kept_done(wb_own)
    wb_far = mv.send(wb.at[0], wb.at[2], Y)
    mv.send(wb.at[0], wb.at[1], CORE)
    wi_near.advance()
    wo_line.advance()
    m0[3] = attend(0, 3)
    wi_far.advance()
    wo_line.advance()
    m0[1] = attend(0, 1)
    wo_line.advance()
    wi_far.advance()
    m0[0] = attend(0, 0)
    wi_far.advance()
    mv.keep(ot.at[0], ot_out.at[0])
    mv.arrive(c1, *near1)
    mv.kept_done(own[1], n_copy[2])
    n_copy.append(project(1, 0))
    mv.arrive(m0[2], m0[1], m0[3])
    mv.kept_done(m0[0])
    mv.send(mo_out.at[0], mp_out.at[0], X)
    mv.kept_done(n_copy[3])
    n_copy.append(project(1, 1))
    wo_line.done()
    wo_far = mv.send(wo.at[0], wo.at[2], Y)
    mv.send(wo.at[0], wo.at[1], CORE)
    mv.kept_done(n_copy[4])
    n_copy.append(project(1, 2))
    mv.kept_done(n_copy[5])
    n_copy.append(project(1, 3))
    wi_near.done()
    mv.kept_done(wi_own[0])
    mv.send(wi.at[0], wi.at[1], CORE)
    mv.keep(qkv.at[1], qkv_out.at[1])
    turn_values(1)
    m1 = {2: attend(1, 2)}
    mv.arrive(wb_far)
    mv.send(wb.at[2], wb.at[3], CORE)
    m1[3] = attend(1, 3)
    mv.arrive(wo_far)
    mv.send(wo.at[2], wo.at[3], CORE)
    m1[1] = attend(1, 1)
    m1[0] = attend(1, 0)
    mv.keep(ot.at[1], ot_out.at[1])
    mv.kept_done(m1[0])
    mv.send(mo_out.at[1, 0], mp_out.at[1, 0], X)
    for m in (1, 2, 3):
        mv.arrive(m1[m])
        mv.send(mo_out.at[1, m], mp_out.at[1, m], X)
    wi_far.done()
    mv.kept_done(wi_own[1])
    mv.send(wi.at[2], wi.at[3], CORE)
    for line in (wq_line, wb_line, wi_near, wo_line, wi_far):
        line.finish()
    mv.finish()


ANY = pl.BlockSpec(memory_space=pl.ANY)


def first_call(x, w_qkv, w_out, w_in, w_back, b, ln, b_out):
    clips, rows, half = x.shape
    width = half // 2
    lanes = half // 4
    hidden = w_in.shape[1] // 4
    outs = [
        ((clips, rows, half), BF),
        ((clips, 4, rows, 2 * half), BF),
        ((clips, 3, 4 * rows, lanes), BF),
        ((clips, lanes, 4 * rows), F32),
        ((clips, lanes // HEAD_DIM, 4 * rows), F32),
        ((clips, 4, rows, lanes), BF),
        ((clips, 4, rows, lanes), BF),
        ((4, width, 3 * lanes), BF),
        ((4, 4, 2, lanes, width), BF),
        ((4, 4, width, hidden), BF),
        ((4, 4, hidden, width), BF),
        (b_out.shape, BF),
        ((2, 4, rows, lanes), F32),
    ]
    out_specs = [ANY] * len(outs)
    out_specs[4] = whole(outs[4][0])
    return pl.pallas_call(
        first_body,
        in_specs=[ANY] * 5 + [whole(b.shape), whole(ln.shape), ANY],
        out_specs=out_specs,
        out_shape=[jax.ShapeDtypeStruct(shape, kind) for shape, kind in outs],
        scratch_shapes=[
            pltpu.VMEM((clips, 2, 4, rows, half), BF),
            pltpu.VMEM((2, rows, 2 * half), BF),
            pltpu.VMEM((clips, 3, 4 * rows, lanes), BF),
            pltpu.VMEM((clips, lanes, 4 * rows), F32),
            pltpu.VMEM((lanes + 16, 4 * rows), BF),
            pltpu.VMEM((clips, 4, rows, lanes), BF),
            pltpu.VMEM((4, width, 3 * lanes), BF),
            pltpu.VMEM((2, 4, rows, lanes), F32),
            pltpu.SemaphoreType.DMA((64,)),
            pltpu.SemaphoreType.DMA((64,)),
            pltpu.SemaphoreType.DMA((40,)),
        ],
        compiler_params=pltpu.CompilerParams(
            vmem_limit_bytes=VMEM_BYTES, collective_id=1, has_side_effects=True
        ),
        name="project_and_attend",
    )(x, w_qkv, w_out, w_in, w_back, b, ln, b_out)


def chunk_of(shard, k):
    found = flip(shard, 2) if k & 2 else shard
    return flip(found, 1) if k & 1 else found


def side_by_side(parts):
    return jnp.concatenate(parts, axis=1)


def second_body(*refs):
    (x_ref, xp_ref, c_ref, mo_ref, mp_ref, wo_hbm, wi_hbm, wb_hbm, qkv_hbm, ot_hbm) = refs[:10]
    (ln_ref, bin_ref, bout_ref, boutp_ref, bback_ref, lse_ref) = refs[10:16]
    (y_out, other_out, gmid_out, d_out, keep_out, near_out, far_out, go_out) = refs[16:24]
    (dqt_out, dk_out, dv_out, midsum_out, insum_out, backsum_out) = refs[24:30]
    (xs, cs, ms, wo, wi, wb, mid, sec, act, gin, outs, ybuf, gs, gsr, gmid, gb, gm) = refs[30:47]
    (wg, wgnear, wgo, turned, ot, dqt, delta, dks, dvs, send_sems, recv_sems, local_sems) = refs[47:]
    clips, rows, half = x_ref.shape
    width = half // 2
    lanes = mo_ref.shape[3]
    hidden = wi.shape[3]
    shard, ctx, tp = place()
    mv = Movers(send_sems, recv_sems, local_sems)
    ks = range(4)
    own_k = [piece_at(shard, tp, 0, j) for j in range(2)]
    other_k = [piece_at(shard, tp, 1, j) for j in range(2)]

    def fetch(b):
        return [
            mv.keep(mo_ref.at[b], ms.at[b, 0]),
            mv.keep(mp_ref.at[b], ms.at[b, 1]),
            mv.keep(x_ref.at[b], xs.at[b, 0]),
            mv.keep(xp_ref.at[b], xs.at[b, 1]),
            mv.keep(c_ref.at[b], cs.at[b, 0]),
        ]

    got = [fetch(0)]
    got_wo = mv.keep(wo_hbm, wo)
    got_wi = [mv.keep(wi_hbm.at[m], wi.at[m]) for m in ks]
    got_wb = [mv.keep(wb_hbm.at[m], wb.at[m]) for m in ks]
    got.append(fetch(1))
    mv.barrier([X, CORE, Y, YCORE])
    cot_in = [mv.send(c_ref.at[b], cs.at[b, 1], X) for b in range(clips)]

    def row(which, k):
        return ln_ref[pl.ds(4 * which + chunk_of(shard, k), 1), :]

    def statistics(b):
        total = 4 * width
        mean = sum(jnp.sum(mid[b, k], 1, keepdims=True) for k in ks) / total
        spread = sum(jnp.sum((mid[b, k] - mean) ** 2, 1, keepdims=True) for k in ks) / total
        return mean, lax.rsqrt(spread + EPSILON)

    y_put = []

    def block(b):
        mv.kept_done(*got[b])
        mv.kept_done(got_wo)
        mixed = side_by_side([ms[b, side, m] for side in range(2) for m in ks])
        for k in ks:
            weight = jnp.concatenate([wo[m, k, side] for side in range(2) for m in ks], axis=0)
            mid[b, k] = dot_nn(mixed, weight)
        for j in range(2):
            part = slice(j * width, (j + 1) * width)
            mid[b, own_k[j]] += xs[b, 0, :, part].astype(F32) + bout_ref[0:1, part].astype(F32)
            mid[b, other_k[j]] += xs[b, 1, :, part].astype(F32) + boutp_ref[0:1, part].astype(F32)
        mean, inv = statistics(b)
        for k in ks:
            sec[b, k] = ((mid[b, k] - mean) * inv * row(0, k) + row(1, k)).astype(BF)
        mv.arrive(cot_in[b])
        for j in range(2):
            part = slice(j * width, (j + 1) * width)
            gb[b, own_k[j]] = cs[b, 0, :, part]
            gb[b, other_k[j]] = cs[b, 1, :, part]
        normed = side_by_side([sec[b, k] for k in ks])
        cot = side_by_side([gb[b, k] for k in ks])
        for m in ks:
            mv.kept_done(got_wi[m])
            at = (ctx, flip(ctx, 1), flip(ctx, 2), flip(flip(ctx, 2), 1))[m]
            inner = bin_ref[pl.ds(at, 1), :] + dot_nn(normed, wi[m].reshape(4 * width, hidden))
            mv.kept_done(got_wb[m])
            grad = dot_nt(cot, side_by_side([wb[m, k] for k in ks]))
            phi = 0.5 + 0.5 * lax.erf(inner * (0.5**0.5))
            act[b, m] = (inner * phi).astype(BF)
            slope = phi + inner * (jnp.exp(-0.5 * inner * inner) * ((2 * math.pi) ** -0.5))
            grad = (grad * slope).astype(BF)
            gin[b, m] = grad
            sums = jnp.sum(grad.astype(F32), axis=0, keepdims=True)
            if b == 0:
                insum_out[pl.ds(at, 1), :] = sums
            else:
                insum_out[pl.ds(at, 1), :] += sums
        back = side_by_side([gin[b, m] for m in ks])
        sent = []
        for k in ks:
            gs[b, k] = dot_nt(back, side_by_side([wi[m, k] for m in ks])).astype(BF)
            sent.append(mv.send(gs.at[b, k], gsr.at[b, k], X))
        active = side_by_side([act[b, m] for m in ks])
        mv.kept_done(*y_put)
        for h, which in enumerate((own_k, other_k)):
            for j in range(2):
                weight = jnp.concatenate([wb[m, which[j]] for m in ks], axis=0)
                part = slice(j * width, (j + 1) * width)
                term = dot_nn(active, weight)
                if h == 0:
                    term = term + mid[b, own_k[j]] + bback_ref[0:1, part].astype(F32)
                    ybuf[:, part] = term
                else:
                    outs[b, :, part] = term.astype(BF)
        y_put.append(mv.keep(ybuf, y_out.at[b]))
        mv.keep(outs.at[b], other_out.at[b])
        return sent

    put = []

    def branch(b, sent):
        mv.arrive(*sent[:4])
        mv.kept_done(*put)
        total = 4 * width
        mean, inv = statistics(b)
        mean_one = mean_two = 0.0
        for k in ks:
            unit = (mid[b, k] - mean) * inv
            grad = gs[b, k].astype(F32) + gsr[b, k].astype(F32)
            gain_sum = jnp.sum(grad * unit, 0, keepdims=True)
            shift_sum = jnp.sum(grad, 0, keepdims=True)
            for i, term in enumerate((gain_sum, shift_sum)):
                place_row = pl.ds(4 * i + chunk_of(shard, k), 1)
                if b == 0:
                    midsum_out[place_row, :] = term
                else:
                    midsum_out[place_row, :] += term
            scaled = grad * row(0, k)
            mean_one = mean_one + jnp.sum(scaled, 1, keepdims=True)
            mean_two = mean_two + jnp.sum(scaled * unit, 1, keepdims=True)
        mean_one, mean_two = mean_one / total, mean_two / total
        for k in ks:
            unit = (mid[b, k] - mean) * inv
            grad = gs[b, k].astype(F32) + gsr[b, k].astype(F32)
            full = gb[b, k].astype(F32) + inv * (grad * row(0, k) - mean_one - unit * mean_two)
            gmid[k] = full
            low = full.astype(BF)
            xs[b, k // 2, :, (k % 2) * width : (k % 2 + 1) * width] = low
            sec_sum = jnp.sum(low.astype(F32), 0, keepdims=True)
            place_row = pl.ds(8 + chunk_of(shard, k), 1)
            if b == 0:
                midsum_out[place_row, :] = sec_sum
            else:
                midsum_out[place_row, :] += sec_sum
        low = side_by_side([xs[b, 0], xs[b, 1]])
        weight = side_by_side([jnp.concatenate([wo[m, k, 0] for m in ks], axis=0) for k in ks])
        mixed = dot_nt(low, weight).astype(BF)
        for m in ks:
            gm[b, m] = mixed[:, m * lanes : (m + 1) * lanes]
        remote = [mv.send(gm.at[b, 2], d_out.at[b, 2], Y)]
        remote.append(mv.send(gm.at[b, 3], d_out.at[b, 3], YCORE))
        remote.append(mv.send(gm.at[b, 1], d_out.at[b, 1], CORE))
        local = mv.keep(gm.at[b, 0], d_out.at[b, 0])
        for j in range(2):
            put.append(mv.keep(gmid.at[own_k[j]], gmid_out.at[b, j]))
        cot_sum = jnp.sum(cs[b, 0].astype(F32), 0, keepdims=True)
        if b == 0:
            backsum_out[...] = cot_sum
        else:
            backsum_out[...] += cot_sum
        return remote, local

    def tokens(ref, *at):
        return jnp.concatenate([ref[(b,) + at] for b in range(clips)], axis=0)

    def big_grads(m, slot):
        cot = side_by_side([tokens(gb, k) for k in ks])
        back = dot_tn(tokens(act, m), cot).astype(BF)
        own = dot_nn(turned[...], tokens(gin, m)).astype(BF)
        for k in ks:
            wg[slot, k, :hidden, :] = back[:, k * width : (k + 1) * width]
            wg[slot, k, hidden : hidden + width, :] = own[k * width : (k + 1) * width, :width]
            wg[slot, k, hidden + width :, :] = own[k * width : (k + 1) * width, width:]

    def held(kind, i):
        place_at = ((0, i, 0), (0, i, 1), (1, i, 0), (1, i, 1))
        m, k, side = place_at[kind]
        return wb.at[m, k, :, side * lanes : (side + 1) * lanes]

    def masked(kind, h, i):
        return wb.at[2 + kind, i, :, h * lanes : (h + 1) * lanes]

    heads = lanes // HEAD_DIM
    scale = HEAD_DIM ** (-0.5)

    def load_attention():
        for i in ks:
            part = slice(i * rows, (i + 1) * rows)
            attention_in.append(mv.keep(qkv_hbm.at[0, 1, part, :], held(0, i)))
            attention_in.append(mv.keep(qkv_hbm.at[0, 2, part, :], held(1, i)))
            attention_in.append(mv.keep(qkv_hbm.at[0, 0, part, :], held(2, i)))
        attention_in.append(mv.keep(ot_hbm.at[0], ot))

    attention_in = []

    def prepare(arrivals):
        remote, local = arrivals
        mv.arrive(*remote)
        mv.kept_done(local)
        mv.kept_done(*[mv.keep(d_out.at[0, i], held(3, i)) for i in ks])
        mv.kept_done(*attention_in)
        head = lax.broadcasted_iota(jnp.int32, (rows, lanes), 1) // HEAD_DIM
        for i in ks:
            part = slice(i * rows, (i + 1) * rows)
            q, grad = held(2, i)[...], held(3, i)[...]
            for h in range(heads):
                masked(0, h, i)[...] = jnp.where(head == h, q, jnp.zeros_like(q))
                masked(1, h, i)[...] = jnp.where(head == h, grad, jnp.zeros_like(grad))
            products = grad.astype(F32).T * ot[:, part]
            for h in range(heads):
                delta[h : h + 1, part] = jnp.sum(
                    products[h * HEAD_DIM : (h + 1) * HEAD_DIM], axis=0, keepdims=True
                )
        dqt[...] = jnp.zeros_like(dqt)

    attention_put = []

    def attend_back(m):
        keys, values = held(0, m)[...], held(1, m)[...]
        dk, dv = attend_back_block(
            keys,
            values,
            lambda h, i: masked(0, h, i)[...],
            lambda h, i: masked(1, h, i)[...],
            lambda h, part: lse_ref[0, h : h + 1, part],
            delta,
            dqt,
            rows,
        )
        if m >= 2:
            mv.kept_done(*attention_put[2 * m - 4 : 2 * m - 2])
        dks[m % 2] = dk * scale
        dvs[m % 2] = dv.astype(BF)
        attention_put.append(mv.keep(dks.at[m % 2], dk_out.at[m]))
        attention_put.append(mv.keep(dvs.at[m % 2], dv_out.at[m]))

    first = block(0)
    second = block(1)
    load_attention()
    for k in ks:
        turned[k * width : (k + 1) * width, :] = tokens(sec, k).T
    big_grads(3, 0)
    near = mv.send(wg.at[0], wgnear, CORE)
    arrivals = branch(0, first)
    big_grads(2, 1)
    mv.arrive(near)
    for k in ks:
        wg[1, k] = (wg[1, k].astype(F32) + wgnear[k].astype(F32)).astype(BF)
    far = mv.send(wg.at[1], far_out, Y)
    prepare(arrivals)
    attend_back(0)
    attend_back(1)
    mv.wait_sent(near)
    big_grads(1, 0)
    mv.send(wg.at[0], near_out, CORE)
    attend_back(2)
    attend_back(3)
    mv.keep(dqt, dqt_out)
    branch(1, second)
    grads = side_by_side([tokens(xs, i) for i in range(2)])
    for m in ks:
        mixed = jnp.concatenate([ms[b, 0, m] for b in range(clips)], axis=0)
        out = dot_tn(mixed, grads).astype(BF)
        for k in ks:
            wgo[m, k] = out[:, k * width : (k + 1) * width]
    mv.keep(wgo, go_out)
    mv.wait_sent(far)
    big_grads(0, 1)
    mv.keep(wg.at[1], keep_out)
    mv.finish()


def attend_back_block(keys, values, query, grad_out, log_total, delta, dqt, rows):
    scale = HEAD_DIM ** (-0.5)
    flat_keys = keys.T
    row = lax.broadcasted_iota(jnp.int32, flat_keys.shape, 0) // HEAD_DIM
    dk = dv = None
    for h in range(keys.shape[1] // HEAD_DIM):
        turned = jnp.where(row == h, flat_keys, jnp.zeros_like(flat_keys))
        for i in range(4):
            part = slice(i * rows, (i + 1) * rows)
            q, grad = query(h, i), grad_out(h, i)
            probs = jnp.exp2(dot_nt(keys, q) * (scale * LOG2E) - log_total(h, part))
            slope = (probs * (dot_nt(values, grad) - delta[h : h + 1, part])).astype(BF)
            value_term, key_term = dot_nn(probs.astype(BF), grad), dot_nn(slope, q)
            dk = key_term if dk is None else dk + key_term
            dv = value_term if dv is None else dv + value_term
            dqt[:, part] += dot_nn(turned, slope)
    return dk, dv


def second_call(x, xp, c, mo, mp, wo, wi, wb, qkv, ot, ln, b_in, b_out, b_other, b_back, lse):
    clips, rows, half = x.shape
    width = half // 2
    lanes = mo.shape[3]
    hidden = wi.shape[3]
    tall = hidden + 2 * width
    heads = lanes // HEAD_DIM
    outs = [
        ((clips, rows, half), F32),
        ((clips, rows, half), BF),
        ((clips, 2, rows, width), F32),
        ((clips, 4, rows, lanes), BF),
        ((4, tall, width), BF),
        ((4, tall, width), BF),
        ((4, tall, width), BF),
        ((4, 4, lanes, width), BF),
        ((lanes, 4 * rows), F32),
        ((4, rows, lanes), F32),
        ((4, rows, lanes), BF),
        ((12, width), F32),
        ((4, hidden), F32),
        ((1, half), F32),
    ]
    small = [ln, b_in, b_out, b_other, b_back, lse]
    vmem = lambda kind, *shape: pltpu.VMEM(shape, kind)
    return pl.pallas_call(
        second_body,
        in_specs=[ANY] * 10 + [whole(a.shape) for a in small],
        out_specs=[ANY] * 11 + [whole(o[0]) for o in outs[11:]],
        out_shape=[jax.ShapeDtypeStruct(shape, kind) for shape, kind in outs],
        scratch_shapes=[
            vmem(BF, clips, 2, rows, half),
            vmem(BF, clips, 2, rows, half),
            vmem(BF, clips, 2, 4, rows, lanes),
            vmem(BF, *wo.shape),
            vmem(BF, *wi.shape),
            vmem(BF, *wb.shape),
            vmem(F32, clips, 4, rows, width),
            vmem(BF, clips, 4, rows, width),
            vmem(BF, clips, 4, rows, hidden),
            vmem(BF, clips, 4, rows, hidden),
            vmem(BF, clips, rows, half),
            vmem(F32, rows, half),
            vmem(BF, clips, 4, rows, width),
            vmem(BF, clips, 4, rows, width),
            vmem(F32, 4, rows, width),
            vmem(BF, clips, 4, rows, width),
            vmem(BF, clips, 4, rows, lanes),
            vmem(BF, 2, 4, tall, width),
            vmem(BF, 4, tall, width),
            vmem(BF, 4, 4, lanes, width),
            vmem(BF, 4 * width, clips * rows),
            vmem(F32, lanes, 4 * rows),
            vmem(F32, lanes, 4 * rows),
            vmem(F32, heads, 4 * rows),
            vmem(F32, 2, rows, lanes),
            vmem(BF, 2, rows, lanes),
            pltpu.SemaphoreType.DMA((24,)),
            pltpu.SemaphoreType.DMA((24,)),
            pltpu.SemaphoreType.DMA((72,)),
        ],
        compiler_params=pltpu.CompilerParams(
            vmem_limit_bytes=VMEM_BYTES, collective_id=2, has_side_effects=True
        ),
        name="layer_middle",
    )(x, xp, c, mo, mp, wo, wi, wb, qkv, ot, *small)


def third_body(*refs):
    (qkv_hbm, ot_hbm, d_hbm, t_hbm, wq_hbm, n_hbm, keep_hbm, near_hbm, far_hbm, go_hbm) = refs[:10]
    (dqt_hbm, dk_hbm, dv_hbm, other_hbm, x_hbm, xp_hbm) = refs[10:16]
    (lse_ref, ln_ref, midsum_ref, insum_ref, backsum_ref) = refs[16:21]
    (ig_out, arrived_out, dense_out, qdense_out, early_out, ln1_out, qsum_out) = refs[21:28]
    (qkv, ot, d, tables, wq, qh, dh, delta, dqt, gj, pk, ps, near, hop, last) = refs[28:43]
    (nbuf, qacc, qs, qz, gk, gnear, gfar, gz, go, gonear, dk0, dqt0, xs, stats) = refs[43:57]
    (stats_in, early, early_in, late, late_in, late_x, send_sems, recv_sems, local_sems) = refs[57:]
    unused, count, lanes = qkv.shape
    clips = x_hbm.shape[0]
    rows = count // 4
    width = wq.shape[1]
    half = 2 * width
    heads = lanes // HEAD_DIM
    cut = rows // 2
    shard, ctx, tp = place()
    mv = Movers(send_sems, recv_sems, local_sems)
    ks = range(4)
    zs = (Z1, Z2, Z3)
    scale = HEAD_DIM ** (-0.5)

    tall = keep_hbm.shape[1]
    got_first = [
        mv.keep(dqt_hbm, dqt0),
        mv.keep(dk_hbm, dk0),
        mv.keep(dv_hbm, gj.at[0, :, :, 2 * lanes :]),
    ]
    got_w = [mv.keep(t_hbm, tables), mv.keep(wq_hbm, wq)]
    got_g = [
        mv.keep(source.at[k], target.at[k, :tall])
        for k in (1, 2, 3, 0)
        for source, target in ((keep_hbm, gk), (near_hbm, gnear), (far_hbm, gfar))
    ]
    got_go = [mv.keep(go_hbm.at[2 * i], go.at[i]) for i in range(2)]
    got = [
        mv.keep(qkv_hbm.at[1], qkv),
        mv.keep(d_hbm.at[1], d),
        mv.keep(ot_hbm.at[1], ot),
    ]
    got_n = [mv.keep(n_hbm.at[0, m], nbuf.at[m]) for m in range(2)]
    got_x = [mv.keep(x_hbm, xs.at[0]), mv.keep(xp_hbm, xs.at[1])]
    mv.barrier([X, CORE, Y, YCORE, Z1, Z2, Z3])
    go_core = [mv.send(go_hbm.at[2 * i + 1], gonear.at[i], CORE) for i in range(2)]

    early[0, :12, :] = midsum_ref[...]
    for m in ks:
        for j in range(2):
            part = slice(j * width, (j + 1) * width)
            early[0, 12 + 2 * m + j : 13 + 2 * m + j, :] = insum_ref[m : m + 1, part]
    for j in range(2):
        early[0, 20 + j : 21 + j, :] = backsum_ref[:, j * width : (j + 1) * width]
    early[0, 22:, :] = jnp.zeros((2, width), F32)
    early_z = [mv.send(early.at[0], early_in.at[i], name) for i, name in enumerate(zs)]

    def prepare():
        mv.kept_done(*got)
        head = lax.broadcasted_iota(jnp.int32, (rows, lanes), 1) // HEAD_DIM
        for m in ks:
            part = slice(m * rows, (m + 1) * rows)
            q, grad = qkv[0, part, :], d[m]
            for h in range(heads):
                qh[h, part, :] = jnp.where(head == h, q, jnp.zeros_like(q))
                dh[h, part, :] = jnp.where(head == h, grad, jnp.zeros_like(grad))
            products = grad.astype(F32).T * ot[:, part]
            for h in range(heads):
                delta[h : h + 1, part] = jnp.sum(
                    products[h * HEAD_DIM : (h + 1) * HEAD_DIM], axis=0, keepdims=True
                )
        dqt[...] = jnp.zeros_like(dqt)

    def attend_back(m):
        mine = slice(m * rows, (m + 1) * rows)
        dk, dv = attend_back_block(
            qkv[1, mine, :],
            qkv[2, mine, :],
            lambda h, i: qh[h, i * rows : (i + 1) * rows, :],
            lambda h, i: dh[h, i * rows : (i + 1) * rows, :],
            lambda h, part: lse_ref[1, h : h + 1, part],
            delta,
            dqt,
            rows,
        )
        dk = dk * scale
        dk = dk * tables[0, m] + partner_lanes(dk * tables[1, m])
        gj[1, m, :, lanes : 2 * lanes] = dk.astype(BF)
        gj[1, m, :, 2 * lanes :] = dv.astype(BF)

    sums = [0.0, 0.0, 0.0]

    def join(b):
        mv.kept_done(*got_w, *got_first)
        sent = {}
        for m in (3, 1, 2, 0):
            part = slice(m * rows, (m + 1) * rows)
            dq = ((dqt0, dqt)[b][:, part] * scale).T
            if b == 0:
                dk = dk0[m]
                dk = dk * tables[0, m] + partner_lanes(dk * tables[1, m])
                gj[0, m, :, lanes : 2 * lanes] = dk.astype(BF)
            dq = dq * tables[0, m] + partner_lanes(dq * tables[1, m])
            gj[b, m, :, :lanes] = dq.astype(BF)
            for i in range(3):
                low = gj[b, m, :, i * lanes : (i + 1) * lanes].astype(F32)
                sums[i] = sums[i] + jnp.sum(low, axis=0, keepdims=True)
            for h in (1, 0):
                target = (pk, ps)[m % 2]
                for j in range(2):
                    term = dot_nt(gj[b, m], wq[piece_at(shard, tp, h, j)])
                    target[b, m // 2, h, :, j * width : (j + 1) * width] = term.astype(BF)
                if m % 2:
                    sent[m // 2, h] = mv.send(ps.at[b, m // 2, h], near.at[b, m // 2, h], CORE)
        return sent

    def first_hop(b, sent):
        mv.arrive(sent[1, 1])
        pk[b, 1, 1] = (pk[b, 1, 1].astype(F32) + near[b, 1, 1].astype(F32)).astype(BF)
        low = mv.send(pk.at[b, 1, 1, :cut], hop.at[b, 0], X)
        high = mv.send(pk.at[b, 1, 1, cut:], hop.at[b, 1], Y)
        return low, high

    def second_hop(b, sent, hops):
        mv.arrive(sent[1, 0], sent[0, 1])
        mv.arrive(hops[0])
        pk[b, 1, 0, :cut] = (
            pk[b, 1, 0, :cut].astype(F32)
            + near[b, 1, 0, :cut].astype(F32)
            + hop[b, 0].astype(F32)
        ).astype(BF)
        pk[b, 1, 0, cut:] = (
            pk[b, 1, 0, cut:].astype(F32) + near[b, 1, 0, cut:].astype(F32)
        ).astype(BF)
        far = mv.send(pk.at[b, 1, 0], last.at[b, 0], Y)
        mv.arrive(hops[1])
        pk[b, 0, 1, :cut] = (
            pk[b, 0, 1, :cut].astype(F32) + near[b, 0, 1, :cut].astype(F32)
        ).astype(BF)
        pk[b, 0, 1, cut:] = (
            pk[b, 0, 1, cut:].astype(F32)
            + near[b, 0, 1, cut:].astype(F32)
            + hop[b, 1].astype(F32)
        ).astype(BF)
        other = mv.send(pk.at[b, 0, 1], last.at[b, 1], X)
        return far, other

    def norm_one(b):
        mv.kept_done(*got_x)
        own, unused, inv = norm_parts(xs[0, b].astype(F32), xs[1, b].astype(F32))
        return own, inv

    gains = [0.0, 0.0]
    gain_own = jnp.where(tp == 0, ln_ref[:, :half], ln_ref[:, half:])

    def finish_sum(b, sent, lasts):
        mv.arrive(sent[0, 0], *lasts)
        own, inv = norm_one(b)
        grad = (
            pk[b, 0, 0].astype(F32)
            + near[b, 0, 0].astype(F32)
            + last[b, 0].astype(F32)
            + last[b, 1].astype(F32)
        )
        gains[0] = gains[0] + jnp.sum(grad * own, axis=0, keepdims=True)
        gains[1] = gains[1] + jnp.sum(grad, axis=0, keepdims=True)
        scaled = grad * gain_own
        ig_out[b] = scaled
        lane = lax.broadcasted_iota(jnp.int32, (rows, 128), 1)
        both = jnp.where(
            lane == 0,
            jnp.sum(scaled, 1, keepdims=True),
            jnp.where(lane == 1, jnp.sum(scaled * own, 1, keepdims=True), 0.0),
        )
        stats[b] = both.T[:8]
        return mv.send(stats.at[b], stats_in.at[b], X)

    def finish_grad(b, sent):
        mv.arrive(sent)
        own, inv = norm_one(b)
        total = stats[b] + stats_in[b]
        both = jnp.concatenate([total, jnp.zeros((120, rows), F32)], axis=0).T / (2 * half)
        grad = inv * (ig_out[b] - both[:, 0:1] - own * both[:, 1:2])
        ig_out[b] = grad

    def qkv_grads(b):
        for m in ks:
            at = 4 * b + m
            mv.kept_done(got_n[at])
            slot = at % 2
            for h, j in CHUNKS:
                cols = slice((2 * h + j) * width, (2 * h + j + 1) * width)
                term = dot_tn(nbuf[slot, :, cols], gj[b, m])
                if at == 0:
                    qacc[2 * h + j] = term
                else:
                    qacc[2 * h + j] += term
            if at + 2 < 8:
                got_n.append(mv.keep(n_hbm.at[(at + 2) // 4, (at + 2) % 4], nbuf.at[slot]))

    def add_far():
        mv.arrive(*go_core)
        mv.kept_done(*got_go)
        go[1] = (go[1].astype(F32) + gonear[1].astype(F32)).astype(BF)
        return mv.send(go.at[1], gonear.at[2], Y)

    def shard_sends():
        sent = []
        for at, k in enumerate((1, 2, 3, 0)):
            mv.kept_done(*got_g[3 * at : 3 * at + 3])
            gk[k, :tall] = (
                gk[k, :tall].astype(F32) + gnear[k].astype(F32) + gfar[k].astype(F32)
            ).astype(BF)
            if k:
                sent.append(mv.send(gk.at[k, :tall], gz.at[k - 1, :tall], zs[k - 1]))
        return sent

    def shard_sends_out(far):
        mv.arrive(far)
        sent = []
        for k in (1, 2, 3, 0):
            gk[k, tall:] = (
                go[0, k].astype(F32) + gonear[0, k].astype(F32) + gonear[2, k].astype(F32)
            ).astype(BF)
            if k:
                sent.append(mv.send(gk.at[k, tall:], gz.at[k - 1, tall:], zs[k - 1]))
        return sent

    def spread_far(ref):
        return mv.send(ref.at[ctx], ref.at[ctx], Y), mv.send(ref.at[ctx], ref.at[ctx], CORE)

    def spread_near(ref, far):
        mv.arrive(far[0])
        mv.send(ref.at[flip(ctx, 2)], ref.at[flip(ctx, 2)], CORE)

    gz_sent = shard_sends()
    sent0 = join(0)
    go_far = add_far()
    prepare()
    hops0 = first_hop(0, sent0)
    attend_back(0)
    lasts0 = second_hop(0, sent0, hops0)
    gz_sent += shard_sends_out(go_far)
    mv.arrive(*early_z)
    early[1] = early[0] + early_in[0] + early_in[1] + early_in[2]
    attend_back(1)
    arrived = [mv.send(other_hbm.at[b], arrived_out.at[b], X) for b in range(clips)]
    attend_back(2)
    stats0 = finish_sum(0, sent0, lasts0)
    attend_back(3)
    sent1 = join(1)
    qkv_grads(0)
    hops1 = first_hop(1, sent1)
    mv.arrive(*gz_sent)
    for part in (slice(0, tall), slice(tall, gz.shape[1])):
        gk[0, part] = (
            gk[0, part].astype(F32)
            + gz[0, part].astype(F32)
            + gz[1, part].astype(F32)
            + gz[2, part].astype(F32)
        ).astype(BF)
    placed = mv.keep(gk.at[0], dense_out.at[ctx])
    qkv_grads(1)
    lasts1 = second_hop(1, sent1, hops1)
    for h, j in CHUNKS:
        qs[piece_at(shard, tp, h, j)] = qacc[2 * h + j].astype(BF)
    q_sent = [mv.send(qs.at[k + 1], qz.at[k], name) for k, name in enumerate(zs)]
    mv.kept_done(placed)
    dense_far = spread_far(dense_out)
    finish_grad(0, stats0)
    mv.arrive(*q_sent)
    qs[0] = sum((qz[i].astype(F32) for i in range(3)), qs[0].astype(F32)).astype(BF)
    q_placed = mv.keep(qs.at[0], qdense_out.at[ctx])
    stats1 = finish_sum(1, sent1, lasts1)
    mv.kept_done(q_placed)
    q_far = spread_far(qdense_out)
    late[...] = jnp.zeros_like(late)
    for i in range(2):
        for j in range(4):
            late[4 * i + j : 4 * i + j + 1, :] = gains[i][:, j * 128 : (j + 1) * 128]
    for i in range(3):
        late[pl.ds(8 + 3 * ctx + i, 1), :] = sums[i]
    late_z = [mv.send(late, late_in.at[i], name) for i, name in enumerate(zs)]
    finish_grad(1, stats1)
    mv.arrive(*late_z)
    late_total = late[...] + late_in[0] + late_in[1] + late_in[2]
    late_x[0] = late_total
    others = (CORE, Y, YCORE)
    late_c = [mv.send(late_x.at[0], late_in.at[3 + i], name) for i, name in enumerate(others)]
    early_x = [mv.send(early.at[1], early_in.at[3 + i], name) for i, name in enumerate(others)]
    spread_near(qdense_out, q_far)
    spread_near(dense_out, dense_far)
    mv.arrive(*late_c)
    late_x[1] = late_x[0] + late_in[3] + late_in[4] + late_in[5]
    crossed = mv.send(late_x.at[1], late_x.at[2], X)
    mv.arrive(*early_x)
    early_out[...] = early[1] + early_in[3] + early_in[4] + early_in[5]
    qsum_out[...] = late_x[1, 8:20, :]
    mv.arrive(crossed)
    for i in range(2):
        part = slice(4 * i, 4 * i + 4)
        ln1_out[i, pl.ds(4 * tp, 4), :] = late_x[1, part, :]
        ln1_out[i, pl.ds(4 * (1 - tp), 4), :] = late_x[2, part, :]
    mv.finish()


def third_call(
    qkv, ot, d, tables, wq, normed, keep, near, far, go, dqt, dk, dv, other, x, xp, *small
):
    unused, unused, count, lanes = qkv.shape
    clips, rows, half = x.shape
    width = half // 2
    tall = keep.shape[1]
    heads = lanes // HEAD_DIM
    outs = [
        ((clips, rows, half), F32),
        ((clips, rows, half), BF),
        ((4, tall + lanes, width), BF),
        ((4, width, 3 * lanes), BF),
        ((24, width), F32),
        ((2, 8, 128), F32),
        ((12, lanes), F32),
    ]
    vmem = lambda kind, *shape: pltpu.VMEM(shape, kind)
    return pl.pallas_call(
        third_body,
        in_specs=[ANY] * 16 + [whole(a.shape) for a in small],
        out_specs=[whole(outs[0][0]), ANY, ANY, ANY] + [whole(o[0]) for o in outs[4:]],
        out_shape=[jax.ShapeDtypeStruct(shape, kind) for shape, kind in outs],
        scratch_shapes=[
            vmem(BF, *qkv.shape[1:]),
            vmem(F32, *ot.shape[1:]),
            vmem(BF, *d.shape[1:]),
            vmem(F32, *tables.shape),
            vmem(BF, *wq.shape),
            vmem(BF, heads, count, lanes),
            vmem(BF, heads, count, lanes),
            vmem(F32, heads, count),
            vmem(F32, lanes, count),
            vmem(BF, clips, 4, rows, 3 * lanes),
            vmem(BF, clips, 2, 2, rows, half),
            vmem(BF, clips, 2, 2, rows, half),
            vmem(BF, clips, 2, 2, rows, half),
            vmem(BF, clips, 2, rows // 2, half),
            vmem(BF, clips, 2, rows, half),
            vmem(BF, 2, rows, 2 * half),
            vmem(F32, 4, width, 3 * lanes),
            vmem(BF, *wq.shape),
            vmem(BF, 3, width, 3 * lanes),
            vmem(BF, 4, tall + lanes, width),
            vmem(BF, 4, tall, width),
            vmem(BF, 4, tall, width),
            vmem(BF, 3, tall + lanes, width),
            vmem(BF, 2, 4, lanes, width),
            vmem(BF, 3, 4, lanes, width),
            vmem(F32, *dk.shape),
            vmem(F32, *dqt.shape),
            vmem(BF, 2, clips, rows, half),
            vmem(F32, clips, 8, rows),
            vmem(F32, clips, 8, rows),
            vmem(F32, 2, 24, width),
            vmem(F32, 6, 24, width),
            vmem(F32, 24, 128),
            vmem(F32, 6, 24, 128),
            vmem(F32, 3, 24, 128),
            pltpu.SemaphoreType.DMA((64,)),
            pltpu.SemaphoreType.DMA((64,)),
            pltpu.SemaphoreType.DMA((48,)),
        ],
        compiler_params=pltpu.CompilerParams(
            vmem_limit_bytes=VMEM_BYTES, collective_id=3, has_side_effects=True
        ),
        name="layer_back",
    )(qkv, ot, d, tables, wq, normed, keep, near, far, go, dqt, dk, dv, other, x, xp, *small)


def fourth_body(
    dense_ref, q_ref, y_ref, other_ref, ig_ref, mid_ref, wb_ref, wi_ref, wo_ref, wq_ref, yo_ref, go_ref
):
    width = q_ref.shape[1]
    hidden = wb_ref.shape[0]
    lanes = wo_ref.shape[0]
    wb_ref[...] = dense_ref[0, :hidden, :].astype(F32)
    for j in range(2):
        at = hidden + j * width
        wi_ref[:, j * width : (j + 1) * width] = dense_ref[0, at : at + width, :].astype(F32)
    wo_ref[...] = dense_ref[0, hidden + 2 * width :, :].astype(F32)
    for i in range(3):
        wq_ref[i] = q_ref[0, :, i * lanes : (i + 1) * lanes].astype(F32)
    yo_ref[...] = (y_ref[...] + other_ref[...].astype(F32)).astype(BF)
    for j in range(2):
        part = slice(j * width, (j + 1) * width)
        go_ref[:, :, part] = ig_ref[:, :, part] + mid_ref[:, j]


def fourth_call(dense, qkv_dense, y, other, input_part, mids):
    four, tall, width = dense.shape
    lanes = qkv_dense.shape[2] // 3
    hidden = tall - 2 * width - lanes
    clips, rows, half = y.shape
    some = pl.BlockSpec((clips, rows // four, half), lambda a: (0, a, 0))
    return pl.pallas_call(
        fourth_body,
        grid=(four,),
        in_specs=[
            pl.BlockSpec((1, tall, width), lambda a: (a, 0, 0)),
            pl.BlockSpec((1, width, 3 * lanes), lambda a: (a, 0, 0)),
            some,
            some,
            some,
            pl.BlockSpec((clips, 2, rows // four, width), lambda a: (0, 0, a, 0)),
        ],
        out_specs=[
            pl.BlockSpec((hidden, width), lambda a: (a, 0)),
            pl.BlockSpec((width, hidden), lambda a: (0, a)),
            pl.BlockSpec((lanes, width), lambda a: (a, 0)),
            pl.BlockSpec((3, width, lanes), lambda a: (0, 0, a)),
            some,
            some,
        ],
        out_shape=[
            jax.ShapeDtypeStruct((four * hidden, width), F32),
            jax.ShapeDtypeStruct((width, four * hidden), F32),
            jax.ShapeDtypeStruct((four * lanes, width), F32),
            jax.ShapeDtypeStruct((3, width, four * lanes), F32),
            jax.ShapeDtypeStruct(y.shape, BF),
            jax.ShapeDtypeStruct(y.shape, F32),
        ],
        compiler_params=pltpu.CompilerParams(vmem_limit_bytes=VMEM_BYTES),
        name="owned_gradients",
    )(dense, qkv_dense, y, other, input_part, mids)


def fast_device(
    inputs,
    ln1_gain,
    ln1_bias,
    w_qkv,
    b_qkv,
    w_out,
    b_out,
    ln2_gain,
    ln2_bias,
    w_in,
    b_in,
    w_back,
    b_back,
    cotangent,
):
    clips, rows, half = inputs.shape
    width = half // 2
    lanes = half // 4
    hidden = w_in.shape[1] // 4
    shard, ctx, tp = (lax.axis_index(name) for name in ("shard", "ctx", "tp"))
    ids = jnp.stack([shard, ctx, tp]).astype(jnp.int32)
    def halves(vector):
        vector = vector.astype(F32)
        return jnp.concatenate(
            [
                lax.dynamic_slice_in_dim(vector, tp * half, half),
                lax.dynamic_slice_in_dim(vector, (1 - tp) * half, half),
            ]
        )

    ln_qkv = jnp.stack([halves(ln1_gain), halves(ln1_bias)])
    bias_qkv = (
        lax.dynamic_slice_in_dim(b_qkv, ctx * lanes, lanes, axis=1)
        .reshape(1, 3 * lanes)
        .astype(F32)
    )
    bias_in = b_in.reshape(4, hidden).astype(F32)

    xp, normed, qkv, ot, lse, mo, mp, wq, wo, wi, wb, bias_other, tables = first_call(
        inputs,
        jnp.transpose(w_qkv, (1, 0, 2)),
        w_out,
        w_in,
        w_back,
        bias_qkv,
        ln_qkv,
        jnp.broadcast_to(b_out, (16, half)),
    )
    ln_two = jnp.concatenate([ln2_gain, ln2_bias]).astype(F32).reshape(8, width)
    middle = second_call(
        inputs,
        xp,
        cotangent,
        mo,
        mp,
        wo,
        wi,
        wb,
        qkv,
        ot,
        ln_two,
        bias_in,
        b_out.reshape(1, half),
        bias_other,
        b_back.reshape(1, half),
        lse,
    )
    y, other, mids, grad_heads, keep, near, far, grads_out, dqt, dk, dv = middle[:11]
    input_part, arrived, dense, qkv_dense, early, grad_ln1, q_sums = third_call(
        qkv,
        ot,
        grad_heads,
        tables,
        wq,
        normed,
        keep,
        near,
        far,
        grads_out,
        dqt,
        dk,
        dv,
        other,
        inputs,
        xp,
        lse,
        ln1_gain.astype(F32).reshape(1, 2 * half),
        *middle[11:],
    )
    mid_total = early[:12].reshape(3, 2 * half)
    grad_b_out = lax.dynamic_slice_in_dim(mid_total[2], tp * half, half)
    grad_b_in = early[12:20].reshape(4 * hidden)
    grad_b_back = early[20:22].reshape(half)
    grad_b_qkv = q_sums.reshape(4, 3, lanes).transpose(1, 0, 2).reshape(3, 4 * lanes)
    grad_w_back, grad_w_in, grad_w_out, grad_w_qkv, output, input_grad = fourth_call(
        dense, qkv_dense, y, arrived, input_part, mids
    )
    grad_w_qkv = jnp.transpose(grad_w_qkv, (1, 0, 2))
    return (
        output,
        input_grad,
        grad_ln1[0].reshape(2 * half),
        grad_ln1[1].reshape(2 * half),
        grad_w_qkv,
        grad_b_qkv,
        grad_w_out,
        grad_b_out,
        mid_total[0],
        mid_total[1],
        grad_w_in,
        grad_b_in,
        grad_w_back,
        grad_b_back,
    )


def quick_form_fits(mesh):
    return (mesh.shape["shard"], mesh.shape["ctx"], mesh.shape["tp"]) == (4, 4, 2)


def solution(mesh):
    placed = (
        P("shard", "ctx", "tp"),
        P(),
        P(),
        P("shard", None, "tp"),
        P(None, "tp"),
        P("tp", "shard"),
        P("tp"),
        P(),
        P(),
        P("shard", "tp"),
        P("tp"),
        P("tp", "shard"),
        P("tp"),
        P("shard", "ctx", "tp"),
    )
    return jax.shard_map(
        fast_device if quick_form_fits(mesh) else per_device,
        mesh=mesh,
        in_specs=placed,
        out_specs=(
            P("shard", "ctx", "tp"),
            P("shard", "ctx", "tp"),
            P(),
            P(),
            P("shard", None, "tp"),
            P(None, "tp"),
            P("tp", "shard"),
            P("tp"),
            P(),
            P(),
            P("shard", "tp"),
            P("tp"),
            P("tp", "shard"),
            P("tp"),
        ),
        check_vma=False,
    )
```

```python
import math

import jax
import jax.numpy as jnp
from jax import lax
from jax.experimental import pallas as pl
from jax.experimental.pallas import tpu as pltpu
from jax.sharding import PartitionSpec as P

HEAD_DIM = 64
GH = 16
GW = 16


EPSILON = 1e-06
NEG_LARGE = -1e30


def rotary_tables(first_row, row_count):
    segment = 2 * (HEAD_DIM // 3 // 2)
    halfway = segment // 2
    places = first_row + jnp.arange(row_count, dtype=jnp.int32)
    frames = places // (GH * GW)
    rows_at = places // GW % GH
    cols_at = places % GW
    column = jnp.arange(HEAD_DIM, dtype=jnp.int32)
    segment_of = column // segment
    within = column % segment
    frequency = jnp.power(10000.0, -(within % halfway).astype(jnp.float32) / halfway)
    position = jnp.where(
        segment_of[None, :] == 0,
        frames[:, None],
        jnp.where(segment_of[None, :] == 1, rows_at[:, None], cols_at[:, None]),
    )
    angles = position.astype(jnp.float32) * frequency[None, :]
    active = (column < 3 * segment)[None, :]
    cosines = jnp.where(active, jnp.cos(angles), 1.0)
    sine_table = jnp.where(
        active, jnp.where((within < halfway)[None, :], -jnp.sin(angles), jnp.sin(angles)), 0.0
    )
    return (cosines, sine_table)


def partner(tensor):
    segment = 2 * (HEAD_DIM // 3 // 2)
    halfway = segment // 2
    pieces = []
    for number in range(3):
        offset = number * segment
        pieces.append(tensor[..., offset + halfway : offset + segment])
        pieces.append(tensor[..., offset : offset + halfway])
    pieces.append(tensor[..., 3 * segment :])
    return jnp.concatenate(pieces, axis=-1)


def rotate(tensor, cosines, sine_table):
    return tensor * cosines + partner(tensor) * sine_table


def rotate_back(gradient, cosines, sine_table):
    return gradient * cosines + partner(gradient * sine_table)


def normalize(tensor, gain, shift):
    center = tensor - jnp.mean(tensor, axis=-1, keepdims=True)
    spread = jnp.mean(center * center, axis=-1, keepdims=True)
    inv_std = lax.rsqrt(spread + EPSILON)
    scaled = center * inv_std
    return (scaled * gain + shift, scaled, inv_std)


def norm_back(grad_out, scaled, inv_std, gain):
    grad_scaled = grad_out * gain
    mean_one = jnp.mean(grad_scaled, axis=-1, keepdims=True)
    mean_two = jnp.mean(grad_scaled * scaled, axis=-1, keepdims=True)
    return inv_std * (grad_scaled - mean_one - scaled * mean_two)


def tp_rows(sharded):
    return lax.all_gather(sharded, "tp", axis=2, tiled=True)


def tensor_sum(summand):
    return lax.psum_scatter(
        summand.astype(jnp.bfloat16), "tp", scatter_dimension=2, tiled=True
    ).astype(jnp.float32)


def back_total(summand):
    return lax.psum(summand.astype(jnp.bfloat16), "tp").astype(jnp.float32)


def fetch_weights(w_qkv, w_out, w_in, w_back):
    return (
        lax.all_gather(w_qkv, "shard", axis=0, tiled=True),
        lax.all_gather(w_out, "shard", axis=1, tiled=True),
        lax.all_gather(w_in, "shard", axis=0, tiled=True),
        lax.all_gather(w_back, "shard", axis=1, tiled=True),
    )


def forward(inputs, params, weights, cosines, sine_table):
    gain_one, shift_one, b_qkv, b_out, gain_two, shift_two, b_in, b_back = params
    w_qkv_all, w_out_all, w_in_all, w_back_all = weights
    clip_count, row_count, width_local = inputs.shape
    heads_local = width_local // HEAD_DIM
    score_scale = HEAD_DIM ** (-0.5)
    tokens = tp_rows(inputs).astype(jnp.float32)
    normed, scaled_one, inv_one = normalize(tokens, gain_one, shift_one)
    normed_low = normed.astype(jnp.bfloat16)
    joined = (
        jnp.einsum("csd,dkh->cskh", normed_low, w_qkv_all, preferred_element_type=jnp.float32)
        + b_qkv
    )
    shaped = joined.reshape(clip_count, row_count, 3, heads_local, HEAD_DIM)
    queries = rotate(shaped[:, :, 0], cosines, sine_table).astype(jnp.bfloat16)
    key_rows = rotate(shaped[:, :, 1], cosines, sine_table).astype(jnp.bfloat16)
    values = shaped[:, :, 2].astype(jnp.bfloat16)
    key_flat = key_rows.reshape(clip_count, row_count, width_local)
    value_flat = values.reshape(clip_count, row_count, width_local)

    def absorb_block(running, block_pair):
        row_max, row_sum, weighted = running
        key_piece, value_piece = block_pair
        scores = (
            jnp.einsum("cqhd,ckhd->chqk", queries, key_piece, preferred_element_type=jnp.float32)
            * score_scale
        )
        next_max = jnp.maximum(row_max, jnp.max(scores, axis=-1))
        factor = jnp.exp(row_max - next_max)
        weights_now = jnp.exp(scores - next_max[..., None])
        row_sum = row_sum * factor + jnp.sum(weights_now, axis=-1)
        weighted = weighted * factor[..., None] + jnp.einsum(
            "chqk,ckhd->chqd",
            weights_now.astype(jnp.bfloat16),
            value_piece,
            preferred_element_type=jnp.float32,
        )
        return ((next_max, row_sum, weighted), None)

    initial = (
        jnp.full((clip_count, heads_local, row_count), NEG_LARGE, jnp.float32),
        jnp.zeros((clip_count, heads_local, row_count), jnp.float32),
        jnp.zeros((clip_count, heads_local, row_count, HEAD_DIM), jnp.float32),
    )
    running = initial
    pieces = (
        lax.all_gather(key_flat, "ctx", axis=1, tiled=True),
        lax.all_gather(value_flat, "ctx", axis=1, tiled=True),
    )
    piece_rows = pieces[0].shape[1]
    block_size = math.gcd(piece_rows, 512)
    block_count = piece_rows // block_size
    key_blocks = jnp.moveaxis(
        pieces[0].reshape(clip_count, block_count, block_size, heads_local, HEAD_DIM), 1, 0
    )
    value_blocks = jnp.moveaxis(
        pieces[1].reshape(clip_count, block_count, block_size, heads_local, HEAD_DIM), 1, 0
    )
    running, unused = lax.scan(absorb_block, running, (key_blocks, value_blocks))
    row_max, row_sum, weighted = running
    log_total = row_max + jnp.log(row_sum)
    mixed_heads = jnp.transpose(weighted / row_sum[..., None], (0, 2, 1, 3))
    mixed_low = mixed_heads.reshape(clip_count, row_count, width_local).astype(jnp.bfloat16)
    branch = tensor_sum(
        jnp.einsum("csh,hd->csd", mixed_low, w_out_all, preferred_element_type=jnp.float32)
    )
    middle = inputs.astype(jnp.float32) + branch + b_out
    middle_all = lax.all_gather(middle.astype(jnp.bfloat16), "tp", axis=2, tiled=True).astype(
        middle.dtype
    )
    second, scaled_two, inv_two = normalize(middle_all, gain_two, shift_two)
    second_low = second.astype(jnp.bfloat16)
    inner_pre = (
        jnp.einsum("csd,df->csf", second_low, w_in_all, preferred_element_type=jnp.float32) + b_in
    )
    active_low = jax.nn.gelu(inner_pre, approximate=False).astype(jnp.bfloat16)
    return {
        "normed_low": normed_low,
        "scaled_one": scaled_one,
        "inv_one": inv_one,
        "queries": queries,
        "key_flat": key_flat,
        "value_flat": value_flat,
        "mixed_heads": mixed_heads,
        "mixed_low": mixed_low,
        "log_total": log_total,
        "middle": middle,
        "scaled_two": scaled_two,
        "inv_two": inv_two,
        "second_low": second_low,
        "inner_pre": inner_pre,
        "active_low": active_low,
    }


def per_device(
    inputs,
    ln1_gain,
    ln1_bias,
    w_qkv,
    b_qkv,
    w_out,
    b_out,
    ln2_gain,
    ln2_bias,
    w_in,
    b_in,
    w_back,
    b_back,
    cotangent,
):
    params = tuple(
        (
            parameter.astype(jnp.float32)
            for parameter in (ln1_gain, ln1_bias, b_qkv, b_out, ln2_gain, ln2_bias, b_in, b_back)
        )
    )
    gain_one = params[0]
    gain_two = params[4]
    clip_count, row_count, width_local = inputs.shape
    heads_local = width_local // HEAD_DIM
    score_scale = HEAD_DIM ** (-0.5)
    tp_index = lax.axis_index("tp")
    share_start = tp_index * width_local
    cosines, sine_table = rotary_tables(lax.axis_index("ctx") * row_count, row_count)
    cosines = cosines[:, None, :]
    sine_table = sine_table[:, None, :]
    weights = fetch_weights(w_qkv, w_out, w_in, w_back)
    stored_acts = forward(inputs, params, weights, cosines, sine_table)
    output = (
        stored_acts["middle"]
        + tensor_sum(
            jnp.einsum(
                "csf,fd->csd",
                stored_acts["active_low"],
                weights[3],
                preferred_element_type=jnp.float32,
            )
        )
        + params[7]
    ).astype(jnp.bfloat16)
    weights = fetch_weights(w_qkv, w_out, w_in, w_back)
    stored_acts = forward(inputs, params, weights, cosines, sine_table)
    w_qkv_all, w_out_all, w_in_all, w_back_all = weights
    grad_low = tp_rows(cotangent)
    grad_full = grad_low.astype(jnp.float32)
    grad_active = jnp.einsum(
        "csd,fd->csf", grad_low, w_back_all, preferred_element_type=jnp.float32
    )
    unused, gelu_back = jax.vjp(
        lambda argument: jax.nn.gelu(argument, approximate=False), stored_acts["inner_pre"]
    )
    grad_inner = gelu_back(grad_active)[0].astype(jnp.bfloat16)
    grad_w_back = jnp.einsum(
        "csf,csd->fd", stored_acts["active_low"], grad_low, preferred_element_type=jnp.float32
    )
    grad_b_back = jnp.sum(cotangent.astype(jnp.float32), axis=(0, 1))
    grad_w_in = jnp.einsum(
        "csd,csf->df", stored_acts["second_low"], grad_inner, preferred_element_type=jnp.float32
    )
    grad_b_in = jnp.sum(grad_inner.astype(jnp.float32), axis=(0, 1))
    grad_second = back_total(
        jnp.einsum("csf,df->csd", grad_inner, w_in_all, preferred_element_type=jnp.float32)
    )
    grad_gain_two = jnp.sum(grad_second * stored_acts["scaled_two"], axis=(0, 1))
    grad_shift_two = jnp.sum(grad_second, axis=(0, 1))
    grad_middle = grad_full + norm_back(
        grad_second, stored_acts["scaled_two"], stored_acts["inv_two"], gain_two
    )
    grad_branch = grad_middle.astype(jnp.bfloat16)
    grad_b_out = lax.dynamic_slice_in_dim(
        jnp.sum(grad_branch.astype(jnp.float32), axis=(0, 1)), share_start, width_local
    )
    grad_w_out = jnp.einsum(
        "csh,csd->hd", stored_acts["mixed_low"], grad_branch, preferred_element_type=jnp.float32
    )
    grad_mixed = jnp.einsum(
        "csd,hd->csh", grad_branch, w_out_all, preferred_element_type=jnp.float32
    ).astype(jnp.bfloat16)
    key_all, value_all = (
        lax.all_gather(stored_acts["key_flat"], "ctx", axis=1, tiled=True),
        lax.all_gather(stored_acts["value_flat"], "ctx", axis=1, tiled=True),
    )
    length = key_all.shape[1]
    block_size = math.gcd(length, 512)
    block_count = length // block_size
    grad_heads = grad_mixed.reshape(clip_count, row_count, heads_local, HEAD_DIM)
    queries = stored_acts["queries"]
    log_total = stored_acts["log_total"]
    row_delta = jnp.einsum(
        "cqhd,chqd->chq",
        grad_heads.astype(jnp.float32),
        jnp.transpose(stored_acts["mixed_heads"], (0, 2, 1, 3)),
    )
    key_blocks = jnp.moveaxis(
        key_all.reshape(clip_count, block_count, block_size, heads_local, HEAD_DIM), 1, 0
    )
    value_blocks = jnp.moveaxis(
        value_all.reshape(clip_count, block_count, block_size, heads_local, HEAD_DIM), 1, 0
    )

    def key_step(grad_query, block_pair):
        key_piece, value_piece = block_pair
        scores = (
            jnp.einsum("cqhd,ckhd->chqk", queries, key_piece, preferred_element_type=jnp.float32)
            * score_scale
        )
        prob_block = jnp.exp(scores - log_total[..., None])
        grad_probs = jnp.einsum(
            "cqhd,ckhd->chqk", grad_heads, value_piece, preferred_element_type=jnp.float32
        )
        grad_scores = (prob_block * (grad_probs - row_delta[..., None])).astype(jnp.bfloat16)
        grad_query = grad_query + jnp.einsum(
            "chqk,ckhd->cqhd", grad_scores, key_piece, preferred_element_type=jnp.float32
        )
        grad_key = (
            jnp.einsum("chqk,cqhd->ckhd", grad_scores, queries, preferred_element_type=jnp.float32)
            * score_scale
        )
        grad_value = jnp.einsum(
            "chqk,cqhd->ckhd",
            prob_block.astype(jnp.bfloat16),
            grad_heads,
            preferred_element_type=jnp.float32,
        )
        return (grad_query, (grad_key, grad_value))

    grad_query, (key_terms, value_terms) = lax.scan(
        key_step,
        jnp.zeros((clip_count, row_count, heads_local, HEAD_DIM), jnp.float32),
        (key_blocks, value_blocks),
    )
    grad_query = grad_query * score_scale
    key_terms = jnp.moveaxis(key_terms, 0, 1).reshape(clip_count, length, width_local)
    value_terms = jnp.moveaxis(value_terms, 0, 1).reshape(clip_count, length, width_local)
    grad_keys, grad_values = (
        lax.psum_scatter(
            key_terms.astype(jnp.bfloat16), "ctx", scatter_dimension=1, tiled=True
        ).astype(jnp.float32),
        lax.psum_scatter(
            value_terms.astype(jnp.bfloat16), "ctx", scatter_dimension=1, tiled=True
        ).astype(jnp.float32),
    )
    grad_q_pre = rotate_back(grad_query, cosines, sine_table).reshape(
        clip_count, row_count, width_local
    )
    grad_k_pre = rotate_back(
        grad_keys.reshape(clip_count, row_count, heads_local, HEAD_DIM), cosines, sine_table
    ).reshape(clip_count, row_count, width_local)
    grad_joined = jnp.stack([grad_q_pre, grad_k_pre, grad_values], axis=2).astype(jnp.bfloat16)
    grad_w_qkv = jnp.einsum(
        "csd,cskh->dkh", stored_acts["normed_low"], grad_joined, preferred_element_type=jnp.float32
    )
    grad_b_qkv = jnp.sum(grad_joined.astype(jnp.float32), axis=(0, 1))
    normed_term = jnp.einsum(
        "cskh,dkh->csd", grad_joined, w_qkv_all, preferred_element_type=jnp.float32
    )
    grad_normed = back_total(normed_term)
    grad_gain_one = jnp.sum(grad_normed * stored_acts["scaled_one"], axis=(0, 1))
    grad_shift_one = jnp.sum(grad_normed, axis=(0, 1))
    grad_tokens = grad_middle + norm_back(
        grad_normed, stored_acts["scaled_one"], stored_acts["inv_one"], gain_one
    )
    input_grad = lax.dynamic_slice_in_dim(grad_tokens, share_start, width_local, axis=2)
    summed = (
        lax.psum(grad_w_qkv.astype(jnp.bfloat16), "ctx").astype(jnp.float32),
        lax.psum(grad_w_out.astype(jnp.bfloat16), "ctx").astype(jnp.float32),
        lax.psum(grad_w_in.astype(jnp.bfloat16), "ctx").astype(jnp.float32),
        lax.psum(grad_w_back.astype(jnp.bfloat16), "ctx").astype(jnp.float32),
    )
    owned_grads = (
        lax.psum_scatter(
            summed[0].astype(jnp.bfloat16), "shard", scatter_dimension=0, tiled=True
        ).astype(jnp.float32),
        lax.psum_scatter(
            summed[1].astype(jnp.bfloat16), "shard", scatter_dimension=1, tiled=True
        ).astype(jnp.float32),
        lax.psum_scatter(
            summed[2].astype(jnp.bfloat16), "shard", scatter_dimension=0, tiled=True
        ).astype(jnp.float32),
        lax.psum_scatter(
            summed[3].astype(jnp.bfloat16), "shard", scatter_dimension=1, tiled=True
        ).astype(jnp.float32),
    )
    small_sums = lax.psum(
        (
            grad_gain_one,
            grad_shift_one,
            grad_b_qkv,
            grad_b_out,
            grad_gain_two,
            grad_shift_two,
            grad_b_in,
            grad_b_back,
        ),
        ("shard", "ctx"),
    )
    return (
        output,
        input_grad,
        small_sums[0],
        small_sums[1],
        owned_grads[0],
        small_sums[2],
        owned_grads[1],
        small_sums[3],
        small_sums[4],
        small_sums[5],
        owned_grads[2],
        small_sums[6],
        owned_grads[3],
        small_sums[7],
    )


LOG2E = 1.4426950408889634
BF = jnp.bfloat16
F32 = jnp.float32
VMEM_BYTES = 60 * 2**20


def dot_nt(a, b):
    return lax.dot_general(a, b, (((1,), (1,)), ((), ())), preferred_element_type=F32)


def dot_nn(a, b):
    return lax.dot_general(a, b, (((1,), (0,)), ((), ())), preferred_element_type=F32)


def dot_tn(a, b):
    return lax.dot_general(a, b, (((0,), (0,)), ((), ())), preferred_element_type=F32)


def whole(shape):
    return pl.BlockSpec(shape, lambda *_: (0,) * len(shape))


CHUNKS = ((0, 0), (0, 1), (1, 0), (1, 1))


def partner_lanes(tensor):
    segment = 2 * (HEAD_DIM // 3 // 2)
    halfway = segment // 2
    width = tensor.shape[1]
    lane = lax.broadcasted_iota(jnp.int32, tensor.shape, 1) % HEAD_DIM
    first = lane % segment < halfway
    return jnp.where(
        first, pltpu.roll(tensor, width - halfway, 1), pltpu.roll(tensor, halfway, 1)
    )


def norm_parts(own, other):
    total = 2 * own.shape[1]
    mean = (jnp.sum(own, 1, keepdims=True) + jnp.sum(other, 1, keepdims=True)) / total
    own, other = own - mean, other - mean
    spread = (
        jnp.sum(own * own, 1, keepdims=True) + jnp.sum(other * other, 1, keepdims=True)
    ) / total
    inv = lax.rsqrt(spread + EPSILON)
    return own * inv, other * inv, inv


def flip(value, bit):
    if bit == 1:
        return value + 1 - 2 * lax.rem(value, 2)
    return lax.rem(value + 2, 4)


def place():
    return tuple(lax.axis_index(name) for name in ("shard", "ctx", "tp"))


def piece_at(shard, tp, half, part):
    found = lax.rem(shard + 2 * lax.rem(tp + half, 2), 4)
    return flip(found, 1) if part else found


X, CORE, Y, YCORE, Z1, Z2, Z3 = range(7)


class Movers:
    def __init__(self, send_sems, recv_sems, local_sems):
        shard, ctx, tp = place()
        self.sems = (send_sems, recv_sems, local_sems)
        self.sent, self.kept = [], []
        self.partners = {
            X: {"tp": 1 - tp},
            CORE: {"ctx": flip(ctx, 1)},
            Y: {"ctx": flip(ctx, 2)},
            YCORE: {"ctx": flip(flip(ctx, 2), 1)},
            Z1: {"shard": flip(shard, 1)},
            Z2: {"shard": flip(shard, 2)},
            Z3: {"shard": flip(flip(shard, 2), 1)},
        }
        self.inner = jnp.logical_or(shard == 1, shard == 2)
        self.used = 0
        self.left = set()

    def barrier(self, names):
        barrier = pltpu.get_barrier_semaphore()
        for name in names:
            pl.semaphore_signal(
                barrier,
                inc=1,
                device_id=self.partners[name],
                device_id_type=pl.DeviceIdType.MESH,
            )
        pl.semaphore_wait(barrier, len(names))

    def remote(self, source, target, name, send_at, recv_at):
        return pltpu.make_async_remote_copy(
            src_ref=source,
            dst_ref=target,
            send_sem=self.sems[0].at[send_at],
            recv_sem=self.sems[1].at[recv_at],
            device_id=self.partners[name],
            device_id_type=pl.DeviceIdType.MESH,
        )

    def send(self, source, target, name):
        copy = self.remote(source, target, name, self.used, self.used)
        self.used += 1
        copy.start()
        self.sent.append([copy, False])
        return len(self.sent) - 1

    def arrive(self, *which):
        for at in which:
            if not self.sent[at][1]:
                self.sent[at][0].wait_recv()
                self.sent[at][1] = True

    def wait_sent(self, *which):
        for at in which:
            if at not in self.left:
                self.sent[at][0].wait_send()
                self.left.add(at)

    def keep(self, source, target):
        at = len(self.kept)
        copy = pltpu.make_async_copy(source, target, self.sems[2].at[at])
        copy.start()
        self.kept.append([copy, False])
        return at

    def kept_done(self, *which):
        for at in which:
            if not self.kept[at][1]:
                self.kept[at][0].wait()
                self.kept[at][1] = True

    def finish(self):
        if self.used > self.sems[0].shape[0] or len(self.kept) > self.sems[2].shape[0]:
            raise ValueError((self.used, len(self.kept)))
        self.arrive(*range(len(self.sent)))
        self.wait_sent(*range(len(self.sent)))
        self.kept_done(*range(len(self.kept)))


class Line:
    def __init__(self, mv, own, slot):
        self.mv, self.step = mv, 0
        at = mv.used
        mv.used += 5
        self.first = mv.remote(own, slot(1), Z1, at, at)
        self.middle = [
            mv.remote(own, slot(3), Z3, at + 1, at + 2),
            mv.remote(slot(1), slot(2), Z3, at + 2, at + 1),
            mv.remote(slot(3), slot(2), Z1, at + 3, at + 1),
            mv.remote(slot(2), slot(3), Z1, at + 4, at + 2),
        ]
        self.arrivals = {2: self.middle[1], 3: self.middle[0]}
        self.first.start()
        pl.when(mv.inner)(self.middle[0].start)

    def advance(self):
        self.step += 1
        if self.step == 1:
            self.first.wait_recv()
            pl.when(self.mv.inner)(self.middle[1].start)
            return
        arrival = self.arrivals[3 if self.step == 2 else 2]

        @pl.when(self.mv.inner)
        def _():
            arrival.wait_recv()
            self.middle[self.step].start()

    def done(self):
        while self.step < 3:
            self.advance()

        @pl.when(jnp.logical_not(self.mv.inner))
        def _():
            self.arrivals[2].wait_recv()
            self.arrivals[3].wait_recv()

    def finish(self):
        self.first.wait_send()

        @pl.when(self.mv.inner)
        def _():
            for copy in self.middle:
                copy.wait_send()


def first_body(*refs):
    (x_ref, cot_ref, wqkv_ref, wout_ref, win_ref, wback_ref, b_ref, ln_ref, bout_ref) = refs[:9]
    (xp_out, cp_out, n_out, qkv_out, ot_out, lse_out, mo_out, mp_out, wq_out, wo, wi, wb, boutp_out, table_out) = refs[
        9:23
    ]
    (xall, nbuf, qkv, ot, vt, osc, wq, tables, send_sems, recv_sems, local_sems) = refs[23:]
    clips, rows, half = x_ref.shape
    width = half // 2
    lanes = tables.shape[3]
    hidden = wi.shape[3]
    shard, ctx, tp = place()
    mv = Movers(send_sems, recv_sems, local_sems)
    mv.barrier([X, CORE, Y, YCORE, Z1, Z2, Z3])
    cut = rows // 2

    x0 = [mv.send(x_ref.at[0], xall.at[0, 1, 0], X)]
    y0 = [mv.send(x_ref.at[0], xall.at[0, 0, 2], Y)]
    qkv_at = pl.ds(pl.multiple_of(ctx * lanes, lanes), lanes)
    wq_own = [
        mv.keep(wqkv_ref.at[i, :, qkv_at], wq.at[0, :, i * lanes : (i + 1) * lanes])
        for i in range(3)
    ]
    mv.kept_done(*wq_own)
    wq_line = Line(mv, wq.at[0], lambda k: wq.at[k])
    c0 = [mv.send(x_ref.at[0], xall.at[0, 0, 1], CORE)]
    own = [mv.keep(x_ref.at[b], xall.at[b, 0, 0]) for b in range(clips)]
    out_piece = wout_ref.at[pl.ds(pl.multiple_of(ctx * lanes, lanes), lanes), :]
    back_piece = wback_ref.at[pl.ds(pl.multiple_of(ctx * hidden, hidden), hidden), :]
    far_ctx = flip(ctx, 2)
    in_pieces = [
        win_ref.at[:, pl.ds(pl.multiple_of(at * hidden, hidden), hidden)] for at in (ctx, far_ctx)
    ]
    wo_x = mv.send(out_piece, wo.at[0, 0, 1], X)
    mv.send(bout_ref, boutp_out, X)
    wo_own = mv.keep(out_piece, wo.at[0, 0, 0])
    wi_own = [mv.keep(in_pieces[i], wi.at[2 * i, 0]) for i in range(2)]
    wb_own = mv.keep(back_piece, wb.at[0, 0])

    def forward(b, x, y):
        mv.arrive(x)
        size = cut if b == 0 else cut // 4
        low = mv.send(xall.at[b, 1, 0, :size], xall.at[b, 1, 2, :size], Y)
        near = [mv.send(xall.at[b, 1, 0], xall.at[b, 1, 1], CORE)]
        mv.arrive(y)
        high = mv.send(xall.at[b, 0, 2, size:], xall.at[b, 1, 2, size:], X)
        near.append(mv.send(xall.at[b, 0, 2], xall.at[b, 0, 3], CORE))
        return low, high, near

    def project(b, m):
        slot = m % 2
        for start in range(0, rows, cut):
            part = slice(start, start + cut)
            one, two, unused = norm_parts(
                xall[b, 0, m, part, :].astype(F32), xall[b, 1, m, part, :].astype(F32)
            )
            nbuf[slot, part, :half] = (one * ln_ref[0:1, :half] + ln_ref[1:2, :half]).astype(BF)
            nbuf[slot, part, half:] = (two * ln_ref[0:1, half:] + ln_ref[1:2, half:]).astype(BF)
        acc = b_ref[...]
        for h, j in CHUNKS:
            at = (2 * h + j) * width
            acc = acc + dot_nn(nbuf[slot, :, at : at + width], wq[piece_at(shard, tp, h, j)])
        cosines, sines = tables[0, m], tables[1, m]
        q, k = acc[:, :lanes], acc[:, lanes : 2 * lanes]
        place_rows = slice(m * rows, (m + 1) * rows)
        qkv[b, 0, place_rows, :] = (q * cosines + partner_lanes(q) * sines).astype(BF)
        qkv[b, 1, place_rows, :] = (k * cosines + partner_lanes(k) * sines).astype(BF)
        qkv[b, 2, place_rows, :] = acc[:, 2 * lanes :].astype(BF)
        return mv.keep(nbuf.at[slot], n_out.at[b, m])

    scale = HEAD_DIM ** (-0.5) * LOG2E
    head = lax.broadcasted_iota(jnp.int32, (rows, lanes), 1) // HEAD_DIM

    def turn_values(b):
        vt[:lanes, :] = qkv[b, 2].T
        vt[lanes:, :] = jnp.ones((vt.shape[0] - lanes, 4 * rows), BF)

    def attend(b, m):
        part = slice(m * rows, (m + 1) * rows)
        q = qkv[b, 0, part, :]
        keys = qkv[b, 1]
        outs = []
        for h in range(lanes // HEAD_DIM):
            q_head = jnp.where(head == h, q, jnp.zeros_like(q))
            scores = dot_nt(keys, q_head)
            top = jnp.max(scores, axis=0, keepdims=True) * scale
            probs = jnp.exp2(scores * scale - top).astype(BF)
            acc = dot_nn(vt[...], probs)
            total = acc[lanes : lanes + 1, :]
            outs.append(acc[h * HEAD_DIM : (h + 1) * HEAD_DIM, :] / total)
            lse_out[b, h : h + 1, part] = top + jnp.log2(total)
        result = jnp.concatenate(outs, axis=0)
        ot[b, :, part] = result
        osc[b, m] = result.T.astype(BF)
        if m == 0:
            return mv.keep(osc.at[b, 0], mo_out.at[b, 0])
        return mv.send(osc.at[b, m], mo_out.at[b, m], (None, CORE, Y, YCORE)[m])

    token = lax.broadcasted_iota(jnp.int32, (rows, lanes), 0)
    column = lax.broadcasted_iota(jnp.int32, (rows, lanes), 1) % HEAD_DIM
    segment = 2 * (HEAD_DIM // 3 // 2)
    halfway = segment // 2
    within = column % segment
    frequency = jnp.exp(
        (within % halfway).astype(F32) * (-math.log(10000.0) / halfway)
    )
    sign = jnp.where(within < halfway, -1.0, 1.0)
    active = column < 3 * segment

    def turn(position):
        angle = position.astype(F32) * frequency
        return jnp.where(active, jnp.cos(angle), 1.0), jnp.where(active, jnp.sin(angle) * sign, 0.0)

    def turn_frame(frame):
        angle = frame.astype(F32) * frequency[:8]
        cosine, sine = jnp.cos(angle)[:1], (jnp.sin(angle) * sign[:8])[:1]
        return cosine, sine

    start = [at * rows for at in (ctx, flip(ctx, 1), flip(ctx, 2), flip(flip(ctx, 2), 1))]
    if rows % (GH * GW) == 0:
        tables_in = turn(
            jnp.where(column < 2 * segment, token // GW % GH, token % GW)
        )
        for m in range(4):
            for at in range(0, rows, GH * GW):
                part = slice(at, at + GH * GW)
                frame = turn_frame((start[m] + at) // (GH * GW))
                first = column[part] < segment
                for i in range(2):
                    tables[i, m, part, :] = jnp.where(first, frame[i], tables_in[i][part])
    else:
        for m in range(4):
            at = start[m] + token
            both = turn(
                jnp.where(
                    column < segment,
                    at // (GH * GW),
                    jnp.where(column < 2 * segment, at // GW % GH, at % GW),
                )
            )
            for i in range(2):
                tables[i, m] = both[i]
    mv.keep(tables, table_out)

    wq_line.advance()
    wb_line = Line(mv, back_piece, lambda k: wb.at[0, k])
    wq_line.advance()
    low0, high0, near0 = forward(0, x0[0], y0[0])
    wq_line.advance()
    x1 = mv.send(x_ref.at[1], xall.at[1, 1, 0], X)
    y1 = mv.send(x_ref.at[1], xall.at[1, 0, 2], Y)
    c1 = mv.send(x_ref.at[1], xall.at[1, 0, 1], CORE)
    mv.keep(xall.at[0, 1, 0], xp_out.at[0])
    wb_line.advance()
    mv.arrive(wo_x)
    mv.kept_done(wo_own)
    wo_line = Line(mv, wo.at[0, 0], lambda k: wo.at[0, k])
    wq_line.done()
    mv.kept_done(own[0])
    mv.keep(wq, wq_out)
    n_copy = [project(0, 0)]
    wb_line.advance()
    wi_near = Line(mv, in_pieces[0], lambda k: wi.at[0, k])
    mv.arrive(c0[0], near0[0])
    n_copy.append(project(0, 1))
    mv.arrive(low0, high0)
    near0.append(mv.send(xall.at[0, 1, 2], xall.at[0, 1, 3], CORE))
    wb_line.advance()
    wo_line.advance()
    mv.kept_done(n_copy[0])
    n_copy.append(project(0, 2))
    wo_line.advance()
    mv.arrive(near0[1], near0[2])
    mv.kept_done(n_copy[1])
    n_copy.append(project(0, 3))
    mv.keep(qkv.at[0], qkv_out.at[0])
    low1, high1, near1 = forward(1, x1, y1)
    mv.keep(xall.at[1, 1, 0], xp_out.at[1])
    mv.send(cot_ref.at[0], cp_out, X)
    wb_line.done()
    mv.kept_done(wb_own)
    wb_far = mv.send(wb.at[0], wb.at[2], Y)
    mv.send(wb.at[0], wb.at[1], CORE)
    wi_near.advance()
    wi_far = Line(mv, in_pieces[1], lambda k: wi.at[2, k])
    turn_values(0)
    m0 = {2: attend(0, 2)}
    mv.arrive(low1, high1)
    near1.append(mv.send(xall.at[1, 1, 2], xall.at[1, 1, 3], CORE))
    wo_line.advance()
    wi_near.advance()
    m0[3] = attend(0, 3)
    wo_line.done()
    wo_far = mv.send(wo.at[0], wo.at[2], Y)
    mv.send(wo.at[0], wo.at[1], CORE)
    wi_near.advance()
    m0[1] = attend(0, 1)
    wi_far.advance()
    m0[0] = attend(0, 0)
    wi_far.advance()
    mv.keep(ot.at[0], ot_out.at[0])
    mv.arrive(c1, *near1)
    mv.kept_done(own[1], n_copy[2])
    n_copy.append(project(1, 0))
    mv.kept_done(n_copy[3])
    n_copy.append(project(1, 1))
    mv.arrive(m0[1])
    mv.kept_done(m0[0])
    for m in (1, 0):
        mv.send(mo_out.at[0, m], mp_out.at[0, m], X)
    mv.kept_done(n_copy[4])
    n_copy.append(project(1, 2))
    mv.kept_done(n_copy[5])
    n_copy.append(project(1, 3))
    mv.keep(qkv.at[1], qkv_out.at[1])
    for m in (2, 3):
        mv.arrive(m0[m])
        mv.send(mo_out.at[0, m], mp_out.at[0, m], X)
    wi_far.advance()
    turn_values(1)
    m1 = {2: attend(1, 2)}
    m1[3] = attend(1, 3)
    wi_near.done()
    mv.kept_done(wi_own[0])
    mv.send(wi.at[0], wi.at[1], CORE)
    m1[1] = attend(1, 1)
    m1[0] = attend(1, 0)
    mv.arrive(m1[1])
    mv.send(mo_out.at[1, 1], mp_out.at[1, 1], X)
    mv.kept_done(m1[0])
    mv.send(mo_out.at[1, 0], mp_out.at[1, 0], X)
    mv.keep(ot.at[1], ot_out.at[1])
    mv.arrive(wb_far)
    mv.send(wb.at[2], wb.at[3], CORE)
    mv.arrive(wo_far)
    mv.send(wo.at[2], wo.at[3], CORE)
    for m in (2, 3):
        mv.arrive(m1[m])
        mv.send(mo_out.at[1, m], mp_out.at[1, m], X)
    wi_far.done()
    mv.kept_done(wi_own[1])
    mv.send(wi.at[2], wi.at[3], CORE)
    for line in (wq_line, wb_line, wi_near, wo_line, wi_far):
        line.finish()
    mv.finish()


ANY = pl.BlockSpec(memory_space=pl.ANY)


def first_call(x, cot, w_qkv, w_out, w_in, w_back, b, ln, b_out):
    clips, rows, half = x.shape
    width = half // 2
    lanes = half // 4
    hidden = w_in.shape[1] // 4
    outs = [
        ((clips, rows, half), BF),
        ((rows, half), BF),
        ((clips, 4, rows, 2 * half), BF),
        ((clips, 3, 4 * rows, lanes), BF),
        ((clips, lanes, 4 * rows), F32),
        ((clips, lanes // HEAD_DIM, 4 * rows), F32),
        ((clips, 4, rows, lanes), BF),
        ((clips, 4, rows, lanes), BF),
        ((4, width, 3 * lanes), BF),
        ((4, 4, 2, lanes, width), BF),
        ((4, 4, width, hidden), BF),
        ((4, 4, hidden, width), BF),
        (b_out.shape, BF),
        ((2, 4, rows, lanes), F32),
    ]
    out_specs = [ANY] * len(outs)
    out_specs[5] = whole(outs[5][0])
    return pl.pallas_call(
        first_body,
        in_specs=[ANY] * 6 + [whole(b.shape), whole(ln.shape), ANY],
        out_specs=out_specs,
        out_shape=[jax.ShapeDtypeStruct(shape, kind) for shape, kind in outs],
        scratch_shapes=[
            pltpu.VMEM((clips, 2, 4, rows, half), BF),
            pltpu.VMEM((2, rows, 2 * half), BF),
            pltpu.VMEM((clips, 3, 4 * rows, lanes), BF),
            pltpu.VMEM((clips, lanes, 4 * rows), F32),
            pltpu.VMEM((lanes + 16, 4 * rows), BF),
            pltpu.VMEM((clips, 4, rows, lanes), BF),
            pltpu.VMEM((4, width, 3 * lanes), BF),
            pltpu.VMEM((2, 4, rows, lanes), F32),
            pltpu.SemaphoreType.DMA((80,)),
            pltpu.SemaphoreType.DMA((80,)),
            pltpu.SemaphoreType.DMA((40,)),
        ],
        compiler_params=pltpu.CompilerParams(
            vmem_limit_bytes=VMEM_BYTES, collective_id=1, has_side_effects=True
        ),
        name="project_and_attend",
    )(x, cot, w_qkv, w_out, w_in, w_back, b, ln, b_out)


def chunk_of(shard, k):
    found = flip(shard, 2) if k & 2 else shard
    return flip(found, 1) if k & 1 else found


def side_by_side(parts):
    return jnp.concatenate(parts, axis=1)


def second_body(*refs):
    (x_ref, xp_ref, c_ref, cp_ref, mo_ref, mp_ref, wo_hbm, wi_hbm, wb_hbm, qkv_hbm, ot_hbm) = refs[:11]
    (ln_ref, bin_ref, bout_ref, boutp_ref, bback_ref, lse_ref) = refs[11:17]
    (y_out, other_out, arrived_out, gmid_out, d_out, keep_out, near_out, far_out, far_own_out, go_out) = refs[17:27]
    (dqt_out, dk_out, dv_out, midsum_out, insum_out, backsum_out) = refs[27:33]
    (xs, cs, ms, wo, wi, wb, mid, sec, act, gin, outs, ybuf, gs, gsr, gmid, gb, gm) = refs[33:50]
    (wg, wgnear, wgo, turned, ot, dqt, delta, dks, dvs, send_sems, recv_sems, local_sems) = refs[50:]
    clips, rows, half = x_ref.shape
    width = half // 2
    lanes = mo_ref.shape[3]
    hidden = wi.shape[3]
    shard, ctx, tp = place()
    mv = Movers(send_sems, recv_sems, local_sems)
    ks = range(4)
    own_k = [piece_at(shard, tp, 0, j) for j in range(2)]
    other_k = [piece_at(shard, tp, 1, j) for j in range(2)]

    def fetch(b):
        return [
            mv.keep(mo_ref.at[b], ms.at[b, 0]),
            mv.keep(mp_ref.at[b], ms.at[b, 1]),
            mv.keep(x_ref.at[b], xs.at[b, 0]),
            mv.keep(xp_ref.at[b], xs.at[b, 1]),
            mv.keep(c_ref.at[b], cs.at[b, 0]),
        ]

    got = [fetch(0)]
    got[0].append(mv.keep(cp_ref, cs.at[0, 1]))
    got_wo = mv.keep(wo_hbm, wo)
    got_wi = [mv.keep(wi_hbm.at[m], wi.at[m]) for m in ks]
    got_wb = [mv.keep(wb_hbm.at[m], wb.at[m]) for m in ks]
    got.append(fetch(1))
    mv.barrier([X, CORE, Y, YCORE])
    cot_in = mv.send(c_ref.at[1], cs.at[1, 1], X)

    def row(which, k):
        return ln_ref[pl.ds(4 * which + chunk_of(shard, k), 1), :]

    def statistics(b):
        total = 4 * width
        mean = sum(jnp.sum(mid[b, k], 1, keepdims=True) for k in ks) / total
        spread = sum(jnp.sum((mid[b, k] - mean) ** 2, 1, keepdims=True) for k in ks) / total
        return mean, lax.rsqrt(spread + EPSILON)

    y_put = []

    def block(b):
        mv.kept_done(*got[b])
        mv.kept_done(got_wo)
        mixed = side_by_side([ms[b, side, m] for side in range(2) for m in ks])
        for k in ks:
            weight = jnp.concatenate([wo[m, k, side] for side in range(2) for m in ks], axis=0)
            mid[b, k] = dot_nn(mixed, weight)
        for j in range(2):
            part = slice(j * width, (j + 1) * width)
            mid[b, own_k[j]] += xs[b, 0, :, part].astype(F32) + bout_ref[0:1, part].astype(F32)
            mid[b, other_k[j]] += xs[b, 1, :, part].astype(F32) + boutp_ref[0:1, part].astype(F32)
        mean, inv = statistics(b)
        for k in ks:
            sec[b, k] = ((mid[b, k] - mean) * inv * row(0, k) + row(1, k)).astype(BF)
        if b == 1:
            mv.arrive(cot_in)
        for j in range(2):
            part = slice(j * width, (j + 1) * width)
            gb[b, own_k[j]] = cs[b, 0, :, part]
            gb[b, other_k[j]] = cs[b, 1, :, part]
        normed = side_by_side([sec[b, k] for k in ks])
        cot = side_by_side([gb[b, k] for k in ks])
        for m in ks:
            mv.kept_done(got_wi[m])
            at = (ctx, flip(ctx, 1), flip(ctx, 2), flip(flip(ctx, 2), 1))[m]
            inner = bin_ref[pl.ds(at, 1), :] + dot_nn(normed, wi[m].reshape(4 * width, hidden))
            mv.kept_done(got_wb[m])
            grad = dot_nt(cot, side_by_side([wb[m, k] for k in ks]))
            phi = 0.5 + 0.5 * lax.erf(inner * (0.5**0.5))
            act[b, m] = (inner * phi).astype(BF)
            slope = phi + inner * (jnp.exp(-0.5 * inner * inner) * ((2 * math.pi) ** -0.5))
            grad = (grad * slope).astype(BF)
            gin[b, m] = grad
            sums = jnp.sum(grad.astype(F32), axis=0, keepdims=True)
            if b == 0:
                insum_out[pl.ds(at, 1), :] = sums
            else:
                insum_out[pl.ds(at, 1), :] += sums
        back = side_by_side([gin[b, m] for m in ks])
        sent = []
        for k in ks:
            gs[b, k] = dot_nt(back, side_by_side([wi[m, k] for m in ks])).astype(BF)
            sent.append(mv.send(gs.at[b, k], gsr.at[b, k], X))
        active = side_by_side([act[b, m] for m in ks])
        mv.kept_done(*y_put)
        for h, which in enumerate((own_k, other_k)):
            for j in range(2):
                weight = jnp.concatenate([wb[m, which[j]] for m in ks], axis=0)
                part = slice(j * width, (j + 1) * width)
                term = dot_nn(active, weight)
                if h == 0:
                    term = term + mid[b, own_k[j]] + bback_ref[0:1, part].astype(F32)
                    ybuf[:, part] = term
                else:
                    outs[b, :, part] = term.astype(BF)
        y_put.append(mv.keep(ybuf, y_out.at[b]))
        if b == 1:
            mv.keep(outs.at[1], other_out)
        return sent

    put = []

    def branch(b, sent):
        mv.arrive(*sent[:4])
        mv.kept_done(*put)
        total = 4 * width
        mean, inv = statistics(b)
        mean_one = mean_two = 0.0
        for k in ks:
            unit = (mid[b, k] - mean) * inv
            grad = gs[b, k].astype(F32) + gsr[b, k].astype(F32)
            gain_sum = jnp.sum(grad * unit, 0, keepdims=True)
            shift_sum = jnp.sum(grad, 0, keepdims=True)
            for i, term in enumerate((gain_sum, shift_sum)):
                place_row = pl.ds(4 * i + chunk_of(shard, k), 1)
                if b == 0:
                    midsum_out[place_row, :] = term
                else:
                    midsum_out[place_row, :] += term
            scaled = grad * row(0, k)
            mean_one = mean_one + jnp.sum(scaled, 1, keepdims=True)
            mean_two = mean_two + jnp.sum(scaled * unit, 1, keepdims=True)
        mean_one, mean_two = mean_one / total, mean_two / total
        for k in ks:
            unit = (mid[b, k] - mean) * inv
            grad = gs[b, k].astype(F32) + gsr[b, k].astype(F32)
            full = gb[b, k].astype(F32) + inv * (grad * row(0, k) - mean_one - unit * mean_two)
            gmid[k] = full
            low = full.astype(BF)
            xs[b, k // 2, :, (k % 2) * width : (k % 2 + 1) * width] = low
            sec_sum = jnp.sum(low.astype(F32), 0, keepdims=True)
            place_row = pl.ds(8 + chunk_of(shard, k), 1)
            if b == 0:
                midsum_out[place_row, :] = sec_sum
            else:
                midsum_out[place_row, :] += sec_sum
        low = side_by_side([xs[b, 0], xs[b, 1]])
        weight = side_by_side([jnp.concatenate([wo[m, k, 0] for m in ks], axis=0) for k in ks])
        mixed = dot_nt(low, weight).astype(BF)
        for m in ks:
            gm[b, m] = mixed[:, m * lanes : (m + 1) * lanes]
        remote = [mv.send(gm.at[b, 2], d_out.at[b, 2], Y)]
        remote.append(mv.send(gm.at[b, 3], d_out.at[b, 3], YCORE))
        remote.append(mv.send(gm.at[b, 1], d_out.at[b, 1], CORE))
        local = mv.keep(gm.at[b, 0], d_out.at[b, 0])
        for j in range(2):
            put.append(mv.keep(gmid.at[own_k[j]], gmid_out.at[b, j]))
        cot_sum = jnp.sum(cs[b, 0].astype(F32), 0, keepdims=True)
        if b == 0:
            backsum_out[...] = cot_sum
        else:
            backsum_out[...] += cot_sum
        return remote, local

    def tokens(ref, *at):
        return jnp.concatenate([ref[(b,) + at] for b in range(clips)], axis=0)

    def big_grads(m, slot):
        cot = side_by_side([tokens(gb, k) for k in ks])
        back = dot_tn(tokens(act, m), cot).astype(BF)
        own = dot_nn(turned[...], tokens(gin, m)).astype(BF)
        for k in ks:
            wg[slot, k, :hidden, :] = back[:, k * width : (k + 1) * width]
            wg[slot, k, hidden : hidden + width, :] = own[k * width : (k + 1) * width, :width]
            wg[slot, k, hidden + width :, :] = own[k * width : (k + 1) * width, width:]

    def held(kind, i):
        place_at = ((0, i, 0), (0, i, 1), (1, i, 0), (1, i, 1))
        m, k, side = place_at[kind]
        return wb.at[m, k, :, side * lanes : (side + 1) * lanes]

    def masked(kind, h, i):
        return wb.at[2 + kind, i, :, h * lanes : (h + 1) * lanes]

    heads = lanes // HEAD_DIM
    scale = HEAD_DIM ** (-0.5)

    def load_attention():
        for i in ks:
            part = slice(i * rows, (i + 1) * rows)
            attention_in.append(mv.keep(qkv_hbm.at[0, 1, part, :], held(0, i)))
            attention_in.append(mv.keep(qkv_hbm.at[0, 2, part, :], held(1, i)))
            attention_in.append(mv.keep(qkv_hbm.at[0, 0, part, :], held(2, i)))
        attention_in.append(mv.keep(ot_hbm.at[0], ot))

    attention_in = []

    def prepare(arrivals):
        remote, local = arrivals
        mv.arrive(*remote)
        mv.kept_done(local)
        mv.kept_done(*[mv.keep(d_out.at[0, i], held(3, i)) for i in ks])
        mv.kept_done(*attention_in)
        head = lax.broadcasted_iota(jnp.int32, (rows, lanes), 1) // HEAD_DIM
        for i in ks:
            part = slice(i * rows, (i + 1) * rows)
            q, grad = held(2, i)[...], held(3, i)[...]
            for h in range(heads):
                masked(0, h, i)[...] = jnp.where(head == h, q, jnp.zeros_like(q))
                masked(1, h, i)[...] = jnp.where(head == h, grad, jnp.zeros_like(grad))
            products = grad.astype(F32).T * ot[:, part]
            for h in range(heads):
                delta[h : h + 1, part] = jnp.sum(
                    products[h * HEAD_DIM : (h + 1) * HEAD_DIM], axis=0, keepdims=True
                )
        dqt[...] = jnp.zeros_like(dqt)

    attention_put = []

    def attend_back(m):
        keys, values = held(0, m)[...], held(1, m)[...]
        dk, dv = attend_back_block(
            keys,
            values,
            lambda h, i: masked(0, h, i)[...],
            lambda h, i: masked(1, h, i)[...],
            lambda h, part: lse_ref[0, h : h + 1, part],
            delta,
            dqt,
            rows,
        )
        if m >= 2:
            mv.kept_done(*attention_put[2 * m - 4 : 2 * m - 2])
        dks[m % 2] = dk * scale
        dvs[m % 2] = dv.astype(BF)
        attention_put.append(mv.keep(dks.at[m % 2], dk_out.at[m]))
        attention_put.append(mv.keep(dvs.at[m % 2], dv_out.at[m]))

    first = block(0)
    second = block(1)
    load_attention()
    for k in ks:
        turned[k * width : (k + 1) * width, :] = tokens(sec, k).T
    big_grads(3, 0)
    near = mv.send(wg.at[0], wgnear, CORE)
    big_grads(2, 1)
    mv.arrive(near)
    for k in ks:
        wg[1, k] = (wg[1, k].astype(F32) + wgnear[k].astype(F32)).astype(BF)
    arrivals = branch(0, first)
    prepare(arrivals)
    far = [mv.send(wg.at[1, k], far_out.at[k - 1], Y) for k in (1, 2)]
    far_own = [mv.keep(wg.at[1, k], far_own_out.at[i]) for i, k in enumerate((3, 0))]
    mv.send(outs.at[0], arrived_out, X)
    attend_back(0)
    attend_back(1)
    mv.wait_sent(near)
    big_grads(1, 0)
    mv.send(wg.at[0], near_out, CORE)
    attend_back(2)
    attend_back(3)
    mv.keep(dqt, dqt_out)
    branch(1, second)
    grads = side_by_side([tokens(xs, i) for i in range(2)])
    for m in ks:
        mixed = jnp.concatenate([ms[b, 0, m] for b in range(clips)], axis=0)
        out = dot_tn(mixed, grads).astype(BF)
        for k in ks:
            wgo[m, k] = out[:, k * width : (k + 1) * width]
    mv.keep(wgo, go_out)
    mv.wait_sent(*far)
    mv.kept_done(*far_own)
    big_grads(0, 1)
    mv.keep(wg.at[1], keep_out)
    mv.finish()


def attend_back_block(keys, values, query, grad_out, log_total, delta, dqt, rows):
    scale = HEAD_DIM ** (-0.5)
    flat_keys = keys.T
    row = lax.broadcasted_iota(jnp.int32, flat_keys.shape, 0) // HEAD_DIM
    dk = dv = None
    for h in range(keys.shape[1] // HEAD_DIM):
        turned = jnp.where(row == h, flat_keys, jnp.zeros_like(flat_keys))
        for i in range(4):
            part = slice(i * rows, (i + 1) * rows)
            q, grad = query(h, i), grad_out(h, i)
            probs = jnp.exp2(dot_nt(keys, q) * (scale * LOG2E) - log_total(h, part))
            slope = (probs * (dot_nt(values, grad) - delta[h : h + 1, part])).astype(BF)
            value_term, key_term = dot_nn(probs.astype(BF), grad), dot_nn(slope, q)
            dk = key_term if dk is None else dk + key_term
            dv = value_term if dv is None else dv + value_term
            dqt[:, part] += dot_nn(turned, slope)
    return dk, dv


def second_call(x, xp, c, cp, mo, mp, wo, wi, wb, qkv, ot, ln, b_in, b_out, b_other, b_back, lse):
    clips, rows, half = x.shape
    width = half // 2
    lanes = mo.shape[3]
    hidden = wi.shape[3]
    tall = hidden + 2 * width
    heads = lanes // HEAD_DIM
    outs = [
        ((clips, rows, half), F32),
        ((rows, half), BF),
        ((rows, half), BF),
        ((clips, 2, rows, width), F32),
        ((clips, 4, rows, lanes), BF),
        ((4, tall, width), BF),
        ((4, tall, width), BF),
        ((2, tall, width), BF),
        ((2, tall, width), BF),
        ((4, 4, lanes, width), BF),
        ((lanes, 4 * rows), F32),
        ((4, rows, lanes), F32),
        ((4, rows, lanes), BF),
        ((12, width), F32),
        ((4, hidden), F32),
        ((1, half), F32),
    ]
    small = [ln, b_in, b_out, b_other, b_back, lse]
    vmem = lambda kind, *shape: pltpu.VMEM(shape, kind)
    return pl.pallas_call(
        second_body,
        in_specs=[ANY] * 11 + [whole(a.shape) for a in small],
        out_specs=[ANY] * 13 + [whole(o[0]) for o in outs[13:]],
        out_shape=[jax.ShapeDtypeStruct(shape, kind) for shape, kind in outs],
        scratch_shapes=[
            vmem(BF, clips, 2, rows, half),
            vmem(BF, clips, 2, rows, half),
            vmem(BF, clips, 2, 4, rows, lanes),
            vmem(BF, *wo.shape),
            vmem(BF, *wi.shape),
            vmem(BF, *wb.shape),
            vmem(F32, clips, 4, rows, width),
            vmem(BF, clips, 4, rows, width),
            vmem(BF, clips, 4, rows, hidden),
            vmem(BF, clips, 4, rows, hidden),
            vmem(BF, clips, rows, half),
            vmem(F32, rows, half),
            vmem(BF, clips, 4, rows, width),
            vmem(BF, clips, 4, rows, width),
            vmem(F32, 4, rows, width),
            vmem(BF, clips, 4, rows, width),
            vmem(BF, clips, 4, rows, lanes),
            vmem(BF, 2, 4, tall, width),
            vmem(BF, 4, tall, width),
            vmem(BF, 4, 4, lanes, width),
            vmem(BF, 4 * width, clips * rows),
            vmem(F32, lanes, 4 * rows),
            vmem(F32, lanes, 4 * rows),
            vmem(F32, heads, 4 * rows),
            vmem(F32, 2, rows, lanes),
            vmem(BF, 2, rows, lanes),
            pltpu.SemaphoreType.DMA((24,)),
            pltpu.SemaphoreType.DMA((24,)),
            pltpu.SemaphoreType.DMA((72,)),
        ],
        compiler_params=pltpu.CompilerParams(
            vmem_limit_bytes=VMEM_BYTES, collective_id=2, has_side_effects=True
        ),
        name="layer_middle",
    )(x, xp, c, cp, mo, mp, wo, wi, wb, qkv, ot, *small)


def third_body(*refs):
    (qkv_hbm, ot_hbm, d_hbm, t_hbm, wq_hbm, n_hbm, keep_hbm, near_hbm, far_hbm, far_own) = refs[:10]
    (go_hbm, dqt_hbm, dk_hbm, dv_hbm, other_hbm, x_hbm, xp_hbm) = refs[10:17]
    (lse_ref, ln_ref, midsum_ref, insum_ref, backsum_ref) = refs[17:22]
    (ig_out, arrived_out, dense_out, qdense_out, early_out, ln1_out, qsum_out) = refs[22:29]
    (qkv, ot, d, tables, wq, qh, dh, delta, dqt, gj, pk, ps, near, hop, last) = refs[29:44]
    (nbuf, qacc, qs, qz, gk, gnear, gfar, gz, go, gonear, dk0, dqt0, xs, stats) = refs[44:58]
    (stats_in, early, early_in, late, late_in, late_x, send_sems, recv_sems, local_sems) = refs[58:]
    unused, count, lanes = qkv.shape
    clips = x_hbm.shape[0]
    rows = count // 4
    width = wq.shape[1]
    half = 2 * width
    heads = lanes // HEAD_DIM
    cut = rows // 2
    shard, ctx, tp = place()
    mv = Movers(send_sems, recv_sems, local_sems)
    ks = range(4)
    zs = (Z1, Z2, Z3)
    scale = HEAD_DIM ** (-0.5)

    tall = keep_hbm.shape[1]
    got_first = [
        mv.keep(dqt_hbm, dqt0),
        mv.keep(dk_hbm, dk0),
        mv.keep(dv_hbm, gj.at[0, :, :, 2 * lanes :]),
    ]
    got_w = [mv.keep(t_hbm, tables), mv.keep(wq_hbm, wq)]
    got_g = [
        [mv.keep(keep_hbm.at[k], gk.at[k, :tall]), mv.keep(near_hbm.at[k], gnear.at[k])]
        for k in (1, 2, 3, 0)
    ]
    for at in range(2):
        got_g[at].append(mv.keep(far_hbm.at[at], gfar.at[at + 1]))
    got_go = [mv.keep(go_hbm.at[2 * i], go.at[i]) for i in range(2)]
    got = [
        mv.keep(qkv_hbm.at[1], qkv),
        mv.keep(d_hbm.at[1], d),
        mv.keep(ot_hbm.at[1], ot),
    ]
    got_n = [mv.keep(n_hbm.at[0, m], nbuf.at[m]) for m in range(2)]
    got_x = [mv.keep(x_hbm, xs.at[0]), mv.keep(xp_hbm, xs.at[1])]
    mv.barrier([X, CORE, Y, YCORE, Z1, Z2, Z3])
    far_late = [mv.send(far_own.at[0], gfar.at[3], Y)]
    go_core = [mv.send(go_hbm.at[2 * i + 1], gonear.at[i], CORE) for i in range(2)]

    early[0, :12, :] = midsum_ref[...]
    for m in ks:
        for j in range(2):
            part = slice(j * width, (j + 1) * width)
            early[0, 12 + 2 * m + j : 13 + 2 * m + j, :] = insum_ref[m : m + 1, part]
    for j in range(2):
        early[0, 20 + j : 21 + j, :] = backsum_ref[:, j * width : (j + 1) * width]
    early[0, 22:, :] = jnp.zeros((2, width), F32)
    early_z = [mv.send(early.at[0], early_in.at[i], name) for i, name in enumerate(zs)]

    def prepare():
        mv.kept_done(*got)
        head = lax.broadcasted_iota(jnp.int32, (rows, lanes), 1) // HEAD_DIM
        for m in ks:
            part = slice(m * rows, (m + 1) * rows)
            q, grad = qkv[0, part, :], d[m]
            for h in range(heads):
                qh[h, part, :] = jnp.where(head == h, q, jnp.zeros_like(q))
                dh[h, part, :] = jnp.where(head == h, grad, jnp.zeros_like(grad))
            products = grad.astype(F32).T * ot[:, part]
            for h in range(heads):
                delta[h : h + 1, part] = jnp.sum(
                    products[h * HEAD_DIM : (h + 1) * HEAD_DIM], axis=0, keepdims=True
                )
        dqt[...] = jnp.zeros_like(dqt)

    def attend_back(m):
        mine = slice(m * rows, (m + 1) * rows)
        dk, dv = attend_back_block(
            qkv[1, mine, :],
            qkv[2, mine, :],
            lambda h, i: qh[h, i * rows : (i + 1) * rows, :],
            lambda h, i: dh[h, i * rows : (i + 1) * rows, :],
            lambda h, part: lse_ref[1, h : h + 1, part],
            delta,
            dqt,
            rows,
        )
        dk = dk * scale
        dk = dk * tables[0, m] + partner_lanes(dk * tables[1, m])
        gj[1, m, :, lanes : 2 * lanes] = dk.astype(BF)
        gj[1, m, :, 2 * lanes :] = dv.astype(BF)

    sums = [0.0, 0.0, 0.0]

    def join(b):
        mv.kept_done(*got_w, *got_first)
        sent = {}
        for m in (3, 2, 1, 0):
            part = slice(m * rows, (m + 1) * rows)
            dq = ((dqt0, dqt)[b][:, part] * scale).T
            if b == 0:
                dk = dk0[m]
                dk = dk * tables[0, m] + partner_lanes(dk * tables[1, m])
                gj[0, m, :, lanes : 2 * lanes] = dk.astype(BF)
            dq = dq * tables[0, m] + partner_lanes(dq * tables[1, m])
            gj[b, m, :, :lanes] = dq.astype(BF)
            for i in range(3):
                low = gj[b, m, :, i * lanes : (i + 1) * lanes].astype(F32)
                sums[i] = sums[i] + jnp.sum(low, axis=0, keepdims=True)
            for h in (1, 0):
                target = (pk, ps)[m % 2]
                for j in range(2):
                    term = dot_nt(gj[b, m], wq[piece_at(shard, tp, h, j)])
                    target[b, m // 2, h, :, j * width : (j + 1) * width] = term.astype(BF)
                if m % 2:
                    sent[m // 2, h] = mv.send(ps.at[b, m // 2, h], near.at[b, m // 2, h], CORE)
            if m == 2:
                hops = first_hop(b, sent)
        return sent, hops

    def first_hop(b, sent):
        mv.arrive(sent[1, 1])
        pk[b, 1, 1] = (pk[b, 1, 1].astype(F32) + near[b, 1, 1].astype(F32)).astype(BF)
        low = mv.send(pk.at[b, 1, 1, :cut], hop.at[b, 0], X)
        high = mv.send(pk.at[b, 1, 1, cut:], hop.at[b, 1], Y)
        return low, high

    def second_hop(b, sent, hops):
        mv.arrive(sent[1, 0], sent[0, 1])
        mv.arrive(hops[0])
        pk[b, 1, 0, :cut] = (
            pk[b, 1, 0, :cut].astype(F32)
            + near[b, 1, 0, :cut].astype(F32)
            + hop[b, 0].astype(F32)
        ).astype(BF)
        pk[b, 1, 0, cut:] = (
            pk[b, 1, 0, cut:].astype(F32) + near[b, 1, 0, cut:].astype(F32)
        ).astype(BF)
        far = mv.send(pk.at[b, 1, 0], last.at[b, 0], Y)
        mv.arrive(hops[1])
        pk[b, 0, 1, :cut] = (
            pk[b, 0, 1, :cut].astype(F32) + near[b, 0, 1, :cut].astype(F32)
        ).astype(BF)
        pk[b, 0, 1, cut:] = (
            pk[b, 0, 1, cut:].astype(F32)
            + near[b, 0, 1, cut:].astype(F32)
            + hop[b, 1].astype(F32)
        ).astype(BF)
        other = mv.send(pk.at[b, 0, 1], last.at[b, 1], X)
        return far, other

    def norm_one(b):
        mv.kept_done(*got_x)
        own, unused, inv = norm_parts(xs[0, b].astype(F32), xs[1, b].astype(F32))
        return own, inv

    gains = [0.0, 0.0]
    gain_own = jnp.where(tp == 0, ln_ref[:, :half], ln_ref[:, half:])

    def finish_sum(b, sent, lasts):
        mv.arrive(sent[0, 0], *lasts)
        own, inv = norm_one(b)
        grad = (
            pk[b, 0, 0].astype(F32)
            + near[b, 0, 0].astype(F32)
            + last[b, 0].astype(F32)
            + last[b, 1].astype(F32)
        )
        gains[0] = gains[0] + jnp.sum(grad * own, axis=0, keepdims=True)
        gains[1] = gains[1] + jnp.sum(grad, axis=0, keepdims=True)
        scaled = grad * gain_own
        ig_out[b] = scaled
        lane = lax.broadcasted_iota(jnp.int32, (rows, 128), 1)
        both = jnp.where(
            lane == 0,
            jnp.sum(scaled, 1, keepdims=True),
            jnp.where(lane == 1, jnp.sum(scaled * own, 1, keepdims=True), 0.0),
        )
        stats[b] = both.T[:8]
        return mv.send(stats.at[b], stats_in.at[b], X)

    def finish_grad(b, sent):
        mv.arrive(sent)
        own, inv = norm_one(b)
        total = stats[b] + stats_in[b]
        both = jnp.concatenate([total, jnp.zeros((120, rows), F32)], axis=0).T / (2 * half)
        grad = inv * (ig_out[b] - both[:, 0:1] - own * both[:, 1:2])
        ig_out[b] = grad

    def qkv_grads(b):
        for m in ks:
            at = 4 * b + m
            mv.kept_done(got_n[at])
            slot = at % 2
            for h, j in CHUNKS:
                cols = slice((2 * h + j) * width, (2 * h + j + 1) * width)
                term = dot_tn(nbuf[slot, :, cols], gj[b, m])
                if at == 0:
                    qacc[2 * h + j] = term
                else:
                    qacc[2 * h + j] += term
            if at + 2 < 8:
                got_n.append(mv.keep(n_hbm.at[(at + 2) // 4, (at + 2) % 4], nbuf.at[slot]))

    def add_far():
        mv.arrive(*go_core)
        mv.kept_done(*got_go)
        go[1] = (go[1].astype(F32) + gonear[1].astype(F32)).astype(BF)
        return mv.send(go.at[1], gonear.at[2], Y)

    def shard_send(at):
        k = (1, 2, 3, 0)[at]
        mv.kept_done(*got_g[at])
        if at >= 2:
            mv.arrive(far_late[at - 2])
        gk[k, :tall] = (
            gk[k, :tall].astype(F32) + gnear[k].astype(F32) + gfar[k].astype(F32)
        ).astype(BF)
        return [mv.send(gk.at[k, :tall], gz.at[k - 1, :tall], zs[k - 1])] if k else []

    def shard_sends_out(far):
        mv.arrive(far)
        sent = []
        for k in (1, 2, 3, 0):
            gk[k, tall:] = (
                go[0, k].astype(F32) + gonear[0, k].astype(F32) + gonear[2, k].astype(F32)
            ).astype(BF)
            if k:
                sent.append(mv.send(gk.at[k, tall:], gz.at[k - 1, tall:], zs[k - 1]))
        return sent

    def spread_far(ref):
        return mv.send(ref.at[ctx], ref.at[ctx], Y), mv.send(ref.at[ctx], ref.at[ctx], CORE)

    def spread_near(ref, far):
        mv.arrive(far[0])
        mv.send(ref.at[flip(ctx, 2)], ref.at[flip(ctx, 2)], CORE)

    gz_sent = shard_send(0) + shard_send(1)
    sent0, hops0 = join(0)
    prepare()
    attend_back(0)
    go_far = add_far()
    gz_sent += shard_send(2)
    lasts0 = second_hop(0, sent0, hops0)
    far_late.append(mv.send(far_own.at[1], gfar.at[0], Y))
    arrived = mv.send(other_hbm, arrived_out, X)
    attend_back(1)
    gz_sent += shard_sends_out(go_far)
    mv.arrive(*early_z)
    early[1] = early[0] + early_in[0] + early_in[1] + early_in[2]
    qkv_grads(0)
    attend_back(2)
    stats0 = finish_sum(0, sent0, lasts0)
    attend_back(3)
    sent1, hops1 = join(1)
    qkv_grads(1)
    for h, j in CHUNKS:
        qs[piece_at(shard, tp, h, j)] = qacc[2 * h + j].astype(BF)
    q_sent = [mv.send(qs.at[k + 1], qz.at[k], name) for k, name in enumerate(zs)]
    lasts1 = second_hop(1, sent1, hops1)
    shard_send(3)
    mv.arrive(*gz_sent)
    for part in (slice(0, tall), slice(tall, gz.shape[1])):
        gk[0, part] = (
            gk[0, part].astype(F32)
            + gz[0, part].astype(F32)
            + gz[1, part].astype(F32)
            + gz[2, part].astype(F32)
        ).astype(BF)
    placed = mv.keep(gk.at[0], dense_out.at[ctx])
    finish_grad(0, stats0)
    mv.kept_done(placed)
    dense_far = spread_far(dense_out)
    stats1 = finish_sum(1, sent1, lasts1)
    late[...] = jnp.zeros_like(late)
    for i in range(2):
        for j in range(4):
            late[4 * i + j : 4 * i + j + 1, :] = gains[i][:, j * 128 : (j + 1) * 128]
    for i in range(3):
        late[pl.ds(8 + 3 * ctx + i, 1), :] = sums[i]
    late_z = [mv.send(late, late_in.at[i], name) for i, name in enumerate(zs)]
    finish_grad(1, stats1)
    mv.arrive(*late_z)
    late_x[0] = late[...] + late_in[0] + late_in[1] + late_in[2]
    others = (CORE, Y, YCORE)
    late_c = [mv.send(late_x.at[0], late_in.at[3 + i], name) for i, name in enumerate(others)]
    mv.arrive(*q_sent)
    qs[0] = sum((qz[i].astype(F32) for i in range(3)), qs[0].astype(F32)).astype(BF)
    q_placed = mv.keep(qs.at[0], qdense_out.at[ctx])
    mv.kept_done(q_placed)
    q_far = spread_far(qdense_out)
    early_x = [mv.send(early.at[1], early_in.at[3 + i], name) for i, name in enumerate(others)]
    mv.arrive(*late_c)
    late_x[1] = late_x[0] + late_in[3] + late_in[4] + late_in[5]
    crossed = mv.send(late_x.at[1], late_x.at[2], X)
    mv.arrive(*early_x)
    early_out[...] = early[1] + early_in[3] + early_in[4] + early_in[5]
    qsum_out[...] = late_x[1, 8:20, :]
    spread_near(dense_out, dense_far)
    spread_near(qdense_out, q_far)
    mv.arrive(crossed)
    for i in range(2):
        part = slice(4 * i, 4 * i + 4)
        ln1_out[i, pl.ds(4 * tp, 4), :] = late_x[1, part, :]
        ln1_out[i, pl.ds(4 * (1 - tp), 4), :] = late_x[2, part, :]
    mv.finish()


def third_call(
    qkv, ot, d, tables, wq, normed, keep, near, far, own, go, dqt, dk, dv, other, x, xp, *small
):
    unused, unused, count, lanes = qkv.shape
    clips, rows, half = x.shape
    width = half // 2
    tall = keep.shape[1]
    heads = lanes // HEAD_DIM
    outs = [
        ((clips, rows, half), F32),
        ((rows, half), BF),
        ((4, tall + lanes, width), BF),
        ((4, width, 3 * lanes), BF),
        ((24, width), F32),
        ((2, 8, 128), F32),
        ((12, lanes), F32),
    ]
    vmem = lambda kind, *shape: pltpu.VMEM(shape, kind)
    return pl.pallas_call(
        third_body,
        in_specs=[ANY] * 17 + [whole(a.shape) for a in small],
        out_specs=[whole(outs[0][0]), ANY, ANY, ANY] + [whole(o[0]) for o in outs[4:]],
        out_shape=[jax.ShapeDtypeStruct(shape, kind) for shape, kind in outs],
        scratch_shapes=[
            vmem(BF, *qkv.shape[1:]),
            vmem(F32, *ot.shape[1:]),
            vmem(BF, *d.shape[1:]),
            vmem(F32, *tables.shape),
            vmem(BF, *wq.shape),
            vmem(BF, heads, count, lanes),
            vmem(BF, heads, count, lanes),
            vmem(F32, heads, count),
            vmem(F32, lanes, count),
            vmem(BF, clips, 4, rows, 3 * lanes),
            vmem(BF, clips, 2, 2, rows, half),
            vmem(BF, clips, 2, 2, rows, half),
            vmem(BF, clips, 2, 2, rows, half),
            vmem(BF, clips, 2, rows // 2, half),
            vmem(BF, clips, 2, rows, half),
            vmem(BF, 2, rows, 2 * half),
            vmem(F32, 4, width, 3 * lanes),
            vmem(BF, *wq.shape),
            vmem(BF, 3, width, 3 * lanes),
            vmem(BF, 4, tall + lanes, width),
            vmem(BF, 4, tall, width),
            vmem(BF, 4, tall, width),
            vmem(BF, 3, tall + lanes, width),
            vmem(BF, 2, 4, lanes, width),
            vmem(BF, 3, 4, lanes, width),
            vmem(F32, *dk.shape),
            vmem(F32, *dqt.shape),
            vmem(BF, 2, clips, rows, half),
            vmem(F32, clips, 8, rows),
            vmem(F32, clips, 8, rows),
            vmem(F32, 2, 24, width),
            vmem(F32, 6, 24, width),
            vmem(F32, 24, 128),
            vmem(F32, 6, 24, 128),
            vmem(F32, 3, 24, 128),
            pltpu.SemaphoreType.DMA((64,)),
            pltpu.SemaphoreType.DMA((64,)),
            pltpu.SemaphoreType.DMA((48,)),
        ],
        compiler_params=pltpu.CompilerParams(
            vmem_limit_bytes=VMEM_BYTES, collective_id=3, has_side_effects=True
        ),
        name="layer_back",
    )(qkv, ot, d, tables, wq, normed, keep, near, far, own, go, dqt, dk, dv, other, x, xp, *small)


def fourth_body(
    dense_ref, q_ref, y_ref, far_ref, ig_ref, mid_ref, other_ref, wb_ref, wi_ref, wo_ref, wq_ref, yo_ref, go_ref
):
    width = q_ref.shape[1]
    hidden = wb_ref.shape[0]
    lanes = wo_ref.shape[0]
    wb_ref[...] = dense_ref[0, :hidden, :].astype(F32)
    for j in range(2):
        at = hidden + j * width
        wi_ref[:, j * width : (j + 1) * width] = dense_ref[0, at : at + width, :].astype(F32)
    wo_ref[...] = dense_ref[0, hidden + 2 * width :, :].astype(F32)
    for i in range(3):
        wq_ref[i] = q_ref[0, :, i * lanes : (i + 1) * lanes].astype(F32)
    for b, ref in enumerate((far_ref, other_ref)):
        yo_ref[b] = (y_ref[b] + ref[...].astype(F32)).astype(BF)
    for j in range(2):
        part = slice(j * width, (j + 1) * width)
        go_ref[:, :, part] = ig_ref[:, :, part] + mid_ref[:, j]


def fourth_call(dense, qkv_dense, y, arrived, input_part, mids):
    four, tall, width = dense.shape
    lanes = qkv_dense.shape[2] // 3
    hidden = tall - 2 * width - lanes
    clips, rows, half = y.shape
    one = pl.BlockSpec((rows // four, half), lambda a: (a, 0))
    some = pl.BlockSpec((clips, rows // four, half), lambda a: (0, a, 0))
    return pl.pallas_call(
        fourth_body,
        grid=(four,),
        in_specs=[
            pl.BlockSpec((1, tall, width), lambda a: (a, 0, 0)),
            pl.BlockSpec((1, width, 3 * lanes), lambda a: (a, 0, 0)),
            some,
            one,
            some,
            pl.BlockSpec((clips, 2, rows // four, width), lambda a: (0, 0, a, 0)),
            one,
        ],
        out_specs=[
            pl.BlockSpec((hidden, width), lambda a: (a, 0)),
            pl.BlockSpec((width, hidden), lambda a: (0, a)),
            pl.BlockSpec((lanes, width), lambda a: (a, 0)),
            pl.BlockSpec((3, width, lanes), lambda a: (0, 0, a)),
            some,
            some,
        ],
        out_shape=[
            jax.ShapeDtypeStruct((four * hidden, width), F32),
            jax.ShapeDtypeStruct((width, four * hidden), F32),
            jax.ShapeDtypeStruct((four * lanes, width), F32),
            jax.ShapeDtypeStruct((3, width, four * lanes), F32),
            jax.ShapeDtypeStruct(y.shape, BF),
            jax.ShapeDtypeStruct(y.shape, F32),
        ],
        compiler_params=pltpu.CompilerParams(vmem_limit_bytes=VMEM_BYTES),
        name="owned_gradients",
    )(dense, qkv_dense, y, arrived[0], input_part, mids, arrived[1])


def fast_device(
    inputs,
    ln1_gain,
    ln1_bias,
    w_qkv,
    b_qkv,
    w_out,
    b_out,
    ln2_gain,
    ln2_bias,
    w_in,
    b_in,
    w_back,
    b_back,
    cotangent,
):
    clips, rows, half = inputs.shape
    width = half // 2
    lanes = half // 4
    hidden = w_in.shape[1] // 4
    shard, ctx, tp = (lax.axis_index(name) for name in ("shard", "ctx", "tp"))
    ids = jnp.stack([shard, ctx, tp]).astype(jnp.int32)
    def halves(vector):
        vector = vector.astype(F32)
        return jnp.concatenate(
            [
                lax.dynamic_slice_in_dim(vector, tp * half, half),
                lax.dynamic_slice_in_dim(vector, (1 - tp) * half, half),
            ]
        )

    ln_qkv = jnp.stack([halves(ln1_gain), halves(ln1_bias)])
    bias_qkv = (
        lax.dynamic_slice_in_dim(b_qkv, ctx * lanes, lanes, axis=1)
        .reshape(1, 3 * lanes)
        .astype(F32)
    )
    bias_in = b_in.reshape(4, hidden).astype(F32)

    xp, cp, normed, qkv, ot, lse, mo, mp, wq, wo, wi, wb, bias_other, tables = first_call(
        inputs,
        cotangent,
        jnp.transpose(w_qkv, (1, 0, 2)),
        w_out,
        w_in,
        w_back,
        bias_qkv,
        ln_qkv,
        jnp.broadcast_to(b_out, (16, half)),
    )
    ln_two = jnp.concatenate([ln2_gain, ln2_bias]).astype(F32).reshape(8, width)
    middle = second_call(
        inputs,
        xp,
        cotangent,
        cp,
        mo,
        mp,
        wo,
        wi,
        wb,
        qkv,
        ot,
        ln_two,
        bias_in,
        b_out.reshape(1, half),
        bias_other,
        b_back.reshape(1, half),
        lse,
    )
    y, other, arrived, mids, grad_heads, keep, near, far, far_own, grads_out, dqt, dk, dv = middle[:13]
    input_part, arrived_late, dense, qkv_dense, early, grad_ln1, q_sums = third_call(
        qkv,
        ot,
        grad_heads,
        tables,
        wq,
        normed,
        keep,
        near,
        far,
        far_own,
        grads_out,
        dqt,
        dk,
        dv,
        other,
        inputs,
        xp,
        lse,
        ln1_gain.astype(F32).reshape(1, 2 * half),
        *middle[13:],
    )
    mid_total = early[:12].reshape(3, 2 * half)
    grad_b_out = lax.dynamic_slice_in_dim(mid_total[2], tp * half, half)
    grad_b_in = early[12:20].reshape(4 * hidden)
    grad_b_back = early[20:22].reshape(half)
    grad_b_qkv = q_sums.reshape(4, 3, lanes).transpose(1, 0, 2).reshape(3, 4 * lanes)
    grad_w_back, grad_w_in, grad_w_out, grad_w_qkv, output, input_grad = fourth_call(
        dense, qkv_dense, y, (arrived, arrived_late), input_part, mids
    )
    grad_w_qkv = jnp.transpose(grad_w_qkv, (1, 0, 2))
    return (
        output,
        input_grad,
        grad_ln1[0].reshape(2 * half),
        grad_ln1[1].reshape(2 * half),
        grad_w_qkv,
        grad_b_qkv,
        grad_w_out,
        grad_b_out,
        mid_total[0],
        mid_total[1],
        grad_w_in,
        grad_b_in,
        grad_w_back,
        grad_b_back,
    )


def quick_form_fits(mesh):
    return (mesh.shape["shard"], mesh.shape["ctx"], mesh.shape["tp"]) == (4, 4, 2)


def solution(mesh):
    placed = (
        P("shard", "ctx", "tp"),
        P(),
        P(),
        P("shard", None, "tp"),
        P(None, "tp"),
        P("tp", "shard"),
        P("tp"),
        P(),
        P(),
        P("shard", "tp"),
        P("tp"),
        P("tp", "shard"),
        P("tp"),
        P("shard", "ctx", "tp"),
    )
    return jax.shard_map(
        fast_device if quick_form_fits(mesh) else per_device,
        mesh=mesh,
        in_specs=placed,
        out_specs=(
            P("shard", "ctx", "tp"),
            P("shard", "ctx", "tp"),
            P(),
            P(),
            P("shard", None, "tp"),
            P(None, "tp"),
            P("tp", "shard"),
            P("tp"),
            P(),
            P(),
            P("shard", "tp"),
            P("tp"),
            P("tp", "shard"),
            P("tp"),
        ),
        check_vma=False,
    )
```

```python
import math

import jax
import jax.numpy as jnp
from jax import lax
from jax.experimental import pallas as pl
from jax.experimental.pallas import tpu as pltpu
from jax.sharding import PartitionSpec as P

HEAD_DIM = 64
GH = 16
GW = 16


EPSILON = 1e-06
NEG_LARGE = -1e30


def rotary_tables(first_row, row_count):
    segment = 2 * (HEAD_DIM // 3 // 2)
    halfway = segment // 2
    places = first_row + jnp.arange(row_count, dtype=jnp.int32)
    frames = places // (GH * GW)
    rows_at = places // GW % GH
    cols_at = places % GW
    column = jnp.arange(HEAD_DIM, dtype=jnp.int32)
    segment_of = column // segment
    within = column % segment
    frequency = jnp.power(10000.0, -(within % halfway).astype(jnp.float32) / halfway)
    position = jnp.where(
        segment_of[None, :] == 0,
        frames[:, None],
        jnp.where(segment_of[None, :] == 1, rows_at[:, None], cols_at[:, None]),
    )
    angles = position.astype(jnp.float32) * frequency[None, :]
    active = (column < 3 * segment)[None, :]
    cosines = jnp.where(active, jnp.cos(angles), 1.0)
    sine_table = jnp.where(
        active, jnp.where((within < halfway)[None, :], -jnp.sin(angles), jnp.sin(angles)), 0.0
    )
    return (cosines, sine_table)


def partner(tensor):
    segment = 2 * (HEAD_DIM // 3 // 2)
    halfway = segment // 2
    pieces = []
    for number in range(3):
        offset = number * segment
        pieces.append(tensor[..., offset + halfway : offset + segment])
        pieces.append(tensor[..., offset : offset + halfway])
    pieces.append(tensor[..., 3 * segment :])
    return jnp.concatenate(pieces, axis=-1)


def rotate(tensor, cosines, sine_table):
    return tensor * cosines + partner(tensor) * sine_table


def rotate_back(gradient, cosines, sine_table):
    return gradient * cosines + partner(gradient * sine_table)


def normalize(tensor, gain, shift):
    center = tensor - jnp.mean(tensor, axis=-1, keepdims=True)
    spread = jnp.mean(center * center, axis=-1, keepdims=True)
    inv_std = lax.rsqrt(spread + EPSILON)
    scaled = center * inv_std
    return (scaled * gain + shift, scaled, inv_std)


def norm_back(grad_out, scaled, inv_std, gain):
    grad_scaled = grad_out * gain
    mean_one = jnp.mean(grad_scaled, axis=-1, keepdims=True)
    mean_two = jnp.mean(grad_scaled * scaled, axis=-1, keepdims=True)
    return inv_std * (grad_scaled - mean_one - scaled * mean_two)


def tp_rows(sharded):
    return lax.all_gather(sharded, "tp", axis=2, tiled=True)


def tensor_sum(summand):
    return lax.psum_scatter(
        summand.astype(jnp.bfloat16), "tp", scatter_dimension=2, tiled=True
    ).astype(jnp.float32)


def back_total(summand):
    return lax.psum(summand.astype(jnp.bfloat16), "tp").astype(jnp.float32)


def fetch_weights(w_qkv, w_out, w_in, w_back):
    return (
        lax.all_gather(w_qkv, "shard", axis=0, tiled=True),
        lax.all_gather(w_out, "shard", axis=1, tiled=True),
        lax.all_gather(w_in, "shard", axis=0, tiled=True),
        lax.all_gather(w_back, "shard", axis=1, tiled=True),
    )


def forward(inputs, params, weights, cosines, sine_table):
    gain_one, shift_one, b_qkv, b_out, gain_two, shift_two, b_in, b_back = params
    w_qkv_all, w_out_all, w_in_all, w_back_all = weights
    clip_count, row_count, width_local = inputs.shape
    heads_local = width_local // HEAD_DIM
    score_scale = HEAD_DIM ** (-0.5)
    tokens = tp_rows(inputs).astype(jnp.float32)
    normed, scaled_one, inv_one = normalize(tokens, gain_one, shift_one)
    normed_low = normed.astype(jnp.bfloat16)
    joined = (
        jnp.einsum("csd,dkh->cskh", normed_low, w_qkv_all, preferred_element_type=jnp.float32)
        + b_qkv
    )
    shaped = joined.reshape(clip_count, row_count, 3, heads_local, HEAD_DIM)
    queries = rotate(shaped[:, :, 0], cosines, sine_table).astype(jnp.bfloat16)
    key_rows = rotate(shaped[:, :, 1], cosines, sine_table).astype(jnp.bfloat16)
    values = shaped[:, :, 2].astype(jnp.bfloat16)
    key_flat = key_rows.reshape(clip_count, row_count, width_local)
    value_flat = values.reshape(clip_count, row_count, width_local)

    def absorb_block(running, block_pair):
        row_max, row_sum, weighted = running
        key_piece, value_piece = block_pair
        scores = (
            jnp.einsum("cqhd,ckhd->chqk", queries, key_piece, preferred_element_type=jnp.float32)
            * score_scale
        )
        next_max = jnp.maximum(row_max, jnp.max(scores, axis=-1))
        factor = jnp.exp(row_max - next_max)
        weights_now = jnp.exp(scores - next_max[..., None])
        row_sum = row_sum * factor + jnp.sum(weights_now, axis=-1)
        weighted = weighted * factor[..., None] + jnp.einsum(
            "chqk,ckhd->chqd",
            weights_now.astype(jnp.bfloat16),
            value_piece,
            preferred_element_type=jnp.float32,
        )
        return ((next_max, row_sum, weighted), None)

    initial = (
        jnp.full((clip_count, heads_local, row_count), NEG_LARGE, jnp.float32),
        jnp.zeros((clip_count, heads_local, row_count), jnp.float32),
        jnp.zeros((clip_count, heads_local, row_count, HEAD_DIM), jnp.float32),
    )
    running = initial
    pieces = (
        lax.all_gather(key_flat, "ctx", axis=1, tiled=True),
        lax.all_gather(value_flat, "ctx", axis=1, tiled=True),
    )
    piece_rows = pieces[0].shape[1]
    block_size = math.gcd(piece_rows, 512)
    block_count = piece_rows // block_size
    key_blocks = jnp.moveaxis(
        pieces[0].reshape(clip_count, block_count, block_size, heads_local, HEAD_DIM), 1, 0
    )
    value_blocks = jnp.moveaxis(
        pieces[1].reshape(clip_count, block_count, block_size, heads_local, HEAD_DIM), 1, 0
    )
    running, unused = lax.scan(absorb_block, running, (key_blocks, value_blocks))
    row_max, row_sum, weighted = running
    log_total = row_max + jnp.log(row_sum)
    mixed_heads = jnp.transpose(weighted / row_sum[..., None], (0, 2, 1, 3))
    mixed_low = mixed_heads.reshape(clip_count, row_count, width_local).astype(jnp.bfloat16)
    branch = tensor_sum(
        jnp.einsum("csh,hd->csd", mixed_low, w_out_all, preferred_element_type=jnp.float32)
    )
    middle = inputs.astype(jnp.float32) + branch + b_out
    middle_all = lax.all_gather(middle.astype(jnp.bfloat16), "tp", axis=2, tiled=True).astype(
        middle.dtype
    )
    second, scaled_two, inv_two = normalize(middle_all, gain_two, shift_two)
    second_low = second.astype(jnp.bfloat16)
    inner_pre = (
        jnp.einsum("csd,df->csf", second_low, w_in_all, preferred_element_type=jnp.float32) + b_in
    )
    active_low = jax.nn.gelu(inner_pre, approximate=False).astype(jnp.bfloat16)
    return {
        "normed_low": normed_low,
        "scaled_one": scaled_one,
        "inv_one": inv_one,
        "queries": queries,
        "key_flat": key_flat,
        "value_flat": value_flat,
        "mixed_heads": mixed_heads,
        "mixed_low": mixed_low,
        "log_total": log_total,
        "middle": middle,
        "scaled_two": scaled_two,
        "inv_two": inv_two,
        "second_low": second_low,
        "inner_pre": inner_pre,
        "active_low": active_low,
    }


def per_device(
    inputs,
    ln1_gain,
    ln1_bias,
    w_qkv,
    b_qkv,
    w_out,
    b_out,
    ln2_gain,
    ln2_bias,
    w_in,
    b_in,
    w_back,
    b_back,
    cotangent,
):
    params = tuple(
        (
            parameter.astype(jnp.float32)
            for parameter in (ln1_gain, ln1_bias, b_qkv, b_out, ln2_gain, ln2_bias, b_in, b_back)
        )
    )
    gain_one = params[0]
    gain_two = params[4]
    clip_count, row_count, width_local = inputs.shape
    heads_local = width_local // HEAD_DIM
    score_scale = HEAD_DIM ** (-0.5)
    tp_index = lax.axis_index("tp")
    share_start = tp_index * width_local
    cosines, sine_table = rotary_tables(lax.axis_index("ctx") * row_count, row_count)
    cosines = cosines[:, None, :]
    sine_table = sine_table[:, None, :]
    weights = fetch_weights(w_qkv, w_out, w_in, w_back)
    stored_acts = forward(inputs, params, weights, cosines, sine_table)
    output = (
        stored_acts["middle"]
        + tensor_sum(
            jnp.einsum(
                "csf,fd->csd",
                stored_acts["active_low"],
                weights[3],
                preferred_element_type=jnp.float32,
            )
        )
        + params[7]
    ).astype(jnp.bfloat16)
    weights = fetch_weights(w_qkv, w_out, w_in, w_back)
    stored_acts = forward(inputs, params, weights, cosines, sine_table)
    w_qkv_all, w_out_all, w_in_all, w_back_all = weights
    grad_low = tp_rows(cotangent)
    grad_full = grad_low.astype(jnp.float32)
    grad_active = jnp.einsum(
        "csd,fd->csf", grad_low, w_back_all, preferred_element_type=jnp.float32
    )
    unused, gelu_back = jax.vjp(
        lambda argument: jax.nn.gelu(argument, approximate=False), stored_acts["inner_pre"]
    )
    grad_inner = gelu_back(grad_active)[0].astype(jnp.bfloat16)
    grad_w_back = jnp.einsum(
        "csf,csd->fd", stored_acts["active_low"], grad_low, preferred_element_type=jnp.float32
    )
    grad_b_back = jnp.sum(cotangent.astype(jnp.float32), axis=(0, 1))
    grad_w_in = jnp.einsum(
        "csd,csf->df", stored_acts["second_low"], grad_inner, preferred_element_type=jnp.float32
    )
    grad_b_in = jnp.sum(grad_inner.astype(jnp.float32), axis=(0, 1))
    grad_second = back_total(
        jnp.einsum("csf,df->csd", grad_inner, w_in_all, preferred_element_type=jnp.float32)
    )
    grad_gain_two = jnp.sum(grad_second * stored_acts["scaled_two"], axis=(0, 1))
    grad_shift_two = jnp.sum(grad_second, axis=(0, 1))
    grad_middle = grad_full + norm_back(
        grad_second, stored_acts["scaled_two"], stored_acts["inv_two"], gain_two
    )
    grad_branch = grad_middle.astype(jnp.bfloat16)
    grad_b_out = lax.dynamic_slice_in_dim(
        jnp.sum(grad_branch.astype(jnp.float32), axis=(0, 1)), share_start, width_local
    )
    grad_w_out = jnp.einsum(
        "csh,csd->hd", stored_acts["mixed_low"], grad_branch, preferred_element_type=jnp.float32
    )
    grad_mixed = jnp.einsum(
        "csd,hd->csh", grad_branch, w_out_all, preferred_element_type=jnp.float32
    ).astype(jnp.bfloat16)
    key_all, value_all = (
        lax.all_gather(stored_acts["key_flat"], "ctx", axis=1, tiled=True),
        lax.all_gather(stored_acts["value_flat"], "ctx", axis=1, tiled=True),
    )
    length = key_all.shape[1]
    block_size = math.gcd(length, 512)
    block_count = length // block_size
    grad_heads = grad_mixed.reshape(clip_count, row_count, heads_local, HEAD_DIM)
    queries = stored_acts["queries"]
    log_total = stored_acts["log_total"]
    row_delta = jnp.einsum(
        "cqhd,chqd->chq",
        grad_heads.astype(jnp.float32),
        jnp.transpose(stored_acts["mixed_heads"], (0, 2, 1, 3)),
    )
    key_blocks = jnp.moveaxis(
        key_all.reshape(clip_count, block_count, block_size, heads_local, HEAD_DIM), 1, 0
    )
    value_blocks = jnp.moveaxis(
        value_all.reshape(clip_count, block_count, block_size, heads_local, HEAD_DIM), 1, 0
    )

    def key_step(grad_query, block_pair):
        key_piece, value_piece = block_pair
        scores = (
            jnp.einsum("cqhd,ckhd->chqk", queries, key_piece, preferred_element_type=jnp.float32)
            * score_scale
        )
        prob_block = jnp.exp(scores - log_total[..., None])
        grad_probs = jnp.einsum(
            "cqhd,ckhd->chqk", grad_heads, value_piece, preferred_element_type=jnp.float32
        )
        grad_scores = (prob_block * (grad_probs - row_delta[..., None])).astype(jnp.bfloat16)
        grad_query = grad_query + jnp.einsum(
            "chqk,ckhd->cqhd", grad_scores, key_piece, preferred_element_type=jnp.float32
        )
        grad_key = (
            jnp.einsum("chqk,cqhd->ckhd", grad_scores, queries, preferred_element_type=jnp.float32)
            * score_scale
        )
        grad_value = jnp.einsum(
            "chqk,cqhd->ckhd",
            prob_block.astype(jnp.bfloat16),
            grad_heads,
            preferred_element_type=jnp.float32,
        )
        return (grad_query, (grad_key, grad_value))

    grad_query, (key_terms, value_terms) = lax.scan(
        key_step,
        jnp.zeros((clip_count, row_count, heads_local, HEAD_DIM), jnp.float32),
        (key_blocks, value_blocks),
    )
    grad_query = grad_query * score_scale
    key_terms = jnp.moveaxis(key_terms, 0, 1).reshape(clip_count, length, width_local)
    value_terms = jnp.moveaxis(value_terms, 0, 1).reshape(clip_count, length, width_local)
    grad_keys, grad_values = (
        lax.psum_scatter(
            key_terms.astype(jnp.bfloat16), "ctx", scatter_dimension=1, tiled=True
        ).astype(jnp.float32),
        lax.psum_scatter(
            value_terms.astype(jnp.bfloat16), "ctx", scatter_dimension=1, tiled=True
        ).astype(jnp.float32),
    )
    grad_q_pre = rotate_back(grad_query, cosines, sine_table).reshape(
        clip_count, row_count, width_local
    )
    grad_k_pre = rotate_back(
        grad_keys.reshape(clip_count, row_count, heads_local, HEAD_DIM), cosines, sine_table
    ).reshape(clip_count, row_count, width_local)
    grad_joined = jnp.stack([grad_q_pre, grad_k_pre, grad_values], axis=2).astype(jnp.bfloat16)
    grad_w_qkv = jnp.einsum(
        "csd,cskh->dkh", stored_acts["normed_low"], grad_joined, preferred_element_type=jnp.float32
    )
    grad_b_qkv = jnp.sum(grad_joined.astype(jnp.float32), axis=(0, 1))
    normed_term = jnp.einsum(
        "cskh,dkh->csd", grad_joined, w_qkv_all, preferred_element_type=jnp.float32
    )
    grad_normed = back_total(normed_term)
    grad_gain_one = jnp.sum(grad_normed * stored_acts["scaled_one"], axis=(0, 1))
    grad_shift_one = jnp.sum(grad_normed, axis=(0, 1))
    grad_tokens = grad_middle + norm_back(
        grad_normed, stored_acts["scaled_one"], stored_acts["inv_one"], gain_one
    )
    input_grad = lax.dynamic_slice_in_dim(grad_tokens, share_start, width_local, axis=2)
    summed = (
        lax.psum(grad_w_qkv.astype(jnp.bfloat16), "ctx").astype(jnp.float32),
        lax.psum(grad_w_out.astype(jnp.bfloat16), "ctx").astype(jnp.float32),
        lax.psum(grad_w_in.astype(jnp.bfloat16), "ctx").astype(jnp.float32),
        lax.psum(grad_w_back.astype(jnp.bfloat16), "ctx").astype(jnp.float32),
    )
    owned_grads = (
        lax.psum_scatter(
            summed[0].astype(jnp.bfloat16), "shard", scatter_dimension=0, tiled=True
        ).astype(jnp.float32),
        lax.psum_scatter(
            summed[1].astype(jnp.bfloat16), "shard", scatter_dimension=1, tiled=True
        ).astype(jnp.float32),
        lax.psum_scatter(
            summed[2].astype(jnp.bfloat16), "shard", scatter_dimension=0, tiled=True
        ).astype(jnp.float32),
        lax.psum_scatter(
            summed[3].astype(jnp.bfloat16), "shard", scatter_dimension=1, tiled=True
        ).astype(jnp.float32),
    )
    small_sums = lax.psum(
        (
            grad_gain_one,
            grad_shift_one,
            grad_b_qkv,
            grad_b_out,
            grad_gain_two,
            grad_shift_two,
            grad_b_in,
            grad_b_back,
        ),
        ("shard", "ctx"),
    )
    return (
        output,
        input_grad,
        small_sums[0],
        small_sums[1],
        owned_grads[0],
        small_sums[2],
        owned_grads[1],
        small_sums[3],
        small_sums[4],
        small_sums[5],
        owned_grads[2],
        small_sums[6],
        owned_grads[3],
        small_sums[7],
    )


LOG2E = 1.4426950408889634
BF = jnp.bfloat16
F32 = jnp.float32
VMEM_BYTES = 60 * 2**20


def dot_nt(a, b):
    return lax.dot_general(a, b, (((1,), (1,)), ((), ())), preferred_element_type=F32)


def dot_nn(a, b):
    return lax.dot_general(a, b, (((1,), (0,)), ((), ())), preferred_element_type=F32)


def dot_tn(a, b):
    return lax.dot_general(a, b, (((0,), (0,)), ((), ())), preferred_element_type=F32)


def whole(shape):
    return pl.BlockSpec(shape, lambda *_: (0,) * len(shape))


CHUNKS = ((0, 0), (0, 1), (1, 0), (1, 1))


def partner_lanes(tensor):
    segment = 2 * (HEAD_DIM // 3 // 2)
    halfway = segment // 2
    width = tensor.shape[1]
    lane = lax.broadcasted_iota(jnp.int32, tensor.shape, 1) % HEAD_DIM
    first = lane % segment < halfway
    return jnp.where(
        first, pltpu.roll(tensor, width - halfway, 1), pltpu.roll(tensor, halfway, 1)
    )


def norm_parts(own, other):
    total = 2 * own.shape[1]
    mean = (jnp.sum(own, 1, keepdims=True) + jnp.sum(other, 1, keepdims=True)) / total
    own, other = own - mean, other - mean
    spread = (
        jnp.sum(own * own, 1, keepdims=True) + jnp.sum(other * other, 1, keepdims=True)
    ) / total
    inv = lax.rsqrt(spread + EPSILON)
    return own * inv, other * inv, inv


def flip(value, bit):
    if bit == 1:
        return value + 1 - 2 * lax.rem(value, 2)
    return lax.rem(value + 2, 4)


def place():
    return tuple(lax.axis_index(name) for name in ("shard", "ctx", "tp"))


def piece_at(shard, tp, half, part):
    found = lax.rem(shard + 2 * lax.rem(tp + half, 2), 4)
    return flip(found, 1) if part else found


X, CORE, Y, YCORE, Z1, Z2, Z3 = range(7)


class Movers:
    def __init__(self, send_sems, recv_sems, local_sems):
        shard, ctx, tp = place()
        self.sems = (send_sems, recv_sems, local_sems)
        self.sent, self.kept = [], []
        self.partners = {
            X: {"tp": 1 - tp},
            CORE: {"ctx": flip(ctx, 1)},
            Y: {"ctx": flip(ctx, 2)},
            YCORE: {"ctx": flip(flip(ctx, 2), 1)},
            Z1: {"shard": flip(shard, 1)},
            Z2: {"shard": flip(shard, 2)},
            Z3: {"shard": flip(flip(shard, 2), 1)},
        }
        self.inner = jnp.logical_or(shard == 1, shard == 2)
        self.used = 0
        self.left = set()

    def barrier(self, names):
        barrier = pltpu.get_barrier_semaphore()
        for name in names:
            pl.semaphore_signal(
                barrier,
                inc=1,
                device_id=self.partners[name],
                device_id_type=pl.DeviceIdType.MESH,
            )
        pl.semaphore_wait(barrier, len(names))

    def remote(self, source, target, name, send_at, recv_at):
        return pltpu.make_async_remote_copy(
            src_ref=source,
            dst_ref=target,
            send_sem=self.sems[0].at[send_at],
            recv_sem=self.sems[1].at[recv_at],
            device_id=self.partners[name],
            device_id_type=pl.DeviceIdType.MESH,
        )

    def send(self, source, target, name):
        copy = self.remote(source, target, name, self.used, self.used)
        self.used += 1
        copy.start()
        self.sent.append([copy, False])
        return len(self.sent) - 1

    def arrive(self, *which):
        for at in which:
            if not self.sent[at][1]:
                self.sent[at][0].wait_recv()
                self.sent[at][1] = True

    def wait_sent(self, *which):
        for at in which:
            if at not in self.left:
                self.sent[at][0].wait_send()
                self.left.add(at)

    def keep(self, source, target):
        at = len(self.kept)
        copy = pltpu.make_async_copy(source, target, self.sems[2].at[at])
        copy.start()
        self.kept.append([copy, False])
        return at

    def kept_done(self, *which):
        for at in which:
            if not self.kept[at][1]:
                self.kept[at][0].wait()
                self.kept[at][1] = True

    def finish(self):
        if self.used > self.sems[0].shape[0] or len(self.kept) > self.sems[2].shape[0]:
            raise ValueError((self.used, len(self.kept)))
        self.arrive(*range(len(self.sent)))
        self.wait_sent(*range(len(self.sent)))
        self.kept_done(*range(len(self.kept)))


class Line:
    def __init__(self, mv, own, slot):
        self.mv, self.step = mv, 0
        at = mv.used
        mv.used += 5
        self.first = mv.remote(own, slot(1), Z1, at, at)
        self.middle = [
            mv.remote(own, slot(3), Z3, at + 1, at + 2),
            mv.remote(slot(1), slot(2), Z3, at + 2, at + 1),
            mv.remote(slot(3), slot(2), Z1, at + 3, at + 1),
            mv.remote(slot(2), slot(3), Z1, at + 4, at + 2),
        ]
        self.arrivals = {2: self.middle[1], 3: self.middle[0]}
        self.first.start()
        pl.when(mv.inner)(self.middle[0].start)

    def advance(self):
        self.step += 1
        if self.step == 1:
            self.first.wait_recv()
            pl.when(self.mv.inner)(self.middle[1].start)
            return
        arrival = self.arrivals[3 if self.step == 2 else 2]

        @pl.when(self.mv.inner)
        def _():
            arrival.wait_recv()
            self.middle[self.step].start()

    def done(self):
        while self.step < 3:
            self.advance()

        @pl.when(jnp.logical_not(self.mv.inner))
        def _():
            self.arrivals[2].wait_recv()
            self.arrivals[3].wait_recv()

    def finish(self):
        self.first.wait_send()

        @pl.when(self.mv.inner)
        def _():
            for copy in self.middle:
                copy.wait_send()


def first_body(*refs):
    (x_ref, cot_ref, wqkv_ref, wout_ref, win_ref, wback_ref, b_ref, ln_ref, bout_ref) = refs[:9]
    (xp_out, cp_out, n_out, qkv_out, ot_out, lse_out, mo_out, mp_out, wq_out, wo, wi, wb, boutp_out, table_out) = refs[
        9:23
    ]
    (xall, nbuf, qkv, ot, vt, osc, wq, tables, send_sems, recv_sems, local_sems) = refs[23:]
    clips, rows, half = x_ref.shape
    width = half // 2
    lanes = tables.shape[3]
    hidden = wi.shape[3]
    shard, ctx, tp = place()
    mv = Movers(send_sems, recv_sems, local_sems)
    mv.barrier([X, CORE, Y, YCORE, Z1, Z2, Z3])
    cut = rows // 2

    x0 = [mv.send(x_ref.at[0], xall.at[0, 1, 0], X)]
    y0 = [mv.send(x_ref.at[0], xall.at[0, 0, 2], Y)]
    qkv_at = pl.ds(pl.multiple_of(ctx * lanes, lanes), lanes)
    wq_own = [
        mv.keep(wqkv_ref.at[i, :, qkv_at], wq.at[0, :, i * lanes : (i + 1) * lanes])
        for i in range(3)
    ]
    mv.kept_done(*wq_own)
    wq_line = Line(mv, wq.at[0], lambda k: wq.at[k])
    c0 = [mv.send(x_ref.at[0], xall.at[0, 0, 1], CORE)]
    own = [mv.keep(x_ref.at[b], xall.at[b, 0, 0]) for b in range(clips)]
    out_piece = wout_ref.at[pl.ds(pl.multiple_of(ctx * lanes, lanes), lanes), :]
    back_piece = wback_ref.at[pl.ds(pl.multiple_of(ctx * hidden, hidden), hidden), :]
    far_ctx = flip(ctx, 2)
    in_pieces = [
        win_ref.at[:, pl.ds(pl.multiple_of(at * hidden, hidden), hidden)] for at in (ctx, far_ctx)
    ]
    wo_x = mv.send(out_piece, wo.at[0, 0, 1], X)
    mv.send(bout_ref, boutp_out, X)
    wo_own = mv.keep(out_piece, wo.at[0, 0, 0])
    wi_own = [mv.keep(in_pieces[i], wi.at[2 * i, 0]) for i in range(2)]
    wb_own = mv.keep(back_piece, wb.at[0, 0])

    def forward(b, x, y):
        mv.arrive(x)
        size = cut if b == 0 else cut // 4
        low = mv.send(xall.at[b, 1, 0, :size], xall.at[b, 1, 2, :size], Y)
        near = [mv.send(xall.at[b, 1, 0], xall.at[b, 1, 1], CORE)]
        mv.arrive(y)
        high = mv.send(xall.at[b, 0, 2, size:], xall.at[b, 1, 2, size:], X)
        near.append(mv.send(xall.at[b, 0, 2], xall.at[b, 0, 3], CORE))
        return low, high, near

    def project(b, m):
        slot = m % 2
        for start in range(0, rows, cut):
            part = slice(start, start + cut)
            one, two, unused = norm_parts(
                xall[b, 0, m, part, :].astype(F32), xall[b, 1, m, part, :].astype(F32)
            )
            nbuf[slot, part, :half] = (one * ln_ref[0:1, :half] + ln_ref[1:2, :half]).astype(BF)
            nbuf[slot, part, half:] = (two * ln_ref[0:1, half:] + ln_ref[1:2, half:]).astype(BF)
        acc = b_ref[...]
        for h, j in CHUNKS:
            at = (2 * h + j) * width
            acc = acc + dot_nn(nbuf[slot, :, at : at + width], wq[piece_at(shard, tp, h, j)])
        cosines, sines = tables[0, m], tables[1, m]
        q, k = acc[:, :lanes], acc[:, lanes : 2 * lanes]
        place_rows = slice(m * rows, (m + 1) * rows)
        qkv[b, 0, place_rows, :] = (q * cosines + partner_lanes(q) * sines).astype(BF)
        qkv[b, 1, place_rows, :] = (k * cosines + partner_lanes(k) * sines).astype(BF)
        qkv[b, 2, place_rows, :] = acc[:, 2 * lanes :].astype(BF)
        return mv.keep(nbuf.at[slot], n_out.at[b, m])

    scale = HEAD_DIM ** (-0.5) * LOG2E
    head = lax.broadcasted_iota(jnp.int32, (rows, lanes), 1) // HEAD_DIM

    def turn_values(b):
        vt[:lanes, :] = qkv[b, 2].T
        vt[lanes:, :] = jnp.ones((vt.shape[0] - lanes, 4 * rows), BF)

    def attend(b, m):
        part = slice(m * rows, (m + 1) * rows)
        q = qkv[b, 0, part, :]
        keys = qkv[b, 1]
        outs = []
        for h in range(lanes // HEAD_DIM):
            q_head = jnp.where(head == h, q, jnp.zeros_like(q))
            scores = dot_nt(keys, q_head)
            top = jnp.max(scores, axis=0, keepdims=True) * scale
            probs = jnp.exp2(scores * scale - top).astype(BF)
            acc = dot_nn(vt[...], probs)
            total = acc[lanes : lanes + 1, :]
            outs.append(acc[h * HEAD_DIM : (h + 1) * HEAD_DIM, :] / total)
            lse_out[b, h : h + 1, part] = top + jnp.log2(total)
        result = jnp.concatenate(outs, axis=0)
        ot[b, :, part] = result
        osc[b, m] = result.T.astype(BF)
        if m == 0 or b == 1:
            return mv.keep(osc.at[b, m], mo_out.at[b, m])
        return mv.send(osc.at[b, m], mo_out.at[b, m], (None, CORE, Y, YCORE)[m])

    token = lax.broadcasted_iota(jnp.int32, (rows, lanes), 0)
    column = lax.broadcasted_iota(jnp.int32, (rows, lanes), 1) % HEAD_DIM
    segment = 2 * (HEAD_DIM // 3 // 2)
    halfway = segment // 2
    within = column % segment
    frequency = jnp.exp(
        (within % halfway).astype(F32) * (-math.log(10000.0) / halfway)
    )
    sign = jnp.where(within < halfway, -1.0, 1.0)
    active = column < 3 * segment

    def turn(position):
        angle = position.astype(F32) * frequency
        return jnp.where(active, jnp.cos(angle), 1.0), jnp.where(active, jnp.sin(angle) * sign, 0.0)

    def turn_frame(frame):
        angle = frame.astype(F32) * frequency[:8]
        cosine, sine = jnp.cos(angle)[:1], (jnp.sin(angle) * sign[:8])[:1]
        return cosine, sine

    start = [at * rows for at in (ctx, flip(ctx, 1), flip(ctx, 2), flip(flip(ctx, 2), 1))]
    if rows % (GH * GW) == 0:
        tables_in = turn(
            jnp.where(column < 2 * segment, token // GW % GH, token % GW)
        )
        for m in range(4):
            for at in range(0, rows, GH * GW):
                part = slice(at, at + GH * GW)
                frame = turn_frame((start[m] + at) // (GH * GW))
                first = column[part] < segment
                for i in range(2):
                    tables[i, m, part, :] = jnp.where(first, frame[i], tables_in[i][part])
    else:
        for m in range(4):
            at = start[m] + token
            both = turn(
                jnp.where(
                    column < segment,
                    at // (GH * GW),
                    jnp.where(column < 2 * segment, at // GW % GH, at % GW),
                )
            )
            for i in range(2):
                tables[i, m] = both[i]
    mv.keep(tables, table_out)

    wq_line.advance()
    wb_line = Line(mv, back_piece, lambda k: wb.at[0, k])
    wq_line.advance()
    low0, high0, near0 = forward(0, x0[0], y0[0])
    wq_line.advance()
    x1 = mv.send(x_ref.at[1], xall.at[1, 1, 0], X)
    y1 = mv.send(x_ref.at[1], xall.at[1, 0, 2], Y)
    c1 = mv.send(x_ref.at[1], xall.at[1, 0, 1], CORE)
    mv.keep(xall.at[0, 1, 0], xp_out.at[0])
    wb_line.advance()
    mv.arrive(wo_x)
    mv.kept_done(wo_own)
    wo_line = Line(mv, wo.at[0, 0], lambda k: wo.at[0, k])
    wq_line.done()
    mv.kept_done(own[0])
    mv.keep(wq, wq_out)
    n_copy = [project(0, 0)]
    wb_line.advance()
    wi_near = Line(mv, in_pieces[0], lambda k: wi.at[0, k])
    mv.arrive(c0[0], near0[0])
    n_copy.append(project(0, 1))
    mv.arrive(low0, high0)
    near0.append(mv.send(xall.at[0, 1, 2], xall.at[0, 1, 3], CORE))
    wb_line.advance()
    wo_line.advance()
    mv.kept_done(n_copy[0])
    n_copy.append(project(0, 2))
    wo_line.advance()
    mv.arrive(near0[1], near0[2])
    mv.kept_done(n_copy[1])
    n_copy.append(project(0, 3))
    mv.keep(qkv.at[0], qkv_out.at[0])
    low1, high1, near1 = forward(1, x1, y1)
    mv.keep(xall.at[1, 1, 0], xp_out.at[1])
    mv.send(cot_ref.at[0], cp_out.at[0], X)
    wb_line.done()
    mv.kept_done(wb_own)
    wb_far = mv.send(wb.at[0], wb.at[2], Y)
    mv.send(wb.at[0], wb.at[1], CORE)
    wi_near.advance()
    wi_far = Line(mv, in_pieces[1], lambda k: wi.at[2, k])
    turn_values(0)
    m0 = {2: attend(0, 2)}
    mv.arrive(low1, high1)
    near1.append(mv.send(xall.at[1, 1, 2], xall.at[1, 1, 3], CORE))
    wo_line.advance()
    wi_near.advance()
    m0[3] = attend(0, 3)
    wo_line.done()
    wo_far = mv.send(wo.at[0], wo.at[2], Y)
    mv.send(wo.at[0], wo.at[1], CORE)
    wi_near.advance()
    m0[1] = attend(0, 1)
    wi_far.advance()
    m0[0] = attend(0, 0)
    wi_far.advance()
    mv.keep(ot.at[0], ot_out.at[0])
    mv.arrive(c1, *near1)
    mv.kept_done(own[1], n_copy[2])
    n_copy.append(project(1, 0))
    mv.kept_done(n_copy[3])
    n_copy.append(project(1, 1))
    mv.arrive(m0[1])
    mv.kept_done(m0[0])
    for m in (1, 0):
        mv.send(mo_out.at[0, m], mp_out.at[0, m], X)
    mv.kept_done(n_copy[4])
    n_copy.append(project(1, 2))
    mv.kept_done(n_copy[5])
    n_copy.append(project(1, 3))
    mv.keep(qkv.at[1], qkv_out.at[1])
    for m in (2, 3):
        mv.arrive(m0[m])
        mv.send(mo_out.at[0, m], mp_out.at[0, m], X)
    wi_far.advance()
    turn_values(1)
    mv.send(cot_ref.at[1], cp_out.at[1], X)
    attend(1, 2)
    attend(1, 3)
    wi_near.done()
    mv.kept_done(wi_own[0])
    mv.send(wi.at[0], wi.at[1], CORE)
    attend(1, 1)
    mv.arrive(wb_far)
    mv.send(wb.at[2], wb.at[3], CORE)
    attend(1, 0)
    mv.keep(ot.at[1], ot_out.at[1])
    mv.arrive(wo_far)
    mv.send(wo.at[2], wo.at[3], CORE)
    wi_far.done()
    mv.kept_done(wi_own[1])
    mv.send(wi.at[2], wi.at[3], CORE)
    for line in (wq_line, wb_line, wi_near, wo_line, wi_far):
        line.finish()
    mv.finish()


ANY = pl.BlockSpec(memory_space=pl.ANY)


def first_call(x, cot, w_qkv, w_out, w_in, w_back, b, ln, b_out):
    clips, rows, half = x.shape
    width = half // 2
    lanes = half // 4
    hidden = w_in.shape[1] // 4
    outs = [
        ((clips, rows, half), BF),
        ((clips, rows, half), BF),
        ((clips, 4, rows, 2 * half), BF),
        ((clips, 3, 4 * rows, lanes), BF),
        ((clips, lanes, 4 * rows), F32),
        ((clips, lanes // HEAD_DIM, 4 * rows), F32),
        ((clips, 4, rows, lanes), BF),
        ((clips, 4, rows, lanes), BF),
        ((4, width, 3 * lanes), BF),
        ((4, 4, 2, lanes, width), BF),
        ((4, 4, width, hidden), BF),
        ((4, 4, hidden, width), BF),
        (b_out.shape, BF),
        ((2, 4, rows, lanes), F32),
    ]
    out_specs = [ANY] * len(outs)
    out_specs[5] = whole(outs[5][0])
    return pl.pallas_call(
        first_body,
        in_specs=[ANY] * 6 + [whole(b.shape), whole(ln.shape), ANY],
        out_specs=out_specs,
        out_shape=[jax.ShapeDtypeStruct(shape, kind) for shape, kind in outs],
        scratch_shapes=[
            pltpu.VMEM((clips, 2, 4, rows, half), BF),
            pltpu.VMEM((2, rows, 2 * half), BF),
            pltpu.VMEM((clips, 3, 4 * rows, lanes), BF),
            pltpu.VMEM((clips, lanes, 4 * rows), F32),
            pltpu.VMEM((lanes + 16, 4 * rows), BF),
            pltpu.VMEM((clips, 4, rows, lanes), BF),
            pltpu.VMEM((4, width, 3 * lanes), BF),
            pltpu.VMEM((2, 4, rows, lanes), F32),
            pltpu.SemaphoreType.DMA((80,)),
            pltpu.SemaphoreType.DMA((80,)),
            pltpu.SemaphoreType.DMA((40,)),
        ],
        compiler_params=pltpu.CompilerParams(
            vmem_limit_bytes=VMEM_BYTES, collective_id=1, has_side_effects=True
        ),
        name="project_and_attend",
    )(x, cot, w_qkv, w_out, w_in, w_back, b, ln, b_out)


def chunk_of(shard, k):
    found = flip(shard, 2) if k & 2 else shard
    return flip(found, 1) if k & 1 else found


def side_by_side(parts):
    return jnp.concatenate(parts, axis=1)


def second_body(*refs):
    (x_ref, xp_ref, c_ref, cp_ref, mo_ref, mp_ref, wo_hbm, wi_hbm, wb_hbm, qkv_hbm, ot_hbm) = refs[:11]
    (ln_ref, bin_ref, bout_ref, boutp_ref, bback_ref, lse_ref) = refs[11:17]
    (y_out, other_out, arrived_out, gmid_out, d_out, keep_out, near_out, far_out, far_own_out, go_out) = refs[17:27]
    (dqt_out, dk_out, dv_out, midsum_out, insum_out, backsum_out) = refs[27:33]
    (xs, cs, ms, wo, wi, wb, mid, sec, act, gin, outs, ybuf, gs, gsr, gmid, gb, gm) = refs[33:50]
    (wg, wgnear, wgo, turned, ot, dqt, delta, dks, dvs, send_sems, recv_sems, local_sems) = refs[50:]
    clips, rows, half = x_ref.shape
    width = half // 2
    lanes = mo_ref.shape[3]
    hidden = wi.shape[3]
    shard, ctx, tp = place()
    mv = Movers(send_sems, recv_sems, local_sems)
    ks = range(4)
    own_k = [piece_at(shard, tp, 0, j) for j in range(2)]
    other_k = [piece_at(shard, tp, 1, j) for j in range(2)]

    def fetch(b):
        mixed = []
        if b == 0:
            mixed.append(mv.keep(mo_ref.at[0], ms.at[0, 0]))
            mixed.append(mv.keep(mp_ref.at[0], ms.at[0, 1]))
        return mixed + [
            mv.keep(x_ref.at[b], xs.at[b, 0]),
            mv.keep(xp_ref.at[b], xs.at[b, 1]),
            mv.keep(c_ref.at[b], cs.at[b, 0]),
            mv.keep(cp_ref.at[b], cs.at[b, 1]),
        ]

    got = [fetch(0)]
    got_wo = mv.keep(wo_hbm, wo)
    got_wi = [mv.keep(wi_hbm.at[m], wi.at[m]) for m in ks]
    got_wb = [mv.keep(wb_hbm.at[m], wb.at[m]) for m in ks]
    got.append(fetch(1))
    mv.barrier([X, CORE, Y, YCORE])
    mixed_in = {
        m: mv.send(mo_ref.at[1, m], ms.at[1, 0, m], name)
        for m, name in ((2, Y), (3, YCORE), (1, CORE))
    }
    got[1].append(mv.keep(mo_ref.at[1, 0], ms.at[1, 0, 0]))
    mixed_far = [mv.send(mo_ref.at[1, 0], ms.at[1, 1, 0], X)]

    def pass_on(m):
        mv.arrive(mixed_in[m])
        mixed_far.append(mv.send(ms.at[1, 0, m], ms.at[1, 1, m], X))

    def row(which, k):
        return ln_ref[pl.ds(4 * which + chunk_of(shard, k), 1), :]

    def statistics(b):
        total = 4 * width
        mean = sum(jnp.sum(mid[b, k], 1, keepdims=True) for k in ks) / total
        spread = sum(jnp.sum((mid[b, k] - mean) ** 2, 1, keepdims=True) for k in ks) / total
        return mean, lax.rsqrt(spread + EPSILON)

    y_put = []

    def block(b):
        mv.kept_done(*got[b])
        mv.kept_done(got_wo)
        if b == 1:
            mv.arrive(*mixed_far)
        mixed = side_by_side([ms[b, side, m] for side in range(2) for m in ks])
        for k in ks:
            weight = jnp.concatenate([wo[m, k, side] for side in range(2) for m in ks], axis=0)
            mid[b, k] = dot_nn(mixed, weight)
        for j in range(2):
            part = slice(j * width, (j + 1) * width)
            mid[b, own_k[j]] += xs[b, 0, :, part].astype(F32) + bout_ref[0:1, part].astype(F32)
            mid[b, other_k[j]] += xs[b, 1, :, part].astype(F32) + boutp_ref[0:1, part].astype(F32)
        mean, inv = statistics(b)
        for k in ks:
            sec[b, k] = ((mid[b, k] - mean) * inv * row(0, k) + row(1, k)).astype(BF)
        if b == 0:
            pass_on(1)
        for j in range(2):
            part = slice(j * width, (j + 1) * width)
            gb[b, own_k[j]] = cs[b, 0, :, part]
            gb[b, other_k[j]] = cs[b, 1, :, part]
        normed = side_by_side([sec[b, k] for k in ks])
        cot = side_by_side([gb[b, k] for k in ks])
        for m in ks:
            if b == 0 and m in (1, 2):
                pass_on(m + 1)
            mv.kept_done(got_wi[m])
            at = (ctx, flip(ctx, 1), flip(ctx, 2), flip(flip(ctx, 2), 1))[m]
            inner = bin_ref[pl.ds(at, 1), :] + dot_nn(normed, wi[m].reshape(4 * width, hidden))
            mv.kept_done(got_wb[m])
            grad = dot_nt(cot, side_by_side([wb[m, k] for k in ks]))
            phi = 0.5 + 0.5 * lax.erf(inner * (0.5**0.5))
            act[b, m] = (inner * phi).astype(BF)
            slope = phi + inner * (jnp.exp(-0.5 * inner * inner) * ((2 * math.pi) ** -0.5))
            grad = (grad * slope).astype(BF)
            gin[b, m] = grad
            sums = jnp.sum(grad.astype(F32), axis=0, keepdims=True)
            if b == 0:
                insum_out[pl.ds(at, 1), :] = sums
            else:
                insum_out[pl.ds(at, 1), :] += sums
        back = side_by_side([gin[b, m] for m in ks])
        sent = []
        for k in ks:
            gs[b, k] = dot_nt(back, side_by_side([wi[m, k] for m in ks])).astype(BF)
            sent.append(mv.send(gs.at[b, k], gsr.at[b, k], X))
        active = side_by_side([act[b, m] for m in ks])
        mv.kept_done(*y_put)
        for h, which in enumerate((own_k, other_k)):
            for j in range(2):
                weight = jnp.concatenate([wb[m, which[j]] for m in ks], axis=0)
                part = slice(j * width, (j + 1) * width)
                term = dot_nn(active, weight)
                if h == 0:
                    term = term + mid[b, own_k[j]] + bback_ref[0:1, part].astype(F32)
                    ybuf[:, part] = term
                else:
                    outs[b, :, part] = term.astype(BF)
        y_put.append(mv.keep(ybuf, y_out.at[b]))
        if b == 1:
            mv.keep(outs.at[1], other_out)
        return sent

    put = []

    def branch(b, sent):
        mv.arrive(*sent[:4])
        mv.kept_done(*put)
        total = 4 * width
        mean, inv = statistics(b)
        mean_one = mean_two = 0.0
        for k in ks:
            unit = (mid[b, k] - mean) * inv
            grad = gs[b, k].astype(F32) + gsr[b, k].astype(F32)
            gain_sum = jnp.sum(grad * unit, 0, keepdims=True)
            shift_sum = jnp.sum(grad, 0, keepdims=True)
            for i, term in enumerate((gain_sum, shift_sum)):
                place_row = pl.ds(4 * i + chunk_of(shard, k), 1)
                if b == 0:
                    midsum_out[place_row, :] = term
                else:
                    midsum_out[place_row, :] += term
            scaled = grad * row(0, k)
            mean_one = mean_one + jnp.sum(scaled, 1, keepdims=True)
            mean_two = mean_two + jnp.sum(scaled * unit, 1, keepdims=True)
        mean_one, mean_two = mean_one / total, mean_two / total
        for k in ks:
            unit = (mid[b, k] - mean) * inv
            grad = gs[b, k].astype(F32) + gsr[b, k].astype(F32)
            full = gb[b, k].astype(F32) + inv * (grad * row(0, k) - mean_one - unit * mean_two)
            gmid[k] = full
            low = full.astype(BF)
            xs[b, k // 2, :, (k % 2) * width : (k % 2 + 1) * width] = low
            sec_sum = jnp.sum(low.astype(F32), 0, keepdims=True)
            place_row = pl.ds(8 + chunk_of(shard, k), 1)
            if b == 0:
                midsum_out[place_row, :] = sec_sum
            else:
                midsum_out[place_row, :] += sec_sum
        low = side_by_side([xs[b, 0], xs[b, 1]])
        weight = side_by_side([jnp.concatenate([wo[m, k, 0] for m in ks], axis=0) for k in ks])
        mixed = dot_nt(low, weight).astype(BF)
        for m in ks:
            gm[b, m] = mixed[:, m * lanes : (m + 1) * lanes]
        remote = [mv.send(gm.at[b, 2], d_out.at[b, 2], Y)]
        remote.append(mv.send(gm.at[b, 3], d_out.at[b, 3], YCORE))
        remote.append(mv.send(gm.at[b, 1], d_out.at[b, 1], CORE))
        local = mv.keep(gm.at[b, 0], d_out.at[b, 0])
        for j in range(2):
            put.append(mv.keep(gmid.at[own_k[j]], gmid_out.at[b, j]))
        cot_sum = jnp.sum(cs[b, 0].astype(F32), 0, keepdims=True)
        if b == 0:
            backsum_out[...] = cot_sum
        else:
            backsum_out[...] += cot_sum
        return remote, local

    def tokens(ref, *at):
        return jnp.concatenate([ref[(b,) + at] for b in range(clips)], axis=0)

    def big_grads(m, slot):
        cot = side_by_side([tokens(gb, k) for k in ks])
        back = dot_tn(tokens(act, m), cot).astype(BF)
        own = dot_nn(turned[...], tokens(gin, m)).astype(BF)
        for k in ks:
            wg[slot, k, :hidden, :] = back[:, k * width : (k + 1) * width]
            wg[slot, k, hidden : hidden + width, :] = own[k * width : (k + 1) * width, :width]
            wg[slot, k, hidden + width :, :] = own[k * width : (k + 1) * width, width:]

    def held(kind, i):
        place_at = ((0, i, 0), (0, i, 1), (1, i, 0), (1, i, 1))
        m, k, side = place_at[kind]
        return wb.at[m, k, :, side * lanes : (side + 1) * lanes]

    def masked(kind, h, i):
        return wb.at[2 + kind, i, :, h * lanes : (h + 1) * lanes]

    heads = lanes // HEAD_DIM
    scale = HEAD_DIM ** (-0.5)

    def load_attention():
        for i in ks:
            part = slice(i * rows, (i + 1) * rows)
            attention_in.append(mv.keep(qkv_hbm.at[0, 1, part, :], held(0, i)))
            attention_in.append(mv.keep(qkv_hbm.at[0, 2, part, :], held(1, i)))
            attention_in.append(mv.keep(qkv_hbm.at[0, 0, part, :], held(2, i)))
        attention_in.append(mv.keep(ot_hbm.at[0], ot))

    attention_in = []

    def prepare(arrivals):
        remote, local = arrivals
        mv.arrive(*remote)
        mv.kept_done(local)
        mv.kept_done(*[mv.keep(d_out.at[0, i], held(3, i)) for i in ks])
        mv.kept_done(*attention_in)
        head = lax.broadcasted_iota(jnp.int32, (rows, lanes), 1) // HEAD_DIM
        for i in ks:
            part = slice(i * rows, (i + 1) * rows)
            q, grad = held(2, i)[...], held(3, i)[...]
            for h in range(heads):
                masked(0, h, i)[...] = jnp.where(head == h, q, jnp.zeros_like(q))
                masked(1, h, i)[...] = jnp.where(head == h, grad, jnp.zeros_like(grad))
            products = grad.astype(F32).T * ot[:, part]
            for h in range(heads):
                delta[h : h + 1, part] = jnp.sum(
                    products[h * HEAD_DIM : (h + 1) * HEAD_DIM], axis=0, keepdims=True
                )
        dqt[...] = jnp.zeros_like(dqt)

    attention_put = []

    def attend_back(m):
        keys, values = held(0, m)[...], held(1, m)[...]
        dk, dv = attend_back_block(
            keys,
            values,
            lambda h, i: masked(0, h, i)[...],
            lambda h, i: masked(1, h, i)[...],
            lambda h, part: lse_ref[0, h : h + 1, part],
            delta,
            dqt,
            rows,
        )
        if m >= 2:
            mv.kept_done(*attention_put[2 * m - 4 : 2 * m - 2])
        dks[m % 2] = dk * scale
        dvs[m % 2] = dv.astype(BF)
        attention_put.append(mv.keep(dks.at[m % 2], dk_out.at[m]))
        attention_put.append(mv.keep(dvs.at[m % 2], dv_out.at[m]))

    first = block(0)
    second = block(1)
    load_attention()
    for k in ks:
        turned[k * width : (k + 1) * width, :] = tokens(sec, k).T
    big_grads(3, 0)
    near = mv.send(wg.at[0], wgnear, CORE)
    big_grads(2, 1)
    mv.arrive(near)
    for k in ks:
        wg[1, k] = (wg[1, k].astype(F32) + wgnear[k].astype(F32)).astype(BF)
    arrivals = branch(0, first)
    prepare(arrivals)
    far = [mv.send(wg.at[1, k], far_out.at[k - 1], Y) for k in (1, 2)]
    far_own = [mv.keep(wg.at[1, k], far_own_out.at[i]) for i, k in enumerate((3, 0))]
    mv.send(outs.at[0], arrived_out, X)
    attend_back(0)
    attend_back(1)
    mv.wait_sent(near)
    big_grads(1, 0)
    mv.send(wg.at[0], near_out, CORE)
    attend_back(2)
    attend_back(3)
    mv.keep(dqt, dqt_out)
    branch(1, second)
    grads = side_by_side([tokens(xs, i) for i in range(2)])
    for m in ks:
        mixed = jnp.concatenate([ms[b, 0, m] for b in range(clips)], axis=0)
        out = dot_tn(mixed, grads).astype(BF)
        for k in ks:
            wgo[m, k] = out[:, k * width : (k + 1) * width]
    mv.keep(wgo, go_out)
    mv.wait_sent(*far)
    mv.kept_done(*far_own)
    big_grads(0, 1)
    mv.keep(wg.at[1], keep_out)
    mv.finish()


def attend_back_block(keys, values, query, grad_out, log_total, delta, dqt, rows):
    scale = HEAD_DIM ** (-0.5)
    flat_keys = keys.T
    row = lax.broadcasted_iota(jnp.int32, flat_keys.shape, 0) // HEAD_DIM
    dk = dv = None
    for h in range(keys.shape[1] // HEAD_DIM):
        turned = jnp.where(row == h, flat_keys, jnp.zeros_like(flat_keys))
        for i in range(4):
            part = slice(i * rows, (i + 1) * rows)
            q, grad = query(h, i), grad_out(h, i)
            probs = jnp.exp2(dot_nt(keys, q) * (scale * LOG2E) - log_total(h, part))
            slope = (probs * (dot_nt(values, grad) - delta[h : h + 1, part])).astype(BF)
            value_term, key_term = dot_nn(probs.astype(BF), grad), dot_nn(slope, q)
            dk = key_term if dk is None else dk + key_term
            dv = value_term if dv is None else dv + value_term
            dqt[:, part] += dot_nn(turned, slope)
    return dk, dv


def second_call(x, xp, c, cp, mo, mp, wo, wi, wb, qkv, ot, ln, b_in, b_out, b_other, b_back, lse):
    clips, rows, half = x.shape
    width = half // 2
    lanes = mo.shape[3]
    hidden = wi.shape[3]
    tall = hidden + 2 * width
    heads = lanes // HEAD_DIM
    outs = [
        ((clips, rows, half), F32),
        ((rows, half), BF),
        ((rows, half), BF),
        ((clips, 2, rows, width), F32),
        ((clips, 4, rows, lanes), BF),
        ((4, tall, width), BF),
        ((4, tall, width), BF),
        ((2, tall, width), BF),
        ((2, tall, width), BF),
        ((4, 4, lanes, width), BF),
        ((lanes, 4 * rows), F32),
        ((4, rows, lanes), F32),
        ((4, rows, lanes), BF),
        ((12, width), F32),
        ((4, hidden), F32),
        ((1, half), F32),
    ]
    small = [ln, b_in, b_out, b_other, b_back, lse]
    vmem = lambda kind, *shape: pltpu.VMEM(shape, kind)
    return pl.pallas_call(
        second_body,
        in_specs=[ANY] * 11 + [whole(a.shape) for a in small],
        out_specs=[ANY] * 13 + [whole(o[0]) for o in outs[13:]],
        out_shape=[jax.ShapeDtypeStruct(shape, kind) for shape, kind in outs],
        scratch_shapes=[
            vmem(BF, clips, 2, rows, half),
            vmem(BF, clips, 2, rows, half),
            vmem(BF, clips, 2, 4, rows, lanes),
            vmem(BF, *wo.shape),
            vmem(BF, *wi.shape),
            vmem(BF, *wb.shape),
            vmem(F32, clips, 4, rows, width),
            vmem(BF, clips, 4, rows, width),
            vmem(BF, clips, 4, rows, hidden),
            vmem(BF, clips, 4, rows, hidden),
            vmem(BF, clips, rows, half),
            vmem(F32, rows, half),
            vmem(BF, clips, 4, rows, width),
            vmem(BF, clips, 4, rows, width),
            vmem(F32, 4, rows, width),
            vmem(BF, clips, 4, rows, width),
            vmem(BF, clips, 4, rows, lanes),
            vmem(BF, 2, 4, tall, width),
            vmem(BF, 4, tall, width),
            vmem(BF, 4, 4, lanes, width),
            vmem(BF, 4 * width, clips * rows),
            vmem(F32, lanes, 4 * rows),
            vmem(F32, lanes, 4 * rows),
            vmem(F32, heads, 4 * rows),
            vmem(F32, 2, rows, lanes),
            vmem(BF, 2, rows, lanes),
            pltpu.SemaphoreType.DMA((32,)),
            pltpu.SemaphoreType.DMA((32,)),
            pltpu.SemaphoreType.DMA((72,)),
        ],
        compiler_params=pltpu.CompilerParams(
            vmem_limit_bytes=VMEM_BYTES, collective_id=2, has_side_effects=True
        ),
        name="layer_middle",
    )(x, xp, c, cp, mo, mp, wo, wi, wb, qkv, ot, *small)


def third_body(*refs):
    (qkv_hbm, ot_hbm, d_hbm, t_hbm, wq_hbm, n_hbm, keep_hbm, near_hbm, far_hbm, far_own) = refs[:10]
    (go_hbm, dqt_hbm, dk_hbm, dv_hbm, other_hbm, x_hbm, xp_hbm) = refs[10:17]
    (lse_ref, ln_ref, midsum_ref, insum_ref, backsum_ref) = refs[17:22]
    (ig_out, arrived_out, dense_out, qdense_out, early_out, ln1_out, qsum_out) = refs[22:29]
    (qkv, ot, d, tables, wq, qh, dh, delta, dqt, gj, pk, ps, near, hop, last) = refs[29:44]
    (nbuf, qacc, qs, qz, gk, gnear, gfar, gz, go, gonear, dk0, dqt0, xs, stats) = refs[44:58]
    (stats_in, early, early_in, late, late_in, late_x, send_sems, recv_sems, local_sems) = refs[58:]
    unused, count, lanes = qkv.shape
    clips = x_hbm.shape[0]
    rows = count // 4
    width = wq.shape[1]
    half = 2 * width
    heads = lanes // HEAD_DIM
    cut = rows // 2
    shard, ctx, tp = place()
    mv = Movers(send_sems, recv_sems, local_sems)
    ks = range(4)
    zs = (Z1, Z2, Z3)
    scale = HEAD_DIM ** (-0.5)

    tall = keep_hbm.shape[1]
    got_first = [
        mv.keep(dqt_hbm, dqt0),
        mv.keep(dk_hbm, dk0),
        mv.keep(dv_hbm, gj.at[0, :, :, 2 * lanes :]),
    ]
    got_w = [mv.keep(t_hbm, tables), mv.keep(wq_hbm, wq)]
    got_g = [
        [mv.keep(keep_hbm.at[k], gk.at[k, :tall]), mv.keep(near_hbm.at[k], gnear.at[k])]
        for k in (1, 2, 3, 0)
    ]
    for at in range(2):
        got_g[at].append(mv.keep(far_hbm.at[at], gfar.at[at + 1]))
    got_go = [mv.keep(go_hbm.at[2 * i], go.at[i]) for i in range(2)]
    got = [
        mv.keep(qkv_hbm.at[1], qkv),
        mv.keep(d_hbm.at[1], d),
        mv.keep(ot_hbm.at[1], ot),
    ]
    got_n = [mv.keep(n_hbm.at[0, m], nbuf.at[m]) for m in range(2)]
    got_x = [mv.keep(x_hbm, xs.at[0]), mv.keep(xp_hbm, xs.at[1])]
    mv.barrier([X, CORE, Y, YCORE, Z1, Z2, Z3])
    far_late = [mv.send(far_own.at[0], gfar.at[3], Y)]
    go_core = [mv.send(go_hbm.at[2 * i + 1], gonear.at[i], CORE) for i in range(2)]

    early[0, :12, :] = midsum_ref[...]
    for m in ks:
        for j in range(2):
            part = slice(j * width, (j + 1) * width)
            early[0, 12 + 2 * m + j : 13 + 2 * m + j, :] = insum_ref[m : m + 1, part]
    for j in range(2):
        early[0, 20 + j : 21 + j, :] = backsum_ref[:, j * width : (j + 1) * width]
    early[0, 22:, :] = jnp.zeros((2, width), F32)
    early_z = [mv.send(early.at[0], early_in.at[i], name) for i, name in enumerate(zs)]

    def prepare():
        mv.kept_done(*got)
        head = lax.broadcasted_iota(jnp.int32, (rows, lanes), 1) // HEAD_DIM
        for m in ks:
            part = slice(m * rows, (m + 1) * rows)
            q, grad = qkv[0, part, :], d[m]
            for h in range(heads):
                qh[h, part, :] = jnp.where(head == h, q, jnp.zeros_like(q))
                dh[h, part, :] = jnp.where(head == h, grad, jnp.zeros_like(grad))
            products = grad.astype(F32).T * ot[:, part]
            for h in range(heads):
                delta[h : h + 1, part] = jnp.sum(
                    products[h * HEAD_DIM : (h + 1) * HEAD_DIM], axis=0, keepdims=True
                )
        dqt[...] = jnp.zeros_like(dqt)

    def attend_back(m):
        mine = slice(m * rows, (m + 1) * rows)
        dk, dv = attend_back_block(
            qkv[1, mine, :],
            qkv[2, mine, :],
            lambda h, i: qh[h, i * rows : (i + 1) * rows, :],
            lambda h, i: dh[h, i * rows : (i + 1) * rows, :],
            lambda h, part: lse_ref[1, h : h + 1, part],
            delta,
            dqt,
            rows,
        )
        dk = dk * scale
        dk = dk * tables[0, m] + partner_lanes(dk * tables[1, m])
        gj[1, m, :, lanes : 2 * lanes] = dk.astype(BF)
        gj[1, m, :, 2 * lanes :] = dv.astype(BF)

    sums = [0.0, 0.0, 0.0]

    def join(b):
        mv.kept_done(*got_w, *got_first)
        sent = {}
        for m in (3, 2, 1, 0):
            part = slice(m * rows, (m + 1) * rows)
            dq = ((dqt0, dqt)[b][:, part] * scale).T
            if b == 0:
                dk = dk0[m]
                dk = dk * tables[0, m] + partner_lanes(dk * tables[1, m])
                gj[0, m, :, lanes : 2 * lanes] = dk.astype(BF)
            dq = dq * tables[0, m] + partner_lanes(dq * tables[1, m])
            gj[b, m, :, :lanes] = dq.astype(BF)
            for i in range(3):
                low = gj[b, m, :, i * lanes : (i + 1) * lanes].astype(F32)
                sums[i] = sums[i] + jnp.sum(low, axis=0, keepdims=True)
            for h in (1, 0):
                target = (pk, ps)[m % 2]
                for j in range(2):
                    term = dot_nt(gj[b, m], wq[piece_at(shard, tp, h, j)])
                    target[b, m // 2, h, :, j * width : (j + 1) * width] = term.astype(BF)
                if m % 2:
                    sent[m // 2, h] = mv.send(ps.at[b, m // 2, h], near.at[b, m // 2, h], CORE)
            if m == 2:
                hops = first_hop(b, sent)
        return sent, hops

    def first_hop(b, sent):
        mv.arrive(sent[1, 1])
        pk[b, 1, 1] = (pk[b, 1, 1].astype(F32) + near[b, 1, 1].astype(F32)).astype(BF)
        low = mv.send(pk.at[b, 1, 1, :cut], hop.at[b, 0], X)
        high = mv.send(pk.at[b, 1, 1, cut:], hop.at[b, 1], Y)
        return low, high

    def second_hop(b, sent, hops):
        mv.arrive(sent[1, 0], sent[0, 1])
        mv.arrive(hops[0])
        pk[b, 1, 0, :cut] = (
            pk[b, 1, 0, :cut].astype(F32)
            + near[b, 1, 0, :cut].astype(F32)
            + hop[b, 0].astype(F32)
        ).astype(BF)
        pk[b, 1, 0, cut:] = (
            pk[b, 1, 0, cut:].astype(F32) + near[b, 1, 0, cut:].astype(F32)
        ).astype(BF)
        far = mv.send(pk.at[b, 1, 0], last.at[b, 0], Y)
        mv.arrive(hops[1])
        pk[b, 0, 1, :cut] = (
            pk[b, 0, 1, :cut].astype(F32) + near[b, 0, 1, :cut].astype(F32)
        ).astype(BF)
        pk[b, 0, 1, cut:] = (
            pk[b, 0, 1, cut:].astype(F32)
            + near[b, 0, 1, cut:].astype(F32)
            + hop[b, 1].astype(F32)
        ).astype(BF)
        other = mv.send(pk.at[b, 0, 1], last.at[b, 1], X)
        return far, other

    def norm_one(b):
        mv.kept_done(*got_x)
        own, unused, inv = norm_parts(xs[0, b].astype(F32), xs[1, b].astype(F32))
        return own, inv

    gains = [0.0, 0.0]
    gain_own = jnp.where(tp == 0, ln_ref[:, :half], ln_ref[:, half:])

    def finish_sum(b, sent, lasts):
        mv.arrive(sent[0, 0], *lasts)
        own, inv = norm_one(b)
        grad = (
            pk[b, 0, 0].astype(F32)
            + near[b, 0, 0].astype(F32)
            + last[b, 0].astype(F32)
            + last[b, 1].astype(F32)
        )
        gains[0] = gains[0] + jnp.sum(grad * own, axis=0, keepdims=True)
        gains[1] = gains[1] + jnp.sum(grad, axis=0, keepdims=True)
        scaled = grad * gain_own
        ig_out[b] = scaled
        lane = lax.broadcasted_iota(jnp.int32, (rows, 128), 1)
        both = jnp.where(
            lane == 0,
            jnp.sum(scaled, 1, keepdims=True),
            jnp.where(lane == 1, jnp.sum(scaled * own, 1, keepdims=True), 0.0),
        )
        stats[b] = both.T[:8]
        return mv.send(stats.at[b], stats_in.at[b], X)

    def finish_grad(b, sent):
        mv.arrive(sent)
        own, inv = norm_one(b)
        total = stats[b] + stats_in[b]
        both = jnp.concatenate([total, jnp.zeros((120, rows), F32)], axis=0).T / (2 * half)
        grad = inv * (ig_out[b] - both[:, 0:1] - own * both[:, 1:2])
        ig_out[b] = grad

    def qkv_grads(b):
        for m in ks:
            at = 4 * b + m
            mv.kept_done(got_n[at])
            slot = at % 2
            for h, j in CHUNKS:
                cols = slice((2 * h + j) * width, (2 * h + j + 1) * width)
                term = dot_tn(nbuf[slot, :, cols], gj[b, m])
                if at == 0:
                    qacc[2 * h + j] = term
                else:
                    qacc[2 * h + j] += term
            if at + 2 < 8:
                got_n.append(mv.keep(n_hbm.at[(at + 2) // 4, (at + 2) % 4], nbuf.at[slot]))

    def add_far():
        mv.arrive(*go_core)
        mv.kept_done(*got_go)
        go[1] = (go[1].astype(F32) + gonear[1].astype(F32)).astype(BF)
        return mv.send(go.at[1], gonear.at[2], Y)

    def shard_send(at):
        k = (1, 2, 3, 0)[at]
        mv.kept_done(*got_g[at])
        if at >= 2:
            mv.arrive(far_late[at - 2])
        gk[k, :tall] = (
            gk[k, :tall].astype(F32) + gnear[k].astype(F32) + gfar[k].astype(F32)
        ).astype(BF)
        return [mv.send(gk.at[k, :tall], gz.at[k - 1, :tall], zs[k - 1])] if k else []

    def shard_sends_out(far):
        mv.arrive(far)
        sent = []
        for k in (1, 2, 3, 0):
            gk[k, tall:] = (
                go[0, k].astype(F32) + gonear[0, k].astype(F32) + gonear[2, k].astype(F32)
            ).astype(BF)
            if k:
                sent.append(mv.send(gk.at[k, tall:], gz.at[k - 1, tall:], zs[k - 1]))
        return sent

    def spread_far(ref):
        return mv.send(ref.at[ctx], ref.at[ctx], Y), mv.send(ref.at[ctx], ref.at[ctx], CORE)

    def spread_near(ref, far):
        mv.arrive(far[0])
        mv.send(ref.at[flip(ctx, 2)], ref.at[flip(ctx, 2)], CORE)

    gz_sent = shard_send(0) + shard_send(1)
    sent0, hops0 = join(0)
    prepare()
    attend_back(0)
    go_far = add_far()
    gz_sent += shard_send(2)
    lasts0 = second_hop(0, sent0, hops0)
    far_late.append(mv.send(far_own.at[1], gfar.at[0], Y))
    arrived = mv.send(other_hbm, arrived_out, X)
    attend_back(1)
    gz_sent += shard_sends_out(go_far)
    mv.arrive(*early_z)
    early[1] = early[0] + early_in[0] + early_in[1] + early_in[2]
    qkv_grads(0)
    attend_back(2)
    stats0 = finish_sum(0, sent0, lasts0)
    attend_back(3)
    sent1, hops1 = join(1)
    qkv_grads(1)
    for h, j in CHUNKS:
        qs[piece_at(shard, tp, h, j)] = qacc[2 * h + j].astype(BF)
    q_sent = [mv.send(qs.at[k + 1], qz.at[k], name) for k, name in enumerate(zs)]
    lasts1 = second_hop(1, sent1, hops1)
    shard_send(3)
    mv.arrive(*gz_sent)
    for part in (slice(0, tall), slice(tall, gz.shape[1])):
        gk[0, part] = (
            gk[0, part].astype(F32)
            + gz[0, part].astype(F32)
            + gz[1, part].astype(F32)
            + gz[2, part].astype(F32)
        ).astype(BF)
    placed = mv.keep(gk.at[0], dense_out.at[ctx])
    finish_grad(0, stats0)
    mv.kept_done(placed)
    dense_far = spread_far(dense_out)
    stats1 = finish_sum(1, sent1, lasts1)
    late[...] = jnp.zeros_like(late)
    for i in range(2):
        for j in range(4):
            late[4 * i + j : 4 * i + j + 1, :] = gains[i][:, j * 128 : (j + 1) * 128]
    for i in range(3):
        late[pl.ds(8 + 3 * ctx + i, 1), :] = sums[i]
    late_z = [mv.send(late, late_in.at[i], name) for i, name in enumerate(zs)]
    finish_grad(1, stats1)
    mv.arrive(*late_z)
    late_x[0] = late[...] + late_in[0] + late_in[1] + late_in[2]
    others = (CORE, Y, YCORE)
    late_c = [mv.send(late_x.at[0], late_in.at[3 + i], name) for i, name in enumerate(others)]
    mv.arrive(*q_sent)
    qs[0] = sum((qz[i].astype(F32) for i in range(3)), qs[0].astype(F32)).astype(BF)
    q_placed = mv.keep(qs.at[0], qdense_out.at[ctx])
    mv.kept_done(q_placed)
    q_far = spread_far(qdense_out)
    early_x = [mv.send(early.at[1], early_in.at[3 + i], name) for i, name in enumerate(others)]
    mv.arrive(*late_c)
    late_x[1] = late_x[0] + late_in[3] + late_in[4] + late_in[5]
    crossed = mv.send(late_x.at[1], late_x.at[2], X)
    mv.arrive(*early_x)
    early_out[...] = early[1] + early_in[3] + early_in[4] + early_in[5]
    qsum_out[...] = late_x[1, 8:20, :]
    spread_near(dense_out, dense_far)
    spread_near(qdense_out, q_far)
    mv.arrive(crossed)
    for i in range(2):
        part = slice(4 * i, 4 * i + 4)
        ln1_out[i, pl.ds(4 * tp, 4), :] = late_x[1, part, :]
        ln1_out[i, pl.ds(4 * (1 - tp), 4), :] = late_x[2, part, :]
    mv.finish()


def third_call(
    qkv, ot, d, tables, wq, normed, keep, near, far, own, go, dqt, dk, dv, other, x, xp, *small
):
    unused, unused, count, lanes = qkv.shape
    clips, rows, half = x.shape
    width = half // 2
    tall = keep.shape[1]
    heads = lanes // HEAD_DIM
    outs = [
        ((clips, rows, half), F32),
        ((rows, half), BF),
        ((4, tall + lanes, width), BF),
        ((4, width, 3 * lanes), BF),
        ((24, width), F32),
        ((2, 8, 128), F32),
        ((12, lanes), F32),
    ]
    vmem = lambda kind, *shape: pltpu.VMEM(shape, kind)
    return pl.pallas_call(
        third_body,
        in_specs=[ANY] * 17 + [whole(a.shape) for a in small],
        out_specs=[whole(outs[0][0]), ANY, ANY, ANY] + [whole(o[0]) for o in outs[4:]],
        out_shape=[jax.ShapeDtypeStruct(shape, kind) for shape, kind in outs],
        scratch_shapes=[
            vmem(BF, *qkv.shape[1:]),
            vmem(F32, *ot.shape[1:]),
            vmem(BF, *d.shape[1:]),
            vmem(F32, *tables.shape),
            vmem(BF, *wq.shape),
            vmem(BF, heads, count, lanes),
            vmem(BF, heads, count, lanes),
            vmem(F32, heads, count),
            vmem(F32, lanes, count),
            vmem(BF, clips, 4, rows, 3 * lanes),
            vmem(BF, clips, 2, 2, rows, half),
            vmem(BF, clips, 2, 2, rows, half),
            vmem(BF, clips, 2, 2, rows, half),
            vmem(BF, clips, 2, rows // 2, half),
            vmem(BF, clips, 2, rows, half),
            vmem(BF, 2, rows, 2 * half),
            vmem(F32, 4, width, 3 * lanes),
            vmem(BF, *wq.shape),
            vmem(BF, 3, width, 3 * lanes),
            vmem(BF, 4, tall + lanes, width),
            vmem(BF, 4, tall, width),
            vmem(BF, 4, tall, width),
            vmem(BF, 3, tall + lanes, width),
            vmem(BF, 2, 4, lanes, width),
            vmem(BF, 3, 4, lanes, width),
            vmem(F32, *dk.shape),
            vmem(F32, *dqt.shape),
            vmem(BF, 2, clips, rows, half),
            vmem(F32, clips, 8, rows),
            vmem(F32, clips, 8, rows),
            vmem(F32, 2, 24, width),
            vmem(F32, 6, 24, width),
            vmem(F32, 24, 128),
            vmem(F32, 6, 24, 128),
            vmem(F32, 3, 24, 128),
            pltpu.SemaphoreType.DMA((64,)),
            pltpu.SemaphoreType.DMA((64,)),
            pltpu.SemaphoreType.DMA((48,)),
        ],
        compiler_params=pltpu.CompilerParams(
            vmem_limit_bytes=VMEM_BYTES, collective_id=3, has_side_effects=True
        ),
        name="layer_back",
    )(qkv, ot, d, tables, wq, normed, keep, near, far, own, go, dqt, dk, dv, other, x, xp, *small)


def fourth_body(
    dense_ref, q_ref, y_ref, far_ref, ig_ref, mid_ref, other_ref, wb_ref, wi_ref, wo_ref, wq_ref, yo_ref, go_ref
):
    width = q_ref.shape[1]
    hidden = wb_ref.shape[0]
    lanes = wo_ref.shape[0]
    wb_ref[...] = dense_ref[0, :hidden, :].astype(F32)
    for j in range(2):
        at = hidden + j * width
        wi_ref[:, j * width : (j + 1) * width] = dense_ref[0, at : at + width, :].astype(F32)
    wo_ref[...] = dense_ref[0, hidden + 2 * width :, :].astype(F32)
    for i in range(3):
        wq_ref[i] = q_ref[0, :, i * lanes : (i + 1) * lanes].astype(F32)
    for b, ref in enumerate((far_ref, other_ref)):
        yo_ref[b] = (y_ref[b] + ref[...].astype(F32)).astype(BF)
    for j in range(2):
        part = slice(j * width, (j + 1) * width)
        go_ref[:, :, part] = ig_ref[:, :, part] + mid_ref[:, j]


def fourth_call(dense, qkv_dense, y, arrived, input_part, mids):
    four, tall, width = dense.shape
    lanes = qkv_dense.shape[2] // 3
    hidden = tall - 2 * width - lanes
    clips, rows, half = y.shape
    one = pl.BlockSpec((rows // four, half), lambda a: (a, 0))
    some = pl.BlockSpec((clips, rows // four, half), lambda a: (0, a, 0))
    return pl.pallas_call(
        fourth_body,
        grid=(four,),
        in_specs=[
            pl.BlockSpec((1, tall, width), lambda a: (a, 0, 0)),
            pl.BlockSpec((1, width, 3 * lanes), lambda a: (a, 0, 0)),
            some,
            one,
            some,
            pl.BlockSpec((clips, 2, rows // four, width), lambda a: (0, 0, a, 0)),
            one,
        ],
        out_specs=[
            pl.BlockSpec((hidden, width), lambda a: (a, 0)),
            pl.BlockSpec((width, hidden), lambda a: (0, a)),
            pl.BlockSpec((lanes, width), lambda a: (a, 0)),
            pl.BlockSpec((3, width, lanes), lambda a: (0, 0, a)),
            some,
            some,
        ],
        out_shape=[
            jax.ShapeDtypeStruct((four * hidden, width), F32),
            jax.ShapeDtypeStruct((width, four * hidden), F32),
            jax.ShapeDtypeStruct((four * lanes, width), F32),
            jax.ShapeDtypeStruct((3, width, four * lanes), F32),
            jax.ShapeDtypeStruct(y.shape, BF),
            jax.ShapeDtypeStruct(y.shape, F32),
        ],
        compiler_params=pltpu.CompilerParams(vmem_limit_bytes=VMEM_BYTES),
        name="owned_gradients",
    )(dense, qkv_dense, y, arrived[0], input_part, mids, arrived[1])


def fast_device(
    inputs,
    ln1_gain,
    ln1_bias,
    w_qkv,
    b_qkv,
    w_out,
    b_out,
    ln2_gain,
    ln2_bias,
    w_in,
    b_in,
    w_back,
    b_back,
    cotangent,
):
    clips, rows, half = inputs.shape
    width = half // 2
    lanes = half // 4
    hidden = w_in.shape[1] // 4
    shard, ctx, tp = (lax.axis_index(name) for name in ("shard", "ctx", "tp"))
    ids = jnp.stack([shard, ctx, tp]).astype(jnp.int32)
    def halves(vector):
        vector = vector.astype(F32)
        return jnp.concatenate(
            [
                lax.dynamic_slice_in_dim(vector, tp * half, half),
                lax.dynamic_slice_in_dim(vector, (1 - tp) * half, half),
            ]
        )

    ln_qkv = jnp.stack([halves(ln1_gain), halves(ln1_bias)])
    bias_qkv = (
        lax.dynamic_slice_in_dim(b_qkv, ctx * lanes, lanes, axis=1)
        .reshape(1, 3 * lanes)
        .astype(F32)
    )
    bias_in = b_in.reshape(4, hidden).astype(F32)

    xp, cp, normed, qkv, ot, lse, mo, mp, wq, wo, wi, wb, bias_other, tables = first_call(
        inputs,
        cotangent,
        jnp.transpose(w_qkv, (1, 0, 2)),
        w_out,
        w_in,
        w_back,
        bias_qkv,
        ln_qkv,
        jnp.broadcast_to(b_out, (16, half)),
    )
    ln_two = jnp.concatenate([ln2_gain, ln2_bias]).astype(F32).reshape(8, width)
    middle = second_call(
        inputs,
        xp,
        cotangent,
        cp,
        mo,
        mp,
        wo,
        wi,
        wb,
        qkv,
        ot,
        ln_two,
        bias_in,
        b_out.reshape(1, half),
        bias_other,
        b_back.reshape(1, half),
        lse,
    )
    y, other, arrived, mids, grad_heads, keep, near, far, far_own, grads_out, dqt, dk, dv = middle[:13]
    input_part, arrived_late, dense, qkv_dense, early, grad_ln1, q_sums = third_call(
        qkv,
        ot,
        grad_heads,
        tables,
        wq,
        normed,
        keep,
        near,
        far,
        far_own,
        grads_out,
        dqt,
        dk,
        dv,
        other,
        inputs,
        xp,
        lse,
        ln1_gain.astype(F32).reshape(1, 2 * half),
        *middle[13:],
    )
    mid_total = early[:12].reshape(3, 2 * half)
    grad_b_out = lax.dynamic_slice_in_dim(mid_total[2], tp * half, half)
    grad_b_in = early[12:20].reshape(4 * hidden)
    grad_b_back = early[20:22].reshape(half)
    grad_b_qkv = q_sums.reshape(4, 3, lanes).transpose(1, 0, 2).reshape(3, 4 * lanes)
    grad_w_back, grad_w_in, grad_w_out, grad_w_qkv, output, input_grad = fourth_call(
        dense, qkv_dense, y, (arrived, arrived_late), input_part, mids
    )
    grad_w_qkv = jnp.transpose(grad_w_qkv, (1, 0, 2))
    return (
        output,
        input_grad,
        grad_ln1[0].reshape(2 * half),
        grad_ln1[1].reshape(2 * half),
        grad_w_qkv,
        grad_b_qkv,
        grad_w_out,
        grad_b_out,
        mid_total[0],
        mid_total[1],
        grad_w_in,
        grad_b_in,
        grad_w_back,
        grad_b_back,
    )


def quick_form_fits(mesh):
    return (mesh.shape["shard"], mesh.shape["ctx"], mesh.shape["tp"]) == (4, 4, 2)


def solution(mesh):
    placed = (
        P("shard", "ctx", "tp"),
        P(),
        P(),
        P("shard", None, "tp"),
        P(None, "tp"),
        P("tp", "shard"),
        P("tp"),
        P(),
        P(),
        P("shard", "tp"),
        P("tp"),
        P("tp", "shard"),
        P("tp"),
        P("shard", "ctx", "tp"),
    )
    return jax.shard_map(
        fast_device if quick_form_fits(mesh) else per_device,
        mesh=mesh,
        in_specs=placed,
        out_specs=(
            P("shard", "ctx", "tp"),
            P("shard", "ctx", "tp"),
            P(),
            P(),
            P("shard", None, "tp"),
            P(None, "tp"),
            P("tp", "shard"),
            P("tp"),
            P(),
            P(),
            P("shard", "tp"),
            P("tp"),
            P("tp", "shard"),
            P("tp"),
        ),
        check_vma=False,
    )
```

```python
import math

import jax
import jax.numpy as jnp
from jax import lax
from jax.experimental import pallas as pl
from jax.experimental.pallas import tpu as pltpu
from jax.sharding import PartitionSpec as P

HEAD_DIM = 64
GH = 16
GW = 16


EPSILON = 1e-06
NEG_LARGE = -1e30


def rotary_tables(first_row, row_count):
    segment = 2 * (HEAD_DIM // 3 // 2)
    halfway = segment // 2
    places = first_row + jnp.arange(row_count, dtype=jnp.int32)
    frames = places // (GH * GW)
    rows_at = places // GW % GH
    cols_at = places % GW
    column = jnp.arange(HEAD_DIM, dtype=jnp.int32)
    segment_of = column // segment
    within = column % segment
    frequency = jnp.power(10000.0, -(within % halfway).astype(jnp.float32) / halfway)
    position = jnp.where(
        segment_of[None, :] == 0,
        frames[:, None],
        jnp.where(segment_of[None, :] == 1, rows_at[:, None], cols_at[:, None]),
    )
    angles = position.astype(jnp.float32) * frequency[None, :]
    active = (column < 3 * segment)[None, :]
    cosines = jnp.where(active, jnp.cos(angles), 1.0)
    sine_table = jnp.where(
        active, jnp.where((within < halfway)[None, :], -jnp.sin(angles), jnp.sin(angles)), 0.0
    )
    return (cosines, sine_table)


def partner(tensor):
    segment = 2 * (HEAD_DIM // 3 // 2)
    halfway = segment // 2
    pieces = []
    for number in range(3):
        offset = number * segment
        pieces.append(tensor[..., offset + halfway : offset + segment])
        pieces.append(tensor[..., offset : offset + halfway])
    pieces.append(tensor[..., 3 * segment :])
    return jnp.concatenate(pieces, axis=-1)


def rotate(tensor, cosines, sine_table):
    return tensor * cosines + partner(tensor) * sine_table


def rotate_back(gradient, cosines, sine_table):
    return gradient * cosines + partner(gradient * sine_table)


def normalize(tensor, gain, shift):
    center = tensor - jnp.mean(tensor, axis=-1, keepdims=True)
    spread = jnp.mean(center * center, axis=-1, keepdims=True)
    inv_std = lax.rsqrt(spread + EPSILON)
    scaled = center * inv_std
    return (scaled * gain + shift, scaled, inv_std)


def norm_back(grad_out, scaled, inv_std, gain):
    grad_scaled = grad_out * gain
    mean_one = jnp.mean(grad_scaled, axis=-1, keepdims=True)
    mean_two = jnp.mean(grad_scaled * scaled, axis=-1, keepdims=True)
    return inv_std * (grad_scaled - mean_one - scaled * mean_two)


def tp_rows(sharded):
    return lax.all_gather(sharded, "tp", axis=2, tiled=True)


def tensor_sum(summand):
    return lax.psum_scatter(
        summand.astype(jnp.bfloat16), "tp", scatter_dimension=2, tiled=True
    ).astype(jnp.float32)


def back_total(summand):
    return lax.psum(summand.astype(jnp.bfloat16), "tp").astype(jnp.float32)


def fetch_weights(w_qkv, w_out, w_in, w_back):
    return (
        lax.all_gather(w_qkv, "shard", axis=0, tiled=True),
        lax.all_gather(w_out, "shard", axis=1, tiled=True),
        lax.all_gather(w_in, "shard", axis=0, tiled=True),
        lax.all_gather(w_back, "shard", axis=1, tiled=True),
    )


def forward(inputs, params, weights, cosines, sine_table):
    gain_one, shift_one, b_qkv, b_out, gain_two, shift_two, b_in, b_back = params
    w_qkv_all, w_out_all, w_in_all, w_back_all = weights
    clip_count, row_count, width_local = inputs.shape
    heads_local = width_local // HEAD_DIM
    score_scale = HEAD_DIM ** (-0.5)
    tokens = tp_rows(inputs).astype(jnp.float32)
    normed, scaled_one, inv_one = normalize(tokens, gain_one, shift_one)
    normed_low = normed.astype(jnp.bfloat16)
    joined = (
        jnp.einsum("csd,dkh->cskh", normed_low, w_qkv_all, preferred_element_type=jnp.float32)
        + b_qkv
    )
    shaped = joined.reshape(clip_count, row_count, 3, heads_local, HEAD_DIM)
    queries = rotate(shaped[:, :, 0], cosines, sine_table).astype(jnp.bfloat16)
    key_rows = rotate(shaped[:, :, 1], cosines, sine_table).astype(jnp.bfloat16)
    values = shaped[:, :, 2].astype(jnp.bfloat16)
    key_flat = key_rows.reshape(clip_count, row_count, width_local)
    value_flat = values.reshape(clip_count, row_count, width_local)

    def absorb_block(running, block_pair):
        row_max, row_sum, weighted = running
        key_piece, value_piece = block_pair
        scores = (
            jnp.einsum("cqhd,ckhd->chqk", queries, key_piece, preferred_element_type=jnp.float32)
            * score_scale
        )
        next_max = jnp.maximum(row_max, jnp.max(scores, axis=-1))
        factor = jnp.exp(row_max - next_max)
        weights_now = jnp.exp(scores - next_max[..., None])
        row_sum = row_sum * factor + jnp.sum(weights_now, axis=-1)
        weighted = weighted * factor[..., None] + jnp.einsum(
            "chqk,ckhd->chqd",
            weights_now.astype(jnp.bfloat16),
            value_piece,
            preferred_element_type=jnp.float32,
        )
        return ((next_max, row_sum, weighted), None)

    initial = (
        jnp.full((clip_count, heads_local, row_count), NEG_LARGE, jnp.float32),
        jnp.zeros((clip_count, heads_local, row_count), jnp.float32),
        jnp.zeros((clip_count, heads_local, row_count, HEAD_DIM), jnp.float32),
    )
    running = initial
    pieces = (
        lax.all_gather(key_flat, "ctx", axis=1, tiled=True),
        lax.all_gather(value_flat, "ctx", axis=1, tiled=True),
    )
    piece_rows = pieces[0].shape[1]
    block_size = math.gcd(piece_rows, 512)
    block_count = piece_rows // block_size
    key_blocks = jnp.moveaxis(
        pieces[0].reshape(clip_count, block_count, block_size, heads_local, HEAD_DIM), 1, 0
    )
    value_blocks = jnp.moveaxis(
        pieces[1].reshape(clip_count, block_count, block_size, heads_local, HEAD_DIM), 1, 0
    )
    running, unused = lax.scan(absorb_block, running, (key_blocks, value_blocks))
    row_max, row_sum, weighted = running
    log_total = row_max + jnp.log(row_sum)
    mixed_heads = jnp.transpose(weighted / row_sum[..., None], (0, 2, 1, 3))
    mixed_low = mixed_heads.reshape(clip_count, row_count, width_local).astype(jnp.bfloat16)
    branch = tensor_sum(
        jnp.einsum("csh,hd->csd", mixed_low, w_out_all, preferred_element_type=jnp.float32)
    )
    middle = inputs.astype(jnp.float32) + branch + b_out
    middle_all = lax.all_gather(middle.astype(jnp.bfloat16), "tp", axis=2, tiled=True).astype(
        middle.dtype
    )
    second, scaled_two, inv_two = normalize(middle_all, gain_two, shift_two)
    second_low = second.astype(jnp.bfloat16)
    inner_pre = (
        jnp.einsum("csd,df->csf", second_low, w_in_all, preferred_element_type=jnp.float32) + b_in
    )
    active_low = jax.nn.gelu(inner_pre, approximate=False).astype(jnp.bfloat16)
    return {
        "normed_low": normed_low,
        "scaled_one": scaled_one,
        "inv_one": inv_one,
        "queries": queries,
        "key_flat": key_flat,
        "value_flat": value_flat,
        "mixed_heads": mixed_heads,
        "mixed_low": mixed_low,
        "log_total": log_total,
        "middle": middle,
        "scaled_two": scaled_two,
        "inv_two": inv_two,
        "second_low": second_low,
        "inner_pre": inner_pre,
        "active_low": active_low,
    }


def per_device(
    inputs,
    ln1_gain,
    ln1_bias,
    w_qkv,
    b_qkv,
    w_out,
    b_out,
    ln2_gain,
    ln2_bias,
    w_in,
    b_in,
    w_back,
    b_back,
    cotangent,
):
    params = tuple(
        (
            parameter.astype(jnp.float32)
            for parameter in (ln1_gain, ln1_bias, b_qkv, b_out, ln2_gain, ln2_bias, b_in, b_back)
        )
    )
    gain_one = params[0]
    gain_two = params[4]
    clip_count, row_count, width_local = inputs.shape
    heads_local = width_local // HEAD_DIM
    score_scale = HEAD_DIM ** (-0.5)
    tp_index = lax.axis_index("tp")
    share_start = tp_index * width_local
    cosines, sine_table = rotary_tables(lax.axis_index("ctx") * row_count, row_count)
    cosines = cosines[:, None, :]
    sine_table = sine_table[:, None, :]
    weights = fetch_weights(w_qkv, w_out, w_in, w_back)
    stored_acts = forward(inputs, params, weights, cosines, sine_table)
    output = (
        stored_acts["middle"]
        + tensor_sum(
            jnp.einsum(
                "csf,fd->csd",
                stored_acts["active_low"],
                weights[3],
                preferred_element_type=jnp.float32,
            )
        )
        + params[7]
    ).astype(jnp.bfloat16)
    weights = fetch_weights(w_qkv, w_out, w_in, w_back)
    stored_acts = forward(inputs, params, weights, cosines, sine_table)
    w_qkv_all, w_out_all, w_in_all, w_back_all = weights
    grad_low = tp_rows(cotangent)
    grad_full = grad_low.astype(jnp.float32)
    grad_active = jnp.einsum(
        "csd,fd->csf", grad_low, w_back_all, preferred_element_type=jnp.float32
    )
    unused, gelu_back = jax.vjp(
        lambda argument: jax.nn.gelu(argument, approximate=False), stored_acts["inner_pre"]
    )
    grad_inner = gelu_back(grad_active)[0].astype(jnp.bfloat16)
    grad_w_back = jnp.einsum(
        "csf,csd->fd", stored_acts["active_low"], grad_low, preferred_element_type=jnp.float32
    )
    grad_b_back = jnp.sum(cotangent.astype(jnp.float32), axis=(0, 1))
    grad_w_in = jnp.einsum(
        "csd,csf->df", stored_acts["second_low"], grad_inner, preferred_element_type=jnp.float32
    )
    grad_b_in = jnp.sum(grad_inner.astype(jnp.float32), axis=(0, 1))
    grad_second = back_total(
        jnp.einsum("csf,df->csd", grad_inner, w_in_all, preferred_element_type=jnp.float32)
    )
    grad_gain_two = jnp.sum(grad_second * stored_acts["scaled_two"], axis=(0, 1))
    grad_shift_two = jnp.sum(grad_second, axis=(0, 1))
    grad_middle = grad_full + norm_back(
        grad_second, stored_acts["scaled_two"], stored_acts["inv_two"], gain_two
    )
    grad_branch = grad_middle.astype(jnp.bfloat16)
    grad_b_out = lax.dynamic_slice_in_dim(
        jnp.sum(grad_branch.astype(jnp.float32), axis=(0, 1)), share_start, width_local
    )
    grad_w_out = jnp.einsum(
        "csh,csd->hd", stored_acts["mixed_low"], grad_branch, preferred_element_type=jnp.float32
    )
    grad_mixed = jnp.einsum(
        "csd,hd->csh", grad_branch, w_out_all, preferred_element_type=jnp.float32
    ).astype(jnp.bfloat16)
    key_all, value_all = (
        lax.all_gather(stored_acts["key_flat"], "ctx", axis=1, tiled=True),
        lax.all_gather(stored_acts["value_flat"], "ctx", axis=1, tiled=True),
    )
    length = key_all.shape[1]
    block_size = math.gcd(length, 512)
    block_count = length // block_size
    grad_heads = grad_mixed.reshape(clip_count, row_count, heads_local, HEAD_DIM)
    queries = stored_acts["queries"]
    log_total = stored_acts["log_total"]
    row_delta = jnp.einsum(
        "cqhd,chqd->chq",
        grad_heads.astype(jnp.float32),
        jnp.transpose(stored_acts["mixed_heads"], (0, 2, 1, 3)),
    )
    key_blocks = jnp.moveaxis(
        key_all.reshape(clip_count, block_count, block_size, heads_local, HEAD_DIM), 1, 0
    )
    value_blocks = jnp.moveaxis(
        value_all.reshape(clip_count, block_count, block_size, heads_local, HEAD_DIM), 1, 0
    )

    def key_step(grad_query, block_pair):
        key_piece, value_piece = block_pair
        scores = (
            jnp.einsum("cqhd,ckhd->chqk", queries, key_piece, preferred_element_type=jnp.float32)
            * score_scale
        )
        prob_block = jnp.exp(scores - log_total[..., None])
        grad_probs = jnp.einsum(
            "cqhd,ckhd->chqk", grad_heads, value_piece, preferred_element_type=jnp.float32
        )
        grad_scores = (prob_block * (grad_probs - row_delta[..., None])).astype(jnp.bfloat16)
        grad_query = grad_query + jnp.einsum(
            "chqk,ckhd->cqhd", grad_scores, key_piece, preferred_element_type=jnp.float32
        )
        grad_key = (
            jnp.einsum("chqk,cqhd->ckhd", grad_scores, queries, preferred_element_type=jnp.float32)
            * score_scale
        )
        grad_value = jnp.einsum(
            "chqk,cqhd->ckhd",
            prob_block.astype(jnp.bfloat16),
            grad_heads,
            preferred_element_type=jnp.float32,
        )
        return (grad_query, (grad_key, grad_value))

    grad_query, (key_terms, value_terms) = lax.scan(
        key_step,
        jnp.zeros((clip_count, row_count, heads_local, HEAD_DIM), jnp.float32),
        (key_blocks, value_blocks),
    )
    grad_query = grad_query * score_scale
    key_terms = jnp.moveaxis(key_terms, 0, 1).reshape(clip_count, length, width_local)
    value_terms = jnp.moveaxis(value_terms, 0, 1).reshape(clip_count, length, width_local)
    grad_keys, grad_values = (
        lax.psum_scatter(
            key_terms.astype(jnp.bfloat16), "ctx", scatter_dimension=1, tiled=True
        ).astype(jnp.float32),
        lax.psum_scatter(
            value_terms.astype(jnp.bfloat16), "ctx", scatter_dimension=1, tiled=True
        ).astype(jnp.float32),
    )
    grad_q_pre = rotate_back(grad_query, cosines, sine_table).reshape(
        clip_count, row_count, width_local
    )
    grad_k_pre = rotate_back(
        grad_keys.reshape(clip_count, row_count, heads_local, HEAD_DIM), cosines, sine_table
    ).reshape(clip_count, row_count, width_local)
    grad_joined = jnp.stack([grad_q_pre, grad_k_pre, grad_values], axis=2).astype(jnp.bfloat16)
    grad_w_qkv = jnp.einsum(
        "csd,cskh->dkh", stored_acts["normed_low"], grad_joined, preferred_element_type=jnp.float32
    )
    grad_b_qkv = jnp.sum(grad_joined.astype(jnp.float32), axis=(0, 1))
    normed_term = jnp.einsum(
        "cskh,dkh->csd", grad_joined, w_qkv_all, preferred_element_type=jnp.float32
    )
    grad_normed = back_total(normed_term)
    grad_gain_one = jnp.sum(grad_normed * stored_acts["scaled_one"], axis=(0, 1))
    grad_shift_one = jnp.sum(grad_normed, axis=(0, 1))
    grad_tokens = grad_middle + norm_back(
        grad_normed, stored_acts["scaled_one"], stored_acts["inv_one"], gain_one
    )
    input_grad = lax.dynamic_slice_in_dim(grad_tokens, share_start, width_local, axis=2)
    summed = (
        lax.psum(grad_w_qkv.astype(jnp.bfloat16), "ctx").astype(jnp.float32),
        lax.psum(grad_w_out.astype(jnp.bfloat16), "ctx").astype(jnp.float32),
        lax.psum(grad_w_in.astype(jnp.bfloat16), "ctx").astype(jnp.float32),
        lax.psum(grad_w_back.astype(jnp.bfloat16), "ctx").astype(jnp.float32),
    )
    owned_grads = (
        lax.psum_scatter(
            summed[0].astype(jnp.bfloat16), "shard", scatter_dimension=0, tiled=True
        ).astype(jnp.float32),
        lax.psum_scatter(
            summed[1].astype(jnp.bfloat16), "shard", scatter_dimension=1, tiled=True
        ).astype(jnp.float32),
        lax.psum_scatter(
            summed[2].astype(jnp.bfloat16), "shard", scatter_dimension=0, tiled=True
        ).astype(jnp.float32),
        lax.psum_scatter(
            summed[3].astype(jnp.bfloat16), "shard", scatter_dimension=1, tiled=True
        ).astype(jnp.float32),
    )
    small_sums = lax.psum(
        (
            grad_gain_one,
            grad_shift_one,
            grad_b_qkv,
            grad_b_out,
            grad_gain_two,
            grad_shift_two,
            grad_b_in,
            grad_b_back,
        ),
        ("shard", "ctx"),
    )
    return (
        output,
        input_grad,
        small_sums[0],
        small_sums[1],
        owned_grads[0],
        small_sums[2],
        owned_grads[1],
        small_sums[3],
        small_sums[4],
        small_sums[5],
        owned_grads[2],
        small_sums[6],
        owned_grads[3],
        small_sums[7],
    )


LOG2E = 1.4426950408889634
BF = jnp.bfloat16
F32 = jnp.float32
VMEM_BYTES = 60 * 2**20


def dot_nt(a, b):
    return lax.dot_general(a, b, (((1,), (1,)), ((), ())), preferred_element_type=F32)


def dot_nn(a, b):
    return lax.dot_general(a, b, (((1,), (0,)), ((), ())), preferred_element_type=F32)


def dot_tn(a, b):
    return lax.dot_general(a, b, (((0,), (0,)), ((), ())), preferred_element_type=F32)


def whole(shape):
    return pl.BlockSpec(shape, lambda *_: (0,) * len(shape))


CHUNKS = ((0, 0), (0, 1), (1, 0), (1, 1))


def partner_lanes(tensor):
    segment = 2 * (HEAD_DIM // 3 // 2)
    halfway = segment // 2
    width = tensor.shape[1]
    lane = lax.broadcasted_iota(jnp.int32, tensor.shape, 1) % HEAD_DIM
    first = lane % segment < halfway
    return jnp.where(
        first, pltpu.roll(tensor, width - halfway, 1), pltpu.roll(tensor, halfway, 1)
    )


def norm_parts(own, other):
    total = 2 * own.shape[1]
    mean = (jnp.sum(own, 1, keepdims=True) + jnp.sum(other, 1, keepdims=True)) / total
    own, other = own - mean, other - mean
    spread = (
        jnp.sum(own * own, 1, keepdims=True) + jnp.sum(other * other, 1, keepdims=True)
    ) / total
    inv = lax.rsqrt(spread + EPSILON)
    return own * inv, other * inv, inv


def flip(value, bit):
    if bit == 1:
        return value + 1 - 2 * lax.rem(value, 2)
    return lax.rem(value + 2, 4)


def place():
    return tuple(lax.axis_index(name) for name in ("shard", "ctx", "tp"))


def piece_at(shard, tp, half, part):
    found = lax.rem(shard + 2 * lax.rem(tp + half, 2), 4)
    return flip(found, 1) if part else found


X, CORE, Y, YCORE, Z1, Z2, Z3 = range(7)


class Movers:
    def __init__(self, send_sems, recv_sems, local_sems):
        shard, ctx, tp = place()
        self.sems = (send_sems, recv_sems, local_sems)
        self.sent, self.kept = [], []
        self.partners = {
            X: {"tp": 1 - tp},
            CORE: {"ctx": flip(ctx, 1)},
            Y: {"ctx": flip(ctx, 2)},
            YCORE: {"ctx": flip(flip(ctx, 2), 1)},
            Z1: {"shard": flip(shard, 1)},
            Z2: {"shard": flip(shard, 2)},
            Z3: {"shard": flip(flip(shard, 2), 1)},
        }
        self.inner = jnp.logical_or(shard == 1, shard == 2)
        self.used = 0
        self.left = set()

    def barrier(self, names):
        barrier = pltpu.get_barrier_semaphore()
        for name in names:
            pl.semaphore_signal(
                barrier,
                inc=1,
                device_id=self.partners[name],
                device_id_type=pl.DeviceIdType.MESH,
            )
        pl.semaphore_wait(barrier, len(names))

    def remote(self, source, target, name, send_at, recv_at):
        return pltpu.make_async_remote_copy(
            src_ref=source,
            dst_ref=target,
            send_sem=self.sems[0].at[send_at],
            recv_sem=self.sems[1].at[recv_at],
            device_id=self.partners[name],
            device_id_type=pl.DeviceIdType.MESH,
        )

    def send(self, source, target, name):
        copy = self.remote(source, target, name, self.used, self.used)
        self.used += 1
        copy.start()
        self.sent.append([copy, False])
        return len(self.sent) - 1

    def arrive(self, *which):
        for at in which:
            if not self.sent[at][1]:
                self.sent[at][0].wait_recv()
                self.sent[at][1] = True

    def wait_sent(self, *which):
        for at in which:
            if at not in self.left:
                self.sent[at][0].wait_send()
                self.left.add(at)

    def keep(self, source, target):
        at = len(self.kept)
        copy = pltpu.make_async_copy(source, target, self.sems[2].at[at])
        copy.start()
        self.kept.append([copy, False])
        return at

    def kept_done(self, *which):
        for at in which:
            if not self.kept[at][1]:
                self.kept[at][0].wait()
                self.kept[at][1] = True

    def finish(self):
        if self.used > self.sems[0].shape[0] or len(self.kept) > self.sems[2].shape[0]:
            raise ValueError((self.used, len(self.kept)))
        self.arrive(*range(len(self.sent)))
        self.wait_sent(*range(len(self.sent)))
        self.kept_done(*range(len(self.kept)))


class Line:
    def __init__(self, mv, own, slot):
        self.mv, self.step = mv, 0
        at = mv.used
        mv.used += 5
        self.first = mv.remote(own, slot(1), Z1, at, at)
        self.middle = [
            mv.remote(own, slot(3), Z3, at + 1, at + 2),
            mv.remote(slot(1), slot(2), Z3, at + 2, at + 1),
            mv.remote(slot(3), slot(2), Z1, at + 3, at + 1),
            mv.remote(slot(2), slot(3), Z1, at + 4, at + 2),
        ]
        self.arrivals = {2: self.middle[1], 3: self.middle[0]}
        self.first.start()
        pl.when(mv.inner)(self.middle[0].start)

    def advance(self):
        self.step += 1
        if self.step == 1:
            self.first.wait_recv()
            pl.when(self.mv.inner)(self.middle[1].start)
            return
        arrival = self.arrivals[3 if self.step == 2 else 2]

        @pl.when(self.mv.inner)
        def _():
            arrival.wait_recv()
            self.middle[self.step].start()

    def done(self):
        while self.step < 3:
            self.advance()

        @pl.when(jnp.logical_not(self.mv.inner))
        def _():
            self.arrivals[2].wait_recv()
            self.arrivals[3].wait_recv()

    def finish(self):
        self.first.wait_send()

        @pl.when(self.mv.inner)
        def _():
            for copy in self.middle:
                copy.wait_send()


def first_body(*refs):
    (x_ref, cot_ref, wqkv_ref, wout_ref, win_ref, wback_ref, b_ref, ln_ref, bout_ref) = refs[:9]
    (xp_out, cp_out, n_out, qkv_out, ot_out, lse_out, mo_out, mp_out, wq_out, wo, wi, wb, boutp_out, table_out) = refs[
        9:23
    ]
    (xall, nbuf, qkv, ot, vt, osc, wq, tables, send_sems, recv_sems, local_sems) = refs[23:]
    clips, rows, half = x_ref.shape
    width = half // 2
    lanes = tables.shape[3]
    hidden = wi.shape[3]
    shard, ctx, tp = place()
    mv = Movers(send_sems, recv_sems, local_sems)
    mv.barrier([X, CORE, Y, YCORE, Z1, Z2, Z3])
    cut = rows // 2

    x0 = [mv.send(x_ref.at[0], xall.at[0, 1, 0], X)]
    y0 = [mv.send(x_ref.at[0], xall.at[0, 0, 2], Y)]
    qkv_at = pl.ds(pl.multiple_of(ctx * lanes, lanes), lanes)
    wq_own = [
        mv.keep(wqkv_ref.at[i, :, qkv_at], wq.at[0, :, i * lanes : (i + 1) * lanes])
        for i in range(3)
    ]
    mv.kept_done(*wq_own)
    wq_line = Line(mv, wq.at[0], lambda k: wq.at[k])
    c0 = [mv.send(x_ref.at[0], xall.at[0, 0, 1], CORE)]
    own = [mv.keep(x_ref.at[b], xall.at[b, 0, 0]) for b in range(clips)]
    out_piece = wout_ref.at[pl.ds(pl.multiple_of(ctx * lanes, lanes), lanes), :]
    back_piece = wback_ref.at[pl.ds(pl.multiple_of(ctx * hidden, hidden), hidden), :]
    far_ctx = flip(ctx, 2)
    in_pieces = [
        win_ref.at[:, pl.ds(pl.multiple_of(at * hidden, hidden), hidden)] for at in (ctx, far_ctx)
    ]
    wo_x = mv.send(out_piece, wo.at[0, 0, 1], X)
    mv.send(bout_ref, boutp_out, X)
    wo_own = mv.keep(out_piece, wo.at[0, 0, 0])
    wi_own = [mv.keep(in_pieces[i], wi.at[2 * i, 0]) for i in range(2)]
    wb_own = mv.keep(back_piece, wb.at[0, 0])

    def forward(b, x, y):
        mv.arrive(x)
        size = cut if b == 0 else cut // 4
        low = mv.send(xall.at[b, 1, 0, :size], xall.at[b, 1, 2, :size], Y)
        near = [mv.send(xall.at[b, 1, 0], xall.at[b, 1, 1], CORE)]
        mv.arrive(y)
        high = mv.send(xall.at[b, 0, 2, size:], xall.at[b, 1, 2, size:], X)
        near.append(mv.send(xall.at[b, 0, 2], xall.at[b, 0, 3], CORE))
        return low, high, near

    def project(b, m):
        slot = m % 2
        for start in range(0, rows, cut):
            part = slice(start, start + cut)
            one, two, unused = norm_parts(
                xall[b, 0, m, part, :].astype(F32), xall[b, 1, m, part, :].astype(F32)
            )
            nbuf[slot, part, :half] = (one * ln_ref[0:1, :half] + ln_ref[1:2, :half]).astype(BF)
            nbuf[slot, part, half:] = (two * ln_ref[0:1, half:] + ln_ref[1:2, half:]).astype(BF)
        acc = b_ref[...]
        for h, j in CHUNKS:
            at = (2 * h + j) * width
            acc = acc + dot_nn(nbuf[slot, :, at : at + width], wq[piece_at(shard, tp, h, j)])
        cosines, sines = tables[0, m], tables[1, m]
        q, k = acc[:, :lanes], acc[:, lanes : 2 * lanes]
        place_rows = slice(m * rows, (m + 1) * rows)
        qkv[b, 0, place_rows, :] = (q * cosines + partner_lanes(q) * sines).astype(BF)
        qkv[b, 1, place_rows, :] = (k * cosines + partner_lanes(k) * sines).astype(BF)
        qkv[b, 2, place_rows, :] = acc[:, 2 * lanes :].astype(BF)
        return mv.keep(nbuf.at[slot], n_out.at[b, m])

    scale = HEAD_DIM ** (-0.5) * LOG2E
    head = lax.broadcasted_iota(jnp.int32, (rows, lanes), 1) // HEAD_DIM

    def turn_values(b):
        vt[:lanes, :] = qkv[b, 2].T
        vt[lanes:, :] = jnp.ones((vt.shape[0] - lanes, 4 * rows), BF)

    def attend(b, m):
        part = slice(m * rows, (m + 1) * rows)
        q = qkv[b, 0, part, :]
        keys = qkv[b, 1]
        outs = []
        for h in range(lanes // HEAD_DIM):
            q_head = jnp.where(head == h, q, jnp.zeros_like(q))
            scores = dot_nt(keys, q_head)
            top = jnp.max(scores, axis=0, keepdims=True) * scale
            probs = jnp.exp2(scores * scale - top).astype(BF)
            acc = dot_nn(vt[...], probs)
            total = acc[lanes : lanes + 1, :]
            outs.append(acc[h * HEAD_DIM : (h + 1) * HEAD_DIM, :] / total)
            lse_out[b, h : h + 1, part] = top + jnp.log2(total)
        result = jnp.concatenate(outs, axis=0)
        ot[b, :, part] = result
        osc[b, m] = result.T.astype(BF)
        if m == 0 or b == 1:
            return mv.keep(osc.at[b, m], mo_out.at[b, m])
        return mv.send(osc.at[b, m], mo_out.at[b, m], (None, CORE, Y, YCORE)[m])

    token = lax.broadcasted_iota(jnp.int32, (rows, lanes), 0)
    column = lax.broadcasted_iota(jnp.int32, (rows, lanes), 1) % HEAD_DIM
    segment = 2 * (HEAD_DIM // 3 // 2)
    halfway = segment // 2
    within = column % segment
    frequency = jnp.exp(
        (within % halfway).astype(F32) * (-math.log(10000.0) / halfway)
    )
    sign = jnp.where(within < halfway, -1.0, 1.0)
    active = column < 3 * segment

    def turn(position):
        angle = position.astype(F32) * frequency
        return jnp.where(active, jnp.cos(angle), 1.0), jnp.where(active, jnp.sin(angle) * sign, 0.0)

    def turn_frame(frame):
        angle = frame.astype(F32) * frequency[:8]
        cosine, sine = jnp.cos(angle)[:1], (jnp.sin(angle) * sign[:8])[:1]
        return cosine, sine

    start = [at * rows for at in (ctx, flip(ctx, 1), flip(ctx, 2), flip(flip(ctx, 2), 1))]
    if rows % (GH * GW) == 0:
        tables_in = turn(
            jnp.where(column < 2 * segment, token // GW % GH, token % GW)
        )
        for m in range(4):
            for at in range(0, rows, GH * GW):
                part = slice(at, at + GH * GW)
                frame = turn_frame((start[m] + at) // (GH * GW))
                first = column[part] < segment
                for i in range(2):
                    tables[i, m, part, :] = jnp.where(first, frame[i], tables_in[i][part])
    else:
        for m in range(4):
            at = start[m] + token
            both = turn(
                jnp.where(
                    column < segment,
                    at // (GH * GW),
                    jnp.where(column < 2 * segment, at // GW % GH, at % GW),
                )
            )
            for i in range(2):
                tables[i, m] = both[i]
    mv.keep(tables, table_out)

    wq_line.advance()
    wb_line = Line(mv, back_piece, lambda k: wb.at[0, k])
    wq_line.advance()
    low0, high0, near0 = forward(0, x0[0], y0[0])
    wq_line.advance()
    x1 = mv.send(x_ref.at[1], xall.at[1, 1, 0], X)
    y1 = mv.send(x_ref.at[1], xall.at[1, 0, 2], Y)
    c1 = mv.send(x_ref.at[1], xall.at[1, 0, 1], CORE)
    mv.keep(xall.at[0, 1, 0], xp_out.at[0])
    wb_line.advance()
    mv.arrive(wo_x)
    mv.kept_done(wo_own)
    wo_line = Line(mv, wo.at[0, 0], lambda k: wo.at[0, k])
    wq_line.done()
    mv.kept_done(own[0])
    mv.keep(wq, wq_out)
    n_copy = [project(0, 0)]
    wb_line.advance()
    wi_near = Line(mv, in_pieces[0], lambda k: wi.at[0, k])
    mv.arrive(c0[0], near0[0])
    n_copy.append(project(0, 1))
    mv.arrive(low0, high0)
    near0.append(mv.send(xall.at[0, 1, 2], xall.at[0, 1, 3], CORE))
    wb_line.advance()
    wo_line.advance()
    wi_far = Line(mv, in_pieces[1], lambda k: wi.at[2, k])
    mv.kept_done(n_copy[0])
    n_copy.append(project(0, 2))
    wo_line.advance()
    mv.arrive(near0[1], near0[2])
    mv.kept_done(n_copy[1])
    n_copy.append(project(0, 3))
    mv.keep(qkv.at[0], qkv_out.at[0])
    low1, high1, near1 = forward(1, x1, y1)
    mv.keep(xall.at[1, 1, 0], xp_out.at[1])
    mv.send(cot_ref.at[0], cp_out.at[0], X)
    mv.kept_done(wb_own)
    wb_far = [mv.send(wb.at[0, :2], wb.at[2, :2], Y)]
    wi_near.advance()
    turn_values(0)
    m0 = {2: attend(0, 2)}
    mv.arrive(low1, high1)
    near1.append(mv.send(xall.at[1, 1, 2], xall.at[1, 1, 3], CORE))
    wb_line.done()
    wb_far.append(mv.send(wb.at[0, 2:], wb.at[2, 2:], Y))
    mv.send(wb.at[0], wb.at[1], CORE)
    wo_line.advance()
    wi_near.advance()
    m0[3] = attend(0, 3)
    wo_line.done()
    wo_far = mv.send(wo.at[0], wo.at[2], Y)
    mv.send(wo.at[0], wo.at[1], CORE)
    wi_near.advance()
    m0[1] = attend(0, 1)
    wi_far.advance()
    m0[0] = attend(0, 0)
    wi_far.advance()
    mv.keep(ot.at[0], ot_out.at[0])
    mv.arrive(c1, *near1)
    mv.kept_done(own[1], n_copy[2])
    n_copy.append(project(1, 0))
    mv.kept_done(n_copy[3])
    n_copy.append(project(1, 1))
    mv.arrive(m0[1])
    mv.kept_done(m0[0])
    for m in (1, 0):
        mv.send(mo_out.at[0, m], mp_out.at[0, m], X)
    wi_far.advance()
    mv.kept_done(n_copy[4])
    n_copy.append(project(1, 2))
    mv.kept_done(n_copy[5])
    n_copy.append(project(1, 3))
    mv.keep(qkv.at[1], qkv_out.at[1])
    for m in (2, 3):
        mv.arrive(m0[m])
        mv.send(mo_out.at[0, m], mp_out.at[0, m], X)
    turn_values(1)
    mv.send(cot_ref.at[1], cp_out.at[1], X)
    attend(1, 2)
    attend(1, 3)
    wi_near.done()
    mv.kept_done(wi_own[0])
    mv.send(wi.at[0], wi.at[1], CORE)
    attend(1, 1)
    mv.arrive(*wb_far)
    mv.send(wb.at[2], wb.at[3], CORE)
    attend(1, 0)
    mv.keep(ot.at[1], ot_out.at[1])
    mv.arrive(wo_far)
    mv.send(wo.at[2], wo.at[3], CORE)
    wi_far.done()
    mv.kept_done(wi_own[1])
    mv.send(wi.at[2], wi.at[3], CORE)
    for line in (wq_line, wb_line, wi_near, wo_line, wi_far):
        line.finish()
    mv.finish()


ANY = pl.BlockSpec(memory_space=pl.ANY)


def first_call(x, cot, w_qkv, w_out, w_in, w_back, b, ln, b_out):
    clips, rows, half = x.shape
    width = half // 2
    lanes = half // 4
    hidden = w_in.shape[1] // 4
    outs = [
        ((clips, rows, half), BF),
        ((clips, rows, half), BF),
        ((clips, 4, rows, 2 * half), BF),
        ((clips, 3, 4 * rows, lanes), BF),
        ((clips, lanes, 4 * rows), F32),
        ((clips, lanes // HEAD_DIM, 4 * rows), F32),
        ((clips, 4, rows, lanes), BF),
        ((clips, 4, rows, lanes), BF),
        ((4, width, 3 * lanes), BF),
        ((4, 4, 2, lanes, width), BF),
        ((4, 4, width, hidden), BF),
        ((4, 4, hidden, width), BF),
        (b_out.shape, BF),
        ((2, 4, rows, lanes), F32),
    ]
    out_specs = [ANY] * len(outs)
    out_specs[5] = whole(outs[5][0])
    return pl.pallas_call(
        first_body,
        in_specs=[ANY] * 6 + [whole(b.shape), whole(ln.shape), ANY],
        out_specs=out_specs,
        out_shape=[jax.ShapeDtypeStruct(shape, kind) for shape, kind in outs],
        scratch_shapes=[
            pltpu.VMEM((clips, 2, 4, rows, half), BF),
            pltpu.VMEM((2, rows, 2 * half), BF),
            pltpu.VMEM((clips, 3, 4 * rows, lanes), BF),
            pltpu.VMEM((clips, lanes, 4 * rows), F32),
            pltpu.VMEM((lanes + 16, 4 * rows), BF),
            pltpu.VMEM((clips, 4, rows, lanes), BF),
            pltpu.VMEM((4, width, 3 * lanes), BF),
            pltpu.VMEM((2, 4, rows, lanes), F32),
            pltpu.SemaphoreType.DMA((80,)),
            pltpu.SemaphoreType.DMA((80,)),
            pltpu.SemaphoreType.DMA((40,)),
        ],
        compiler_params=pltpu.CompilerParams(
            vmem_limit_bytes=VMEM_BYTES, collective_id=1, has_side_effects=True
        ),
        name="project_and_attend",
    )(x, cot, w_qkv, w_out, w_in, w_back, b, ln, b_out)


def chunk_of(shard, k):
    found = flip(shard, 2) if k & 2 else shard
    return flip(found, 1) if k & 1 else found


def side_by_side(parts):
    return jnp.concatenate(parts, axis=1)


def second_body(*refs):
    (x_ref, xp_ref, c_ref, cp_ref, mo_ref, mp_ref, wo_hbm, wi_hbm, wb_hbm, qkv_hbm, ot_hbm) = refs[:11]
    (ln_ref, bin_ref, bout_ref, boutp_ref, bback_ref, lse_ref) = refs[11:17]
    (y_out, other_out, arrived_out, gmid_out, d_out, keep_out, near_out, far_out, far_own_out, go_out) = refs[17:27]
    (dqt_out, dk_out, dv_out, midsum_out, insum_out, backsum_out) = refs[27:33]
    (xs, cs, ms, wo, wi, wb, mid, sec, act, gin, outs, ybuf, gs, gsr, gmid, gb, gm) = refs[33:50]
    (wg, wgnear, wgo, turned, ot, dqt, delta, dks, dvs, send_sems, recv_sems, local_sems) = refs[50:]
    clips, rows, half = x_ref.shape
    width = half // 2
    lanes = mo_ref.shape[3]
    hidden = wi.shape[3]
    shard, ctx, tp = place()
    mv = Movers(send_sems, recv_sems, local_sems)
    ks = range(4)
    own_k = [piece_at(shard, tp, 0, j) for j in range(2)]
    other_k = [piece_at(shard, tp, 1, j) for j in range(2)]

    def fetch(b):
        mixed = []
        if b == 0:
            mixed.append(mv.keep(mo_ref.at[0], ms.at[0, 0]))
            mixed.append(mv.keep(mp_ref.at[0], ms.at[0, 1]))
        return mixed + [
            mv.keep(x_ref.at[b], xs.at[b, 0]),
            mv.keep(xp_ref.at[b], xs.at[b, 1]),
            mv.keep(c_ref.at[b], cs.at[b, 0]),
            mv.keep(cp_ref.at[b], cs.at[b, 1]),
        ]

    got = [fetch(0)]
    got_wo = mv.keep(wo_hbm, wo)
    got_wi = [mv.keep(wi_hbm.at[m], wi.at[m]) for m in ks]
    got_wb = [mv.keep(wb_hbm.at[m], wb.at[m]) for m in ks]
    got.append(fetch(1))
    mv.barrier([X, CORE, Y, YCORE])
    mixed_in = {
        m: mv.send(mo_ref.at[1, m], ms.at[1, 0, m], name)
        for m, name in ((2, Y), (3, YCORE), (1, CORE))
    }
    got[1].append(mv.keep(mo_ref.at[1, 0], ms.at[1, 0, 0]))
    mixed_far = [mv.send(mo_ref.at[1, 0], ms.at[1, 1, 0], X)]

    def pass_on(m):
        mv.arrive(mixed_in[m])
        mixed_far.append(mv.send(ms.at[1, 0, m], ms.at[1, 1, m], X))

    def row(which, k):
        return ln_ref[pl.ds(4 * which + chunk_of(shard, k), 1), :]

    def statistics(b):
        total = 4 * width
        mean = sum(jnp.sum(mid[b, k], 1, keepdims=True) for k in ks) / total
        spread = sum(jnp.sum((mid[b, k] - mean) ** 2, 1, keepdims=True) for k in ks) / total
        return mean, lax.rsqrt(spread + EPSILON)

    y_put = []

    def block(b):
        mv.kept_done(*got[b])
        mv.kept_done(got_wo)
        if b == 1:
            mv.arrive(*mixed_far)
        mixed = side_by_side([ms[b, side, m] for side in range(2) for m in ks])
        for k in ks:
            weight = jnp.concatenate([wo[m, k, side] for side in range(2) for m in ks], axis=0)
            mid[b, k] = dot_nn(mixed, weight)
        for j in range(2):
            part = slice(j * width, (j + 1) * width)
            mid[b, own_k[j]] += xs[b, 0, :, part].astype(F32) + bout_ref[0:1, part].astype(F32)
            mid[b, other_k[j]] += xs[b, 1, :, part].astype(F32) + boutp_ref[0:1, part].astype(F32)
        mean, inv = statistics(b)
        for k in ks:
            sec[b, k] = ((mid[b, k] - mean) * inv * row(0, k) + row(1, k)).astype(BF)
        if b == 0:
            pass_on(1)
        for j in range(2):
            part = slice(j * width, (j + 1) * width)
            gb[b, own_k[j]] = cs[b, 0, :, part]
            gb[b, other_k[j]] = cs[b, 1, :, part]
        normed = side_by_side([sec[b, k] for k in ks])
        cot = side_by_side([gb[b, k] for k in ks])
        for m in ks:
            if b == 0 and m in (1, 2):
                pass_on(m + 1)
            mv.kept_done(got_wi[m])
            at = (ctx, flip(ctx, 1), flip(ctx, 2), flip(flip(ctx, 2), 1))[m]
            inner = bin_ref[pl.ds(at, 1), :] + dot_nn(normed, wi[m].reshape(4 * width, hidden))
            mv.kept_done(got_wb[m])
            grad = dot_nt(cot, side_by_side([wb[m, k] for k in ks]))
            phi = 0.5 + 0.5 * lax.erf(inner * (0.5**0.5))
            act[b, m] = (inner * phi).astype(BF)
            slope = phi + inner * (jnp.exp(-0.5 * inner * inner) * ((2 * math.pi) ** -0.5))
            grad = (grad * slope).astype(BF)
            gin[b, m] = grad
            sums = jnp.sum(grad.astype(F32), axis=0, keepdims=True)
            if b == 0:
                insum_out[pl.ds(at, 1), :] = sums
            else:
                insum_out[pl.ds(at, 1), :] += sums
        back = side_by_side([gin[b, m] for m in ks])
        sent = []
        for k in ks:
            gs[b, k] = dot_nt(back, side_by_side([wi[m, k] for m in ks])).astype(BF)
            sent.append(mv.send(gs.at[b, k], gsr.at[b, k], X))
        active = side_by_side([act[b, m] for m in ks])
        mv.kept_done(*y_put)
        for h, which in enumerate((own_k, other_k)):
            for j in range(2):
                weight = jnp.concatenate([wb[m, which[j]] for m in ks], axis=0)
                part = slice(j * width, (j + 1) * width)
                term = dot_nn(active, weight)
                if h == 0:
                    term = term + mid[b, own_k[j]] + bback_ref[0:1, part].astype(F32)
                    ybuf[:, part] = term
                else:
                    outs[b, :, part] = term.astype(BF)
        y_put.append(mv.keep(ybuf, y_out.at[b]))
        if b == 1:
            mv.keep(outs.at[1], other_out)
        return sent

    put = []

    def branch(b, sent):
        mv.arrive(*sent[:4])
        mv.kept_done(*put)
        total = 4 * width
        mean, inv = statistics(b)
        mean_one = mean_two = 0.0
        for k in ks:
            unit = (mid[b, k] - mean) * inv
            grad = gs[b, k].astype(F32) + gsr[b, k].astype(F32)
            gain_sum = jnp.sum(grad * unit, 0, keepdims=True)
            shift_sum = jnp.sum(grad, 0, keepdims=True)
            for i, term in enumerate((gain_sum, shift_sum)):
                place_row = pl.ds(4 * i + chunk_of(shard, k), 1)
                if b == 0:
                    midsum_out[place_row, :] = term
                else:
                    midsum_out[place_row, :] += term
            scaled = grad * row(0, k)
            mean_one = mean_one + jnp.sum(scaled, 1, keepdims=True)
            mean_two = mean_two + jnp.sum(scaled * unit, 1, keepdims=True)
        mean_one, mean_two = mean_one / total, mean_two / total
        for k in ks:
            unit = (mid[b, k] - mean) * inv
            grad = gs[b, k].astype(F32) + gsr[b, k].astype(F32)
            full = gb[b, k].astype(F32) + inv * (grad * row(0, k) - mean_one - unit * mean_two)
            gmid[k] = full
            low = full.astype(BF)
            xs[b, k // 2, :, (k % 2) * width : (k % 2 + 1) * width] = low
            sec_sum = jnp.sum(low.astype(F32), 0, keepdims=True)
            place_row = pl.ds(8 + chunk_of(shard, k), 1)
            if b == 0:
                midsum_out[place_row, :] = sec_sum
            else:
                midsum_out[place_row, :] += sec_sum
        low = side_by_side([xs[b, 0], xs[b, 1]])
        weight = side_by_side([jnp.concatenate([wo[m, k, 0] for m in ks], axis=0) for k in ks])
        mixed = dot_nt(low, weight).astype(BF)
        for m in ks:
            gm[b, m] = mixed[:, m * lanes : (m + 1) * lanes]
        remote = [mv.send(gm.at[b, 2], d_out.at[b, 2], Y)]
        remote.append(mv.send(gm.at[b, 3], d_out.at[b, 3], YCORE))
        remote.append(mv.send(gm.at[b, 1], d_out.at[b, 1], CORE))
        local = mv.keep(gm.at[b, 0], d_out.at[b, 0])
        for j in range(2):
            put.append(mv.keep(gmid.at[own_k[j]], gmid_out.at[b, j]))
        cot_sum = jnp.sum(cs[b, 0].astype(F32), 0, keepdims=True)
        if b == 0:
            backsum_out[...] = cot_sum
        else:
            backsum_out[...] += cot_sum
        return remote, local

    def tokens(ref, *at):
        return jnp.concatenate([ref[(b,) + at] for b in range(clips)], axis=0)

    def big_grads(m, slot):
        cot = side_by_side([tokens(gb, k) for k in ks])
        back = dot_tn(tokens(act, m), cot).astype(BF)
        own = dot_nn(turned[...], tokens(gin, m)).astype(BF)
        for k in ks:
            wg[slot, k, :hidden, :] = back[:, k * width : (k + 1) * width]
            wg[slot, k, hidden : hidden + width, :] = own[k * width : (k + 1) * width, :width]
            wg[slot, k, hidden + width :, :] = own[k * width : (k + 1) * width, width:]

    def held(kind, i):
        place_at = ((0, i, 0), (0, i, 1), (1, i, 0), (1, i, 1))
        m, k, side = place_at[kind]
        return wb.at[m, k, :, side * lanes : (side + 1) * lanes]

    def masked(kind, h, i):
        return wb.at[2 + kind, i, :, h * lanes : (h + 1) * lanes]

    heads = lanes // HEAD_DIM
    scale = HEAD_DIM ** (-0.5)

    def load_attention():
        for i in ks:
            part = slice(i * rows, (i + 1) * rows)
            attention_in.append(mv.keep(qkv_hbm.at[0, 1, part, :], held(0, i)))
            attention_in.append(mv.keep(qkv_hbm.at[0, 2, part, :], held(1, i)))
            attention_in.append(mv.keep(qkv_hbm.at[0, 0, part, :], held(2, i)))
        attention_in.append(mv.keep(ot_hbm.at[0], ot))

    attention_in = []

    def prepare(arrivals):
        remote, local = arrivals
        mv.arrive(*remote)
        mv.kept_done(local)
        mv.kept_done(*[mv.keep(d_out.at[0, i], held(3, i)) for i in ks])
        mv.kept_done(*attention_in)
        head = lax.broadcasted_iota(jnp.int32, (rows, lanes), 1) // HEAD_DIM
        for i in ks:
            part = slice(i * rows, (i + 1) * rows)
            q, grad = held(2, i)[...], held(3, i)[...]
            for h in range(heads):
                masked(0, h, i)[...] = jnp.where(head == h, q, jnp.zeros_like(q))
                masked(1, h, i)[...] = jnp.where(head == h, grad, jnp.zeros_like(grad))
            products = grad.astype(F32).T * ot[:, part]
            for h in range(heads):
                delta[h : h + 1, part] = jnp.sum(
                    products[h * HEAD_DIM : (h + 1) * HEAD_DIM], axis=0, keepdims=True
                )
        dqt[...] = jnp.zeros_like(dqt)

    attention_put = []

    def attend_back(m):
        keys, values = held(0, m)[...], held(1, m)[...]
        dk, dv = attend_back_block(
            keys,
            values,
            lambda h, i: masked(0, h, i)[...],
            lambda h, i: masked(1, h, i)[...],
            lambda h, part: lse_ref[0, h : h + 1, part],
            delta,
            dqt,
            rows,
        )
        if m >= 2:
            mv.kept_done(*attention_put[2 * m - 4 : 2 * m - 2])
        dks[m % 2] = dk * scale
        dvs[m % 2] = dv.astype(BF)
        attention_put.append(mv.keep(dks.at[m % 2], dk_out.at[m]))
        attention_put.append(mv.keep(dvs.at[m % 2], dv_out.at[m]))

    first = block(0)
    second = block(1)
    load_attention()
    for k in ks:
        turned[k * width : (k + 1) * width, :] = tokens(sec, k).T
    big_grads(3, 0)
    near = mv.send(wg.at[0], wgnear, CORE)
    big_grads(2, 1)
    mv.arrive(near)
    for k in ks:
        wg[1, k] = (wg[1, k].astype(F32) + wgnear[k].astype(F32)).astype(BF)
    arrivals = branch(0, first)
    prepare(arrivals)
    far = [mv.send(wg.at[1, k], far_out.at[k - 1], Y) for k in (1, 2)]
    far_own = [mv.keep(wg.at[1, k], far_own_out.at[i]) for i, k in enumerate((3, 0))]
    mv.send(outs.at[0], arrived_out, X)
    attend_back(0)
    attend_back(1)
    mv.wait_sent(near)
    big_grads(1, 0)
    mv.send(wg.at[0], near_out, CORE)
    attend_back(2)
    attend_back(3)
    mv.keep(dqt, dqt_out)
    branch(1, second)
    grads = side_by_side([tokens(xs, i) for i in range(2)])
    for m in ks:
        mixed = jnp.concatenate([ms[b, 0, m] for b in range(clips)], axis=0)
        out = dot_tn(mixed, grads).astype(BF)
        for k in ks:
            wgo[m, k] = out[:, k * width : (k + 1) * width]
    mv.keep(wgo, go_out)
    mv.wait_sent(*far)
    mv.kept_done(*far_own)
    big_grads(0, 1)
    mv.keep(wg.at[1], keep_out)
    mv.finish()


def attend_back_block(keys, values, query, grad_out, log_total, delta, dqt, rows):
    scale = HEAD_DIM ** (-0.5)
    flat_keys = keys.T
    row = lax.broadcasted_iota(jnp.int32, flat_keys.shape, 0) // HEAD_DIM
    dk = dv = None
    for h in range(keys.shape[1] // HEAD_DIM):
        turned = jnp.where(row == h, flat_keys, jnp.zeros_like(flat_keys))
        for i in range(4):
            part = slice(i * rows, (i + 1) * rows)
            q, grad = query(h, i), grad_out(h, i)
            probs = jnp.exp2(dot_nt(keys, q) * (scale * LOG2E) - log_total(h, part))
            slope = (probs * (dot_nt(values, grad) - delta[h : h + 1, part])).astype(BF)
            value_term, key_term = dot_nn(probs.astype(BF), grad), dot_nn(slope, q)
            dk = key_term if dk is None else dk + key_term
            dv = value_term if dv is None else dv + value_term
            dqt[:, part] += dot_nn(turned, slope)
    return dk, dv


def second_call(x, xp, c, cp, mo, mp, wo, wi, wb, qkv, ot, ln, b_in, b_out, b_other, b_back, lse):
    clips, rows, half = x.shape
    width = half // 2
    lanes = mo.shape[3]
    hidden = wi.shape[3]
    tall = hidden + 2 * width
    heads = lanes // HEAD_DIM
    outs = [
        ((clips, rows, half), F32),
        ((rows, half), BF),
        ((rows, half), BF),
        ((clips, 2, rows, width), F32),
        ((clips, 4, rows, lanes), BF),
        ((4, tall, width), BF),
        ((4, tall, width), BF),
        ((2, tall, width), BF),
        ((2, tall, width), BF),
        ((4, 4, lanes, width), BF),
        ((lanes, 4 * rows), F32),
        ((4, rows, lanes), F32),
        ((4, rows, lanes), BF),
        ((12, width), F32),
        ((4, hidden), F32),
        ((1, half), F32),
    ]
    small = [ln, b_in, b_out, b_other, b_back, lse]
    vmem = lambda kind, *shape: pltpu.VMEM(shape, kind)
    return pl.pallas_call(
        second_body,
        in_specs=[ANY] * 11 + [whole(a.shape) for a in small],
        out_specs=[ANY] * 13 + [whole(o[0]) for o in outs[13:]],
        out_shape=[jax.ShapeDtypeStruct(shape, kind) for shape, kind in outs],
        scratch_shapes=[
            vmem(BF, clips, 2, rows, half),
            vmem(BF, clips, 2, rows, half),
            vmem(BF, clips, 2, 4, rows, lanes),
            vmem(BF, *wo.shape),
            vmem(BF, *wi.shape),
            vmem(BF, *wb.shape),
            vmem(F32, clips, 4, rows, width),
            vmem(BF, clips, 4, rows, width),
            vmem(BF, clips, 4, rows, hidden),
            vmem(BF, clips, 4, rows, hidden),
            vmem(BF, clips, rows, half),
            vmem(F32, rows, half),
            vmem(BF, clips, 4, rows, width),
            vmem(BF, clips, 4, rows, width),
            vmem(F32, 4, rows, width),
            vmem(BF, clips, 4, rows, width),
            vmem(BF, clips, 4, rows, lanes),
            vmem(BF, 2, 4, tall, width),
            vmem(BF, 4, tall, width),
            vmem(BF, 4, 4, lanes, width),
            vmem(BF, 4 * width, clips * rows),
            vmem(F32, lanes, 4 * rows),
            vmem(F32, lanes, 4 * rows),
            vmem(F32, heads, 4 * rows),
            vmem(F32, 2, rows, lanes),
            vmem(BF, 2, rows, lanes),
            pltpu.SemaphoreType.DMA((32,)),
            pltpu.SemaphoreType.DMA((32,)),
            pltpu.SemaphoreType.DMA((72,)),
        ],
        compiler_params=pltpu.CompilerParams(
            vmem_limit_bytes=VMEM_BYTES, collective_id=2, has_side_effects=True
        ),
        name="layer_middle",
    )(x, xp, c, cp, mo, mp, wo, wi, wb, qkv, ot, *small)


def third_body(*refs):
    (qkv_hbm, ot_hbm, d_hbm, t_hbm, wq_hbm, n_hbm, keep_hbm, near_hbm, far_hbm, far_own) = refs[:10]
    (go_hbm, dqt_hbm, dk_hbm, dv_hbm, other_hbm, x_hbm, xp_hbm) = refs[10:17]
    (lse_ref, ln_ref, midsum_ref, insum_ref, backsum_ref) = refs[17:22]
    (ig_out, arrived_out, dense_out, qdense_out, early_out, ln1_out, qsum_out) = refs[22:29]
    (qkv, ot, d, tables, wq, qh, dh, delta, dqt, gj, pk, ps, near, hop, last) = refs[29:44]
    (nbuf, qacc, qs, qz, gk, gnear, gfar, gz, go, gonear, dk0, dqt0, xs, stats) = refs[44:58]
    (stats_in, early, early_in, late, late_in, late_x, send_sems, recv_sems, local_sems) = refs[58:]
    unused, count, lanes = qkv.shape
    clips = x_hbm.shape[0]
    rows = count // 4
    width = wq.shape[1]
    half = 2 * width
    heads = lanes // HEAD_DIM
    cut = rows // 2
    shard, ctx, tp = place()
    mv = Movers(send_sems, recv_sems, local_sems)
    ks = range(4)
    zs = (Z1, Z2, Z3)
    scale = HEAD_DIM ** (-0.5)

    tall = keep_hbm.shape[1]
    got_first = [
        mv.keep(dqt_hbm, dqt0),
        mv.keep(dk_hbm, dk0),
        mv.keep(dv_hbm, gj.at[0, :, :, 2 * lanes :]),
    ]
    got_w = [mv.keep(t_hbm, tables), mv.keep(wq_hbm, wq)]
    got_g = [
        [mv.keep(keep_hbm.at[k], gk.at[k, :tall]), mv.keep(near_hbm.at[k], gnear.at[k])]
        for k in (1, 2, 3, 0)
    ]
    for at in range(2):
        got_g[at].append(mv.keep(far_hbm.at[at], gfar.at[at + 1]))
    got_go = [mv.keep(go_hbm.at[2 * i], go.at[i]) for i in range(2)]
    got = [
        mv.keep(qkv_hbm.at[1], qkv),
        mv.keep(d_hbm.at[1], d),
        mv.keep(ot_hbm.at[1], ot),
    ]
    got_n = [mv.keep(n_hbm.at[0, m], nbuf.at[m]) for m in range(2)]
    got_x = [mv.keep(x_hbm, xs.at[0]), mv.keep(xp_hbm, xs.at[1])]
    mv.barrier([X, CORE, Y, YCORE, Z1, Z2, Z3])
    far_late = [mv.send(far_own.at[0], gfar.at[3], Y)]
    go_core = [mv.send(go_hbm.at[2 * i + 1], gonear.at[i], CORE) for i in range(2)]

    early[0, :12, :] = midsum_ref[...]
    for m in ks:
        for j in range(2):
            part = slice(j * width, (j + 1) * width)
            early[0, 12 + 2 * m + j : 13 + 2 * m + j, :] = insum_ref[m : m + 1, part]
    for j in range(2):
        early[0, 20 + j : 21 + j, :] = backsum_ref[:, j * width : (j + 1) * width]
    early[0, 22:, :] = jnp.zeros((2, width), F32)
    early_z = [mv.send(early.at[0], early_in.at[i], name) for i, name in enumerate(zs)]

    def prepare():
        mv.kept_done(*got)
        head = lax.broadcasted_iota(jnp.int32, (rows, lanes), 1) // HEAD_DIM
        for m in ks:
            part = slice(m * rows, (m + 1) * rows)
            q, grad = qkv[0, part, :], d[m]
            for h in range(heads):
                qh[h, part, :] = jnp.where(head == h, q, jnp.zeros_like(q))
                dh[h, part, :] = jnp.where(head == h, grad, jnp.zeros_like(grad))
            products = grad.astype(F32).T * ot[:, part]
            for h in range(heads):
                delta[h : h + 1, part] = jnp.sum(
                    products[h * HEAD_DIM : (h + 1) * HEAD_DIM], axis=0, keepdims=True
                )
        dqt[...] = jnp.zeros_like(dqt)

    def attend_back(m):
        mine = slice(m * rows, (m + 1) * rows)
        dk, dv = attend_back_block(
            qkv[1, mine, :],
            qkv[2, mine, :],
            lambda h, i: qh[h, i * rows : (i + 1) * rows, :],
            lambda h, i: dh[h, i * rows : (i + 1) * rows, :],
            lambda h, part: lse_ref[1, h : h + 1, part],
            delta,
            dqt,
            rows,
        )
        dk = dk * scale
        dk = dk * tables[0, m] + partner_lanes(dk * tables[1, m])
        gj[1, m, :, lanes : 2 * lanes] = dk.astype(BF)
        gj[1, m, :, 2 * lanes :] = dv.astype(BF)

    sums = [0.0, 0.0, 0.0]

    def join(b):
        mv.kept_done(*got_w, *got_first)
        sent = {}
        for m in (3, 2, 1, 0):
            part = slice(m * rows, (m + 1) * rows)
            dq = ((dqt0, dqt)[b][:, part] * scale).T
            if b == 0:
                dk = dk0[m]
                dk = dk * tables[0, m] + partner_lanes(dk * tables[1, m])
                gj[0, m, :, lanes : 2 * lanes] = dk.astype(BF)
            dq = dq * tables[0, m] + partner_lanes(dq * tables[1, m])
            gj[b, m, :, :lanes] = dq.astype(BF)
            for i in range(3):
                low = gj[b, m, :, i * lanes : (i + 1) * lanes].astype(F32)
                sums[i] = sums[i] + jnp.sum(low, axis=0, keepdims=True)
            for h in (1, 0):
                target = (pk, ps)[m % 2]
                for j in range(2):
                    term = dot_nt(gj[b, m], wq[piece_at(shard, tp, h, j)])
                    target[b, m // 2, h, :, j * width : (j + 1) * width] = term.astype(BF)
                if m % 2:
                    sent[m // 2, h] = mv.send(ps.at[b, m // 2, h], near.at[b, m // 2, h], CORE)
            if m == 2:
                hops = first_hop(b, sent)
        return sent, hops

    def first_hop(b, sent):
        mv.arrive(sent[1, 1])
        pk[b, 1, 1] = (pk[b, 1, 1].astype(F32) + near[b, 1, 1].astype(F32)).astype(BF)
        low = mv.send(pk.at[b, 1, 1, :cut], hop.at[b, 0], X)
        high = mv.send(pk.at[b, 1, 1, cut:], hop.at[b, 1], Y)
        return low, high

    def second_hop(b, sent, hops):
        mv.arrive(sent[1, 0], sent[0, 1])
        mv.arrive(hops[0])
        pk[b, 1, 0, :cut] = (
            pk[b, 1, 0, :cut].astype(F32)
            + near[b, 1, 0, :cut].astype(F32)
            + hop[b, 0].astype(F32)
        ).astype(BF)
        pk[b, 1, 0, cut:] = (
            pk[b, 1, 0, cut:].astype(F32) + near[b, 1, 0, cut:].astype(F32)
        ).astype(BF)
        far = mv.send(pk.at[b, 1, 0], last.at[b, 0], Y)
        mv.arrive(hops[1])
        pk[b, 0, 1, :cut] = (
            pk[b, 0, 1, :cut].astype(F32) + near[b, 0, 1, :cut].astype(F32)
        ).astype(BF)
        pk[b, 0, 1, cut:] = (
            pk[b, 0, 1, cut:].astype(F32)
            + near[b, 0, 1, cut:].astype(F32)
            + hop[b, 1].astype(F32)
        ).astype(BF)
        other = mv.send(pk.at[b, 0, 1], last.at[b, 1], X)
        return far, other

    def norm_one(b):
        mv.kept_done(*got_x)
        own, unused, inv = norm_parts(xs[0, b].astype(F32), xs[1, b].astype(F32))
        return own, inv

    gains = [0.0, 0.0]
    gain_own = jnp.where(tp == 0, ln_ref[:, :half], ln_ref[:, half:])

    def finish_sum(b, sent, lasts):
        mv.arrive(sent[0, 0], *lasts)
        own, inv = norm_one(b)
        grad = (
            pk[b, 0, 0].astype(F32)
            + near[b, 0, 0].astype(F32)
            + last[b, 0].astype(F32)
            + last[b, 1].astype(F32)
        )
        gains[0] = gains[0] + jnp.sum(grad * own, axis=0, keepdims=True)
        gains[1] = gains[1] + jnp.sum(grad, axis=0, keepdims=True)
        scaled = grad * gain_own
        ig_out[b] = scaled
        lane = lax.broadcasted_iota(jnp.int32, (rows, 128), 1)
        both = jnp.where(
            lane == 0,
            jnp.sum(scaled, 1, keepdims=True),
            jnp.where(lane == 1, jnp.sum(scaled * own, 1, keepdims=True), 0.0),
        )
        stats[b] = both.T[:8]
        return mv.send(stats.at[b], stats_in.at[b], X)

    def finish_grad(b, sent):
        mv.arrive(sent)
        own, inv = norm_one(b)
        total = stats[b] + stats_in[b]
        both = jnp.concatenate([total, jnp.zeros((120, rows), F32)], axis=0).T / (2 * half)
        grad = inv * (ig_out[b] - both[:, 0:1] - own * both[:, 1:2])
        ig_out[b] = grad

    def qkv_grads(b):
        for m in ks:
            at = 4 * b + m
            mv.kept_done(got_n[at])
            slot = at % 2
            for h, j in CHUNKS:
                cols = slice((2 * h + j) * width, (2 * h + j + 1) * width)
                term = dot_tn(nbuf[slot, :, cols], gj[b, m])
                if at == 0:
                    qacc[2 * h + j] = term
                else:
                    qacc[2 * h + j] += term
            if at + 2 < 8:
                got_n.append(mv.keep(n_hbm.at[(at + 2) // 4, (at + 2) % 4], nbuf.at[slot]))

    def add_far():
        mv.arrive(*go_core)
        mv.kept_done(*got_go)
        go[1] = (go[1].astype(F32) + gonear[1].astype(F32)).astype(BF)
        return mv.send(go.at[1], gonear.at[2], Y)

    def shard_send(at):
        k = (1, 2, 3, 0)[at]
        mv.kept_done(*got_g[at])
        if at >= 2:
            mv.arrive(far_late[at - 2])
        gk[k, :tall] = (
            gk[k, :tall].astype(F32) + gnear[k].astype(F32) + gfar[k].astype(F32)
        ).astype(BF)
        return [mv.send(gk.at[k, :tall], gz.at[k - 1, :tall], zs[k - 1])] if k else []

    def shard_sends_out(far):
        mv.arrive(far)
        sent = []
        for k in (1, 2, 3, 0):
            gk[k, tall:] = (
                go[0, k].astype(F32) + gonear[0, k].astype(F32) + gonear[2, k].astype(F32)
            ).astype(BF)
            if k:
                sent.append(mv.send(gk.at[k, tall:], gz.at[k - 1, tall:], zs[k - 1]))
        return sent

    def spread_far(ref):
        return mv.send(ref.at[ctx], ref.at[ctx], Y), mv.send(ref.at[ctx], ref.at[ctx], CORE)

    def spread_near(ref, far):
        mv.arrive(far[0])
        mv.send(ref.at[flip(ctx, 2)], ref.at[flip(ctx, 2)], CORE)

    gz_sent = shard_send(0) + shard_send(1)
    sent0, hops0 = join(0)
    prepare()
    attend_back(0)
    go_far = add_far()
    gz_sent += shard_send(2)
    lasts0 = second_hop(0, sent0, hops0)
    far_late.append(mv.send(far_own.at[1], gfar.at[0], Y))
    arrived = mv.send(other_hbm, arrived_out, X)
    attend_back(1)
    gz_sent += shard_sends_out(go_far)
    mv.arrive(*early_z)
    early[1] = early[0] + early_in[0] + early_in[1] + early_in[2]
    qkv_grads(0)
    attend_back(2)
    stats0 = finish_sum(0, sent0, lasts0)
    attend_back(3)
    sent1, hops1 = join(1)
    qkv_grads(1)
    for h, j in CHUNKS:
        qs[piece_at(shard, tp, h, j)] = qacc[2 * h + j].astype(BF)
    q_sent = [mv.send(qs.at[k + 1], qz.at[k], name) for k, name in enumerate(zs)]
    lasts1 = second_hop(1, sent1, hops1)
    shard_send(3)
    mv.arrive(*gz_sent)
    for part in (slice(0, tall), slice(tall, gz.shape[1])):
        gk[0, part] = (
            gk[0, part].astype(F32)
            + gz[0, part].astype(F32)
            + gz[1, part].astype(F32)
            + gz[2, part].astype(F32)
        ).astype(BF)
    placed = mv.keep(gk.at[0], dense_out.at[ctx])
    finish_grad(0, stats0)
    mv.kept_done(placed)
    dense_far = spread_far(dense_out)
    stats1 = finish_sum(1, sent1, lasts1)
    late[...] = jnp.zeros_like(late)
    for i in range(2):
        for j in range(4):
            late[4 * i + j : 4 * i + j + 1, :] = gains[i][:, j * 128 : (j + 1) * 128]
    for i in range(3):
        late[pl.ds(8 + 3 * ctx + i, 1), :] = sums[i]
    late_z = [mv.send(late, late_in.at[i], name) for i, name in enumerate(zs)]
    finish_grad(1, stats1)
    mv.arrive(*late_z)
    late_x[0] = late[...] + late_in[0] + late_in[1] + late_in[2]
    others = (CORE, Y, YCORE)
    late_c = [mv.send(late_x.at[0], late_in.at[3 + i], name) for i, name in enumerate(others)]
    mv.arrive(*q_sent)
    qs[0] = sum((qz[i].astype(F32) for i in range(3)), qs[0].astype(F32)).astype(BF)
    q_placed = mv.keep(qs.at[0], qdense_out.at[ctx])
    mv.kept_done(q_placed)
    q_far = spread_far(qdense_out)
    early_x = [mv.send(early.at[1], early_in.at[3 + i], name) for i, name in enumerate(others)]
    mv.arrive(*late_c)
    late_x[1] = late_x[0] + late_in[3] + late_in[4] + late_in[5]
    crossed = mv.send(late_x.at[1], late_x.at[2], X)
    mv.arrive(*early_x)
    early_out[...] = early[1] + early_in[3] + early_in[4] + early_in[5]
    qsum_out[...] = late_x[1, 8:20, :]
    spread_near(dense_out, dense_far)
    spread_near(qdense_out, q_far)
    mv.arrive(crossed)
    for i in range(2):
        part = slice(4 * i, 4 * i + 4)
        ln1_out[i, pl.ds(4 * tp, 4), :] = late_x[1, part, :]
        ln1_out[i, pl.ds(4 * (1 - tp), 4), :] = late_x[2, part, :]
    mv.finish()


def third_call(
    qkv, ot, d, tables, wq, normed, keep, near, far, own, go, dqt, dk, dv, other, x, xp, *small
):
    unused, unused, count, lanes = qkv.shape
    clips, rows, half = x.shape
    width = half // 2
    tall = keep.shape[1]
    heads = lanes // HEAD_DIM
    outs = [
        ((clips, rows, half), F32),
        ((rows, half), BF),
        ((4, tall + lanes, width), BF),
        ((4, width, 3 * lanes), BF),
        ((24, width), F32),
        ((2, 8, 128), F32),
        ((12, lanes), F32),
    ]
    vmem = lambda kind, *shape: pltpu.VMEM(shape, kind)
    return pl.pallas_call(
        third_body,
        in_specs=[ANY] * 17 + [whole(a.shape) for a in small],
        out_specs=[whole(outs[0][0]), ANY, ANY, ANY] + [whole(o[0]) for o in outs[4:]],
        out_shape=[jax.ShapeDtypeStruct(shape, kind) for shape, kind in outs],
        scratch_shapes=[
            vmem(BF, *qkv.shape[1:]),
            vmem(F32, *ot.shape[1:]),
            vmem(BF, *d.shape[1:]),
            vmem(F32, *tables.shape),
            vmem(BF, *wq.shape),
            vmem(BF, heads, count, lanes),
            vmem(BF, heads, count, lanes),
            vmem(F32, heads, count),
            vmem(F32, lanes, count),
            vmem(BF, clips, 4, rows, 3 * lanes),
            vmem(BF, clips, 2, 2, rows, half),
            vmem(BF, clips, 2, 2, rows, half),
            vmem(BF, clips, 2, 2, rows, half),
            vmem(BF, clips, 2, rows // 2, half),
            vmem(BF, clips, 2, rows, half),
            vmem(BF, 2, rows, 2 * half),
            vmem(F32, 4, width, 3 * lanes),
            vmem(BF, *wq.shape),
            vmem(BF, 3, width, 3 * lanes),
            vmem(BF, 4, tall + lanes, width),
            vmem(BF, 4, tall, width),
            vmem(BF, 4, tall, width),
            vmem(BF, 3, tall + lanes, width),
            vmem(BF, 2, 4, lanes, width),
            vmem(BF, 3, 4, lanes, width),
            vmem(F32, *dk.shape),
            vmem(F32, *dqt.shape),
            vmem(BF, 2, clips, rows, half),
            vmem(F32, clips, 8, rows),
            vmem(F32, clips, 8, rows),
            vmem(F32, 2, 24, width),
            vmem(F32, 6, 24, width),
            vmem(F32, 24, 128),
            vmem(F32, 6, 24, 128),
            vmem(F32, 3, 24, 128),
            pltpu.SemaphoreType.DMA((64,)),
            pltpu.SemaphoreType.DMA((64,)),
            pltpu.SemaphoreType.DMA((48,)),
        ],
        compiler_params=pltpu.CompilerParams(
            vmem_limit_bytes=VMEM_BYTES, collective_id=3, has_side_effects=True
        ),
        name="layer_back",
    )(qkv, ot, d, tables, wq, normed, keep, near, far, own, go, dqt, dk, dv, other, x, xp, *small)


def fourth_body(
    dense_ref, q_ref, y_ref, far_ref, ig_ref, mid_ref, other_ref, wb_ref, wi_ref, wo_ref, wq_ref, yo_ref, go_ref
):
    width = q_ref.shape[1]
    hidden = wb_ref.shape[0]
    lanes = wo_ref.shape[0]
    wb_ref[...] = dense_ref[0, :hidden, :].astype(F32)
    for j in range(2):
        at = hidden + j * width
        wi_ref[:, j * width : (j + 1) * width] = dense_ref[0, at : at + width, :].astype(F32)
    wo_ref[...] = dense_ref[0, hidden + 2 * width :, :].astype(F32)
    for i in range(3):
        wq_ref[i] = q_ref[0, :, i * lanes : (i + 1) * lanes].astype(F32)
    for b, ref in enumerate((far_ref, other_ref)):
        yo_ref[b] = (y_ref[b] + ref[...].astype(F32)).astype(BF)
    for j in range(2):
        part = slice(j * width, (j + 1) * width)
        go_ref[:, :, part] = ig_ref[:, :, part] + mid_ref[:, j]


def fourth_call(dense, qkv_dense, y, arrived, input_part, mids):
    four, tall, width = dense.shape
    lanes = qkv_dense.shape[2] // 3
    hidden = tall - 2 * width - lanes
    clips, rows, half = y.shape
    one = pl.BlockSpec((rows // four, half), lambda a: (a, 0))
    some = pl.BlockSpec((clips, rows // four, half), lambda a: (0, a, 0))
    return pl.pallas_call(
        fourth_body,
        grid=(four,),
        in_specs=[
            pl.BlockSpec((1, tall, width), lambda a: (a, 0, 0)),
            pl.BlockSpec((1, width, 3 * lanes), lambda a: (a, 0, 0)),
            some,
            one,
            some,
            pl.BlockSpec((clips, 2, rows // four, width), lambda a: (0, 0, a, 0)),
            one,
        ],
        out_specs=[
            pl.BlockSpec((hidden, width), lambda a: (a, 0)),
            pl.BlockSpec((width, hidden), lambda a: (0, a)),
            pl.BlockSpec((lanes, width), lambda a: (a, 0)),
            pl.BlockSpec((3, width, lanes), lambda a: (0, 0, a)),
            some,
            some,
        ],
        out_shape=[
            jax.ShapeDtypeStruct((four * hidden, width), F32),
            jax.ShapeDtypeStruct((width, four * hidden), F32),
            jax.ShapeDtypeStruct((four * lanes, width), F32),
            jax.ShapeDtypeStruct((3, width, four * lanes), F32),
            jax.ShapeDtypeStruct(y.shape, BF),
            jax.ShapeDtypeStruct(y.shape, F32),
        ],
        compiler_params=pltpu.CompilerParams(vmem_limit_bytes=VMEM_BYTES),
        name="owned_gradients",
    )(dense, qkv_dense, y, arrived[0], input_part, mids, arrived[1])


def fast_device(
    inputs,
    ln1_gain,
    ln1_bias,
    w_qkv,
    b_qkv,
    w_out,
    b_out,
    ln2_gain,
    ln2_bias,
    w_in,
    b_in,
    w_back,
    b_back,
    cotangent,
):
    clips, rows, half = inputs.shape
    width = half // 2
    lanes = half // 4
    hidden = w_in.shape[1] // 4
    shard, ctx, tp = (lax.axis_index(name) for name in ("shard", "ctx", "tp"))
    ids = jnp.stack([shard, ctx, tp]).astype(jnp.int32)
    def halves(vector):
        vector = vector.astype(F32)
        return jnp.concatenate(
            [
                lax.dynamic_slice_in_dim(vector, tp * half, half),
                lax.dynamic_slice_in_dim(vector, (1 - tp) * half, half),
            ]
        )

    ln_qkv = jnp.stack([halves(ln1_gain), halves(ln1_bias)])
    bias_qkv = (
        lax.dynamic_slice_in_dim(b_qkv, ctx * lanes, lanes, axis=1)
        .reshape(1, 3 * lanes)
        .astype(F32)
    )
    bias_in = b_in.reshape(4, hidden).astype(F32)

    xp, cp, normed, qkv, ot, lse, mo, mp, wq, wo, wi, wb, bias_other, tables = first_call(
        inputs,
        cotangent,
        jnp.transpose(w_qkv, (1, 0, 2)),
        w_out,
        w_in,
        w_back,
        bias_qkv,
        ln_qkv,
        jnp.broadcast_to(b_out, (16, half)),
    )
    ln_two = jnp.concatenate([ln2_gain, ln2_bias]).astype(F32).reshape(8, width)
    middle = second_call(
        inputs,
        xp,
        cotangent,
        cp,
        mo,
        mp,
        wo,
        wi,
        wb,
        qkv,
        ot,
        ln_two,
        bias_in,
        b_out.reshape(1, half),
        bias_other,
        b_back.reshape(1, half),
        lse,
    )
    y, other, arrived, mids, grad_heads, keep, near, far, far_own, grads_out, dqt, dk, dv = middle[:13]
    input_part, arrived_late, dense, qkv_dense, early, grad_ln1, q_sums = third_call(
        qkv,
        ot,
        grad_heads,
        tables,
        wq,
        normed,
        keep,
        near,
        far,
        far_own,
        grads_out,
        dqt,
        dk,
        dv,
        other,
        inputs,
        xp,
        lse,
        ln1_gain.astype(F32).reshape(1, 2 * half),
        *middle[13:],
    )
    mid_total = early[:12].reshape(3, 2 * half)
    grad_b_out = lax.dynamic_slice_in_dim(mid_total[2], tp * half, half)
    grad_b_in = early[12:20].reshape(4 * hidden)
    grad_b_back = early[20:22].reshape(half)
    grad_b_qkv = q_sums.reshape(4, 3, lanes).transpose(1, 0, 2).reshape(3, 4 * lanes)
    grad_w_back, grad_w_in, grad_w_out, grad_w_qkv, output, input_grad = fourth_call(
        dense, qkv_dense, y, (arrived, arrived_late), input_part, mids
    )
    grad_w_qkv = jnp.transpose(grad_w_qkv, (1, 0, 2))
    return (
        output,
        input_grad,
        grad_ln1[0].reshape(2 * half),
        grad_ln1[1].reshape(2 * half),
        grad_w_qkv,
        grad_b_qkv,
        grad_w_out,
        grad_b_out,
        mid_total[0],
        mid_total[1],
        grad_w_in,
        grad_b_in,
        grad_w_back,
        grad_b_back,
    )


def quick_form_fits(mesh):
    return (mesh.shape["shard"], mesh.shape["ctx"], mesh.shape["tp"]) == (4, 4, 2)


def solution(mesh):
    placed = (
        P("shard", "ctx", "tp"),
        P(),
        P(),
        P("shard", None, "tp"),
        P(None, "tp"),
        P("tp", "shard"),
        P("tp"),
        P(),
        P(),
        P("shard", "tp"),
        P("tp"),
        P("tp", "shard"),
        P("tp"),
        P("shard", "ctx", "tp"),
    )
    return jax.shard_map(
        fast_device if quick_form_fits(mesh) else per_device,
        mesh=mesh,
        in_specs=placed,
        out_specs=(
            P("shard", "ctx", "tp"),
            P("shard", "ctx", "tp"),
            P(),
            P(),
            P("shard", None, "tp"),
            P(None, "tp"),
            P("tp", "shard"),
            P("tp"),
            P(),
            P(),
            P("shard", "tp"),
            P("tp"),
            P("tp", "shard"),
            P("tp"),
        ),
        check_vma=False,
    )
```
